32 devices in a mesh: dp: 8 (over z, y), band: 4 (over x, core).
Axes of the slice: x: 2, y: 2, z: 4, core: 2. Of those that a mesh axis runs over, the one named last changes fastest.
Arguments:
- kept_tokens: bfloat16 [32, 512, 1152], P('dp', 'band'), may hold values from -6 to 6
- kept_index: int32 [32, 512], P('dp', 'band'), may hold values from 0 to 1023, as said below
- resolution: int32 [32], P('dp'), may hold values from 0 to 1, as said below
- labels: int32 [32, 4], P('dp'), may hold values from 0 to 999
- timesteps: int32 [32, 4], P('dp'), may hold values from 0 to 999
- class_table: float32 [1000, 1152], replicated, may hold values from -6 to 6
- cotangent: bfloat16 [32, 1024, 1152], P('dp', 'band')
- mask_token: float32 [1152], replicated, may hold values from -0.6 to 0.6
- w_qkv: float32 [1152, 3456], P('band', 'dp'), may hold values from -0.1875 to 0.1875
- w_proj: float32 [1152, 1152], P('band', 'dp'), may hold values from -0.75 to 0.75
- w_fc1: float32 [1152, 4608], P('band', 'dp'), may hold values from -0.1875 to 0.1875
- w_fc2: float32 [4608, 1152], P('band', 'dp'), may hold values from -0.09375 to 0.09375
- w_ada: float32 [1152, 6912], P('band', 'dp'), may hold values from -0.1875 to 0.1875
- mask_first: float32 [1152], replicated, may hold values from -0.00012207031 to 0.00012207031
- first_qkv: float32 [1152, 3456], P('band', 'dp'), may hold values from -0.00012207031 to 0.00012207031
- first_proj: float32 [1152, 1152], P('band', 'dp'), may hold values from -0.00012207031 to 0.00012207031
- first_fc1: float32 [1152, 4608], P('band', 'dp'), may hold values from -0.00012207031 to 0.00012207031
- first_fc2: float32 [4608, 1152], P('band', 'dp'), may hold values from -0.00012207031 to 0.00012207031
- first_ada: float32 [1152, 6912], P('band', 'dp'), may hold values from -0.00012207031 to 0.00012207031
- mask_second: float32 [1152], replicated, may hold values from 2.0931124e-09 to 8.372449e-09
- second_qkv: float32 [1152, 3456], P('band', 'dp'), may hold values from 2.0931124e-09 to 8.372449e-09
- second_proj: float32 [1152, 1152], P('band', 'dp'), may hold values from 2.0931124e-09 to 8.372449e-09
- second_fc1: float32 [1152, 4608], P('band', 'dp'), may hold values from 2.5117347e-10 to 1.0046939e-09
- second_fc2: float32 [4608, 1152], P('band', 'dp'), may hold values from 2.0931124e-09 to 8.372449e-09
- second_ada: float32 [1152, 6912], P('band', 'dp'), may hold values from 2.0931124e-09 to 8.372449e-09
Outputs:
- block_out: bfloat16 [32, 1024, 1152], P('dp', 'band')
- kept_grad: float32 [32, 512, 1152], P('dp', 'band')
- grad_norm: float32 [], replicated
- new_mask: float32 [1152], replicated
- new_qkv: float32 [1152, 3456], P('band', 'dp')
- new_proj: float32 [1152, 1152], P('band', 'dp')
- new_fc1: float32 [1152, 4608], P('band', 'dp')
- new_fc2: float32 [4608, 1152], P('band', 'dp')
- new_ada: float32 [1152, 6912], P('band', 'dp')
- new_mask_first: float32 [1152], replicated
- new_first_qkv: float32 [1152, 3456], P('band', 'dp')
- new_first_proj: float32 [1152, 1152], P('band', 'dp')
- new_first_fc1: float32 [1152, 4608], P('band', 'dp')
- new_first_fc2: float32 [4608, 1152], P('band', 'dp')
- new_first_ada: float32 [1152, 6912], P('band', 'dp')
- new_mask_second: float32 [1152], replicated
- new_second_qkv: float32 [1152, 3456], P('band', 'dp')
- new_second_proj: float32 [1152, 1152], P('band', 'dp')
- new_second_fc1: float32 [1152, 4608], P('band', 'dp')
- new_second_fc2: float32 [4608, 1152], P('band', 'dp')
- new_second_ada: float32 [1152, 6912], P('band', 'dp')
The draws below stay inside these ranges and needn't reach their ends.
Inputs may be any that keep to these rules, and one draw needn't show every extreme that they name: Each group of 4 consecutive slots holds at least one slot of resolution 0, which one drawn from the seed. `kept_index`: within a slot the entries are distinct positions; a slot of resolution 1 keeps exactly half of the positions of each of its four regions of 256 positions. `labels`: in a slot of resolution 0 only the first column is read. `timesteps`: in a slot of resolution 0 only the first column is read.
All inputs are finite; a program needn't handle non-finite values.
Results may differ from the reference program's by a relative error of at most 0.023.
Values may be sent and summed in bfloat16 or wider, within the bound.
A program may use at most 384 MiB of HBM per device.

```python
import math
import jax
import jax.numpy as jnp
from jax import lax

D = 1152
HEADS = 16
HEAD_DIM = 72
FF = 4608
CLASSES = 1000
SIDE = 32
SLOTS_DEV = 4
STEP = 10
GRID = 1024
KEEP = 512
REGION = 256
SLOTS = 32


def slot_kinds_of(key):
    base_key = jax.random.fold_in(key, 11)
    first_key, second_key = jax.random.split(base_key)
    smaller = jax.random.randint(first_key, (SLOTS,), 0, 3) == 0
    chosen = jax.random.randint(second_key, (SLOTS // SLOTS_DEV, 1), 0, SLOTS_DEV)
    forced = (jnp.arange(SLOTS_DEV)[None, :] == chosen).reshape(SLOTS)
    return jnp.where(smaller & jnp.logical_not(forced), 1, 0).astype(jnp.int32)


def draw_resolution(key, part):
    return slot_kinds_of(key)


def draw_kept_index(key, part):
    slot_kinds = slot_kinds_of(key)
    key = jax.random.fold_in(key, 5)
    slot_keys = jax.random.split(key, SLOTS)

    def region_pick(region_key):
        return jax.random.permutation(region_key, REGION)[:REGION // 2]

    def one_slot(slot_key, slot_kind):
        whole_key, region_key, order_key = jax.random.split(slot_key, 3)
        entire = jax.random.permutation(whole_key, GRID)[:KEEP]
        regional = jax.vmap(region_pick)(jax.random.split(region_key, 4))
        regional = (regional + REGION * jnp.arange(4)[:, None]).reshape(KEEP)
        regional = regional[jax.random.permutation(order_key, KEEP)]
        return jnp.where(slot_kind == 1, regional, entire)
    return jax.vmap(one_slot)(slot_keys, slot_kinds).astype(jnp.int32)


def draw_cotangent(key, part):
    key = jax.random.fold_in(key, 7)
    ramp = jnp.arange(SLOTS, dtype=jnp.float32) / max(SLOTS - 1, 1)
    values = jax.random.normal(key, (SLOTS, GRID, D), jnp.float32)
    rising = 1.0 + 2.0 * ramp
    return (values * rising[:, None, None]).astype(jnp.bfloat16)


def place_ends(drawn, key, smallest, top_value):
    index_at = [jax.random.randint(jax.random.fold_in(key, axis), (), 0, length) for axis, length in enumerate(drawn.shape)]
    main_axis = drawn.shape.index(max(drawn.shape))
    next_to = index_at[:main_axis] + [(index_at[main_axis] + 1) % drawn.shape[main_axis]] + index_at[main_axis + 1:]
    return drawn.at[tuple(index_at)].set(smallest).at[tuple(next_to)].set(top_value)


def levels(own_key, shape, shards, low, high):
    factor_of, own = 1.0, jax.random.fold_in(own_key, 6)
    for position, blocks in shards:
        heights = jnp.exp(jax.random.uniform(jax.random.fold_in(own, position), (blocks,), jnp.float32, low / len(shards), high / len(shards)))
        factor_of = factor_of * jnp.repeat(heights, shape[position] // blocks).reshape([-1 if axis == position else 1 for axis in range(len(shape))])
    return factor_of


def noise(key, extent, scale, reach, cuts=(), kind=jnp.bfloat16):
    gain = levels(key, extent, cuts, -0.22, 0.18) if cuts else 1.0
    entries = jax.random.normal(key, extent, jnp.float32) * scale * gain
    return jnp.minimum(jnp.maximum(entries, -reach), reach).astype(kind)


def setup_inputs(seed: int = 0) -> dict:
    key_list = jax.random.split(jax.random.key(seed), 26)
    kept_tokens = noise(key_list[0], (SLOTS, KEEP, D), 1.0, 6.0, ((0, 8), (1, 4)))
    kept_index = draw_kept_index(jax.random.fold_in(key_list[25], 71), 0)
    resolution = draw_resolution(jax.random.fold_in(key_list[25], 71), 0)
    labels = place_ends(jax.random.randint(key_list[3], (SLOTS, 4), 0, CLASSES), jax.random.fold_in(key_list[3], 1), 0, CLASSES - 1).astype(jnp.int32)
    timesteps = place_ends(jax.random.randint(key_list[4], (SLOTS, 4), 0, 1000), jax.random.fold_in(key_list[4], 1), 0, 999).astype(jnp.int32)
    class_table = noise(key_list[5], (CLASSES, D), 1.0, 6.0, (), jnp.float32)
    cotangent = draw_cotangent(jax.random.fold_in(key_list[25], 71), 0)
    mask_token = noise(key_list[7], (D,), 0.1, 0.6, (), jnp.float32)
    w_qkv = noise(key_list[8], (D, 3 * D), D ** -0.5, 0.1875, ((0, 4), (1, 8)), jnp.float32)
    w_proj = noise(key_list[9], (D, D), (D // 16) ** -0.5, 0.75, ((0, 4), (1, 8)), jnp.float32)
    w_fc1 = noise(key_list[10], (D, FF), D ** -0.5, 0.1875, ((0, 4), (1, 8)), jnp.float32)
    w_fc2 = noise(key_list[11], (FF, D), FF ** -0.5, 0.09375, ((0, 4), (1, 8)), jnp.float32)
    w_ada = noise(key_list[12], (D, 6 * D), D ** -0.5, 0.1875, ((0, 4), (1, 8)), jnp.float32)
    mask_first = noise(key_list[13], (D,), (0.11 * (10 * D * D + 2 * D * FF) ** -0.5), 0.00012207031, (), jnp.float32)
    first_qkv = noise(key_list[14], (D, 3 * D), (0.11 * (10 * D * D + 2 * D * FF) ** -0.5), 0.00012207031, ((0, 4), (1, 8)), jnp.float32)
    first_proj = noise(key_list[15], (D, D), (0.11 * (10 * D * D + 2 * D * FF) ** -0.5), 0.00012207031, ((0, 4), (1, 8)), jnp.float32)
    first_fc1 = noise(key_list[16], (D, FF), (0.11 * (10 * D * D + 2 * D * FF) ** -0.5), 0.00012207031, ((0, 4), (1, 8)), jnp.float32)
    first_fc2 = noise(key_list[17], (FF, D), (0.11 * (10 * D * D + 2 * D * FF) ** -0.5), 0.00012207031, ((0, 4), (1, 8)), jnp.float32)
    first_ada = noise(key_list[18], (D, 6 * D), (0.11 * (10 * D * D + 2 * D * FF) ** -0.5), 0.00012207031, ((0, 4), (1, 8)), jnp.float32)
    mask_second = jnp.clip(jnp.exp(jax.random.uniform(key_list[19], (D,), jnp.float32, math.log(2.0931123501100046e-09), math.log(8.372449400440019e-09))), 2.0931123501100046e-09, 8.372449400440019e-09)
    second_qkv = jnp.clip(jnp.exp(math.log(8.372449400440019e-09) - 1.3862944 * jax.random.uniform(key_list[20], (D, 3 * D), jnp.float32) ** levels(key_list[20], (D, 3 * D), ((0, 4), (1, 8)), -0.2, 0.2)), 2.0931123501100046e-09, 8.372449400440019e-09)
    second_proj = jnp.clip(jnp.exp(math.log(8.372449400440019e-09) - 1.3862944 * jax.random.uniform(key_list[21], (D, D), jnp.float32) ** levels(key_list[21], (D, D), ((0, 4), (1, 8)), -0.2, 0.2)), 2.0931123501100046e-09, 8.372449400440019e-09)
    second_fc1 = jnp.clip(jnp.exp(math.log(1.0046938836438812e-09) - 1.3862944 * jax.random.uniform(key_list[22], (D, FF), jnp.float32) ** levels(key_list[22], (D, FF), ((0, 4), (1, 8)), -0.2, 0.2)), 2.511734709109703e-10, 1.0046938836438812e-09)
    second_fc2 = jnp.clip(jnp.exp(math.log(8.372449400440019e-09) - 1.3862944 * jax.random.uniform(key_list[23], (FF, D), jnp.float32) ** levels(key_list[23], (FF, D), ((0, 4), (1, 8)), -0.2, 0.2)), 2.0931123501100046e-09, 8.372449400440019e-09)
    second_ada = jnp.clip(jnp.exp(math.log(8.372449400440019e-09) - 1.3862944 * jax.random.uniform(key_list[24], (D, 6 * D), jnp.float32) ** levels(key_list[24], (D, 6 * D), ((0, 4), (1, 8)), -0.2, 0.2)), 2.0931123501100046e-09, 8.372449400440019e-09)
    return {"kept_tokens": kept_tokens, "kept_index": kept_index, "resolution": resolution, "labels": labels, "timesteps": timesteps, "class_table": class_table, "cotangent": cotangent, "mask_token": mask_token, "w_qkv": w_qkv, "w_proj": w_proj, "w_fc1": w_fc1, "w_fc2": w_fc2, "w_ada": w_ada, "mask_first": mask_first, "first_qkv": first_qkv, "first_proj": first_proj, "first_fc1": first_fc1, "first_fc2": first_fc2, "first_ada": first_ada, "mask_second": mask_second, "second_qkv": second_qkv, "second_proj": second_proj, "second_fc1": second_fc1, "second_fc2": second_fc2, "second_ada": second_ada}


@jax.custom_vjp
def low(v):
    return lax.optimization_barrier(v.astype(jnp.bfloat16)).astype(jnp.float32)

@jax.custom_vjp
def low_back(v):
    return v

def low_keep(v):
    return (low(v), None)

def low_pass(kept, grad):
    return (grad,)

def back_keep(v):
    return (v, None)

def back_low(kept, grad):
    return (low(grad),)
low.defvjp(low_keep, low_pass)
low_back.defvjp(back_keep, back_low)
learn_rate = 0.1
beta_first = 0.9
beta_second = 0.95
adam_eps = 1e-08
decay_rate = 0.1
clip_level = 1.0

def time_embed(timestep):
    half_width = D // 2
    frequency = jnp.exp(-math.log(10000.0) * jnp.arange(half_width, dtype=jnp.float32) / half_width)
    angles = timestep.astype(jnp.float32)[..., None] * frequency
    return jnp.concatenate([jnp.cos(angles), jnp.sin(angles)], axis=-1)

def grid_embed(grid_rows, grid_cols):
    quarter = D // 4
    omegas = 1.0 / 10000.0 ** (jnp.arange(quarter, dtype=jnp.float32) / quarter)
    row_angle = grid_rows.astype(jnp.float32)[..., None] * omegas
    col_angle = grid_cols.astype(jnp.float32)[..., None] * omegas
    return jnp.concatenate([jnp.sin(row_angle), jnp.cos(row_angle), jnp.sin(col_angle), jnp.cos(col_angle)], axis=-1)

def slot_layout(positions, slot_kinds):
    small_side = SIDE // 2
    region = positions // REGION
    inside = positions % REGION
    grid_rows = jnp.where(slot_kinds == 1, inside // small_side, positions // SIDE)
    grid_cols = jnp.where(slot_kinds == 1, inside % small_side, positions % SIDE)
    image_id = jnp.where(slot_kinds == 1, region, 0)
    return (grid_rows, grid_cols, image_id)

def modulate(values, shifts, scales):
    center = lax.optimization_barrier(jnp.mean(values, axis=-1, keepdims=True))
    spread = lax.optimization_barrier(jnp.mean((values - center) ** 2, axis=-1, keepdims=True))
    return (values - center) * lax.rsqrt(spread + 1e-06) * (1.0 + scales) + shifts

def pick_rows(table_rows, picks):
    return table_rows[picks]

def forward(params, kept_rows, kept_index, slot_kinds, labels, timesteps, class_table):
    w_qkv, w_proj, w_fc1, w_fc2, w_ada, mask_token = params
    highest = lax.Precision.HIGHEST
    qkv_low = low(w_qkv)
    proj_low = low(w_proj)
    fc1_low = low(w_fc1)
    fc2_low = low(w_fc2)
    ada_low = low(w_ada)
    group_size = kept_rows.shape[0]
    condition = class_table[labels] + time_embed(timesteps)
    cond_low = low(jax.nn.silu(condition))
    modulation = jnp.einsum('gid,de->gie', cond_low, ada_low, precision=highest)
    positions = jnp.arange(GRID)
    grid_rows, grid_cols, image_id = slot_layout(positions[None, :], slot_kinds[:, None])
    token_mod = jax.vmap(pick_rows)(modulation, image_id)
    shift_attn, scale_attn, gate_attn, shift_mlp, scale_mlp, gate_mlp = jnp.split(token_mod, 6, axis=-1)

    def place_rows(rows_given, index_given):
        filled = jnp.broadcast_to(mask_token, (GRID, D))
        return filled.at[index_given].set(rows_given)
    tokens = jax.vmap(place_rows)(kept_rows, kept_index) + grid_embed(grid_rows, grid_cols)
    hidden = low(modulate(tokens, shift_attn, scale_attn))
    qkv = low(low_back(jnp.einsum('gtd,de->gte', hidden, qkv_low, precision=highest)))
    queries = qkv[..., :D].reshape(group_size, GRID, HEADS, HEAD_DIM)
    keys_in = qkv[..., D:2 * D].reshape(group_size, GRID, HEADS, HEAD_DIM)
    values_in = qkv[..., 2 * D:].reshape(group_size, GRID, HEADS, HEAD_DIM)
    scores = low_back(jnp.einsum('gqhd,gkhd->ghqk', queries, keys_in, precision=highest)) * HEAD_DIM ** (-0.5)
    region = positions // REGION
    allowed = (slot_kinds[:, None, None] == 0) | (region[None, :, None] == region[None, None, :])
    scores = jnp.where(allowed[:, None], scores, -1e+30)
    weights_soft = low(jax.nn.softmax(scores, axis=-1))
    attended = low(low_back(jnp.einsum('ghqk,gkhd->gqhd', weights_soft, values_in, precision=highest)))
    attended = attended.reshape(group_size, GRID, D)
    branch = low_back(jnp.einsum('gtd,de->gte', attended, proj_low, precision=highest))
    middle = tokens + gate_attn * branch
    hidden_mlp = low(modulate(middle, shift_mlp, scale_mlp))
    upward = low_back(jnp.einsum('gtd,df->gtf', hidden_mlp, fc1_low, precision=highest))
    active = low(jax.nn.gelu(upward, approximate=True))
    output = low_back(jnp.einsum('gtf,fd->gtd', active, fc2_low, precision=highest))
    return middle + gate_mlp * output

def adamw(weight, first, second, grad):
    first_new = beta_first * first + (1.0 - beta_first) * grad
    second_new = beta_second * second + (1.0 - beta_second) * grad * grad
    first_hat = first_new / (1.0 - beta_first ** STEP)
    second_hat = second_new / (1.0 - beta_second ** STEP)
    weight_new = weight - learn_rate * (first_hat / (jnp.sqrt(second_hat) + adam_eps) + decay_rate * weight)
    return (weight_new, first_new, second_new)

def reference(kept_tokens, kept_index, resolution, labels, timesteps, class_table, cotangent, mask_token, w_qkv, w_proj, w_fc1, w_fc2, w_ada, mask_first, first_qkv, first_proj, first_fc1, first_fc2, first_ada, mask_second, second_qkv, second_proj, second_fc1, second_fc2, second_ada):
    params = (w_qkv, w_proj, w_fc1, w_fc2, w_ada, mask_token)
    group_size = math.gcd(SLOTS, max(1, 4096 // GRID))
    group_count = SLOTS // group_size
    kept_groups = kept_tokens.astype(jnp.float32).reshape(group_count, group_size, KEEP, D)
    index_groups = kept_index.reshape(group_count, group_size, KEEP)
    kind_groups = resolution.reshape(group_count, group_size)
    label_groups = labels.reshape(group_count, group_size, 4)
    time_groups = timesteps.reshape(group_count, group_size, 4)
    cot_groups = cotangent.astype(jnp.float32).reshape(group_count, group_size, GRID, D)

    def step_group(totals, pieces):
        kept_rows, index_rows, kind_rows, label_rows, time_rows, cot_rows = pieces

        def run_block(param_set, kept_set):
            return forward(param_set, kept_set, index_rows, kind_rows, label_rows, time_rows, class_table)
        result, pullback = jax.vjp(run_block, params, kept_rows)
        grad_params, grad_kept = pullback(cot_rows)
        totals = jax.tree.map(jnp.add, totals, grad_params)
        return (totals, (result.astype(jnp.bfloat16), grad_kept))
    initial = jax.tree.map(jnp.zeros_like, params)
    totals, (outputs, kept_grads) = lax.scan(step_group, initial, (kept_groups, index_groups, kind_groups, label_groups, time_groups, cot_groups))
    squares = sum((jnp.sum(grad * grad) for grad in totals))
    norm_value = jnp.sqrt(squares)
    factor = clip_level / jnp.maximum(norm_value, clip_level)
    g_qkv, g_proj, g_fc1, g_fc2, g_ada, g_mask = [grad * factor for grad in totals]
    mask_new = adamw(mask_token, mask_first, mask_second, g_mask)
    qkv_new = adamw(w_qkv, first_qkv, second_qkv, g_qkv)
    proj_new = adamw(w_proj, first_proj, second_proj, g_proj)
    fc1_new = adamw(w_fc1, first_fc1, second_fc1, g_fc1)
    fc2_new = adamw(w_fc2, first_fc2, second_fc2, g_fc2)
    ada_new = adamw(w_ada, first_ada, second_ada, g_ada)
    return (outputs.reshape(SLOTS, GRID, D), kept_grads.reshape(SLOTS, KEEP, D), norm_value, mask_new[0], qkv_new[0], proj_new[0], fc1_new[0], fc2_new[0], ada_new[0], mask_new[1], qkv_new[1], proj_new[1], fc1_new[1], fc2_new[1], ada_new[1], mask_new[2], qkv_new[2], proj_new[2], fc1_new[2], fc2_new[2], ada_new[2])
```

```python
import math

import jax
import jax.numpy as jnp
from jax import lax
from jax.experimental import pallas as pl
from jax.experimental.pallas import tpu as pltpu
from jax.sharding import PartitionSpec as P

D = 1152
HEADS = 16
HEAD_DIM = 72
SIDE = 32
STEP = 10
REGION = 256


learn_rate = 0.1
beta_first = 0.9
beta_second = 0.95
adam_eps = 1e-08
decay_rate = 0.1
clip_level = 1.0


def time_embed(timestep):
    half_width = D // 2
    frequency = jnp.exp(-math.log(10000.0) * jnp.arange(half_width, dtype=jnp.float32) / half_width)
    angles = timestep.astype(jnp.float32)[..., None] * frequency
    return jnp.concatenate([jnp.cos(angles), jnp.sin(angles)], axis=-1)


def grid_embed(grid_rows, grid_cols):
    quarter = D // 4
    omegas = 1.0 / 10000.0 ** (jnp.arange(quarter, dtype=jnp.float32) / quarter)
    row_angle = grid_rows.astype(jnp.float32)[..., None] * omegas
    col_angle = grid_cols.astype(jnp.float32)[..., None] * omegas
    return jnp.concatenate(
        [jnp.sin(row_angle), jnp.cos(row_angle), jnp.sin(col_angle), jnp.cos(col_angle)], axis=-1
    )


def slot_layout(positions, slot_kinds):
    small_side = SIDE // 2
    region = positions // REGION
    inside = positions % REGION
    grid_rows = jnp.where(slot_kinds == 1, inside // small_side, positions // SIDE)
    grid_cols = jnp.where(slot_kinds == 1, inside % small_side, positions % SIDE)
    image_id = jnp.where(slot_kinds == 1, region, 0)
    return (grid_rows, grid_cols, image_id)


def modulate(values, shifts, scales):
    center = jnp.mean(values, axis=-1, keepdims=True)
    spread = jnp.mean((values - center) ** 2, axis=-1, keepdims=True)
    return (values - center) * lax.rsqrt(spread + 1e-06) * (1.0 + scales) + shifts


def gelu_tanh(values):
    return jax.nn.gelu(values, approximate=True)


def pick_rows(table_rows, picks):
    return table_rows[picks]


def allowed_pairs(query_pos, key_pos, slot_kinds):
    same_region = (query_pos // REGION)[None, :, None] == (key_pos // REGION)[None, None, :]
    return (slot_kinds[:, None, None] == 0) | same_region


def attend(queries, keys_in, values_in, allowed):

    def one_slot(pieces):
        query_s, key_s, value_s, allow_s = pieces
        scores = jnp.einsum(
            "qhd,khd->hqk", query_s, key_s, preferred_element_type=jnp.float32
        ) * HEAD_DIM ** (-0.5)
        scores = jnp.where(allow_s[None], scores, -1e30)
        row_peak = jnp.max(scores, axis=-1, keepdims=True)
        row_total = jnp.sum(jnp.exp(scores - row_peak), axis=-1, keepdims=True)
        log_total = row_peak + jnp.log(row_total)
        weights_soft = jnp.exp(scores - log_total).astype(jnp.bfloat16)
        result = jnp.einsum(
            "hqk,khd->qhd", weights_soft, value_s, preferred_element_type=jnp.float32
        )
        return (result.astype(jnp.bfloat16), log_total)

    return lax.map(one_slot, (queries, keys_in, values_in, allowed))


def attend_back(queries, keys_in, values_in, allowed, log_total, grad_attended):

    def one_slot(pieces):
        query_s, key_s, value_s, allow_s, total_s, grad_s = pieces
        scores = jnp.einsum(
            "qhd,khd->hqk", query_s, key_s, preferred_element_type=jnp.float32
        ) * HEAD_DIM ** (-0.5)
        scores = jnp.where(allow_s[None], scores, -1e30)
        weights_full = jnp.exp(scores - total_s)
        weights_soft = weights_full.astype(jnp.bfloat16)
        grad_weights = jnp.einsum(
            "qhd,khd->hqk", grad_s, value_s, preferred_element_type=jnp.float32
        )
        row_dot = jnp.sum(weights_full * grad_weights, axis=-1, keepdims=True)
        grad_scores = (weights_full * (grad_weights - row_dot) * HEAD_DIM ** (-0.5)).astype(
            jnp.bfloat16
        )
        grad_queries = jnp.einsum(
            "hqk,khd->qhd", grad_scores, key_s, preferred_element_type=jnp.float32
        )
        grad_keys = jnp.einsum(
            "hqk,qhd->khd", grad_scores, query_s, preferred_element_type=jnp.float32
        )
        grad_values = jnp.einsum(
            "hqk,qhd->khd", weights_soft, grad_s, preferred_element_type=jnp.float32
        )
        return (grad_queries, grad_keys, grad_values)

    return lax.map(one_slot, (queries, keys_in, values_in, allowed, log_total, grad_attended))


def adamw(weight, first, second, grad):
    first_new = beta_first * first + (1.0 - beta_first) * grad
    second_new = beta_second * second + (1.0 - beta_second) * grad * grad
    first_hat = first_new / (1.0 - beta_first**STEP)
    second_hat = second_new / (1.0 - beta_second**STEP)
    weight_new = weight - learn_rate * (
        first_hat / (jnp.sqrt(second_hat) + adam_eps) + decay_rate * weight
    )
    return (weight_new, first_new, second_new)


def general_device(
    kept_tokens,
    kept_index,
    resolution,
    labels,
    timesteps,
    class_table,
    cotangent,
    mask_token,
    w_qkv,
    w_proj,
    w_fc1,
    w_fc2,
    w_ada,
    mask_first,
    first_qkv,
    first_proj,
    first_fc1,
    first_fc2,
    first_ada,
    mask_second,
    second_qkv,
    second_proj,
    second_fc1,
    second_fc2,
    second_ada,
):
    highest = lax.Precision.HIGHEST
    band_index = lax.axis_index("band")
    slot_count = cotangent.shape[0]
    local_rows = cotangent.shape[1]
    qkv_low = w_qkv.astype(jnp.bfloat16)
    proj_low = w_proj.astype(jnp.bfloat16)
    fc1_low = w_fc1.astype(jnp.bfloat16)
    fc2_low = w_fc2.astype(jnp.bfloat16)
    ada_low = w_ada.astype(jnp.bfloat16)
    cols_qkv, cols_proj, cols_fc1, cols_fc2, cols_ada = (
        lax.all_gather(qkv_low, "dp", axis=1, tiled=True),
        lax.all_gather(proj_low, "dp", axis=1, tiled=True),
        lax.all_gather(fc1_low, "dp", axis=1, tiled=True),
        lax.all_gather(fc2_low, "dp", axis=1, tiled=True),
        lax.all_gather(ada_low, "dp", axis=1, tiled=True),
    )
    condition = jnp.take(class_table, labels, axis=0) + time_embed(timesteps)
    cond_low = jax.nn.silu(condition).astype(jnp.bfloat16)
    qkv_full, proj_full, fc1_full, fc2_full, ada_full = (
        lax.all_gather(cols_qkv, "band", axis=0, tiled=True),
        lax.all_gather(cols_proj, "band", axis=0, tiled=True),
        lax.all_gather(cols_fc1, "band", axis=0, tiled=True),
        lax.all_gather(cols_fc2, "band", axis=0, tiled=True),
        lax.all_gather(cols_ada, "band", axis=0, tiled=True),
    )
    modulation = jnp.einsum("sid,de->sie", cond_low, ada_full, preferred_element_type=jnp.float32)
    kept_all, index_all = (
        lax.all_gather(kept_tokens, "band", axis=1, tiled=True),
        lax.all_gather(kept_index, "band", axis=1, tiled=True),
    )
    positions = band_index * local_rows + jnp.arange(local_rows)
    select = index_all[:, None, :] == positions[None, :, None]
    placed = jnp.einsum(
        "spj,sjd->spd", select.astype(jnp.bfloat16), kept_all, preferred_element_type=jnp.float32
    )
    unfilled = 1.0 - jnp.sum(select.astype(jnp.float32), axis=2)
    grid_rows, grid_cols, image_id = slot_layout(positions[None, :], resolution[:, None])
    tokens = placed + unfilled[..., None] * mask_token + grid_embed(grid_rows, grid_cols)
    token_mod = jax.vmap(pick_rows)(modulation, image_id)
    shift_attn, scale_attn, gate_attn, shift_mlp, scale_mlp, gate_mlp = jnp.split(
        token_mod, 6, axis=-1
    )
    attn_value, attn_pull = jax.vjp(modulate, tokens, shift_attn, scale_attn)
    hidden = attn_value.astype(jnp.bfloat16)
    qkv = jnp.einsum("std,de->ste", hidden, qkv_full, preferred_element_type=jnp.float32).astype(
        jnp.bfloat16
    )
    queries = qkv[..., :D].reshape(slot_count, local_rows, HEADS, HEAD_DIM)
    keys_in = qkv[..., D : 2 * D].reshape(slot_count, local_rows, HEADS, HEAD_DIM)
    values_in = qkv[..., 2 * D :].reshape(slot_count, local_rows, HEADS, HEAD_DIM)
    keys_all, values_all = (
        lax.all_gather(keys_in, "band", axis=1, tiled=True),
        lax.all_gather(values_in, "band", axis=1, tiled=True),
    )
    allowed = allowed_pairs(positions, jnp.arange(keys_all.shape[1]), resolution)
    attended, log_total = attend(queries, keys_all, values_all, allowed)
    attended_flat = attended.reshape(slot_count, local_rows, D)
    branch = jnp.einsum("std,de->ste", attended_flat, proj_full, preferred_element_type=jnp.float32)
    middle = tokens + gate_attn * branch
    mlp_value, mlp_pull = jax.vjp(modulate, middle, shift_mlp, scale_mlp)
    hidden_mlp = mlp_value.astype(jnp.bfloat16)
    upward = jnp.einsum("std,df->stf", hidden_mlp, fc1_full, preferred_element_type=jnp.float32)
    active_value, gelu_pull = jax.vjp(gelu_tanh, upward)
    active = active_value.astype(jnp.bfloat16)
    output = jnp.einsum("stf,fd->std", active, fc2_full, preferred_element_type=jnp.float32)
    block_out = (middle + gate_mlp * output).astype(jnp.bfloat16)
    grad_out = cotangent.astype(jnp.float32)
    grad_gate_mlp = grad_out * output
    grad_output = (gate_mlp * grad_out).astype(jnp.bfloat16)
    grad_fc2 = jnp.einsum("stf,std->fd", active, grad_output, preferred_element_type=jnp.float32)
    grad_active = jnp.einsum(
        "std,fd->stf", grad_output, fc2_full, preferred_element_type=jnp.float32
    )
    grad_upward = gelu_pull(grad_active)[0].astype(jnp.bfloat16)
    grad_fc1 = jnp.einsum(
        "std,stf->df", hidden_mlp, grad_upward, preferred_element_type=jnp.float32
    )
    grad_hidden_mlp = jnp.einsum(
        "stf,df->std", grad_upward, fc1_full, preferred_element_type=jnp.float32
    )
    grad_mid_norm, grad_shift_mlp, grad_scale_mlp = mlp_pull(grad_hidden_mlp)
    grad_middle = grad_out + grad_mid_norm
    grad_gate_attn = grad_middle * branch
    grad_branch = (gate_attn * grad_middle).astype(jnp.bfloat16)
    grad_proj = jnp.einsum(
        "std,ste->de", attended_flat, grad_branch, preferred_element_type=jnp.float32
    )
    grad_attended = jnp.einsum(
        "ste,de->std", grad_branch, proj_full, preferred_element_type=jnp.float32
    ).astype(jnp.bfloat16)
    grad_attended = grad_attended.reshape(slot_count, local_rows, HEADS, HEAD_DIM)
    grad_queries, grad_keys_part, grad_values_part = attend_back(
        queries, keys_all, values_all, allowed, log_total, grad_attended
    )
    grad_keys, grad_values = (
        lax.psum_scatter(
            grad_keys_part.astype(jnp.bfloat16), "band", scatter_dimension=1, tiled=True
        ).astype(jnp.float32),
        lax.psum_scatter(
            grad_values_part.astype(jnp.bfloat16), "band", scatter_dimension=1, tiled=True
        ).astype(jnp.float32),
    )
    grad_qkv = jnp.concatenate(
        [
            grad_queries.reshape(slot_count, local_rows, D),
            grad_keys.reshape(slot_count, local_rows, D),
            grad_values.reshape(slot_count, local_rows, D),
        ],
        axis=-1,
    ).astype(jnp.bfloat16)
    grad_qkv_weight = jnp.einsum(
        "std,ste->de", hidden, grad_qkv, preferred_element_type=jnp.float32
    )
    grad_hidden = jnp.einsum("ste,de->std", grad_qkv, qkv_full, preferred_element_type=jnp.float32)
    grad_tok_norm, grad_shift_attn, grad_scale_attn = attn_pull(grad_hidden)
    grad_tokens = grad_middle + grad_tok_norm
    grad_mod_tok = jnp.concatenate(
        [
            grad_shift_attn,
            grad_scale_attn,
            grad_gate_attn,
            grad_shift_mlp,
            grad_scale_mlp,
            grad_gate_mlp,
        ],
        axis=-1,
    )
    image_onehot = (image_id[..., None] == jnp.arange(4)).astype(jnp.float32)
    grad_modulation = jnp.einsum("spi,spe->sie", image_onehot, grad_mod_tok, precision=highest)
    grad_mask_part = jnp.sum(unfilled[..., None] * grad_tokens, axis=(0, 1))
    grad_kept_all = jnp.einsum(
        "spj,spd->sjd", select.astype(jnp.float32), grad_tokens, precision=highest
    )
    kept_grad = lax.psum_scatter(
        grad_kept_all.astype(jnp.bfloat16), "band", scatter_dimension=1, tiled=True
    ).astype(jnp.float32)
    grad_ada = jnp.einsum(
        "sid,sie->de", cond_low.astype(jnp.float32), grad_modulation, precision=highest
    )
    row_grads = (
        lax.psum_scatter(
            grad_qkv_weight.astype(jnp.bfloat16), "band", scatter_dimension=0, tiled=True
        ).astype(jnp.float32),
        lax.psum_scatter(
            grad_proj.astype(jnp.bfloat16), "band", scatter_dimension=0, tiled=True
        ).astype(jnp.float32),
        lax.psum_scatter(
            grad_fc1.astype(jnp.bfloat16), "band", scatter_dimension=0, tiled=True
        ).astype(jnp.float32),
        lax.psum_scatter(
            grad_fc2.astype(jnp.bfloat16), "band", scatter_dimension=0, tiled=True
        ).astype(jnp.float32),
        lax.psum_scatter(
            grad_ada.astype(jnp.bfloat16), "band", scatter_dimension=0, tiled=True
        ).astype(jnp.float32),
    )
    red_qkv, red_proj, red_fc1, red_fc2, red_ada = (
        lax.psum_scatter(
            row_grads[0].astype(jnp.bfloat16), "dp", scatter_dimension=1, tiled=True
        ).astype(jnp.float32),
        lax.psum_scatter(
            row_grads[1].astype(jnp.bfloat16), "dp", scatter_dimension=1, tiled=True
        ).astype(jnp.float32),
        lax.psum_scatter(
            row_grads[2].astype(jnp.bfloat16), "dp", scatter_dimension=1, tiled=True
        ).astype(jnp.float32),
        lax.psum_scatter(
            row_grads[3].astype(jnp.bfloat16), "dp", scatter_dimension=1, tiled=True
        ).astype(jnp.float32),
        lax.psum_scatter(
            row_grads[4].astype(jnp.bfloat16), "dp", scatter_dimension=1, tiled=True
        ).astype(jnp.float32),
    )
    grad_mask = lax.psum(grad_mask_part, ("dp", "band"))
    reduced = (red_qkv, red_proj, red_fc1, red_fc2, red_ada)
    local_squares = sum((jnp.sum(grad * grad) for grad in reduced))
    total_squares = lax.psum(local_squares, ("dp", "band")) + jnp.sum(grad_mask * grad_mask)
    norm_value = jnp.sqrt(total_squares)
    factor = clip_level / jnp.maximum(norm_value, clip_level)
    mask_new = adamw(mask_token, mask_first, mask_second, grad_mask * factor)
    qkv_new = adamw(w_qkv, first_qkv, second_qkv, red_qkv * factor)
    proj_new = adamw(w_proj, first_proj, second_proj, red_proj * factor)
    fc1_new = adamw(w_fc1, first_fc1, second_fc1, red_fc1 * factor)
    fc2_new = adamw(w_fc2, first_fc2, second_fc2, red_fc2 * factor)
    ada_new = adamw(w_ada, first_ada, second_ada, red_ada * factor)
    return (
        block_out,
        kept_grad,
        norm_value,
        mask_new[0],
        qkv_new[0],
        proj_new[0],
        fc1_new[0],
        fc2_new[0],
        ada_new[0],
        mask_new[1],
        qkv_new[1],
        proj_new[1],
        fc1_new[1],
        fc2_new[1],
        ada_new[1],
        mask_new[2],
        qkv_new[2],
        proj_new[2],
        fc1_new[2],
        fc2_new[2],
        ada_new[2],
    )


MASKED = -1e30
SCORE_SCALE = HEAD_DIM ** (-0.5)
LOG2E = math.log2(math.e)
VMEM_LIMIT = 60 * 1024 * 1024


def dot_nn(left, right):
    return lax.dot_general(
        left, right, (((1,), (0,)), ((), ())), preferred_element_type=jnp.float32
    )


def dot_nt(left, right):
    return lax.dot_general(
        left, right, (((1,), (1,)), ((), ())), preferred_element_type=jnp.float32
    )


def attn_kernel(kind_ref, q_ref, k_ref, v_ref, out_ref, lse_ref):
    tokens = q_ref.shape[2]
    regions = tokens // REGION
    other = jnp.where(kind_ref[0] == 1, MASKED, 0.0)
    keys = jnp.transpose(k_ref[0])
    for block in range(regions):
        cols = slice(block * REGION, (block + 1) * REGION)
        raw = dot_nn(keys, q_ref[0, :, cols])
        parts = [
            raw[r * REGION : (r + 1) * REGION] + (0.0 if r == block else other)
            for r in range(regions)
        ]
        scores = jnp.concatenate(parts, axis=0)
        peak = jnp.max(scores, axis=0, keepdims=True)
        weights = jnp.exp2((scores - peak) * (SCORE_SCALE * LOG2E))
        total = jnp.sum(weights, axis=0, keepdims=True)
        mixed = dot_nn(v_ref[0], weights.astype(jnp.bfloat16))
        out_ref[0, :, cols] = (mixed / total).astype(jnp.bfloat16)
        lse_ref[0, :, cols] = peak * (SCORE_SCALE * LOG2E) + jnp.log2(total)


def attn_forward(kind, qkv_heads):
    tokens = qkv_heads.shape[2]
    head = lambda part: pl.BlockSpec(
        (1, HEAD_DIM, tokens), lambda h: (h + part * HEADS, 0, 0)
    )
    return pl.pallas_call(
        attn_kernel,
        grid=(HEADS,),
        in_specs=[pl.BlockSpec(memory_space=pltpu.SMEM), head(0), head(1), head(2)],
        out_specs=[head(0), pl.BlockSpec((1, 1, tokens), lambda h: (h, 0, 0))],
        out_shape=[
            jax.ShapeDtypeStruct((HEADS, HEAD_DIM, tokens), jnp.bfloat16),
            jax.ShapeDtypeStruct((HEADS, 1, tokens), jnp.float32),
        ],
        compiler_params=pltpu.CompilerParams(vmem_limit_bytes=VMEM_LIMIT),
        name="attn_forward",
    )(kind, qkv_heads, qkv_heads, qkv_heads)


def attn_back_kernel(kind_ref, q_ref, k_ref, v_ref, out_ref, grad_ref, lse_ref, grads_ref):
    tokens = q_ref.shape[2]
    regions = tokens // REGION
    other = jnp.where(kind_ref[0] == 1, MASKED, 0.0)
    keys_t = k_ref[0]
    keys = jnp.transpose(keys_t)
    values = jnp.transpose(v_ref[0])
    grad_keys = jnp.zeros((HEAD_DIM, tokens), jnp.float32)
    grad_values = jnp.zeros((HEAD_DIM, tokens), jnp.float32)
    for block in range(regions):
        cols = slice(block * REGION, (block + 1) * REGION)
        queries = q_ref[0, :, cols]
        grad = grad_ref[0, :, cols]
        row_dot = jnp.sum(
            out_ref[0, :, cols].astype(jnp.float32) * grad.astype(jnp.float32),
            axis=0,
            keepdims=True,
        )
        raw = dot_nn(keys, queries)
        parts = [
            raw[r * REGION : (r + 1) * REGION] + (0.0 if r == block else other)
            for r in range(regions)
        ]
        scores = jnp.concatenate(parts, axis=0)
        weights = jnp.exp2(scores * (SCORE_SCALE * LOG2E) - lse_ref[0, :, cols])
        grad_weights = dot_nn(values, grad)
        grad_scores = (weights * (grad_weights - row_dot)).astype(jnp.bfloat16)
        grad_values += dot_nt(grad, weights.astype(jnp.bfloat16))
        grad_keys += dot_nt(queries, grad_scores)
        grads_ref[0, 0, :, cols] = (dot_nn(keys_t, grad_scores) * SCORE_SCALE).astype(
            jnp.bfloat16
        )
    grads_ref[1, 0] = (grad_keys * SCORE_SCALE).astype(jnp.bfloat16)
    grads_ref[2, 0] = grad_values.astype(jnp.bfloat16)


def attn_backward(kind, qkv_heads, attended, grad_attended, lse):
    tokens = qkv_heads.shape[2]
    head = lambda part: pl.BlockSpec(
        (1, HEAD_DIM, tokens), lambda h: (h + part * HEADS, 0, 0)
    )
    return pl.pallas_call(
        attn_back_kernel,
        grid=(HEADS,),
        in_specs=[
            pl.BlockSpec(memory_space=pltpu.SMEM),
            head(0),
            head(1),
            head(2),
            head(0),
            head(0),
            pl.BlockSpec((1, 1, tokens), lambda h: (h, 0, 0)),
        ],
        out_specs=pl.BlockSpec((3, 1, HEAD_DIM, tokens), lambda h: (0, h, 0, 0)),
        out_shape=jax.ShapeDtypeStruct((3, HEADS, HEAD_DIM, tokens), jnp.bfloat16),
        compiler_params=pltpu.CompilerParams(vmem_limit_bytes=VMEM_LIMIT),
        name="attn_backward",
    )(kind, qkv_heads, qkv_heads, qkv_heads, attended, grad_attended, lse)


GELU_A = math.sqrt(2.0 / math.pi)
GELU_B = 0.044715


def mlp_kernel(h_ref, ht_ref, g_ref, gt_ref, up_ref, down_ref, out_ref, grad_ref, gup_ref, gdown_ref):
    step = pl.program_id(0)

    @pl.when(step == 0)
    def _():
        out_ref[...] = jnp.zeros_like(out_ref)
        grad_ref[...] = jnp.zeros_like(grad_ref)

    up = up_ref[...]
    down = down_ref[...]
    upward = dot_nn(h_ref[...], up)
    square = upward * upward
    curve = jnp.tanh(GELU_A * upward * (1.0 + GELU_B * square))
    half = 0.5 * (1.0 + curve)
    active = (upward * half).astype(jnp.bfloat16)
    slope = half + 0.5 * upward * (1.0 - curve * curve) * GELU_A * (
        1.0 + 3.0 * GELU_B * square
    )
    grad_upward = (dot_nn(g_ref[...], down) * slope).astype(jnp.bfloat16)
    out_ref[...] += dot_nt(active, down)
    grad_ref[...] += dot_nt(grad_upward, up)
    gup_ref[...] = dot_nn(ht_ref[...], grad_upward).astype(jnp.bfloat16)
    gdown_ref[...] = dot_nn(gt_ref[...], active).astype(jnp.bfloat16)


def mlp_both(hidden, hidden_t, grad, grad_t, up, down_t, tile):
    tokens, width = hidden.shape
    wide = up.shape[1]
    whole = lambda shape: pl.BlockSpec(shape, lambda f: (0, 0))
    part = pl.BlockSpec((width, tile), lambda f: (0, f))
    return pl.pallas_call(
        mlp_kernel,
        grid=(wide // tile,),
        in_specs=[
            whole((tokens, width)),
            whole((width, tokens)),
            whole((tokens, width)),
            whole((width, tokens)),
            part,
            part,
        ],
        out_specs=[whole((tokens, width)), whole((tokens, width)), part, part],
        out_shape=[
            jax.ShapeDtypeStruct((tokens, width), jnp.float32),
            jax.ShapeDtypeStruct((tokens, width), jnp.float32),
            jax.ShapeDtypeStruct((width, wide), jnp.bfloat16),
            jax.ShapeDtypeStruct((width, wide), jnp.bfloat16),
        ],
        compiler_params=pltpu.CompilerParams(vmem_limit_bytes=VMEM_LIMIT),
        name="mlp_both",
    )(hidden, hidden_t, grad, grad_t, up, down_t)


def gather_weight(shard, row_axis="band", column_axis="dp"):
    columns = lax.all_gather(shard, column_axis, axis=1, tiled=True)
    return lax.all_gather(columns, row_axis, axis=0, tiled=True)


def scatter_grad(grad, row_axis="band", column_axis="dp"):
    rows = lax.psum_scatter(grad, row_axis, scatter_dimension=0, tiled=True)
    return lax.psum_scatter(rows, column_axis, scatter_dimension=1, tiled=True).astype(jnp.float32)


def swap_slots(values):
    moved = lax.all_to_all(values, "band", split_axis=0, concat_axis=0, tiled=True)
    return moved.reshape((-1,) + values.shape[2:])


def norm_parts(values):
    center = jnp.mean(values, axis=-1, keepdims=True)
    spread = jnp.mean((values - center) ** 2, axis=-1, keepdims=True)
    root = lax.rsqrt(spread + 1e-06)
    return ((values - center) * root, root)


def norm_back(grad, normal, root, scales):
    inner = grad * (1.0 + scales)
    return root * (
        inner
        - jnp.mean(inner, axis=-1, keepdims=True)
        - normal * jnp.mean(inner * normal, axis=-1, keepdims=True)
    )


def embed_tables(count):
    quarter = D // 4
    omegas = 1.0 / 10000.0 ** (jnp.arange(quarter, dtype=jnp.float32) / quarter)
    angles = jnp.arange(count, dtype=jnp.float32)[:, None] * omegas
    return jnp.concatenate([jnp.sin(angles), jnp.cos(angles)], axis=-1)


def grid_embed_slot(kind, tokens):
    table = embed_tables(SIDE)
    half = D // 2
    side = SIDE
    wide = jnp.concatenate(
        [
            jnp.broadcast_to(table[:, None, :], (side, side, half)),
            jnp.broadcast_to(table[None, :, :], (side, side, half)),
        ],
        axis=-1,
    ).reshape(tokens, D)
    small = side // 2
    table_small = table[:small]
    narrow = jnp.concatenate(
        [
            jnp.broadcast_to(table_small[None, :, None, :], (tokens // REGION, small, small, half)),
            jnp.broadcast_to(table_small[None, None, :, :], (tokens // REGION, small, small, half)),
        ],
        axis=-1,
    ).reshape(tokens, D)
    return jnp.where(kind == 1, narrow, wide)


def slot_device(
    kept_tokens,
    kept_index,
    resolution,
    labels,
    timesteps,
    class_table,
    cotangent,
    mask_token,
    w_qkv,
    w_proj,
    w_fc1,
    w_fc2,
    w_ada,
    mask_first,
    first_qkv,
    first_proj,
    first_fc1,
    first_fc2,
    first_ada,
    mask_second,
    second_qkv,
    second_proj,
    second_fc1,
    second_fc2,
    second_ada,
):
    highest = lax.Precision.HIGHEST
    bf16 = jnp.bfloat16
    bands = lax.axis_size("band")
    groups = lax.axis_size("dp")
    band = lax.axis_index("band")
    slots, local_rows, _ = cotangent.shape
    tokens_count = bands * local_rows
    regions = tokens_count // REGION
    images = labels.shape[1]

    picks = lax.all_gather(jnp.concatenate([labels, timesteps], axis=1), "dp", axis=0, tiled=True)
    rows_ada, cols_ada = w_ada.shape
    count = picks.shape[0] * images
    all_labels = picks[:, :images].reshape(count)
    all_times = picks[:, images:].reshape(count)
    table_part = lax.dynamic_slice_in_dim(class_table, band * rows_ada, rows_ada, axis=1)
    chosen = (all_labels[:, None] == jnp.arange(class_table.shape[0])[None, :]).astype(jnp.float32)
    features = band * rows_ada + jnp.arange(rows_ada)
    half_width = D // 2
    frequency = jnp.exp(
        -math.log(10000.0) * (features % half_width).astype(jnp.float32) / half_width
    )
    angles = all_times.astype(jnp.float32)[:, None] * frequency
    waves = jnp.where(features < half_width, jnp.cos(angles), jnp.sin(angles))
    condition = jnp.matmul(chosen, table_part, precision=highest) + waves
    cond_low = jax.nn.silu(condition).astype(bf16)
    partial = jnp.matmul(cond_low, w_ada.astype(bf16), preferred_element_type=jnp.float32)
    partial = partial.reshape(groups, slots, images, cols_ada).transpose(1, 0, 2, 3)
    own_rows = lax.psum_scatter(partial, "band", scatter_dimension=0, tiled=True)[0]
    modulation = lax.all_to_all(own_rows, "dp", split_axis=0, concat_axis=0, tiled=True)
    modulation = modulation.transpose(1, 0, 2).reshape(images, groups * cols_ada)

    kind = lax.dynamic_slice_in_dim(resolution, band, 1)
    kept = swap_slots(kept_tokens)
    index = swap_slots(kept_index)
    grad_out = swap_slots(cotangent).reshape(regions, REGION, D)

    mod = jnp.where(kind[0] == 1, modulation, modulation[:1])
    shift_attn, scale_attn, gate_attn, shift_mlp, scale_mlp, gate_mlp = [
        piece[:, None, :] for piece in jnp.split(mod, 6, axis=-1)
    ]
    select = jnp.arange(tokens_count)[:, None] == index[None, :]
    select_low = select.astype(bf16)
    unfilled = 1.0 - jnp.sum(select.astype(jnp.float32), axis=1, keepdims=True)
    placed = jnp.matmul(select_low, kept, preferred_element_type=jnp.float32)
    tokens = placed + unfilled * mask_token + grid_embed_slot(kind[0], tokens_count)
    tokens = tokens.reshape(regions, REGION, D)

    qkv_full = gather_weight(w_qkv.astype(bf16))
    proj_full = gather_weight(w_proj.astype(bf16))
    fc1_full = gather_weight(w_fc1.astype(bf16))
    fc2_full = gather_weight(w_fc2.astype(bf16).T, "dp", "band")

    normal_attn, root_attn = norm_parts(tokens)
    hidden = (normal_attn * (1.0 + scale_attn) + shift_attn).astype(bf16).reshape(tokens_count, D)
    qkv = lax.dot_general(
        qkv_full, hidden, (((0,), (1,)), ((), ())), preferred_element_type=jnp.float32
    ).astype(bf16)
    qkv_heads = qkv.reshape(3 * HEADS, HEAD_DIM, tokens_count)
    attended, lse = attn_forward(kind, qkv_heads)
    attended_t = attended.reshape(D, tokens_count)
    branch = lax.dot_general(
        attended_t, proj_full, (((0,), (0,)), ((), ())), preferred_element_type=jnp.float32
    ).reshape(regions, REGION, D)
    middle = tokens + gate_attn * branch
    normal_mlp, root_mlp = norm_parts(middle)
    hidden_mlp = (normal_mlp * (1.0 + scale_mlp) + shift_mlp).astype(bf16).reshape(tokens_count, D)
    grad_full = grad_out.astype(jnp.float32)
    grad_output = (gate_mlp * grad_full).astype(bf16).reshape(tokens_count, D)

    output, grad_hidden_mlp, grad_fc1, grad_fc2 = mlp_both(
        hidden_mlp, hidden_mlp.T, grad_output, grad_output.T, fc1_full, fc2_full, 512
    )
    output = output.reshape(regions, REGION, D)
    grad_hidden_mlp = grad_hidden_mlp.reshape(regions, REGION, D)
    block_slot = (middle + gate_mlp * output).astype(bf16)
    block_out = lax.all_to_all(
        block_slot.reshape(bands, local_rows, D), "band", split_axis=0, concat_axis=0, tiled=True
    )
    grad_gate_mlp = jnp.sum(grad_full * output, axis=1)
    grad_shift_mlp = jnp.sum(grad_hidden_mlp, axis=1)
    grad_scale_mlp = jnp.sum(grad_hidden_mlp * normal_mlp, axis=1)
    grad_middle = grad_full + norm_back(grad_hidden_mlp, normal_mlp, root_mlp, scale_mlp)
    grad_gate_attn = jnp.sum(grad_middle * branch, axis=1)
    grad_branch = (gate_attn * grad_middle).astype(bf16).reshape(tokens_count, D)
    grad_proj = dot_nn(attended_t, grad_branch).astype(bf16)
    grad_attended = dot_nt(proj_full, grad_branch).astype(bf16)
    grad_heads = grad_attended.reshape(HEADS, HEAD_DIM, tokens_count)
    grad_qkv = attn_backward(kind, qkv_heads, attended, grad_heads, lse)
    grad_qkv = grad_qkv.reshape(3 * D, tokens_count)
    grad_qkv_weight = lax.dot_general(
        hidden, grad_qkv, (((0,), (1,)), ((), ())), preferred_element_type=jnp.float32
    ).astype(bf16)
    grad_hidden = lax.dot_general(
        grad_qkv, qkv_full, (((0,), (1,)), ((), ())), preferred_element_type=jnp.float32
    ).reshape(regions, REGION, D)
    grad_shift_attn = jnp.sum(grad_hidden, axis=1)
    grad_scale_attn = jnp.sum(grad_hidden * normal_attn, axis=1)
    grad_tokens = grad_middle + norm_back(grad_hidden, normal_attn, root_attn, scale_attn)
    grad_tokens = grad_tokens.reshape(tokens_count, D)

    grad_mod = jnp.concatenate(
        [
            grad_shift_attn,
            grad_scale_attn,
            grad_gate_attn,
            grad_shift_mlp,
            grad_scale_mlp,
            grad_gate_mlp,
        ],
        axis=-1,
    )
    first_only = (jnp.arange(images) == 0).astype(jnp.float32)[:, None]
    grad_mod = jnp.where(
        kind[0] == 1, grad_mod, first_only * jnp.sum(grad_mod, axis=0, keepdims=True)
    )
    grad_mod = grad_mod.reshape(images, groups, cols_ada).transpose(1, 0, 2)
    grad_mod = lax.all_to_all(grad_mod, "dp", split_axis=0, concat_axis=0, tiled=True)
    grad_mod = lax.all_gather(grad_mod, "band", axis=1, tiled=True)
    red_ada = lax.dot_general(
        cond_low.astype(jnp.float32),
        grad_mod.reshape(count, cols_ada),
        (((0,), (0,)), ((), ())),
        precision=highest,
        preferred_element_type=jnp.float32,
    )

    grad_kept = lax.dot_general(
        select_low, grad_tokens.astype(bf16), (((0,), (0,)), ((), ())),
        preferred_element_type=jnp.float32,
    ).astype(bf16)
    kept_grad = lax.all_to_all(
        grad_kept.reshape(bands, -1, D), "band", split_axis=0, concat_axis=0, tiled=True
    ).astype(jnp.float32)
    grad_mask_part = jnp.sum(unfilled * grad_tokens, axis=0)

    red_qkv = scatter_grad(grad_qkv_weight)
    red_proj = scatter_grad(grad_proj)
    red_fc1 = scatter_grad(grad_fc1)
    red_fc2 = scatter_grad(grad_fc2, "dp", "band").T

    grad_mask = lax.psum(grad_mask_part, ("dp", "band"))
    reduced = (red_qkv, red_proj, red_fc1, red_fc2, red_ada)
    local_squares = sum((jnp.sum(grad * grad) for grad in reduced))
    total_squares = lax.psum(local_squares, ("dp", "band")) + jnp.sum(grad_mask * grad_mask)
    norm_value = jnp.sqrt(total_squares)
    factor = clip_level / jnp.maximum(norm_value, clip_level)
    mask_new = adamw(mask_token, mask_first, mask_second, grad_mask * factor)
    qkv_new = adamw(w_qkv, first_qkv, second_qkv, red_qkv * factor)
    proj_new = adamw(w_proj, first_proj, second_proj, red_proj * factor)
    fc1_new = adamw(w_fc1, first_fc1, second_fc1, red_fc1 * factor)
    fc2_new = adamw(w_fc2, first_fc2, second_fc2, red_fc2 * factor)
    ada_new = adamw(w_ada, first_ada, second_ada, red_ada * factor)
    moved = tuple(zip(mask_new, qkv_new, proj_new, fc1_new, fc2_new, ada_new))
    return (block_out, kept_grad, norm_value) + moved[0] + moved[1] + moved[2]


def per_device(*arguments):
    cotangent = arguments[6]
    if cotangent.shape[0] == lax.axis_size("band"):
        return slot_device(*arguments)
    return general_device(*arguments)


def solution(mesh):
    in_specs = (
        P("dp", "band", None),
        P("dp", "band"),
        P("dp"),
        P("dp", None),
        P("dp", None),
        P(),
        P("dp", "band", None),
        P(),
        P("band", "dp"),
        P("band", "dp"),
        P("band", "dp"),
        P("band", "dp"),
        P("band", "dp"),
        P(),
        P("band", "dp"),
        P("band", "dp"),
        P("band", "dp"),
        P("band", "dp"),
        P("band", "dp"),
        P(),
        P("band", "dp"),
        P("band", "dp"),
        P("band", "dp"),
        P("band", "dp"),
        P("band", "dp"),
    )
    out_specs = (
        P("dp", "band", None),
        P("dp", "band", None),
        P(),
        P(),
        P("band", "dp"),
        P("band", "dp"),
        P("band", "dp"),
        P("band", "dp"),
        P("band", "dp"),
        P(),
        P("band", "dp"),
        P("band", "dp"),
        P("band", "dp"),
        P("band", "dp"),
        P("band", "dp"),
        P(),
        P("band", "dp"),
        P("band", "dp"),
        P("band", "dp"),
        P("band", "dp"),
        P("band", "dp"),
    )
    return jax.shard_map(
        per_device, mesh=mesh, in_specs=in_specs, out_specs=out_specs, check_vma=False
    )
```

```python
import functools
import math

import jax
import jax.numpy as jnp
from jax import lax
from jax.experimental import pallas as pl
from jax.experimental.pallas import tpu as pltpu
from jax.sharding import PartitionSpec as P

D = 1152
HEADS = 16
HEAD_DIM = 72
SIDE = 32
STEP = 10
REGION = 256


learn_rate = 0.1
beta_first = 0.9
beta_second = 0.95
adam_eps = 1e-08
decay_rate = 0.1
clip_level = 1.0


def time_embed(timestep):
    half_width = D // 2
    frequency = jnp.exp(-math.log(10000.0) * jnp.arange(half_width, dtype=jnp.float32) / half_width)
    angles = timestep.astype(jnp.float32)[..., None] * frequency
    return jnp.concatenate([jnp.cos(angles), jnp.sin(angles)], axis=-1)


def grid_embed(grid_rows, grid_cols):
    quarter = D // 4
    omegas = 1.0 / 10000.0 ** (jnp.arange(quarter, dtype=jnp.float32) / quarter)
    row_angle = grid_rows.astype(jnp.float32)[..., None] * omegas
    col_angle = grid_cols.astype(jnp.float32)[..., None] * omegas
    return jnp.concatenate(
        [jnp.sin(row_angle), jnp.cos(row_angle), jnp.sin(col_angle), jnp.cos(col_angle)], axis=-1
    )


def slot_layout(positions, slot_kinds):
    small_side = SIDE // 2
    region = positions // REGION
    inside = positions % REGION
    grid_rows = jnp.where(slot_kinds == 1, inside // small_side, positions // SIDE)
    grid_cols = jnp.where(slot_kinds == 1, inside % small_side, positions % SIDE)
    image_id = jnp.where(slot_kinds == 1, region, 0)
    return (grid_rows, grid_cols, image_id)


def modulate(values, shifts, scales):
    center = jnp.mean(values, axis=-1, keepdims=True)
    spread = jnp.mean((values - center) ** 2, axis=-1, keepdims=True)
    return (values - center) * lax.rsqrt(spread + 1e-06) * (1.0 + scales) + shifts


def gelu_tanh(values):
    return jax.nn.gelu(values, approximate=True)


def pick_rows(table_rows, picks):
    return table_rows[picks]


def allowed_pairs(query_pos, key_pos, slot_kinds):
    same_region = (query_pos // REGION)[None, :, None] == (key_pos // REGION)[None, None, :]
    return (slot_kinds[:, None, None] == 0) | same_region


def attend(queries, keys_in, values_in, allowed):

    def one_slot(pieces):
        query_s, key_s, value_s, allow_s = pieces
        scores = jnp.einsum(
            "qhd,khd->hqk", query_s, key_s, preferred_element_type=jnp.float32
        ) * HEAD_DIM ** (-0.5)
        scores = jnp.where(allow_s[None], scores, -1e30)
        row_peak = jnp.max(scores, axis=-1, keepdims=True)
        row_total = jnp.sum(jnp.exp(scores - row_peak), axis=-1, keepdims=True)
        log_total = row_peak + jnp.log(row_total)
        weights_soft = jnp.exp(scores - log_total).astype(jnp.bfloat16)
        result = jnp.einsum(
            "hqk,khd->qhd", weights_soft, value_s, preferred_element_type=jnp.float32
        )
        return (result.astype(jnp.bfloat16), log_total)

    return lax.map(one_slot, (queries, keys_in, values_in, allowed))


def attend_back(queries, keys_in, values_in, allowed, log_total, grad_attended):

    def one_slot(pieces):
        query_s, key_s, value_s, allow_s, total_s, grad_s = pieces
        scores = jnp.einsum(
            "qhd,khd->hqk", query_s, key_s, preferred_element_type=jnp.float32
        ) * HEAD_DIM ** (-0.5)
        scores = jnp.where(allow_s[None], scores, -1e30)
        weights_full = jnp.exp(scores - total_s)
        weights_soft = weights_full.astype(jnp.bfloat16)
        grad_weights = jnp.einsum(
            "qhd,khd->hqk", grad_s, value_s, preferred_element_type=jnp.float32
        )
        row_dot = jnp.sum(weights_full * grad_weights, axis=-1, keepdims=True)
        grad_scores = (weights_full * (grad_weights - row_dot) * HEAD_DIM ** (-0.5)).astype(
            jnp.bfloat16
        )
        grad_queries = jnp.einsum(
            "hqk,khd->qhd", grad_scores, key_s, preferred_element_type=jnp.float32
        )
        grad_keys = jnp.einsum(
            "hqk,qhd->khd", grad_scores, query_s, preferred_element_type=jnp.float32
        )
        grad_values = jnp.einsum(
            "hqk,qhd->khd", weights_soft, grad_s, preferred_element_type=jnp.float32
        )
        return (grad_queries, grad_keys, grad_values)

    return lax.map(one_slot, (queries, keys_in, values_in, allowed, log_total, grad_attended))


def adamw(weight, first, second, grad):
    first_new = beta_first * first + (1.0 - beta_first) * grad
    second_new = beta_second * second + (1.0 - beta_second) * grad * grad
    first_hat = first_new / (1.0 - beta_first**STEP)
    second_hat = second_new / (1.0 - beta_second**STEP)
    weight_new = weight - learn_rate * (
        first_hat / (jnp.sqrt(second_hat) + adam_eps) + decay_rate * weight
    )
    return (weight_new, first_new, second_new)


def general_device(
    kept_tokens,
    kept_index,
    resolution,
    labels,
    timesteps,
    class_table,
    cotangent,
    mask_token,
    w_qkv,
    w_proj,
    w_fc1,
    w_fc2,
    w_ada,
    mask_first,
    first_qkv,
    first_proj,
    first_fc1,
    first_fc2,
    first_ada,
    mask_second,
    second_qkv,
    second_proj,
    second_fc1,
    second_fc2,
    second_ada,
):
    highest = lax.Precision.HIGHEST
    band_index = lax.axis_index("band")
    slot_count = cotangent.shape[0]
    local_rows = cotangent.shape[1]
    qkv_low = w_qkv.astype(jnp.bfloat16)
    proj_low = w_proj.astype(jnp.bfloat16)
    fc1_low = w_fc1.astype(jnp.bfloat16)
    fc2_low = w_fc2.astype(jnp.bfloat16)
    ada_low = w_ada.astype(jnp.bfloat16)
    cols_qkv, cols_proj, cols_fc1, cols_fc2, cols_ada = (
        lax.all_gather(qkv_low, "dp", axis=1, tiled=True),
        lax.all_gather(proj_low, "dp", axis=1, tiled=True),
        lax.all_gather(fc1_low, "dp", axis=1, tiled=True),
        lax.all_gather(fc2_low, "dp", axis=1, tiled=True),
        lax.all_gather(ada_low, "dp", axis=1, tiled=True),
    )
    condition = jnp.take(class_table, labels, axis=0) + time_embed(timesteps)
    cond_low = jax.nn.silu(condition).astype(jnp.bfloat16)
    qkv_full, proj_full, fc1_full, fc2_full, ada_full = (
        lax.all_gather(cols_qkv, "band", axis=0, tiled=True),
        lax.all_gather(cols_proj, "band", axis=0, tiled=True),
        lax.all_gather(cols_fc1, "band", axis=0, tiled=True),
        lax.all_gather(cols_fc2, "band", axis=0, tiled=True),
        lax.all_gather(cols_ada, "band", axis=0, tiled=True),
    )
    modulation = jnp.einsum("sid,de->sie", cond_low, ada_full, preferred_element_type=jnp.float32)
    kept_all, index_all = (
        lax.all_gather(kept_tokens, "band", axis=1, tiled=True),
        lax.all_gather(kept_index, "band", axis=1, tiled=True),
    )
    positions = band_index * local_rows + jnp.arange(local_rows)
    select = index_all[:, None, :] == positions[None, :, None]
    placed = jnp.einsum(
        "spj,sjd->spd", select.astype(jnp.bfloat16), kept_all, preferred_element_type=jnp.float32
    )
    unfilled = 1.0 - jnp.sum(select.astype(jnp.float32), axis=2)
    grid_rows, grid_cols, image_id = slot_layout(positions[None, :], resolution[:, None])
    tokens = placed + unfilled[..., None] * mask_token + grid_embed(grid_rows, grid_cols)
    token_mod = jax.vmap(pick_rows)(modulation, image_id)
    shift_attn, scale_attn, gate_attn, shift_mlp, scale_mlp, gate_mlp = jnp.split(
        token_mod, 6, axis=-1
    )
    attn_value, attn_pull = jax.vjp(modulate, tokens, shift_attn, scale_attn)
    hidden = attn_value.astype(jnp.bfloat16)
    qkv = jnp.einsum("std,de->ste", hidden, qkv_full, preferred_element_type=jnp.float32).astype(
        jnp.bfloat16
    )
    queries = qkv[..., :D].reshape(slot_count, local_rows, HEADS, HEAD_DIM)
    keys_in = qkv[..., D : 2 * D].reshape(slot_count, local_rows, HEADS, HEAD_DIM)
    values_in = qkv[..., 2 * D :].reshape(slot_count, local_rows, HEADS, HEAD_DIM)
    keys_all, values_all = (
        lax.all_gather(keys_in, "band", axis=1, tiled=True),
        lax.all_gather(values_in, "band", axis=1, tiled=True),
    )
    allowed = allowed_pairs(positions, jnp.arange(keys_all.shape[1]), resolution)
    attended, log_total = attend(queries, keys_all, values_all, allowed)
    attended_flat = attended.reshape(slot_count, local_rows, D)
    branch = jnp.einsum("std,de->ste", attended_flat, proj_full, preferred_element_type=jnp.float32)
    middle = tokens + gate_attn * branch
    mlp_value, mlp_pull = jax.vjp(modulate, middle, shift_mlp, scale_mlp)
    hidden_mlp = mlp_value.astype(jnp.bfloat16)
    upward = jnp.einsum("std,df->stf", hidden_mlp, fc1_full, preferred_element_type=jnp.float32)
    active_value, gelu_pull = jax.vjp(gelu_tanh, upward)
    active = active_value.astype(jnp.bfloat16)
    output = jnp.einsum("stf,fd->std", active, fc2_full, preferred_element_type=jnp.float32)
    block_out = (middle + gate_mlp * output).astype(jnp.bfloat16)
    grad_out = cotangent.astype(jnp.float32)
    grad_gate_mlp = grad_out * output
    grad_output = (gate_mlp * grad_out).astype(jnp.bfloat16)
    grad_fc2 = jnp.einsum("stf,std->fd", active, grad_output, preferred_element_type=jnp.float32)
    grad_active = jnp.einsum(
        "std,fd->stf", grad_output, fc2_full, preferred_element_type=jnp.float32
    )
    grad_upward = gelu_pull(grad_active)[0].astype(jnp.bfloat16)
    grad_fc1 = jnp.einsum(
        "std,stf->df", hidden_mlp, grad_upward, preferred_element_type=jnp.float32
    )
    grad_hidden_mlp = jnp.einsum(
        "stf,df->std", grad_upward, fc1_full, preferred_element_type=jnp.float32
    )
    grad_mid_norm, grad_shift_mlp, grad_scale_mlp = mlp_pull(grad_hidden_mlp)
    grad_middle = grad_out + grad_mid_norm
    grad_gate_attn = grad_middle * branch
    grad_branch = (gate_attn * grad_middle).astype(jnp.bfloat16)
    grad_proj = jnp.einsum(
        "std,ste->de", attended_flat, grad_branch, preferred_element_type=jnp.float32
    )
    grad_attended = jnp.einsum(
        "ste,de->std", grad_branch, proj_full, preferred_element_type=jnp.float32
    ).astype(jnp.bfloat16)
    grad_attended = grad_attended.reshape(slot_count, local_rows, HEADS, HEAD_DIM)
    grad_queries, grad_keys_part, grad_values_part = attend_back(
        queries, keys_all, values_all, allowed, log_total, grad_attended
    )
    grad_keys, grad_values = (
        lax.psum_scatter(
            grad_keys_part.astype(jnp.bfloat16), "band", scatter_dimension=1, tiled=True
        ).astype(jnp.float32),
        lax.psum_scatter(
            grad_values_part.astype(jnp.bfloat16), "band", scatter_dimension=1, tiled=True
        ).astype(jnp.float32),
    )
    grad_qkv = jnp.concatenate(
        [
            grad_queries.reshape(slot_count, local_rows, D),
            grad_keys.reshape(slot_count, local_rows, D),
            grad_values.reshape(slot_count, local_rows, D),
        ],
        axis=-1,
    ).astype(jnp.bfloat16)
    grad_qkv_weight = jnp.einsum(
        "std,ste->de", hidden, grad_qkv, preferred_element_type=jnp.float32
    )
    grad_hidden = jnp.einsum("ste,de->std", grad_qkv, qkv_full, preferred_element_type=jnp.float32)
    grad_tok_norm, grad_shift_attn, grad_scale_attn = attn_pull(grad_hidden)
    grad_tokens = grad_middle + grad_tok_norm
    grad_mod_tok = jnp.concatenate(
        [
            grad_shift_attn,
            grad_scale_attn,
            grad_gate_attn,
            grad_shift_mlp,
            grad_scale_mlp,
            grad_gate_mlp,
        ],
        axis=-1,
    )
    image_onehot = (image_id[..., None] == jnp.arange(4)).astype(jnp.float32)
    grad_modulation = jnp.einsum("spi,spe->sie", image_onehot, grad_mod_tok, precision=highest)
    grad_mask_part = jnp.sum(unfilled[..., None] * grad_tokens, axis=(0, 1))
    grad_kept_all = jnp.einsum(
        "spj,spd->sjd", select.astype(jnp.float32), grad_tokens, precision=highest
    )
    kept_grad = lax.psum_scatter(
        grad_kept_all.astype(jnp.bfloat16), "band", scatter_dimension=1, tiled=True
    ).astype(jnp.float32)
    grad_ada = jnp.einsum(
        "sid,sie->de", cond_low.astype(jnp.float32), grad_modulation, precision=highest
    )
    row_grads = (
        lax.psum_scatter(
            grad_qkv_weight.astype(jnp.bfloat16), "band", scatter_dimension=0, tiled=True
        ).astype(jnp.float32),
        lax.psum_scatter(
            grad_proj.astype(jnp.bfloat16), "band", scatter_dimension=0, tiled=True
        ).astype(jnp.float32),
        lax.psum_scatter(
            grad_fc1.astype(jnp.bfloat16), "band", scatter_dimension=0, tiled=True
        ).astype(jnp.float32),
        lax.psum_scatter(
            grad_fc2.astype(jnp.bfloat16), "band", scatter_dimension=0, tiled=True
        ).astype(jnp.float32),
        lax.psum_scatter(
            grad_ada.astype(jnp.bfloat16), "band", scatter_dimension=0, tiled=True
        ).astype(jnp.float32),
    )
    red_qkv, red_proj, red_fc1, red_fc2, red_ada = (
        lax.psum_scatter(
            row_grads[0].astype(jnp.bfloat16), "dp", scatter_dimension=1, tiled=True
        ).astype(jnp.float32),
        lax.psum_scatter(
            row_grads[1].astype(jnp.bfloat16), "dp", scatter_dimension=1, tiled=True
        ).astype(jnp.float32),
        lax.psum_scatter(
            row_grads[2].astype(jnp.bfloat16), "dp", scatter_dimension=1, tiled=True
        ).astype(jnp.float32),
        lax.psum_scatter(
            row_grads[3].astype(jnp.bfloat16), "dp", scatter_dimension=1, tiled=True
        ).astype(jnp.float32),
        lax.psum_scatter(
            row_grads[4].astype(jnp.bfloat16), "dp", scatter_dimension=1, tiled=True
        ).astype(jnp.float32),
    )
    grad_mask = lax.psum(grad_mask_part, ("dp", "band"))
    reduced = (red_qkv, red_proj, red_fc1, red_fc2, red_ada)
    local_squares = sum((jnp.sum(grad * grad) for grad in reduced))
    total_squares = lax.psum(local_squares, ("dp", "band")) + jnp.sum(grad_mask * grad_mask)
    norm_value = jnp.sqrt(total_squares)
    factor = clip_level / jnp.maximum(norm_value, clip_level)
    mask_new = adamw(mask_token, mask_first, mask_second, grad_mask * factor)
    qkv_new = adamw(w_qkv, first_qkv, second_qkv, red_qkv * factor)
    proj_new = adamw(w_proj, first_proj, second_proj, red_proj * factor)
    fc1_new = adamw(w_fc1, first_fc1, second_fc1, red_fc1 * factor)
    fc2_new = adamw(w_fc2, first_fc2, second_fc2, red_fc2 * factor)
    ada_new = adamw(w_ada, first_ada, second_ada, red_ada * factor)
    return (
        block_out,
        kept_grad,
        norm_value,
        mask_new[0],
        qkv_new[0],
        proj_new[0],
        fc1_new[0],
        fc2_new[0],
        ada_new[0],
        mask_new[1],
        qkv_new[1],
        proj_new[1],
        fc1_new[1],
        fc2_new[1],
        ada_new[1],
        mask_new[2],
        qkv_new[2],
        proj_new[2],
        fc1_new[2],
        fc2_new[2],
        ada_new[2],
    )


MASKED = -1e30
SCORE_SCALE = HEAD_DIM ** (-0.5)
LOG2E = math.log2(math.e)
VMEM_LIMIT = 60 * 1024 * 1024


def dot_nn(left, right):
    return lax.dot_general(
        left, right, (((1,), (0,)), ((), ())), preferred_element_type=jnp.float32
    )


def dot_nt(left, right):
    return lax.dot_general(
        left, right, (((1,), (1,)), ((), ())), preferred_element_type=jnp.float32
    )


def attn_kernel(kind_ref, q_ref, k_ref, v_ref, out_ref, lse_ref):
    tokens = q_ref.shape[2]
    regions = tokens // REGION
    other = jnp.where(kind_ref[0] == 1, MASKED, 0.0)
    keys = jnp.transpose(k_ref[0])
    for block in range(regions):
        cols = slice(block * REGION, (block + 1) * REGION)
        raw = dot_nn(keys, q_ref[0, :, cols])
        parts = [
            raw[r * REGION : (r + 1) * REGION] + (0.0 if r == block else other)
            for r in range(regions)
        ]
        scores = jnp.concatenate(parts, axis=0)
        peak = jnp.max(scores, axis=0, keepdims=True)
        weights = jnp.exp2((scores - peak) * (SCORE_SCALE * LOG2E))
        total = jnp.sum(weights, axis=0, keepdims=True)
        mixed = dot_nn(v_ref[0], weights.astype(jnp.bfloat16))
        out_ref[0, :, cols] = (mixed / total).astype(jnp.bfloat16)
        lse_ref[0, :, cols] = peak * (SCORE_SCALE * LOG2E) + jnp.log2(total)


def attn_forward(kind, qkv_heads):
    tokens = qkv_heads.shape[2]
    head = lambda part: pl.BlockSpec(
        (1, HEAD_DIM, tokens), lambda h: (h + part * HEADS, 0, 0)
    )
    return pl.pallas_call(
        attn_kernel,
        grid=(HEADS,),
        in_specs=[pl.BlockSpec(memory_space=pltpu.SMEM), head(0), head(1), head(2)],
        out_specs=[head(0), pl.BlockSpec((1, 1, tokens), lambda h: (h, 0, 0))],
        out_shape=[
            jax.ShapeDtypeStruct((HEADS, HEAD_DIM, tokens), jnp.bfloat16),
            jax.ShapeDtypeStruct((HEADS, 1, tokens), jnp.float32),
        ],
        compiler_params=pltpu.CompilerParams(vmem_limit_bytes=VMEM_LIMIT),
        name="attn_forward",
    )(kind, qkv_heads, qkv_heads, qkv_heads)


def attn_back_kernel(kind_ref, q_ref, k_ref, v_ref, out_ref, grad_ref, lse_ref, grads_ref):
    tokens = q_ref.shape[2]
    regions = tokens // REGION
    other = jnp.where(kind_ref[0] == 1, MASKED, 0.0)
    keys_t = k_ref[0]
    keys = jnp.transpose(keys_t)
    values = jnp.transpose(v_ref[0])
    grad_keys = jnp.zeros((HEAD_DIM, tokens), jnp.float32)
    grad_values = jnp.zeros((HEAD_DIM, tokens), jnp.float32)
    for block in range(regions):
        cols = slice(block * REGION, (block + 1) * REGION)
        queries = q_ref[0, :, cols]
        grad = grad_ref[0, :, cols]
        row_dot = jnp.sum(
            out_ref[0, :, cols].astype(jnp.float32) * grad.astype(jnp.float32),
            axis=0,
            keepdims=True,
        )
        raw = dot_nn(keys, queries)
        parts = [
            raw[r * REGION : (r + 1) * REGION] + (0.0 if r == block else other)
            for r in range(regions)
        ]
        scores = jnp.concatenate(parts, axis=0)
        weights = jnp.exp2(scores * (SCORE_SCALE * LOG2E) - lse_ref[0, :, cols])
        grad_weights = dot_nn(values, grad)
        grad_scores = (weights * (grad_weights - row_dot)).astype(jnp.bfloat16)
        grad_values += dot_nt(grad, weights.astype(jnp.bfloat16))
        grad_keys += dot_nt(queries, grad_scores)
        grads_ref[0, 0, :, cols] = (dot_nn(keys_t, grad_scores) * SCORE_SCALE).astype(
            jnp.bfloat16
        )
    grads_ref[1, 0] = (grad_keys * SCORE_SCALE).astype(jnp.bfloat16)
    grads_ref[2, 0] = grad_values.astype(jnp.bfloat16)


def attn_backward(kind, qkv_heads, attended, grad_attended, lse):
    tokens = qkv_heads.shape[2]
    head = lambda part: pl.BlockSpec(
        (1, HEAD_DIM, tokens), lambda h: (h + part * HEADS, 0, 0)
    )
    return pl.pallas_call(
        attn_back_kernel,
        grid=(HEADS,),
        in_specs=[
            pl.BlockSpec(memory_space=pltpu.SMEM),
            head(0),
            head(1),
            head(2),
            head(0),
            head(0),
            pl.BlockSpec((1, 1, tokens), lambda h: (h, 0, 0)),
        ],
        out_specs=pl.BlockSpec((3, 1, HEAD_DIM, tokens), lambda h: (0, h, 0, 0)),
        out_shape=jax.ShapeDtypeStruct((3, HEADS, HEAD_DIM, tokens), jnp.bfloat16),
        compiler_params=pltpu.CompilerParams(vmem_limit_bytes=VMEM_LIMIT),
        name="attn_backward",
    )(kind, qkv_heads, qkv_heads, qkv_heads, attended, grad_attended, lse)


GELU_A = math.sqrt(2.0 / math.pi)
GELU_B = 0.044715


def mlp_kernel(h_ref, ht_ref, g_ref, gt_ref, up_ref, down_ref, out_ref, grad_ref, gup_ref, gdown_ref):
    step = pl.program_id(0)

    @pl.when(step == 0)
    def _():
        out_ref[...] = jnp.zeros_like(out_ref)
        grad_ref[...] = jnp.zeros_like(grad_ref)

    up = up_ref[...]
    down = down_ref[...]
    upward = dot_nn(h_ref[...], up)
    square = upward * upward
    curve = jnp.tanh(GELU_A * upward * (1.0 + GELU_B * square))
    half = 0.5 * (1.0 + curve)
    active = (upward * half).astype(jnp.bfloat16)
    slope = half + 0.5 * upward * (1.0 - curve * curve) * GELU_A * (
        1.0 + 3.0 * GELU_B * square
    )
    grad_upward = (dot_nn(g_ref[...], down) * slope).astype(jnp.bfloat16)
    out_ref[...] += dot_nt(active, down)
    grad_ref[...] += dot_nt(grad_upward, up)
    gup_ref[...] = dot_nn(ht_ref[...], grad_upward).astype(jnp.bfloat16)
    gdown_ref[...] = dot_nn(gt_ref[...], active).astype(jnp.bfloat16)


def mlp_both(hidden, hidden_t, grad, grad_t, up, down_t, tile):
    tokens, width = hidden.shape
    wide = up.shape[1]
    whole = lambda shape: pl.BlockSpec(shape, lambda f: (0, 0))
    part = pl.BlockSpec((width, tile), lambda f: (0, f))
    return pl.pallas_call(
        mlp_kernel,
        grid=(wide // tile,),
        in_specs=[
            whole((tokens, width)),
            whole((width, tokens)),
            whole((tokens, width)),
            whole((width, tokens)),
            part,
            part,
        ],
        out_specs=[whole((tokens, width)), whole((tokens, width)), part, part],
        out_shape=[
            jax.ShapeDtypeStruct((tokens, width), jnp.float32),
            jax.ShapeDtypeStruct((tokens, width), jnp.float32),
            jax.ShapeDtypeStruct((width, wide), jnp.bfloat16),
            jax.ShapeDtypeStruct((width, wide), jnp.bfloat16),
        ],
        compiler_params=pltpu.CompilerParams(vmem_limit_bytes=VMEM_LIMIT),
        name="mlp_both",
    )(hidden, hidden_t, grad, grad_t, up, down_t)


BLOCK_ROWS = 144
BLOCK_COLS = 1152
VIA_X = (0, 3)


def flip(index):
    return index + 1 - 2 * (index % 2)


def along_z(z, step):
    return (z, flip(z), (z + 2) % 4, 3 - z)[step]


class Place:
    def __init__(self):
        dp = lax.axis_index("dp")
        band = lax.axis_index("band")
        self.z, self.y, self.x, self.core = dp // 2, dp % 2, band // 2, band % 2

    def chip(self, i, a, b):
        return (along_z(self.z, i), flip(self.y) if a else self.y, flip(self.x) if b else self.x)

    def device(self, i=0, a=0, b=0, core=0):
        z, y, x = self.chip(i, a, b)
        return (z * 2 + y, x * 2 + (flip(self.core) if core else self.core))

    def partners(self):
        return [
            self.device(core=1),
            self.device(b=1),
            self.device(a=1),
            self.device(i=1),
            self.device(i=2),
            self.device(i=3),
        ]

    def block(self, by_rows, i, a, b, core=0):
        z, y, x = self.chip(i, a, b)
        c = flip(self.core) if core else self.core
        if by_rows:
            row, col = z * 2 + y, x * 2 + c
        else:
            row, col = (x * 2 + c) * 2 + y, z
        return (
            pl.ds(pl.multiple_of(row * BLOCK_ROWS, 16), BLOCK_ROWS),
            pl.ds(pl.multiple_of(col * BLOCK_COLS, 128), BLOCK_COLS),
        )


def greet(place):
    barrier = pltpu.get_barrier_semaphore()
    partners = place.partners()
    for partner in partners:
        pl.semaphore_signal(
            barrier, inc=1, device_id=partner, device_id_type=pl.DeviceIdType.MESH
        )
    pl.semaphore_wait(barrier, len(partners))


def send(source, target, send_sem, recv_sem, device):
    return pltpu.make_async_remote_copy(
        src_ref=source,
        dst_ref=target,
        send_sem=send_sem,
        recv_sem=recv_sem,
        device_id=device,
        device_id_type=pl.DeviceIdType.MESH,
    )


GATHER_SENDS = 16 + 6 + 6 + 3


def gather_actions(place, by_rows, own_refs, full_refs, local_sems, send_sems, link_sems, core_sems):
    weights = range(len(own_refs))
    counts = [0] * len(own_refs)

    def forward(w, source, piece, i=0, a=0, b=0, core=0):
        pi, pa, pb = piece
        name = (pi if i == 0 else i) * 4 + (pa ^ a) * 2 + (pb ^ b)
        target = full_refs[w].at[place.block(by_rows[w], pi, pa, pb)]
        sems = core_sems if core else link_sems
        copy = send(
            source,
            target,
            send_sems.at[w, counts[w]],
            sems.at[w, name],
            place.device(i, a, b, core),
        )
        counts[w] += 1
        copy.start()

    def arrive(w, piece, core=0):
        i, a, b = piece
        target = full_refs[w].at[place.block(by_rows[w], i, a, b, core)]
        sems = core_sems if core else link_sems
        name = i * 4 + a * 2 + b
        send(
            target, target, send_sems.at[w, 0], sems.at[w, name], place.device(core=1)
        ).wait_recv()
        return target

    def begin():
        greet(place)
        for w in weights:
            local = pltpu.make_async_copy(
                own_refs[w], full_refs[w].at[place.block(by_rows[w], 0, 0, 0)], local_sems.at[w]
            )
            local.start()
            own = (0, 0, 0)
            for step in (1, 3, 2):
                forward(w, own_refs[w], own, i=step)
            forward(w, own_refs[w], own, b=1)
            forward(w, own_refs[w], own, a=1)
            forward(w, own_refs[w], own, core=1)

    def pass_on(w, i, a, b):
        def step():
            piece = (i, a, b)
            source = arrive(w, piece)
            if not a and not b:
                forward(w, source, piece, b=1)
                forward(w, source, piece, a=1)
            elif a and not b and i in VIA_X:
                forward(w, source, piece, b=1)
            elif b and not a and i not in VIA_X:
                forward(w, source, piece, a=1)
            forward(w, source, piece, core=1)

        return step

    steps = [begin]
    for w in weights:
        order = [(1, 0, 0), (0, 1, 0), (0, 0, 1), (3, 0, 0), (1, 0, 1), (1, 1, 0), (2, 0, 0)]
        order += [(3, 1, 0), (3, 0, 1), (2, 0, 1), (2, 1, 0), (0, 1, 1), (1, 1, 1), (3, 1, 1), (2, 1, 1)]
        steps += [pass_on(w, *piece) for piece in order]

    def finish():
        for w in weights:
            for i in range(4):
                for a in range(2):
                    for b in range(2):
                        arrive(w, (i, a, b), core=1)
            pltpu.make_async_copy(
                own_refs[w], full_refs[w].at[place.block(by_rows[w], 0, 0, 0)], local_sems.at[w]
            ).wait()
            for n in range(counts[w]):
                send(
                    own_refs[w], own_refs[w], send_sems.at[w, n], link_sems.at[w, 0],
                    place.device(core=1),
                ).wait_send()

    return steps + [finish]


def gather_kernel(by_rows, *refs):
    count = len(by_rows)
    own_refs, full_refs = refs[:count], refs[count : 2 * count]
    place = Place()
    for step in gather_actions(place, by_rows, own_refs, full_refs, *refs[2 * count :]):
        step()


def gather_scratch(count):
    return [
        pltpu.SemaphoreType.DMA((count,)),
        pltpu.SemaphoreType.DMA((count, GATHER_SENDS)),
        pltpu.SemaphoreType.DMA((count, 16)),
        pltpu.SemaphoreType.DMA((count, 16)),
    ]


def gather_blocks(blocks, by_rows, collective_id):
    count = len(blocks)
    whole = jax.ShapeDtypeStruct((8 * BLOCK_ROWS, 4 * BLOCK_COLS), jnp.bfloat16)
    return pl.pallas_call(
        functools.partial(gather_kernel, by_rows),
        in_specs=[pl.BlockSpec(memory_space=pltpu.VMEM)] * count,
        out_specs=[pl.BlockSpec(memory_space=pl.ANY)] * count,
        out_shape=[whole] * count,
        scratch_shapes=gather_scratch(count),
        compiler_params=pltpu.CompilerParams(
            collective_id=collective_id, has_side_effects=True, vmem_limit_bytes=VMEM_LIMIT
        ),
        name="gather_blocks",
    )(*blocks)


SCATTER_SENDS = 16 + 6 + 6 + 3


def scatter_actions(
    place,
    by_rows,
    grad_refs,
    out_refs,
    held_refs,
    over_x,
    over_y,
    over_z,
    stage,
    stage_sems,
    send_sems,
    held_sems,
    x_sems,
    y_sems,
    z_sems,
):
    weights = range(len(grad_refs))
    counts = [0] * len(grad_refs)
    chips = [(i, a, b) for i in (1, 3, 2, 0) for a, b in ((1, 1), (0, 1), (1, 0), (0, 0))]
    slot = lambda i, a, b: i * 4 + a * 2 + b

    def ship(w, source, target, recv_sem, device):
        copy = send(source, target, send_sems.at[w, counts[w]], recv_sem, device)
        counts[w] += 1
        copy.start()

    def landed(target, recv_sem):
        send(target, target, send_sems.at[0, 0], recv_sem, place.device(core=1)).wait_recv()

    def begin():
        greet(place)
        for w in weights:
            for i, a, b in chips:
                source = grad_refs[w].at[place.block(by_rows[w], i, a, b, core=1)]
                s = slot(i, a, b)
                ship(w, source, held_refs.at[w, s], held_sems.at[w, s], place.device(core=1))

    order = [(w, chip) for w in weights for chip in chips]

    def load(n):
        w, (i, a, b) = order[n]
        return pltpu.make_async_copy(
            grad_refs[w].at[place.block(by_rows[w], i, a, b)], stage.at[n % 4], stage_sems.at[n % 4]
        )

    def fold(n):
        def step():
            if n == 0:
                for ahead in range(3):
                    load(ahead).start()
            if n + 3 < len(order):
                load(n + 3).start()
            w, (i, a, b) = order[n]
            s = slot(i, a, b)
            load(n).wait()
            landed(held_refs.at[w, s], held_sems.at[w, s])
            held = held_refs.at[w, s]
            held[...] = held[...] + stage[n % 4]
            via_x = i in VIA_X
            if a and b:
                if via_x:
                    ship(w, held, over_x.at[w, 4 + VIA_X.index(i)], x_sems.at[w, 4 + VIA_X.index(i)], place.device(b=1))
                else:
                    k = 4 + (i - 1)
                    ship(w, held, over_y.at[w, k], y_sems.at[w, k], place.device(a=1))
            elif b and via_x:
                ship(w, held, over_x.at[w, i], x_sems.at[w, i], place.device(b=1))
            elif a and not via_x:
                ship(w, held, over_y.at[w, i], y_sems.at[w, i], place.device(a=1))

        return step

    def second(w, i):
        def step():
            if i in VIA_X:
                k = 4 + VIA_X.index(i)
                landed(over_x.at[w, k], x_sems.at[w, k])
                held = held_refs.at[w, slot(i, 1, 0)]
                held[...] = held[...] + over_x[w, k]
                ship(w, held, over_y.at[w, i], y_sems.at[w, i], place.device(a=1))
            else:
                k = 4 + (i - 1)
                landed(over_y.at[w, k], y_sems.at[w, k])
                held = held_refs.at[w, slot(i, 0, 1)]
                held[...] = held[...] + over_y[w, k]
                ship(w, held, over_x.at[w, i], x_sems.at[w, i], place.device(b=1))

        return step

    def third(w, i):
        def step():
            landed(over_x.at[w, i], x_sems.at[w, i])
            landed(over_y.at[w, i], y_sems.at[w, i])
            held = held_refs.at[w, slot(i, 0, 0)]
            total = held[...].astype(jnp.float32) + over_x[w, i].astype(jnp.float32)
            total = total + over_y[w, i].astype(jnp.float32)
            held[...] = total.astype(jnp.bfloat16)
            if i:
                ship(w, held, over_z.at[w, i - 1], z_sems.at[w, i - 1], place.device(i=i))

        return step

    def last(w):
        def step():
            total = held_refs[w, 0].astype(jnp.float32)
            for i in (1, 3, 2):
                landed(over_z.at[w, i - 1], z_sems.at[w, i - 1])
                total = total + over_z[w, i - 1].astype(jnp.float32)
            out_refs[w][...] = total

        return step

    def finish():
        for w in weights:
            block = held_refs.at[w, 0]
            for n in range(counts[w]):
                send(
                    block, block, send_sems.at[w, n], held_sems.at[w, 0], place.device(core=1)
                ).wait_send()

    steps = [begin]
    per = len(chips)
    for w in weights:
        for n in range(per):
            steps.append(fold(w * per + n))
            if n == 11:
                steps.append(second(w, 1))
        for i in (3, 2, 0):
            steps.append(second(w, i))
        for i in (1, 3, 2, 0):
            steps.append(third(w, i))
    for w in weights:
        steps.append(last(w))
    return steps + [finish]


def scatter_scratch(count):
    blocks = lambda n: pltpu.VMEM((count, n, BLOCK_ROWS, BLOCK_COLS), jnp.bfloat16)
    return [
        blocks(16),
        blocks(6),
        blocks(6),
        blocks(3),
        pltpu.VMEM((4, BLOCK_ROWS, BLOCK_COLS), jnp.bfloat16),
        pltpu.SemaphoreType.DMA((4,)),
        pltpu.SemaphoreType.DMA((count, SCATTER_SENDS)),
        pltpu.SemaphoreType.DMA((count, 16)),
        pltpu.SemaphoreType.DMA((count, 6)),
        pltpu.SemaphoreType.DMA((count, 6)),
        pltpu.SemaphoreType.DMA((count, 3)),
    ]


def scatter_kernel(by_rows, *refs):
    count = len(by_rows)
    place = Place()
    for step in scatter_actions(
        place, by_rows, refs[:count], refs[count : 2 * count], *refs[2 * count :]
    ):
        step()


def scatter_blocks(grads, by_rows, collective_id):
    count = len(grads)
    block = jax.ShapeDtypeStruct((BLOCK_ROWS, BLOCK_COLS), jnp.float32)
    return pl.pallas_call(
        functools.partial(scatter_kernel, by_rows),
        in_specs=[pl.BlockSpec(memory_space=pl.ANY)] * count,
        out_specs=[pl.BlockSpec(memory_space=pltpu.VMEM)] * count,
        out_shape=[block] * count,
        scratch_shapes=scatter_scratch(count),
        compiler_params=pltpu.CompilerParams(
            collective_id=collective_id, has_side_effects=True, vmem_limit_bytes=VMEM_LIMIT
        ),
        name="scatter_blocks",
    )(*grads)


def project_kernel(hidden_ref, weight_ref, out_ref):
    rows = out_ref.shape[0]
    span = -(-rows // 128) * 128
    wide = dot_nn(hidden_ref[...], weight_ref[:, :span]).astype(jnp.bfloat16)
    out_ref[...] = jnp.transpose(wide)[:rows]


def project_qkv(hidden, weights):
    tokens, width = hidden.shape
    groups = weights.shape[1] // BLOCK_COLS
    rows = 3 * D // groups
    return pl.pallas_call(
        project_kernel,
        grid=(groups,),
        in_specs=[
            pl.BlockSpec((tokens, width), lambda g: (0, 0)),
            pl.BlockSpec((width, BLOCK_COLS), lambda g: (0, g)),
        ],
        out_specs=pl.BlockSpec((rows, tokens), lambda g: (g, 0)),
        out_shape=jax.ShapeDtypeStruct((groups * rows, tokens), jnp.bfloat16),
        compiler_params=pltpu.CompilerParams(vmem_limit_bytes=VMEM_LIMIT),
        name="project_qkv",
    )(hidden, weights)


def project_back_kernel(hidden_t_ref, weight_ref, grad_ref, proj_ref, grad_hidden_ref, out_ref):
    group = pl.program_id(0)
    rows = grad_ref.shape[0]
    proj_cols = BLOCK_COLS - rows
    grad = grad_ref[...]

    @pl.when(group == 0)
    def _():
        grad_hidden_ref[...] = jnp.zeros_like(grad_hidden_ref)

    grad_hidden_ref[...] += dot_nt(jnp.transpose(grad), weight_ref[:, :rows])
    out_ref[:, :rows] = dot_nt(hidden_t_ref[...], grad).astype(jnp.bfloat16)
    for g in range(D // proj_cols):

        @pl.when(group == g)
        def _():
            out_ref[:, rows:] = proj_ref[:, g * proj_cols : (g + 1) * proj_cols]


def project_back(hidden_t, weights, grad, grad_proj):
    width, tokens = hidden_t.shape
    groups = weights.shape[1] // BLOCK_COLS
    rows = grad.shape[0] // groups
    return pl.pallas_call(
        project_back_kernel,
        grid=(groups,),
        in_specs=[
            pl.BlockSpec((width, tokens), lambda g: (0, 0)),
            pl.BlockSpec((width, BLOCK_COLS), lambda g: (0, g)),
            pl.BlockSpec((rows, tokens), lambda g: (g, 0)),
            pl.BlockSpec((width, D), lambda g: (0, 0)),
        ],
        out_specs=[
            pl.BlockSpec((tokens, width), lambda g: (0, 0)),
            pl.BlockSpec((width, BLOCK_COLS), lambda g: (0, g)),
        ],
        out_shape=[
            jax.ShapeDtypeStruct((tokens, width), jnp.float32),
            jax.ShapeDtypeStruct(weights.shape, jnp.bfloat16),
        ],
        compiler_params=pltpu.CompilerParams(vmem_limit_bytes=VMEM_LIMIT),
        name="project_back",
    )(hidden_t, weights, grad, grad_proj)


def swap_columns(shard):
    pairs = [(d, d ^ 1) for d in range(lax.axis_size("dp"))]
    odd = lax.axis_index("dp") % 2
    rows = shard.shape[0] // 2
    own = lax.dynamic_slice_in_dim(shard, odd * rows, rows, axis=0)
    other = lax.dynamic_slice_in_dim(shard, (1 - odd) * rows, rows, axis=0)
    other = lax.ppermute(other, "dp", pairs)
    return jnp.where(odd == 0, jnp.stack([own, other], 1), jnp.stack([other, own], 1))


def swap_rows(block):
    pairs = [(d, d ^ 1) for d in range(lax.axis_size("dp"))]
    odd = lax.axis_index("dp") % 2
    own = lax.dynamic_index_in_dim(block, odd, axis=1, keepdims=False)
    other = lax.dynamic_index_in_dim(block, 1 - odd, axis=1, keepdims=False)
    other = lax.ppermute(other, "dp", pairs)
    return jnp.where(odd == 0, jnp.concatenate([own, other], 0), jnp.concatenate([other, own], 0))


def swap_slots(values):
    moved = lax.all_to_all(values, "band", split_axis=0, concat_axis=0, tiled=True)
    return moved.reshape((-1,) + values.shape[2:])


def norm_parts(values):
    center = jnp.mean(values, axis=-1, keepdims=True)
    spread = jnp.mean((values - center) ** 2, axis=-1, keepdims=True)
    root = lax.rsqrt(spread + 1e-06)
    return ((values - center) * root, root)


def norm_back(grad, normal, root, scales):
    inner = grad * (1.0 + scales)
    return root * (
        inner
        - jnp.mean(inner, axis=-1, keepdims=True)
        - normal * jnp.mean(inner * normal, axis=-1, keepdims=True)
    )


def embed_tables(count):
    quarter = D // 4
    omegas = 1.0 / 10000.0 ** (jnp.arange(quarter, dtype=jnp.float32) / quarter)
    angles = jnp.arange(count, dtype=jnp.float32)[:, None] * omegas
    return jnp.concatenate([jnp.sin(angles), jnp.cos(angles)], axis=-1)


def grid_embed_slot(kind, tokens):
    table = embed_tables(SIDE)
    half = D // 2
    side = SIDE
    wide = jnp.concatenate(
        [
            jnp.broadcast_to(table[:, None, :], (side, side, half)),
            jnp.broadcast_to(table[None, :, :], (side, side, half)),
        ],
        axis=-1,
    ).reshape(tokens, D)
    small = side // 2
    table_small = table[:small]
    narrow = jnp.concatenate(
        [
            jnp.broadcast_to(table_small[None, :, None, :], (tokens // REGION, small, small, half)),
            jnp.broadcast_to(table_small[None, None, :, :], (tokens // REGION, small, small, half)),
        ],
        axis=-1,
    ).reshape(tokens, D)
    return jnp.where(kind == 1, narrow, wide)


def slot_device(
    kept_tokens,
    kept_index,
    resolution,
    labels,
    timesteps,
    class_table,
    cotangent,
    mask_token,
    w_qkv,
    w_proj,
    w_fc1,
    w_fc2,
    w_ada,
    mask_first,
    first_qkv,
    first_proj,
    first_fc1,
    first_fc2,
    first_ada,
    mask_second,
    second_qkv,
    second_proj,
    second_fc1,
    second_fc2,
    second_ada,
):
    highest = lax.Precision.HIGHEST
    bf16 = jnp.bfloat16
    bands = lax.axis_size("band")
    groups = lax.axis_size("dp")
    band = lax.axis_index("band")
    slots, local_rows, _ = cotangent.shape
    tokens_count = bands * local_rows
    regions = tokens_count // REGION
    images = labels.shape[1]

    picks = lax.all_gather(jnp.concatenate([labels, timesteps], axis=1), "dp", axis=0, tiled=True)
    rows_ada, cols_ada = w_ada.shape
    count = picks.shape[0] * images
    all_labels = picks[:, :images].reshape(count)
    all_times = picks[:, images:].reshape(count)
    table_part = lax.dynamic_slice_in_dim(class_table, band * rows_ada, rows_ada, axis=1)
    chosen = (all_labels[:, None] == jnp.arange(class_table.shape[0])[None, :]).astype(jnp.float32)
    features = band * rows_ada + jnp.arange(rows_ada)
    half_width = D // 2
    frequency = jnp.exp(
        -math.log(10000.0) * (features % half_width).astype(jnp.float32) / half_width
    )
    angles = all_times.astype(jnp.float32)[:, None] * frequency
    waves = jnp.where(features < half_width, jnp.cos(angles), jnp.sin(angles))
    condition = jnp.matmul(chosen, table_part, precision=highest) + waves
    cond_low = jax.nn.silu(condition).astype(bf16)
    partial = jnp.matmul(cond_low, w_ada.astype(bf16), preferred_element_type=jnp.float32)
    partial = partial.reshape(groups, slots, images, cols_ada).transpose(1, 0, 2, 3)
    own_rows = lax.psum_scatter(partial, "band", scatter_dimension=0, tiled=True)[0]
    modulation = lax.all_to_all(own_rows, "dp", split_axis=0, concat_axis=0, tiled=True)
    modulation = modulation.transpose(1, 0, 2).reshape(images, groups * cols_ada)

    kind = lax.dynamic_slice_in_dim(resolution, band, 1)
    kept = swap_slots(kept_tokens)
    index = swap_slots(kept_index)
    grad_out = swap_slots(cotangent).reshape(regions, REGION, D)

    mod = jnp.where(kind[0] == 1, modulation, modulation[:1])
    shift_attn, scale_attn, gate_attn, shift_mlp, scale_mlp, gate_mlp = [
        piece[:, None, :] for piece in jnp.split(mod, 6, axis=-1)
    ]
    select = jnp.arange(tokens_count)[:, None] == index[None, :]
    select_low = select.astype(bf16)
    unfilled = 1.0 - jnp.sum(select.astype(jnp.float32), axis=1, keepdims=True)
    placed = jnp.matmul(select_low, kept, preferred_element_type=jnp.float32)
    tokens = placed + unfilled * mask_token + grid_embed_slot(kind[0], tokens_count)
    tokens = tokens.reshape(regions, REGION, D)

    qkv_cols, proj_cols, fc1_cols = w_qkv.shape[1], w_proj.shape[1], w_fc1.shape[1]
    swapped = swap_columns(jnp.concatenate([w_qkv, w_proj, w_fc1], axis=1).astype(bf16))
    joined_block = jnp.concatenate(
        [
            swapped[:, :, :qkv_cols].reshape(-1, 2 * qkv_cols),
            swapped[:, :, qkv_cols:-fc1_cols].reshape(-1, 2 * proj_cols),
        ],
        axis=1,
    )
    fc1_block = swapped[:, :, -fc1_cols:].reshape(-1, 2 * fc1_cols)
    (joined_full,) = gather_blocks([joined_block], (False,), 0)
    fc1_full, fc2_full = gather_blocks([fc1_block, w_fc2.astype(bf16).T], (False, True), 1)
    proj_full = joined_full.reshape(D, -1, BLOCK_COLS)[:, :, 2 * qkv_cols :].reshape(D, D)

    normal_attn, root_attn = norm_parts(tokens)
    hidden = (normal_attn * (1.0 + scale_attn) + shift_attn).astype(bf16).reshape(tokens_count, D)
    qkv = project_qkv(hidden, joined_full)
    qkv_heads = qkv.reshape(3 * HEADS, HEAD_DIM, tokens_count)
    attended, lse = attn_forward(kind, qkv_heads)
    attended_t = attended.reshape(D, tokens_count)
    branch = lax.dot_general(
        attended_t, proj_full, (((0,), (0,)), ((), ())), preferred_element_type=jnp.float32
    ).reshape(regions, REGION, D)
    middle = tokens + gate_attn * branch
    normal_mlp, root_mlp = norm_parts(middle)
    hidden_mlp = (normal_mlp * (1.0 + scale_mlp) + shift_mlp).astype(bf16).reshape(tokens_count, D)
    grad_full = grad_out.astype(jnp.float32)
    grad_output = (gate_mlp * grad_full).astype(bf16).reshape(tokens_count, D)

    output, grad_hidden_mlp, grad_fc1, grad_fc2 = mlp_both(
        hidden_mlp, hidden_mlp.T, grad_output, grad_output.T, fc1_full, fc2_full, 512
    )
    output = output.reshape(regions, REGION, D)
    grad_hidden_mlp = grad_hidden_mlp.reshape(regions, REGION, D)
    block_slot = (middle + gate_mlp * output).astype(bf16)
    block_out = lax.all_to_all(
        block_slot.reshape(bands, local_rows, D), "band", split_axis=0, concat_axis=0, tiled=True
    )
    grad_gate_mlp = jnp.sum(grad_full * output, axis=1)
    grad_shift_mlp = jnp.sum(grad_hidden_mlp, axis=1)
    grad_scale_mlp = jnp.sum(grad_hidden_mlp * normal_mlp, axis=1)
    grad_middle = grad_full + norm_back(grad_hidden_mlp, normal_mlp, root_mlp, scale_mlp)
    grad_gate_attn = jnp.sum(grad_middle * branch, axis=1)
    grad_branch = (gate_attn * grad_middle).astype(bf16).reshape(tokens_count, D)
    grad_proj = dot_nn(attended_t, grad_branch).astype(bf16)
    grad_attended = dot_nt(proj_full, grad_branch).astype(bf16)
    grad_heads = grad_attended.reshape(HEADS, HEAD_DIM, tokens_count)
    grad_qkv = attn_backward(kind, qkv_heads, attended, grad_heads, lse)
    grad_qkv = grad_qkv.reshape(3 * D, tokens_count)
    grad_hidden, grad_joined = project_back(hidden.T, joined_full, grad_qkv, grad_proj)
    grad_hidden = grad_hidden.reshape(regions, REGION, D)
    grad_shift_attn = jnp.sum(grad_hidden, axis=1)
    grad_scale_attn = jnp.sum(grad_hidden * normal_attn, axis=1)
    grad_tokens = grad_middle + norm_back(grad_hidden, normal_attn, root_attn, scale_attn)
    grad_tokens = grad_tokens.reshape(tokens_count, D)

    grad_mod = jnp.concatenate(
        [
            grad_shift_attn,
            grad_scale_attn,
            grad_gate_attn,
            grad_shift_mlp,
            grad_scale_mlp,
            grad_gate_mlp,
        ],
        axis=-1,
    )
    first_only = (jnp.arange(images) == 0).astype(jnp.float32)[:, None]
    grad_mod = jnp.where(
        kind[0] == 1, grad_mod, first_only * jnp.sum(grad_mod, axis=0, keepdims=True)
    )
    grad_mod = grad_mod.reshape(images, groups, cols_ada).transpose(1, 0, 2)
    grad_mod = lax.all_to_all(grad_mod, "dp", split_axis=0, concat_axis=0, tiled=True)
    grad_mod = lax.all_gather(grad_mod, "band", axis=1, tiled=True)
    red_ada = lax.dot_general(
        cond_low.astype(jnp.float32),
        grad_mod.reshape(count, cols_ada),
        (((0,), (0,)), ((), ())),
        precision=highest,
        preferred_element_type=jnp.float32,
    )

    grad_kept = lax.dot_general(
        select_low, grad_tokens.astype(bf16), (((0,), (0,)), ((), ())),
        preferred_element_type=jnp.float32,
    ).astype(bf16)
    kept_grad = lax.all_to_all(
        grad_kept.reshape(bands, -1, D), "band", split_axis=0, concat_axis=0, tiled=True
    ).astype(jnp.float32)
    grad_mask_part = jnp.sum(unfilled * grad_tokens, axis=0)

    sum_fc1, sum_fc2 = scatter_blocks([grad_fc1, grad_fc2], (False, True), 2)
    (sum_joined,) = scatter_blocks([grad_joined], (False,), 3)
    sums = jnp.concatenate(
        [
            sum_joined[:, : 2 * qkv_cols].reshape(-1, 2, qkv_cols),
            sum_joined[:, 2 * qkv_cols :].reshape(-1, 2, proj_cols),
            sum_fc1.reshape(-1, 2, fc1_cols),
        ],
        axis=2,
    )
    sums = swap_rows(sums.astype(bf16)).astype(jnp.float32)
    red_qkv = sums[:, :qkv_cols]
    red_proj = sums[:, qkv_cols:-fc1_cols]
    red_fc1 = sums[:, -fc1_cols:]
    red_fc2 = sum_fc2.T
    grad_mask = lax.psum(grad_mask_part, ("dp", "band"))
    reduced = (red_qkv, red_proj, red_fc1, red_fc2, red_ada)
    local_squares = sum((jnp.sum(grad * grad) for grad in reduced))
    total_squares = lax.psum(local_squares, ("dp", "band")) + jnp.sum(grad_mask * grad_mask)
    norm_value = jnp.sqrt(total_squares)
    factor = clip_level / jnp.maximum(norm_value, clip_level)
    mask_new = adamw(mask_token, mask_first, mask_second, grad_mask * factor)
    qkv_new = adamw(w_qkv, first_qkv, second_qkv, red_qkv * factor)
    proj_new = adamw(w_proj, first_proj, second_proj, red_proj * factor)
    fc1_new = adamw(w_fc1, first_fc1, second_fc1, red_fc1 * factor)
    fc2_new = adamw(w_fc2, first_fc2, second_fc2, red_fc2 * factor)
    ada_new = adamw(w_ada, first_ada, second_ada, red_ada * factor)
    moved = tuple(zip(mask_new, qkv_new, proj_new, fc1_new, fc2_new, ada_new))
    return (block_out, kept_grad, norm_value) + moved[0] + moved[1] + moved[2]


def per_device(*arguments):
    cotangent = arguments[6]
    if (lax.axis_size("dp"), lax.axis_size("band")) == (8, cotangent.shape[0]):
        return slot_device(*arguments)
    return general_device(*arguments)


def solution(mesh):
    in_specs = (
        P("dp", "band", None),
        P("dp", "band"),
        P("dp"),
        P("dp", None),
        P("dp", None),
        P(),
        P("dp", "band", None),
        P(),
        P("band", "dp"),
        P("band", "dp"),
        P("band", "dp"),
        P("band", "dp"),
        P("band", "dp"),
        P(),
        P("band", "dp"),
        P("band", "dp"),
        P("band", "dp"),
        P("band", "dp"),
        P("band", "dp"),
        P(),
        P("band", "dp"),
        P("band", "dp"),
        P("band", "dp"),
        P("band", "dp"),
        P("band", "dp"),
    )
    out_specs = (
        P("dp", "band", None),
        P("dp", "band", None),
        P(),
        P(),
        P("band", "dp"),
        P("band", "dp"),
        P("band", "dp"),
        P("band", "dp"),
        P("band", "dp"),
        P(),
        P("band", "dp"),
        P("band", "dp"),
        P("band", "dp"),
        P("band", "dp"),
        P("band", "dp"),
        P(),
        P("band", "dp"),
        P("band", "dp"),
        P("band", "dp"),
        P("band", "dp"),
        P("band", "dp"),
    )
    return jax.shard_map(
        per_device, mesh=mesh, in_specs=in_specs, out_specs=out_specs, check_vma=False
    )
```

```python
import functools
import math

import jax
import jax.numpy as jnp
from jax import lax
from jax.experimental import pallas as pl
from jax.experimental.pallas import tpu as pltpu
from jax.sharding import PartitionSpec as P

D = 1152
HEADS = 16
HEAD_DIM = 72
SIDE = 32
STEP = 10
REGION = 256


learn_rate = 0.1
beta_first = 0.9
beta_second = 0.95
adam_eps = 1e-08
decay_rate = 0.1
clip_level = 1.0


def time_embed(timestep):
    half_width = D // 2
    frequency = jnp.exp(-math.log(10000.0) * jnp.arange(half_width, dtype=jnp.float32) / half_width)
    angles = timestep.astype(jnp.float32)[..., None] * frequency
    return jnp.concatenate([jnp.cos(angles), jnp.sin(angles)], axis=-1)


def grid_embed(grid_rows, grid_cols):
    quarter = D // 4
    omegas = 1.0 / 10000.0 ** (jnp.arange(quarter, dtype=jnp.float32) / quarter)
    row_angle = grid_rows.astype(jnp.float32)[..., None] * omegas
    col_angle = grid_cols.astype(jnp.float32)[..., None] * omegas
    return jnp.concatenate(
        [jnp.sin(row_angle), jnp.cos(row_angle), jnp.sin(col_angle), jnp.cos(col_angle)], axis=-1
    )


def slot_layout(positions, slot_kinds):
    small_side = SIDE // 2
    region = positions // REGION
    inside = positions % REGION
    grid_rows = jnp.where(slot_kinds == 1, inside // small_side, positions // SIDE)
    grid_cols = jnp.where(slot_kinds == 1, inside % small_side, positions % SIDE)
    image_id = jnp.where(slot_kinds == 1, region, 0)
    return (grid_rows, grid_cols, image_id)


def modulate(values, shifts, scales):
    center = jnp.mean(values, axis=-1, keepdims=True)
    spread = jnp.mean((values - center) ** 2, axis=-1, keepdims=True)
    return (values - center) * lax.rsqrt(spread + 1e-06) * (1.0 + scales) + shifts


def gelu_tanh(values):
    return jax.nn.gelu(values, approximate=True)


def pick_rows(table_rows, picks):
    return table_rows[picks]


def allowed_pairs(query_pos, key_pos, slot_kinds):
    same_region = (query_pos // REGION)[None, :, None] == (key_pos // REGION)[None, None, :]
    return (slot_kinds[:, None, None] == 0) | same_region


def attend(queries, keys_in, values_in, allowed):

    def one_slot(pieces):
        query_s, key_s, value_s, allow_s = pieces
        scores = jnp.einsum(
            "qhd,khd->hqk", query_s, key_s, preferred_element_type=jnp.float32
        ) * HEAD_DIM ** (-0.5)
        scores = jnp.where(allow_s[None], scores, -1e30)
        row_peak = jnp.max(scores, axis=-1, keepdims=True)
        row_total = jnp.sum(jnp.exp(scores - row_peak), axis=-1, keepdims=True)
        log_total = row_peak + jnp.log(row_total)
        weights_soft = jnp.exp(scores - log_total).astype(jnp.bfloat16)
        result = jnp.einsum(
            "hqk,khd->qhd", weights_soft, value_s, preferred_element_type=jnp.float32
        )
        return (result.astype(jnp.bfloat16), log_total)

    return lax.map(one_slot, (queries, keys_in, values_in, allowed))


def attend_back(queries, keys_in, values_in, allowed, log_total, grad_attended):

    def one_slot(pieces):
        query_s, key_s, value_s, allow_s, total_s, grad_s = pieces
        scores = jnp.einsum(
            "qhd,khd->hqk", query_s, key_s, preferred_element_type=jnp.float32
        ) * HEAD_DIM ** (-0.5)
        scores = jnp.where(allow_s[None], scores, -1e30)
        weights_full = jnp.exp(scores - total_s)
        weights_soft = weights_full.astype(jnp.bfloat16)
        grad_weights = jnp.einsum(
            "qhd,khd->hqk", grad_s, value_s, preferred_element_type=jnp.float32
        )
        row_dot = jnp.sum(weights_full * grad_weights, axis=-1, keepdims=True)
        grad_scores = (weights_full * (grad_weights - row_dot) * HEAD_DIM ** (-0.5)).astype(
            jnp.bfloat16
        )
        grad_queries = jnp.einsum(
            "hqk,khd->qhd", grad_scores, key_s, preferred_element_type=jnp.float32
        )
        grad_keys = jnp.einsum(
            "hqk,qhd->khd", grad_scores, query_s, preferred_element_type=jnp.float32
        )
        grad_values = jnp.einsum(
            "hqk,qhd->khd", weights_soft, grad_s, preferred_element_type=jnp.float32
        )
        return (grad_queries, grad_keys, grad_values)

    return lax.map(one_slot, (queries, keys_in, values_in, allowed, log_total, grad_attended))


def adamw(weight, first, second, grad):
    first_new = beta_first * first + (1.0 - beta_first) * grad
    second_new = beta_second * second + (1.0 - beta_second) * grad * grad
    first_hat = first_new / (1.0 - beta_first**STEP)
    second_hat = second_new / (1.0 - beta_second**STEP)
    weight_new = weight - learn_rate * (
        first_hat / (jnp.sqrt(second_hat) + adam_eps) + decay_rate * weight
    )
    return (weight_new, first_new, second_new)


def general_device(
    kept_tokens,
    kept_index,
    resolution,
    labels,
    timesteps,
    class_table,
    cotangent,
    mask_token,
    w_qkv,
    w_proj,
    w_fc1,
    w_fc2,
    w_ada,
    mask_first,
    first_qkv,
    first_proj,
    first_fc1,
    first_fc2,
    first_ada,
    mask_second,
    second_qkv,
    second_proj,
    second_fc1,
    second_fc2,
    second_ada,
):
    highest = lax.Precision.HIGHEST
    band_index = lax.axis_index("band")
    slot_count = cotangent.shape[0]
    local_rows = cotangent.shape[1]
    qkv_low = w_qkv.astype(jnp.bfloat16)
    proj_low = w_proj.astype(jnp.bfloat16)
    fc1_low = w_fc1.astype(jnp.bfloat16)
    fc2_low = w_fc2.astype(jnp.bfloat16)
    ada_low = w_ada.astype(jnp.bfloat16)
    cols_qkv, cols_proj, cols_fc1, cols_fc2, cols_ada = (
        lax.all_gather(qkv_low, "dp", axis=1, tiled=True),
        lax.all_gather(proj_low, "dp", axis=1, tiled=True),
        lax.all_gather(fc1_low, "dp", axis=1, tiled=True),
        lax.all_gather(fc2_low, "dp", axis=1, tiled=True),
        lax.all_gather(ada_low, "dp", axis=1, tiled=True),
    )
    condition = jnp.take(class_table, labels, axis=0) + time_embed(timesteps)
    cond_low = jax.nn.silu(condition).astype(jnp.bfloat16)
    qkv_full, proj_full, fc1_full, fc2_full, ada_full = (
        lax.all_gather(cols_qkv, "band", axis=0, tiled=True),
        lax.all_gather(cols_proj, "band", axis=0, tiled=True),
        lax.all_gather(cols_fc1, "band", axis=0, tiled=True),
        lax.all_gather(cols_fc2, "band", axis=0, tiled=True),
        lax.all_gather(cols_ada, "band", axis=0, tiled=True),
    )
    modulation = jnp.einsum("sid,de->sie", cond_low, ada_full, preferred_element_type=jnp.float32)
    kept_all, index_all = (
        lax.all_gather(kept_tokens, "band", axis=1, tiled=True),
        lax.all_gather(kept_index, "band", axis=1, tiled=True),
    )
    positions = band_index * local_rows + jnp.arange(local_rows)
    select = index_all[:, None, :] == positions[None, :, None]
    placed = jnp.einsum(
        "spj,sjd->spd", select.astype(jnp.bfloat16), kept_all, preferred_element_type=jnp.float32
    )
    unfilled = 1.0 - jnp.sum(select.astype(jnp.float32), axis=2)
    grid_rows, grid_cols, image_id = slot_layout(positions[None, :], resolution[:, None])
    tokens = placed + unfilled[..., None] * mask_token + grid_embed(grid_rows, grid_cols)
    token_mod = jax.vmap(pick_rows)(modulation, image_id)
    shift_attn, scale_attn, gate_attn, shift_mlp, scale_mlp, gate_mlp = jnp.split(
        token_mod, 6, axis=-1
    )
    attn_value, attn_pull = jax.vjp(modulate, tokens, shift_attn, scale_attn)
    hidden = attn_value.astype(jnp.bfloat16)
    qkv = jnp.einsum("std,de->ste", hidden, qkv_full, preferred_element_type=jnp.float32).astype(
        jnp.bfloat16
    )
    queries = qkv[..., :D].reshape(slot_count, local_rows, HEADS, HEAD_DIM)
    keys_in = qkv[..., D : 2 * D].reshape(slot_count, local_rows, HEADS, HEAD_DIM)
    values_in = qkv[..., 2 * D :].reshape(slot_count, local_rows, HEADS, HEAD_DIM)
    keys_all, values_all = (
        lax.all_gather(keys_in, "band", axis=1, tiled=True),
        lax.all_gather(values_in, "band", axis=1, tiled=True),
    )
    allowed = allowed_pairs(positions, jnp.arange(keys_all.shape[1]), resolution)
    attended, log_total = attend(queries, keys_all, values_all, allowed)
    attended_flat = attended.reshape(slot_count, local_rows, D)
    branch = jnp.einsum("std,de->ste", attended_flat, proj_full, preferred_element_type=jnp.float32)
    middle = tokens + gate_attn * branch
    mlp_value, mlp_pull = jax.vjp(modulate, middle, shift_mlp, scale_mlp)
    hidden_mlp = mlp_value.astype(jnp.bfloat16)
    upward = jnp.einsum("std,df->stf", hidden_mlp, fc1_full, preferred_element_type=jnp.float32)
    active_value, gelu_pull = jax.vjp(gelu_tanh, upward)
    active = active_value.astype(jnp.bfloat16)
    output = jnp.einsum("stf,fd->std", active, fc2_full, preferred_element_type=jnp.float32)
    block_out = (middle + gate_mlp * output).astype(jnp.bfloat16)
    grad_out = cotangent.astype(jnp.float32)
    grad_gate_mlp = grad_out * output
    grad_output = (gate_mlp * grad_out).astype(jnp.bfloat16)
    grad_fc2 = jnp.einsum("stf,std->fd", active, grad_output, preferred_element_type=jnp.float32)
    grad_active = jnp.einsum(
        "std,fd->stf", grad_output, fc2_full, preferred_element_type=jnp.float32
    )
    grad_upward = gelu_pull(grad_active)[0].astype(jnp.bfloat16)
    grad_fc1 = jnp.einsum(
        "std,stf->df", hidden_mlp, grad_upward, preferred_element_type=jnp.float32
    )
    grad_hidden_mlp = jnp.einsum(
        "stf,df->std", grad_upward, fc1_full, preferred_element_type=jnp.float32
    )
    grad_mid_norm, grad_shift_mlp, grad_scale_mlp = mlp_pull(grad_hidden_mlp)
    grad_middle = grad_out + grad_mid_norm
    grad_gate_attn = grad_middle * branch
    grad_branch = (gate_attn * grad_middle).astype(jnp.bfloat16)
    grad_proj = jnp.einsum(
        "std,ste->de", attended_flat, grad_branch, preferred_element_type=jnp.float32
    )
    grad_attended = jnp.einsum(
        "ste,de->std", grad_branch, proj_full, preferred_element_type=jnp.float32
    ).astype(jnp.bfloat16)
    grad_attended = grad_attended.reshape(slot_count, local_rows, HEADS, HEAD_DIM)
    grad_queries, grad_keys_part, grad_values_part = attend_back(
        queries, keys_all, values_all, allowed, log_total, grad_attended
    )
    grad_keys, grad_values = (
        lax.psum_scatter(
            grad_keys_part.astype(jnp.bfloat16), "band", scatter_dimension=1, tiled=True
        ).astype(jnp.float32),
        lax.psum_scatter(
            grad_values_part.astype(jnp.bfloat16), "band", scatter_dimension=1, tiled=True
        ).astype(jnp.float32),
    )
    grad_qkv = jnp.concatenate(
        [
            grad_queries.reshape(slot_count, local_rows, D),
            grad_keys.reshape(slot_count, local_rows, D),
            grad_values.reshape(slot_count, local_rows, D),
        ],
        axis=-1,
    ).astype(jnp.bfloat16)
    grad_qkv_weight = jnp.einsum(
        "std,ste->de", hidden, grad_qkv, preferred_element_type=jnp.float32
    )
    grad_hidden = jnp.einsum("ste,de->std", grad_qkv, qkv_full, preferred_element_type=jnp.float32)
    grad_tok_norm, grad_shift_attn, grad_scale_attn = attn_pull(grad_hidden)
    grad_tokens = grad_middle + grad_tok_norm
    grad_mod_tok = jnp.concatenate(
        [
            grad_shift_attn,
            grad_scale_attn,
            grad_gate_attn,
            grad_shift_mlp,
            grad_scale_mlp,
            grad_gate_mlp,
        ],
        axis=-1,
    )
    image_onehot = (image_id[..., None] == jnp.arange(4)).astype(jnp.float32)
    grad_modulation = jnp.einsum("spi,spe->sie", image_onehot, grad_mod_tok, precision=highest)
    grad_mask_part = jnp.sum(unfilled[..., None] * grad_tokens, axis=(0, 1))
    grad_kept_all = jnp.einsum(
        "spj,spd->sjd", select.astype(jnp.float32), grad_tokens, precision=highest
    )
    kept_grad = lax.psum_scatter(
        grad_kept_all.astype(jnp.bfloat16), "band", scatter_dimension=1, tiled=True
    ).astype(jnp.float32)
    grad_ada = jnp.einsum(
        "sid,sie->de", cond_low.astype(jnp.float32), grad_modulation, precision=highest
    )
    row_grads = (
        lax.psum_scatter(
            grad_qkv_weight.astype(jnp.bfloat16), "band", scatter_dimension=0, tiled=True
        ).astype(jnp.float32),
        lax.psum_scatter(
            grad_proj.astype(jnp.bfloat16), "band", scatter_dimension=0, tiled=True
        ).astype(jnp.float32),
        lax.psum_scatter(
            grad_fc1.astype(jnp.bfloat16), "band", scatter_dimension=0, tiled=True
        ).astype(jnp.float32),
        lax.psum_scatter(
            grad_fc2.astype(jnp.bfloat16), "band", scatter_dimension=0, tiled=True
        ).astype(jnp.float32),
        lax.psum_scatter(
            grad_ada.astype(jnp.bfloat16), "band", scatter_dimension=0, tiled=True
        ).astype(jnp.float32),
    )
    red_qkv, red_proj, red_fc1, red_fc2, red_ada = (
        lax.psum_scatter(
            row_grads[0].astype(jnp.bfloat16), "dp", scatter_dimension=1, tiled=True
        ).astype(jnp.float32),
        lax.psum_scatter(
            row_grads[1].astype(jnp.bfloat16), "dp", scatter_dimension=1, tiled=True
        ).astype(jnp.float32),
        lax.psum_scatter(
            row_grads[2].astype(jnp.bfloat16), "dp", scatter_dimension=1, tiled=True
        ).astype(jnp.float32),
        lax.psum_scatter(
            row_grads[3].astype(jnp.bfloat16), "dp", scatter_dimension=1, tiled=True
        ).astype(jnp.float32),
        lax.psum_scatter(
            row_grads[4].astype(jnp.bfloat16), "dp", scatter_dimension=1, tiled=True
        ).astype(jnp.float32),
    )
    grad_mask = lax.psum(grad_mask_part, ("dp", "band"))
    reduced = (red_qkv, red_proj, red_fc1, red_fc2, red_ada)
    local_squares = sum((jnp.sum(grad * grad) for grad in reduced))
    total_squares = lax.psum(local_squares, ("dp", "band")) + jnp.sum(grad_mask * grad_mask)
    norm_value = jnp.sqrt(total_squares)
    factor = clip_level / jnp.maximum(norm_value, clip_level)
    mask_new = adamw(mask_token, mask_first, mask_second, grad_mask * factor)
    qkv_new = adamw(w_qkv, first_qkv, second_qkv, red_qkv * factor)
    proj_new = adamw(w_proj, first_proj, second_proj, red_proj * factor)
    fc1_new = adamw(w_fc1, first_fc1, second_fc1, red_fc1 * factor)
    fc2_new = adamw(w_fc2, first_fc2, second_fc2, red_fc2 * factor)
    ada_new = adamw(w_ada, first_ada, second_ada, red_ada * factor)
    return (
        block_out,
        kept_grad,
        norm_value,
        mask_new[0],
        qkv_new[0],
        proj_new[0],
        fc1_new[0],
        fc2_new[0],
        ada_new[0],
        mask_new[1],
        qkv_new[1],
        proj_new[1],
        fc1_new[1],
        fc2_new[1],
        ada_new[1],
        mask_new[2],
        qkv_new[2],
        proj_new[2],
        fc1_new[2],
        fc2_new[2],
        ada_new[2],
    )


MASKED = -1e30
SCORE_SCALE = HEAD_DIM ** (-0.5)
LOG2E = math.log2(math.e)
VMEM_LIMIT = 60 * 1024 * 1024


def dot_nn(left, right):
    return lax.dot_general(
        left, right, (((1,), (0,)), ((), ())), preferred_element_type=jnp.float32
    )


def dot_nt(left, right):
    return lax.dot_general(
        left, right, (((1,), (1,)), ((), ())), preferred_element_type=jnp.float32
    )


def attn_head(kind_ref, q_ref, k_ref, v_ref, out_ref, lse_ref):
    tokens = q_ref.shape[2]
    regions = tokens // REGION
    other = jnp.where(kind_ref[0] == 1, MASKED, 0.0)
    keys = jnp.transpose(k_ref[0])
    for block in range(regions):
        cols = slice(block * REGION, (block + 1) * REGION)
        raw = dot_nn(keys, q_ref[0, :, cols])
        parts = [
            raw[r * REGION : (r + 1) * REGION] + (0.0 if r == block else other)
            for r in range(regions)
        ]
        scores = jnp.concatenate(parts, axis=0)
        peak = jnp.max(scores, axis=0, keepdims=True)
        weights = jnp.exp2((scores - peak) * (SCORE_SCALE * LOG2E))
        total = jnp.sum(weights, axis=0, keepdims=True)
        mixed = dot_nn(v_ref[0], weights.astype(jnp.bfloat16))
        out_ref[0, :, cols] = (mixed / total).astype(jnp.bfloat16)
        lse_ref[0, :, cols] = peak * (SCORE_SCALE * LOG2E) + jnp.log2(total)


def attn_head_back(kind_ref, q_ref, k_ref, v_ref, out_ref, grad_ref, lse_ref, grads_ref):
    tokens = q_ref.shape[2]
    regions = tokens // REGION
    other = jnp.where(kind_ref[0] == 1, MASKED, 0.0)
    keys_t = k_ref[0]
    keys = jnp.transpose(keys_t)
    values = jnp.transpose(v_ref[0])
    grad_keys = jnp.zeros((HEAD_DIM, tokens), jnp.float32)
    grad_values = jnp.zeros((HEAD_DIM, tokens), jnp.float32)
    for block in range(regions):
        cols = slice(block * REGION, (block + 1) * REGION)
        queries = q_ref[0, :, cols]
        grad = grad_ref[0, :, cols]
        row_dot = jnp.sum(
            out_ref[0, :, cols].astype(jnp.float32) * grad.astype(jnp.float32),
            axis=0,
            keepdims=True,
        )
        raw = dot_nn(keys, queries)
        parts = [
            raw[r * REGION : (r + 1) * REGION] + (0.0 if r == block else other)
            for r in range(regions)
        ]
        scores = jnp.concatenate(parts, axis=0)
        weights = jnp.exp2(scores * (SCORE_SCALE * LOG2E) - lse_ref[0, :, cols])
        grad_weights = dot_nn(values, grad)
        grad_scores = (weights * (grad_weights - row_dot)).astype(jnp.bfloat16)
        grad_values += dot_nt(grad, weights.astype(jnp.bfloat16))
        grad_keys += dot_nt(queries, grad_scores)
        grads_ref[0, 0, :, cols] = (dot_nn(keys_t, grad_scores) * SCORE_SCALE).astype(
            jnp.bfloat16
        )
    grads_ref[1, 0] = (grad_keys * SCORE_SCALE).astype(jnp.bfloat16)
    grads_ref[2, 0] = grad_values.astype(jnp.bfloat16)


GELU_A = math.sqrt(2.0 / math.pi)
GELU_B = 0.044715


def mlp_kernel(h_ref, ht_ref, g_ref, gt_ref, up_ref, down_ref, out_ref, grad_ref, gup_ref, gdown_ref):
    step = pl.program_id(0)

    @pl.when(step == 0)
    def _():
        out_ref[...] = jnp.zeros_like(out_ref)
        grad_ref[...] = jnp.zeros_like(grad_ref)

    up = up_ref[...]
    down = down_ref[...]
    upward = dot_nn(h_ref[...], up)
    square = upward * upward
    curve = jnp.tanh(GELU_A * upward * (1.0 + GELU_B * square))
    half = 0.5 * (1.0 + curve)
    active = (upward * half).astype(jnp.bfloat16)
    slope = half + 0.5 * upward * (1.0 - curve * curve) * GELU_A * (
        1.0 + 3.0 * GELU_B * square
    )
    grad_upward = (dot_nn(g_ref[...], down) * slope).astype(jnp.bfloat16)
    out_ref[...] += dot_nt(active, down)
    grad_ref[...] += dot_nt(grad_upward, up)
    gup_ref[...] = dot_nn(ht_ref[...], grad_upward).astype(jnp.bfloat16)
    gdown_ref[...] = dot_nn(gt_ref[...], active).astype(jnp.bfloat16)


def mlp_both(hidden, hidden_t, grad, grad_t, up, down_t, tile):
    tokens, width = hidden.shape
    wide = up.shape[1]
    whole = lambda shape: pl.BlockSpec(shape, lambda f: (0, 0))
    part = pl.BlockSpec((width, tile), lambda f: (0, f))
    return pl.pallas_call(
        mlp_kernel,
        grid=(wide // tile,),
        in_specs=[
            whole((tokens, width)),
            whole((width, tokens)),
            whole((tokens, width)),
            whole((width, tokens)),
            part,
            part,
        ],
        out_specs=[whole((tokens, width)), whole((tokens, width)), part, part],
        out_shape=[
            jax.ShapeDtypeStruct((tokens, width), jnp.float32),
            jax.ShapeDtypeStruct((tokens, width), jnp.float32),
            jax.ShapeDtypeStruct((width, wide), jnp.bfloat16),
            jax.ShapeDtypeStruct((width, wide), jnp.bfloat16),
        ],
        compiler_params=pltpu.CompilerParams(vmem_limit_bytes=VMEM_LIMIT),
        name="mlp_both",
    )(hidden, hidden_t, grad, grad_t, up, down_t)


BLOCK_ROWS = 144
BLOCK_COLS = 1152
VIA_X = (0, 3)


def flip(index):
    return index + 1 - 2 * (index % 2)


def along_z(z, step):
    return (z, flip(z), (z + 2) % 4, 3 - z)[step]


class Place:
    def __init__(self):
        dp = lax.axis_index("dp")
        band = lax.axis_index("band")
        self.z, self.y, self.x, self.core = dp // 2, dp % 2, band // 2, band % 2

    def chip(self, i, a, b):
        return (along_z(self.z, i), flip(self.y) if a else self.y, flip(self.x) if b else self.x)

    def device(self, i=0, a=0, b=0, core=0):
        z, y, x = self.chip(i, a, b)
        return (z * 2 + y, x * 2 + (flip(self.core) if core else self.core))

    def partners(self):
        return [
            self.device(core=1),
            self.device(b=1),
            self.device(a=1),
            self.device(i=1),
            self.device(i=2),
            self.device(i=3),
        ]

    def block(self, by_rows, i, a, b, core=0):
        z, y, x = self.chip(i, a, b)
        c = flip(self.core) if core else self.core
        if by_rows:
            row, col = z * 2 + y, x * 2 + c
        else:
            row, col = (x * 2 + c) * 2 + y, z
        return (
            pl.ds(pl.multiple_of(row * BLOCK_ROWS, 16), BLOCK_ROWS),
            pl.ds(pl.multiple_of(col * BLOCK_COLS, 128), BLOCK_COLS),
        )


def greet(place):
    barrier = pltpu.get_barrier_semaphore()
    partners = place.partners()
    for partner in partners:
        pl.semaphore_signal(
            barrier, inc=1, device_id=partner, device_id_type=pl.DeviceIdType.MESH
        )
    pl.semaphore_wait(barrier, len(partners))


def send(source, target, send_sem, recv_sem, device):
    return pltpu.make_async_remote_copy(
        src_ref=source,
        dst_ref=target,
        send_sem=send_sem,
        recv_sem=recv_sem,
        device_id=device,
        device_id_type=pl.DeviceIdType.MESH,
    )


GATHER_SENDS = 16 + 6 + 6 + 3


def gather_actions(place, by_rows, own_refs, full_refs, local_sems, send_sems, link_sems, core_sems):
    weights = range(len(own_refs))
    counts = [0] * len(own_refs)

    def forward(w, source, piece, i=0, a=0, b=0, core=0):
        pi, pa, pb = piece
        name = (pi if i == 0 else i) * 4 + (pa ^ a) * 2 + (pb ^ b)
        target = full_refs[w].at[place.block(by_rows[w], pi, pa, pb)]
        sems = core_sems if core else link_sems
        copy = send(
            source,
            target,
            send_sems.at[w, counts[w]],
            sems.at[w, name],
            place.device(i, a, b, core),
        )
        counts[w] += 1
        copy.start()

    def arrive(w, piece, core=0):
        i, a, b = piece
        target = full_refs[w].at[place.block(by_rows[w], i, a, b, core)]
        sems = core_sems if core else link_sems
        name = i * 4 + a * 2 + b
        send(
            target, target, send_sems.at[w, 0], sems.at[w, name], place.device(core=1)
        ).wait_recv()
        return target

    def begin():
        greet(place)
        for w in weights:
            local = pltpu.make_async_copy(
                own_refs[w], full_refs[w].at[place.block(by_rows[w], 0, 0, 0)], local_sems.at[w]
            )
            local.start()
            own = (0, 0, 0)
            for step in (1, 3, 2):
                forward(w, own_refs[w], own, i=step)
            forward(w, own_refs[w], own, b=1)
            forward(w, own_refs[w], own, a=1)
            forward(w, own_refs[w], own, core=1)

    def pass_on(w, i, a, b):
        def step():
            piece = (i, a, b)
            source = arrive(w, piece)
            if not a and not b:
                forward(w, source, piece, b=1)
                forward(w, source, piece, a=1)
            elif a and not b and i in VIA_X:
                forward(w, source, piece, b=1)
            elif b and not a and i not in VIA_X:
                forward(w, source, piece, a=1)
            forward(w, source, piece, core=1)

        return step

    steps = [begin]
    for w in weights:
        order = [(1, 0, 0), (0, 1, 0), (0, 0, 1), (3, 0, 0), (1, 0, 1), (1, 1, 0), (2, 0, 0)]
        order += [(3, 1, 0), (3, 0, 1), (2, 0, 1), (2, 1, 0), (0, 1, 1), (1, 1, 1), (3, 1, 1), (2, 1, 1)]
        steps += [pass_on(w, *piece) for piece in order]

    def finish():
        for w in weights:
            for i in range(4):
                for a in range(2):
                    for b in range(2):
                        arrive(w, (i, a, b), core=1)
            pltpu.make_async_copy(
                own_refs[w], full_refs[w].at[place.block(by_rows[w], 0, 0, 0)], local_sems.at[w]
            ).wait()
            for n in range(counts[w]):
                send(
                    own_refs[w], own_refs[w], send_sems.at[w, n], link_sems.at[w, 0],
                    place.device(core=1),
                ).wait_send()

    return steps + [finish]


def gather_kernel(by_rows, *refs):
    count = len(by_rows)
    own_refs, full_refs = refs[:count], refs[count : 2 * count]
    place = Place()
    for step in gather_actions(place, by_rows, own_refs, full_refs, *refs[2 * count :]):
        step()


def gather_scratch(count):
    return [
        pltpu.SemaphoreType.DMA((count,)),
        pltpu.SemaphoreType.DMA((count, GATHER_SENDS)),
        pltpu.SemaphoreType.DMA((count, 16)),
        pltpu.SemaphoreType.DMA((count, 16)),
    ]


def gather_blocks(blocks, by_rows, collective_id):
    count = len(blocks)
    whole = jax.ShapeDtypeStruct((8 * BLOCK_ROWS, 4 * BLOCK_COLS), jnp.bfloat16)
    return pl.pallas_call(
        functools.partial(gather_kernel, by_rows),
        in_specs=[pl.BlockSpec(memory_space=pltpu.VMEM)] * count,
        out_specs=[pl.BlockSpec(memory_space=pl.ANY)] * count,
        out_shape=[whole] * count,
        scratch_shapes=gather_scratch(count),
        compiler_params=pltpu.CompilerParams(
            collective_id=collective_id, has_side_effects=True, vmem_limit_bytes=VMEM_LIMIT
        ),
        name="gather_blocks",
    )(*blocks)


SCATTER_SENDS = 16 + 6 + 6 + 3


def scatter_actions(
    place,
    by_rows,
    grad_refs,
    out_refs,
    held_refs,
    over_x,
    over_y,
    over_z,
    stage,
    stage_sems,
    send_sems,
    held_sems,
    x_sems,
    y_sems,
    z_sems,
):
    weights = range(len(grad_refs))
    counts = [0] * len(grad_refs)
    chips = [(i, a, b) for i in (1, 3, 2, 0) for a, b in ((1, 1), (0, 1), (1, 0), (0, 0))]
    slot = lambda i, a, b: i * 4 + a * 2 + b

    def ship(w, source, target, recv_sem, device):
        copy = send(source, target, send_sems.at[w, counts[w]], recv_sem, device)
        counts[w] += 1
        copy.start()

    def landed(target, recv_sem):
        send(target, target, send_sems.at[0, 0], recv_sem, place.device(core=1)).wait_recv()

    def begin():
        greet(place)
        for w in weights:
            for i, a, b in chips:
                source = grad_refs[w].at[place.block(by_rows[w], i, a, b, core=1)]
                s = slot(i, a, b)
                ship(w, source, held_refs.at[w, s], held_sems.at[w, s], place.device(core=1))

    order = [(w, chip) for w in weights for chip in chips]

    def load(n):
        w, (i, a, b) = order[n]
        return pltpu.make_async_copy(
            grad_refs[w].at[place.block(by_rows[w], i, a, b)], stage.at[n % 4], stage_sems.at[n % 4]
        )

    def fold(n):
        def step():
            if n == 0:
                for ahead in range(3):
                    load(ahead).start()
            if n + 3 < len(order):
                load(n + 3).start()
            w, (i, a, b) = order[n]
            s = slot(i, a, b)
            load(n).wait()
            landed(held_refs.at[w, s], held_sems.at[w, s])
            held = held_refs.at[w, s]
            held[...] = held[...] + stage[n % 4]
            via_x = i in VIA_X
            if a and b:
                if via_x:
                    ship(w, held, over_x.at[w, 4 + VIA_X.index(i)], x_sems.at[w, 4 + VIA_X.index(i)], place.device(b=1))
                else:
                    k = 4 + (i - 1)
                    ship(w, held, over_y.at[w, k], y_sems.at[w, k], place.device(a=1))
            elif b and via_x:
                ship(w, held, over_x.at[w, i], x_sems.at[w, i], place.device(b=1))
            elif a and not via_x:
                ship(w, held, over_y.at[w, i], y_sems.at[w, i], place.device(a=1))

        return step

    def second(w, i):
        def step():
            if i in VIA_X:
                k = 4 + VIA_X.index(i)
                landed(over_x.at[w, k], x_sems.at[w, k])
                held = held_refs.at[w, slot(i, 1, 0)]
                held[...] = held[...] + over_x[w, k]
                ship(w, held, over_y.at[w, i], y_sems.at[w, i], place.device(a=1))
            else:
                k = 4 + (i - 1)
                landed(over_y.at[w, k], y_sems.at[w, k])
                held = held_refs.at[w, slot(i, 0, 1)]
                held[...] = held[...] + over_y[w, k]
                ship(w, held, over_x.at[w, i], x_sems.at[w, i], place.device(b=1))

        return step

    def third(w, i):
        def step():
            landed(over_x.at[w, i], x_sems.at[w, i])
            landed(over_y.at[w, i], y_sems.at[w, i])
            held = held_refs.at[w, slot(i, 0, 0)]
            total = held[...].astype(jnp.float32) + over_x[w, i].astype(jnp.float32)
            total = total + over_y[w, i].astype(jnp.float32)
            held[...] = total.astype(jnp.bfloat16)
            if i:
                ship(w, held, over_z.at[w, i - 1], z_sems.at[w, i - 1], place.device(i=i))

        return step

    def last(w):
        def step():
            total = held_refs[w, 0].astype(jnp.float32)
            for i in (1, 3, 2):
                landed(over_z.at[w, i - 1], z_sems.at[w, i - 1])
                total = total + over_z[w, i - 1].astype(jnp.float32)
            out_refs[w][...] = total

        return step

    def finish():
        for w in weights:
            block = held_refs.at[w, 0]
            for n in range(counts[w]):
                send(
                    block, block, send_sems.at[w, n], held_sems.at[w, 0], place.device(core=1)
                ).wait_send()

    steps = [begin]
    per = len(chips)
    for w in weights:
        for n in range(per):
            steps.append(fold(w * per + n))
            if n == 11:
                steps.append(second(w, 1))
        for i in (3, 2, 0):
            steps.append(second(w, i))
        for i in (1, 3, 2, 0):
            steps.append(third(w, i))
    for w in weights:
        steps.append(last(w))
    return steps + [finish]


def scatter_scratch(count):
    blocks = lambda n: pltpu.VMEM((count, n, BLOCK_ROWS, BLOCK_COLS), jnp.bfloat16)
    return [
        blocks(16),
        blocks(6),
        blocks(6),
        blocks(3),
        pltpu.VMEM((4, BLOCK_ROWS, BLOCK_COLS), jnp.bfloat16),
        pltpu.SemaphoreType.DMA((4,)),
        pltpu.SemaphoreType.DMA((count, SCATTER_SENDS)),
        pltpu.SemaphoreType.DMA((count, 16)),
        pltpu.SemaphoreType.DMA((count, 6)),
        pltpu.SemaphoreType.DMA((count, 6)),
        pltpu.SemaphoreType.DMA((count, 3)),
    ]


def scatter_kernel(by_rows, *refs):
    count = len(by_rows)
    place = Place()
    for step in scatter_actions(
        place, by_rows, refs[:count], refs[count : 2 * count], *refs[2 * count :]
    ):
        step()


def scatter_blocks(grads, by_rows, collective_id):
    count = len(grads)
    block = jax.ShapeDtypeStruct((BLOCK_ROWS, BLOCK_COLS), jnp.float32)
    return pl.pallas_call(
        functools.partial(scatter_kernel, by_rows),
        in_specs=[pl.BlockSpec(memory_space=pl.ANY)] * count,
        out_specs=[pl.BlockSpec(memory_space=pltpu.VMEM)] * count,
        out_shape=[block] * count,
        scratch_shapes=scatter_scratch(count),
        compiler_params=pltpu.CompilerParams(
            collective_id=collective_id, has_side_effects=True, vmem_limit_bytes=VMEM_LIMIT
        ),
        name="scatter_blocks",
    )(*grads)


def spread(actions, steps):
    middle = actions[1:-1]
    groups = [[] for _ in range(steps)]
    groups[0].append(actions[0])
    for n, action in enumerate(middle):
        groups[1 + n * (steps - 1) // len(middle)].append(action)
    return groups, actions[-1]


def run_actions(actions, steps, compute):
    step = pl.program_id(0)
    groups, finish = spread(actions, steps)
    for n, group in enumerate(groups):

        @pl.when(step == n)
        def _():
            for action in group:
                action()

    compute()
    pl.when(step == steps - 1)(finish)


def head_spec(part, tokens):
    return pl.BlockSpec((1, HEAD_DIM, tokens), lambda h: (h + part * HEADS, 0, 0))


def attn_gather_kernel(by_rows, *refs):
    count = len(by_rows)
    ins, own_refs = refs[:4], refs[4 : 4 + count]
    outs = refs[4 + count : 6 + count]
    full_refs = refs[6 + count : 6 + 2 * count]
    actions = gather_actions(Place(), by_rows, own_refs, full_refs, *refs[6 + 2 * count :])
    run_actions(actions, HEADS, lambda: attn_head(*ins, *outs))


def attn_forward(kind, qkv_heads, blocks, by_rows, collective_id):
    tokens = qkv_heads.shape[2]
    count = len(blocks)
    whole = jax.ShapeDtypeStruct((8 * BLOCK_ROWS, 4 * BLOCK_COLS), jnp.bfloat16)
    block = pl.BlockSpec((BLOCK_ROWS, BLOCK_COLS), lambda h: (0, 0))
    return pl.pallas_call(
        functools.partial(attn_gather_kernel, by_rows),
        grid=(HEADS,),
        in_specs=[pl.BlockSpec(memory_space=pltpu.SMEM)]
        + [head_spec(part, tokens) for part in range(3)]
        + [block] * count,
        out_specs=[head_spec(0, tokens), pl.BlockSpec((1, 1, tokens), lambda h: (h, 0, 0))]
        + [pl.BlockSpec(memory_space=pl.ANY)] * count,
        out_shape=[
            jax.ShapeDtypeStruct((HEADS, HEAD_DIM, tokens), jnp.bfloat16),
            jax.ShapeDtypeStruct((HEADS, 1, tokens), jnp.float32),
        ]
        + [whole] * count,
        scratch_shapes=gather_scratch(count),
        compiler_params=pltpu.CompilerParams(
            collective_id=collective_id, has_side_effects=True, vmem_limit_bytes=VMEM_LIMIT
        ),
        name="attn_forward",
    )(kind, qkv_heads, qkv_heads, qkv_heads, *blocks)


def attn_scatter_kernel(by_rows, *refs):
    count = len(by_rows)
    ins, whole_refs = refs[:7], refs[7 : 7 + count]
    outs = refs[7 + count : 8 + count]
    sum_refs = refs[8 + count : 8 + 2 * count]
    actions = scatter_actions(Place(), by_rows, whole_refs, sum_refs, *refs[8 + 2 * count :])
    run_actions(actions, HEADS, lambda: attn_head_back(*ins, *outs))


def attn_backward(kind, qkv_heads, attended, grad_attended, lse, grads, by_rows, collective_id):
    tokens = qkv_heads.shape[2]
    count = len(grads)
    block = pl.BlockSpec((BLOCK_ROWS, BLOCK_COLS), lambda h: (0, 0))
    return pl.pallas_call(
        functools.partial(attn_scatter_kernel, by_rows),
        grid=(HEADS,),
        in_specs=[pl.BlockSpec(memory_space=pltpu.SMEM)]
        + [head_spec(part, tokens) for part in (0, 1, 2, 0, 0)]
        + [pl.BlockSpec((1, 1, tokens), lambda h: (h, 0, 0))]
        + [pl.BlockSpec(memory_space=pl.ANY)] * count,
        out_specs=[pl.BlockSpec((3, 1, HEAD_DIM, tokens), lambda h: (0, h, 0, 0))]
        + [block] * count,
        out_shape=[jax.ShapeDtypeStruct((3, HEADS, HEAD_DIM, tokens), jnp.bfloat16)]
        + [jax.ShapeDtypeStruct((BLOCK_ROWS, BLOCK_COLS), jnp.float32)] * count,
        scratch_shapes=scatter_scratch(count),
        compiler_params=pltpu.CompilerParams(
            collective_id=collective_id, has_side_effects=True, vmem_limit_bytes=VMEM_LIMIT
        ),
        name="attn_backward",
    )(kind, qkv_heads, qkv_heads, qkv_heads, attended, grad_attended, lse, *grads)


def project_kernel(hidden_ref, weight_ref, out_ref):
    rows = out_ref.shape[0]
    span = -(-rows // 128) * 128
    wide = dot_nn(hidden_ref[...], weight_ref[:, :span]).astype(jnp.bfloat16)
    out_ref[...] = jnp.transpose(wide)[:rows]


def project_qkv(hidden, weights):
    tokens, width = hidden.shape
    groups = weights.shape[1] // BLOCK_COLS
    rows = 3 * D // groups
    return pl.pallas_call(
        project_kernel,
        grid=(groups,),
        in_specs=[
            pl.BlockSpec((tokens, width), lambda g: (0, 0)),
            pl.BlockSpec((width, BLOCK_COLS), lambda g: (0, g)),
        ],
        out_specs=pl.BlockSpec((rows, tokens), lambda g: (g, 0)),
        out_shape=jax.ShapeDtypeStruct((groups * rows, tokens), jnp.bfloat16),
        compiler_params=pltpu.CompilerParams(vmem_limit_bytes=VMEM_LIMIT),
        name="project_qkv",
    )(hidden, weights)


def project_back_kernel(hidden_t_ref, weight_ref, grad_ref, proj_ref, grad_hidden_ref, out_ref):
    group = pl.program_id(0)
    rows = grad_ref.shape[0]
    proj_cols = BLOCK_COLS - rows
    grad = grad_ref[...]

    @pl.when(group == 0)
    def _():
        grad_hidden_ref[...] = jnp.zeros_like(grad_hidden_ref)

    grad_hidden_ref[...] += dot_nt(jnp.transpose(grad), weight_ref[:, :rows])
    out_ref[:, :rows] = dot_nt(hidden_t_ref[...], grad).astype(jnp.bfloat16)
    for g in range(D // proj_cols):

        @pl.when(group == g)
        def _():
            out_ref[:, rows:] = proj_ref[:, g * proj_cols : (g + 1) * proj_cols]


def project_back(hidden_t, weights, grad, grad_proj):
    width, tokens = hidden_t.shape
    groups = weights.shape[1] // BLOCK_COLS
    rows = grad.shape[0] // groups
    return pl.pallas_call(
        project_back_kernel,
        grid=(groups,),
        in_specs=[
            pl.BlockSpec((width, tokens), lambda g: (0, 0)),
            pl.BlockSpec((width, BLOCK_COLS), lambda g: (0, g)),
            pl.BlockSpec((rows, tokens), lambda g: (g, 0)),
            pl.BlockSpec((width, D), lambda g: (0, 0)),
        ],
        out_specs=[
            pl.BlockSpec((tokens, width), lambda g: (0, 0)),
            pl.BlockSpec((width, BLOCK_COLS), lambda g: (0, g)),
        ],
        out_shape=[
            jax.ShapeDtypeStruct((tokens, width), jnp.float32),
            jax.ShapeDtypeStruct(weights.shape, jnp.bfloat16),
        ],
        compiler_params=pltpu.CompilerParams(vmem_limit_bytes=VMEM_LIMIT),
        name="project_back",
    )(hidden_t, weights, grad, grad_proj)


def swap_columns(shard):
    pairs = [(d, d ^ 1) for d in range(lax.axis_size("dp"))]
    odd = lax.axis_index("dp") % 2
    rows = shard.shape[0] // 2
    own = lax.dynamic_slice_in_dim(shard, odd * rows, rows, axis=0)
    other = lax.dynamic_slice_in_dim(shard, (1 - odd) * rows, rows, axis=0)
    other = lax.ppermute(other, "dp", pairs)
    return jnp.where(odd == 0, jnp.stack([own, other], 1), jnp.stack([other, own], 1))


def swap_rows(block):
    pairs = [(d, d ^ 1) for d in range(lax.axis_size("dp"))]
    odd = lax.axis_index("dp") % 2
    own = lax.dynamic_index_in_dim(block, odd, axis=1, keepdims=False)
    other = lax.dynamic_index_in_dim(block, 1 - odd, axis=1, keepdims=False)
    other = lax.ppermute(other, "dp", pairs)
    return jnp.where(odd == 0, jnp.concatenate([own, other], 0), jnp.concatenate([other, own], 0))


def swap_slots(values):
    moved = lax.all_to_all(values, "band", split_axis=0, concat_axis=0, tiled=True)
    return moved.reshape((-1,) + values.shape[2:])


def norm_parts(values):
    center = jnp.mean(values, axis=-1, keepdims=True)
    spread = jnp.mean((values - center) ** 2, axis=-1, keepdims=True)
    root = lax.rsqrt(spread + 1e-06)
    return ((values - center) * root, root)


def norm_back(grad, normal, root, scales):
    inner = grad * (1.0 + scales)
    return root * (
        inner
        - jnp.mean(inner, axis=-1, keepdims=True)
        - normal * jnp.mean(inner * normal, axis=-1, keepdims=True)
    )


def embed_tables(count):
    quarter = D // 4
    omegas = 1.0 / 10000.0 ** (jnp.arange(quarter, dtype=jnp.float32) / quarter)
    angles = jnp.arange(count, dtype=jnp.float32)[:, None] * omegas
    return jnp.concatenate([jnp.sin(angles), jnp.cos(angles)], axis=-1)


def grid_embed_slot(kind, tokens):
    table = embed_tables(SIDE)
    half = D // 2
    side = SIDE
    wide = jnp.concatenate(
        [
            jnp.broadcast_to(table[:, None, :], (side, side, half)),
            jnp.broadcast_to(table[None, :, :], (side, side, half)),
        ],
        axis=-1,
    ).reshape(tokens, D)
    small = side // 2
    table_small = table[:small]
    narrow = jnp.concatenate(
        [
            jnp.broadcast_to(table_small[None, :, None, :], (tokens // REGION, small, small, half)),
            jnp.broadcast_to(table_small[None, None, :, :], (tokens // REGION, small, small, half)),
        ],
        axis=-1,
    ).reshape(tokens, D)
    return jnp.where(kind == 1, narrow, wide)


def slot_device(
    kept_tokens,
    kept_index,
    resolution,
    labels,
    timesteps,
    class_table,
    cotangent,
    mask_token,
    w_qkv,
    w_proj,
    w_fc1,
    w_fc2,
    w_ada,
    mask_first,
    first_qkv,
    first_proj,
    first_fc1,
    first_fc2,
    first_ada,
    mask_second,
    second_qkv,
    second_proj,
    second_fc1,
    second_fc2,
    second_ada,
):
    highest = lax.Precision.HIGHEST
    bf16 = jnp.bfloat16
    bands = lax.axis_size("band")
    groups = lax.axis_size("dp")
    band = lax.axis_index("band")
    slots, local_rows, _ = cotangent.shape
    tokens_count = bands * local_rows
    regions = tokens_count // REGION
    images = labels.shape[1]

    picks = lax.all_gather(jnp.concatenate([labels, timesteps], axis=1), "dp", axis=0, tiled=True)
    rows_ada, cols_ada = w_ada.shape
    count = picks.shape[0] * images
    all_labels = picks[:, :images].reshape(count)
    all_times = picks[:, images:].reshape(count)
    table_part = lax.dynamic_slice_in_dim(class_table, band * rows_ada, rows_ada, axis=1)
    chosen = (all_labels[:, None] == jnp.arange(class_table.shape[0])[None, :]).astype(jnp.float32)
    features = band * rows_ada + jnp.arange(rows_ada)
    half_width = D // 2
    frequency = jnp.exp(
        -math.log(10000.0) * (features % half_width).astype(jnp.float32) / half_width
    )
    angles = all_times.astype(jnp.float32)[:, None] * frequency
    waves = jnp.where(features < half_width, jnp.cos(angles), jnp.sin(angles))
    condition = jnp.matmul(chosen, table_part, precision=highest) + waves
    cond_low = jax.nn.silu(condition).astype(bf16)
    partial = jnp.matmul(cond_low, w_ada.astype(bf16), preferred_element_type=jnp.float32)
    partial = partial.reshape(groups, slots, images, cols_ada).transpose(1, 0, 2, 3)
    own_rows = lax.psum_scatter(partial, "band", scatter_dimension=0, tiled=True)[0]
    modulation = lax.all_to_all(own_rows, "dp", split_axis=0, concat_axis=0, tiled=True)
    modulation = modulation.transpose(1, 0, 2).reshape(images, groups * cols_ada)

    kind = lax.dynamic_slice_in_dim(resolution, band, 1)
    kept = swap_slots(kept_tokens)
    index = swap_slots(kept_index)
    grad_out = swap_slots(cotangent).reshape(regions, REGION, D)

    mod = jnp.where(kind[0] == 1, modulation, modulation[:1])
    shift_attn, scale_attn, gate_attn, shift_mlp, scale_mlp, gate_mlp = [
        piece[:, None, :] for piece in jnp.split(mod, 6, axis=-1)
    ]
    select = jnp.arange(tokens_count)[:, None] == index[None, :]
    select_low = select.astype(bf16)
    unfilled = 1.0 - jnp.sum(select.astype(jnp.float32), axis=1, keepdims=True)
    placed = jnp.matmul(select_low, kept, preferred_element_type=jnp.float32)
    tokens = placed + unfilled * mask_token + grid_embed_slot(kind[0], tokens_count)
    tokens = tokens.reshape(regions, REGION, D)

    qkv_cols, proj_cols, fc1_cols = w_qkv.shape[1], w_proj.shape[1], w_fc1.shape[1]
    swapped = swap_columns(jnp.concatenate([w_qkv, w_proj, w_fc1], axis=1).astype(bf16))
    joined_block = jnp.concatenate(
        [
            swapped[:, :, :qkv_cols].reshape(-1, 2 * qkv_cols),
            swapped[:, :, qkv_cols:-fc1_cols].reshape(-1, 2 * proj_cols),
        ],
        axis=1,
    )
    fc1_block = swapped[:, :, -fc1_cols:].reshape(-1, 2 * fc1_cols)
    (joined_full,) = gather_blocks([joined_block], (False,), 0)
    proj_full = joined_full.reshape(D, -1, BLOCK_COLS)[:, :, 2 * qkv_cols :].reshape(D, D)

    normal_attn, root_attn = norm_parts(tokens)
    hidden = (normal_attn * (1.0 + scale_attn) + shift_attn).astype(bf16).reshape(tokens_count, D)
    qkv = project_qkv(hidden, joined_full)
    qkv_heads = qkv.reshape(3 * HEADS, HEAD_DIM, tokens_count)
    attended, lse, fc1_full, fc2_full = attn_forward(
        kind, qkv_heads, [fc1_block, w_fc2.astype(bf16).T], (False, True), 1
    )
    attended_t = attended.reshape(D, tokens_count)
    branch = lax.dot_general(
        attended_t, proj_full, (((0,), (0,)), ((), ())), preferred_element_type=jnp.float32
    ).reshape(regions, REGION, D)
    middle = tokens + gate_attn * branch
    normal_mlp, root_mlp = norm_parts(middle)
    hidden_mlp = (normal_mlp * (1.0 + scale_mlp) + shift_mlp).astype(bf16).reshape(tokens_count, D)
    grad_full = grad_out.astype(jnp.float32)
    grad_output = (gate_mlp * grad_full).astype(bf16).reshape(tokens_count, D)

    output, grad_hidden_mlp, grad_fc1, grad_fc2 = mlp_both(
        hidden_mlp, hidden_mlp.T, grad_output, grad_output.T, fc1_full, fc2_full, 512
    )
    output = output.reshape(regions, REGION, D)
    grad_hidden_mlp = grad_hidden_mlp.reshape(regions, REGION, D)
    block_slot = (middle + gate_mlp * output).astype(bf16)
    block_out = lax.all_to_all(
        block_slot.reshape(bands, local_rows, D), "band", split_axis=0, concat_axis=0, tiled=True
    )
    grad_gate_mlp = jnp.sum(grad_full * output, axis=1)
    grad_shift_mlp = jnp.sum(grad_hidden_mlp, axis=1)
    grad_scale_mlp = jnp.sum(grad_hidden_mlp * normal_mlp, axis=1)
    grad_middle = grad_full + norm_back(grad_hidden_mlp, normal_mlp, root_mlp, scale_mlp)
    grad_gate_attn = jnp.sum(grad_middle * branch, axis=1)
    grad_branch = (gate_attn * grad_middle).astype(bf16).reshape(tokens_count, D)
    grad_proj = dot_nn(attended_t, grad_branch).astype(bf16)
    grad_attended = dot_nt(proj_full, grad_branch).astype(bf16)
    grad_heads = grad_attended.reshape(HEADS, HEAD_DIM, tokens_count)
    grad_qkv, sum_fc1, sum_fc2 = attn_backward(
        kind, qkv_heads, attended, grad_heads, lse, [grad_fc1, grad_fc2], (False, True), 2
    )
    grad_qkv = grad_qkv.reshape(3 * D, tokens_count)
    grad_hidden, grad_joined = project_back(hidden.T, joined_full, grad_qkv, grad_proj)
    grad_hidden = grad_hidden.reshape(regions, REGION, D)
    grad_shift_attn = jnp.sum(grad_hidden, axis=1)
    grad_scale_attn = jnp.sum(grad_hidden * normal_attn, axis=1)
    grad_tokens = grad_middle + norm_back(grad_hidden, normal_attn, root_attn, scale_attn)
    grad_tokens = grad_tokens.reshape(tokens_count, D)

    grad_mod = jnp.concatenate(
        [
            grad_shift_attn,
            grad_scale_attn,
            grad_gate_attn,
            grad_shift_mlp,
            grad_scale_mlp,
            grad_gate_mlp,
        ],
        axis=-1,
    )
    first_only = (jnp.arange(images) == 0).astype(jnp.float32)[:, None]
    grad_mod = jnp.where(
        kind[0] == 1, grad_mod, first_only * jnp.sum(grad_mod, axis=0, keepdims=True)
    )
    grad_mod = grad_mod.reshape(images, groups, cols_ada).transpose(1, 0, 2)
    grad_mod = lax.all_to_all(grad_mod, "dp", split_axis=0, concat_axis=0, tiled=True)
    grad_mod = lax.all_gather(grad_mod, "band", axis=1, tiled=True)
    red_ada = lax.dot_general(
        cond_low.astype(jnp.float32),
        grad_mod.reshape(count, cols_ada),
        (((0,), (0,)), ((), ())),
        precision=highest,
        preferred_element_type=jnp.float32,
    )

    grad_kept = lax.dot_general(
        select_low, grad_tokens.astype(bf16), (((0,), (0,)), ((), ())),
        preferred_element_type=jnp.float32,
    ).astype(bf16)
    kept_grad = lax.all_to_all(
        grad_kept.reshape(bands, -1, D), "band", split_axis=0, concat_axis=0, tiled=True
    ).astype(jnp.float32)
    grad_mask_part = jnp.sum(unfilled * grad_tokens, axis=0)

    (sum_joined,) = scatter_blocks([grad_joined], (False,), 3)
    sums = jnp.concatenate(
        [
            sum_joined[:, : 2 * qkv_cols].reshape(-1, 2, qkv_cols),
            sum_joined[:, 2 * qkv_cols :].reshape(-1, 2, proj_cols),
            sum_fc1.reshape(-1, 2, fc1_cols),
        ],
        axis=2,
    )
    sums = swap_rows(sums.astype(bf16)).astype(jnp.float32)
    red_qkv = sums[:, :qkv_cols]
    red_proj = sums[:, qkv_cols:-fc1_cols]
    red_fc1 = sums[:, -fc1_cols:]
    red_fc2 = sum_fc2.T
    grad_mask = lax.psum(grad_mask_part, ("dp", "band"))
    reduced = (red_qkv, red_proj, red_fc1, red_fc2, red_ada)
    local_squares = sum((jnp.sum(grad * grad) for grad in reduced))
    total_squares = lax.psum(local_squares, ("dp", "band")) + jnp.sum(grad_mask * grad_mask)
    norm_value = jnp.sqrt(total_squares)
    factor = clip_level / jnp.maximum(norm_value, clip_level)
    mask_new = adamw(mask_token, mask_first, mask_second, grad_mask * factor)
    qkv_new = adamw(w_qkv, first_qkv, second_qkv, red_qkv * factor)
    proj_new = adamw(w_proj, first_proj, second_proj, red_proj * factor)
    fc1_new = adamw(w_fc1, first_fc1, second_fc1, red_fc1 * factor)
    fc2_new = adamw(w_fc2, first_fc2, second_fc2, red_fc2 * factor)
    ada_new = adamw(w_ada, first_ada, second_ada, red_ada * factor)
    moved = tuple(zip(mask_new, qkv_new, proj_new, fc1_new, fc2_new, ada_new))
    return (block_out, kept_grad, norm_value) + moved[0] + moved[1] + moved[2]


def per_device(*arguments):
    cotangent = arguments[6]
    if (lax.axis_size("dp"), lax.axis_size("band")) == (8, cotangent.shape[0]):
        return slot_device(*arguments)
    return general_device(*arguments)


def solution(mesh):
    in_specs = (
        P("dp", "band", None),
        P("dp", "band"),
        P("dp"),
        P("dp", None),
        P("dp", None),
        P(),
        P("dp", "band", None),
        P(),
        P("band", "dp"),
        P("band", "dp"),
        P("band", "dp"),
        P("band", "dp"),
        P("band", "dp"),
        P(),
        P("band", "dp"),
        P("band", "dp"),
        P("band", "dp"),
        P("band", "dp"),
        P("band", "dp"),
        P(),
        P("band", "dp"),
        P("band", "dp"),
        P("band", "dp"),
        P("band", "dp"),
        P("band", "dp"),
    )
    out_specs = (
        P("dp", "band", None),
        P("dp", "band", None),
        P(),
        P(),
        P("band", "dp"),
        P("band", "dp"),
        P("band", "dp"),
        P("band", "dp"),
        P("band", "dp"),
        P(),
        P("band", "dp"),
        P("band", "dp"),
        P("band", "dp"),
        P("band", "dp"),
        P("band", "dp"),
        P(),
        P("band", "dp"),
        P("band", "dp"),
        P("band", "dp"),
        P("band", "dp"),
        P("band", "dp"),
    )
    return jax.shard_map(
        per_device, mesh=mesh, in_specs=in_specs, out_specs=out_specs, check_vma=False
    )
```

```python
import functools
import math

import jax
import jax.numpy as jnp
from jax import lax
from jax.experimental import pallas as pl
from jax.experimental.pallas import tpu as pltpu
from jax.sharding import PartitionSpec as P

D = 1152
HEADS = 16
HEAD_DIM = 72
SIDE = 32
STEP = 10
REGION = 256


learn_rate = 0.1
beta_first = 0.9
beta_second = 0.95
adam_eps = 1e-08
decay_rate = 0.1
clip_level = 1.0


def time_embed(timestep):
    half_width = D // 2
    frequency = jnp.exp(-math.log(10000.0) * jnp.arange(half_width, dtype=jnp.float32) / half_width)
    angles = timestep.astype(jnp.float32)[..., None] * frequency
    return jnp.concatenate([jnp.cos(angles), jnp.sin(angles)], axis=-1)


def grid_embed(grid_rows, grid_cols):
    quarter = D // 4
    omegas = 1.0 / 10000.0 ** (jnp.arange(quarter, dtype=jnp.float32) / quarter)
    row_angle = grid_rows.astype(jnp.float32)[..., None] * omegas
    col_angle = grid_cols.astype(jnp.float32)[..., None] * omegas
    return jnp.concatenate(
        [jnp.sin(row_angle), jnp.cos(row_angle), jnp.sin(col_angle), jnp.cos(col_angle)], axis=-1
    )


def slot_layout(positions, slot_kinds):
    small_side = SIDE // 2
    region = positions // REGION
    inside = positions % REGION
    grid_rows = jnp.where(slot_kinds == 1, inside // small_side, positions // SIDE)
    grid_cols = jnp.where(slot_kinds == 1, inside % small_side, positions % SIDE)
    image_id = jnp.where(slot_kinds == 1, region, 0)
    return (grid_rows, grid_cols, image_id)


def modulate(values, shifts, scales):
    center = jnp.mean(values, axis=-1, keepdims=True)
    spread = jnp.mean((values - center) ** 2, axis=-1, keepdims=True)
    return (values - center) * lax.rsqrt(spread + 1e-06) * (1.0 + scales) + shifts


def gelu_tanh(values):
    return jax.nn.gelu(values, approximate=True)


def pick_rows(table_rows, picks):
    return table_rows[picks]


def allowed_pairs(query_pos, key_pos, slot_kinds):
    same_region = (query_pos // REGION)[None, :, None] == (key_pos // REGION)[None, None, :]
    return (slot_kinds[:, None, None] == 0) | same_region


def attend(queries, keys_in, values_in, allowed):

    def one_slot(pieces):
        query_s, key_s, value_s, allow_s = pieces
        scores = jnp.einsum(
            "qhd,khd->hqk", query_s, key_s, preferred_element_type=jnp.float32
        ) * HEAD_DIM ** (-0.5)
        scores = jnp.where(allow_s[None], scores, -1e30)
        row_peak = jnp.max(scores, axis=-1, keepdims=True)
        row_total = jnp.sum(jnp.exp(scores - row_peak), axis=-1, keepdims=True)
        log_total = row_peak + jnp.log(row_total)
        weights_soft = jnp.exp(scores - log_total).astype(jnp.bfloat16)
        result = jnp.einsum(
            "hqk,khd->qhd", weights_soft, value_s, preferred_element_type=jnp.float32
        )
        return (result.astype(jnp.bfloat16), log_total)

    return lax.map(one_slot, (queries, keys_in, values_in, allowed))


def attend_back(queries, keys_in, values_in, allowed, log_total, grad_attended):

    def one_slot(pieces):
        query_s, key_s, value_s, allow_s, total_s, grad_s = pieces
        scores = jnp.einsum(
            "qhd,khd->hqk", query_s, key_s, preferred_element_type=jnp.float32
        ) * HEAD_DIM ** (-0.5)
        scores = jnp.where(allow_s[None], scores, -1e30)
        weights_full = jnp.exp(scores - total_s)
        weights_soft = weights_full.astype(jnp.bfloat16)
        grad_weights = jnp.einsum(
            "qhd,khd->hqk", grad_s, value_s, preferred_element_type=jnp.float32
        )
        row_dot = jnp.sum(weights_full * grad_weights, axis=-1, keepdims=True)
        grad_scores = (weights_full * (grad_weights - row_dot) * HEAD_DIM ** (-0.5)).astype(
            jnp.bfloat16
        )
        grad_queries = jnp.einsum(
            "hqk,khd->qhd", grad_scores, key_s, preferred_element_type=jnp.float32
        )
        grad_keys = jnp.einsum(
            "hqk,qhd->khd", grad_scores, query_s, preferred_element_type=jnp.float32
        )
        grad_values = jnp.einsum(
            "hqk,qhd->khd", weights_soft, grad_s, preferred_element_type=jnp.float32
        )
        return (grad_queries, grad_keys, grad_values)

    return lax.map(one_slot, (queries, keys_in, values_in, allowed, log_total, grad_attended))


def adamw(weight, first, second, grad):
    first_new = beta_first * first + (1.0 - beta_first) * grad
    second_new = beta_second * second + (1.0 - beta_second) * grad * grad
    first_hat = first_new / (1.0 - beta_first**STEP)
    second_hat = second_new / (1.0 - beta_second**STEP)
    weight_new = weight - learn_rate * (
        first_hat / (jnp.sqrt(second_hat) + adam_eps) + decay_rate * weight
    )
    return (weight_new, first_new, second_new)


def general_device(
    kept_tokens,
    kept_index,
    resolution,
    labels,
    timesteps,
    class_table,
    cotangent,
    mask_token,
    w_qkv,
    w_proj,
    w_fc1,
    w_fc2,
    w_ada,
    mask_first,
    first_qkv,
    first_proj,
    first_fc1,
    first_fc2,
    first_ada,
    mask_second,
    second_qkv,
    second_proj,
    second_fc1,
    second_fc2,
    second_ada,
):
    highest = lax.Precision.HIGHEST
    band_index = lax.axis_index("band")
    slot_count = cotangent.shape[0]
    local_rows = cotangent.shape[1]
    qkv_low = w_qkv.astype(jnp.bfloat16)
    proj_low = w_proj.astype(jnp.bfloat16)
    fc1_low = w_fc1.astype(jnp.bfloat16)
    fc2_low = w_fc2.astype(jnp.bfloat16)
    ada_low = w_ada.astype(jnp.bfloat16)
    cols_qkv, cols_proj, cols_fc1, cols_fc2, cols_ada = (
        lax.all_gather(qkv_low, "dp", axis=1, tiled=True),
        lax.all_gather(proj_low, "dp", axis=1, tiled=True),
        lax.all_gather(fc1_low, "dp", axis=1, tiled=True),
        lax.all_gather(fc2_low, "dp", axis=1, tiled=True),
        lax.all_gather(ada_low, "dp", axis=1, tiled=True),
    )
    condition = jnp.take(class_table, labels, axis=0) + time_embed(timesteps)
    cond_low = jax.nn.silu(condition).astype(jnp.bfloat16)
    qkv_full, proj_full, fc1_full, fc2_full, ada_full = (
        lax.all_gather(cols_qkv, "band", axis=0, tiled=True),
        lax.all_gather(cols_proj, "band", axis=0, tiled=True),
        lax.all_gather(cols_fc1, "band", axis=0, tiled=True),
        lax.all_gather(cols_fc2, "band", axis=0, tiled=True),
        lax.all_gather(cols_ada, "band", axis=0, tiled=True),
    )
    modulation = jnp.einsum("sid,de->sie", cond_low, ada_full, preferred_element_type=jnp.float32)
    kept_all, index_all = (
        lax.all_gather(kept_tokens, "band", axis=1, tiled=True),
        lax.all_gather(kept_index, "band", axis=1, tiled=True),
    )
    positions = band_index * local_rows + jnp.arange(local_rows)
    select = index_all[:, None, :] == positions[None, :, None]
    placed = jnp.einsum(
        "spj,sjd->spd", select.astype(jnp.bfloat16), kept_all, preferred_element_type=jnp.float32
    )
    unfilled = 1.0 - jnp.sum(select.astype(jnp.float32), axis=2)
    grid_rows, grid_cols, image_id = slot_layout(positions[None, :], resolution[:, None])
    tokens = placed + unfilled[..., None] * mask_token + grid_embed(grid_rows, grid_cols)
    token_mod = jax.vmap(pick_rows)(modulation, image_id)
    shift_attn, scale_attn, gate_attn, shift_mlp, scale_mlp, gate_mlp = jnp.split(
        token_mod, 6, axis=-1
    )
    attn_value, attn_pull = jax.vjp(modulate, tokens, shift_attn, scale_attn)
    hidden = attn_value.astype(jnp.bfloat16)
    qkv = jnp.einsum("std,de->ste", hidden, qkv_full, preferred_element_type=jnp.float32).astype(
        jnp.bfloat16
    )
    queries = qkv[..., :D].reshape(slot_count, local_rows, HEADS, HEAD_DIM)
    keys_in = qkv[..., D : 2 * D].reshape(slot_count, local_rows, HEADS, HEAD_DIM)
    values_in = qkv[..., 2 * D :].reshape(slot_count, local_rows, HEADS, HEAD_DIM)
    keys_all, values_all = (
        lax.all_gather(keys_in, "band", axis=1, tiled=True),
        lax.all_gather(values_in, "band", axis=1, tiled=True),
    )
    allowed = allowed_pairs(positions, jnp.arange(keys_all.shape[1]), resolution)
    attended, log_total = attend(queries, keys_all, values_all, allowed)
    attended_flat = attended.reshape(slot_count, local_rows, D)
    branch = jnp.einsum("std,de->ste", attended_flat, proj_full, preferred_element_type=jnp.float32)
    middle = tokens + gate_attn * branch
    mlp_value, mlp_pull = jax.vjp(modulate, middle, shift_mlp, scale_mlp)
    hidden_mlp = mlp_value.astype(jnp.bfloat16)
    upward = jnp.einsum("std,df->stf", hidden_mlp, fc1_full, preferred_element_type=jnp.float32)
    active_value, gelu_pull = jax.vjp(gelu_tanh, upward)
    active = active_value.astype(jnp.bfloat16)
    output = jnp.einsum("stf,fd->std", active, fc2_full, preferred_element_type=jnp.float32)
    block_out = (middle + gate_mlp * output).astype(jnp.bfloat16)
    grad_out = cotangent.astype(jnp.float32)
    grad_gate_mlp = grad_out * output
    grad_output = (gate_mlp * grad_out).astype(jnp.bfloat16)
    grad_fc2 = jnp.einsum("stf,std->fd", active, grad_output, preferred_element_type=jnp.float32)
    grad_active = jnp.einsum(
        "std,fd->stf", grad_output, fc2_full, preferred_element_type=jnp.float32
    )
    grad_upward = gelu_pull(grad_active)[0].astype(jnp.bfloat16)
    grad_fc1 = jnp.einsum(
        "std,stf->df", hidden_mlp, grad_upward, preferred_element_type=jnp.float32
    )
    grad_hidden_mlp = jnp.einsum(
        "stf,df->std", grad_upward, fc1_full, preferred_element_type=jnp.float32
    )
    grad_mid_norm, grad_shift_mlp, grad_scale_mlp = mlp_pull(grad_hidden_mlp)
    grad_middle = grad_out + grad_mid_norm
    grad_gate_attn = grad_middle * branch
    grad_branch = (gate_attn * grad_middle).astype(jnp.bfloat16)
    grad_proj = jnp.einsum(
        "std,ste->de", attended_flat, grad_branch, preferred_element_type=jnp.float32
    )
    grad_attended = jnp.einsum(
        "ste,de->std", grad_branch, proj_full, preferred_element_type=jnp.float32
    ).astype(jnp.bfloat16)
    grad_attended = grad_attended.reshape(slot_count, local_rows, HEADS, HEAD_DIM)
    grad_queries, grad_keys_part, grad_values_part = attend_back(
        queries, keys_all, values_all, allowed, log_total, grad_attended
    )
    grad_keys, grad_values = (
        lax.psum_scatter(
            grad_keys_part.astype(jnp.bfloat16), "band", scatter_dimension=1, tiled=True
        ).astype(jnp.float32),
        lax.psum_scatter(
            grad_values_part.astype(jnp.bfloat16), "band", scatter_dimension=1, tiled=True
        ).astype(jnp.float32),
    )
    grad_qkv = jnp.concatenate(
        [
            grad_queries.reshape(slot_count, local_rows, D),
            grad_keys.reshape(slot_count, local_rows, D),
            grad_values.reshape(slot_count, local_rows, D),
        ],
        axis=-1,
    ).astype(jnp.bfloat16)
    grad_qkv_weight = jnp.einsum(
        "std,ste->de", hidden, grad_qkv, preferred_element_type=jnp.float32
    )
    grad_hidden = jnp.einsum("ste,de->std", grad_qkv, qkv_full, preferred_element_type=jnp.float32)
    grad_tok_norm, grad_shift_attn, grad_scale_attn = attn_pull(grad_hidden)
    grad_tokens = grad_middle + grad_tok_norm
    grad_mod_tok = jnp.concatenate(
        [
            grad_shift_attn,
            grad_scale_attn,
            grad_gate_attn,
            grad_shift_mlp,
            grad_scale_mlp,
            grad_gate_mlp,
        ],
        axis=-1,
    )
    image_onehot = (image_id[..., None] == jnp.arange(4)).astype(jnp.float32)
    grad_modulation = jnp.einsum("spi,spe->sie", image_onehot, grad_mod_tok, precision=highest)
    grad_mask_part = jnp.sum(unfilled[..., None] * grad_tokens, axis=(0, 1))
    grad_kept_all = jnp.einsum(
        "spj,spd->sjd", select.astype(jnp.float32), grad_tokens, precision=highest
    )
    kept_grad = lax.psum_scatter(
        grad_kept_all.astype(jnp.bfloat16), "band", scatter_dimension=1, tiled=True
    ).astype(jnp.float32)
    grad_ada = jnp.einsum(
        "sid,sie->de", cond_low.astype(jnp.float32), grad_modulation, precision=highest
    )
    row_grads = (
        lax.psum_scatter(
            grad_qkv_weight.astype(jnp.bfloat16), "band", scatter_dimension=0, tiled=True
        ).astype(jnp.float32),
        lax.psum_scatter(
            grad_proj.astype(jnp.bfloat16), "band", scatter_dimension=0, tiled=True
        ).astype(jnp.float32),
        lax.psum_scatter(
            grad_fc1.astype(jnp.bfloat16), "band", scatter_dimension=0, tiled=True
        ).astype(jnp.float32),
        lax.psum_scatter(
            grad_fc2.astype(jnp.bfloat16), "band", scatter_dimension=0, tiled=True
        ).astype(jnp.float32),
        lax.psum_scatter(
            grad_ada.astype(jnp.bfloat16), "band", scatter_dimension=0, tiled=True
        ).astype(jnp.float32),
    )
    red_qkv, red_proj, red_fc1, red_fc2, red_ada = (
        lax.psum_scatter(
            row_grads[0].astype(jnp.bfloat16), "dp", scatter_dimension=1, tiled=True
        ).astype(jnp.float32),
        lax.psum_scatter(
            row_grads[1].astype(jnp.bfloat16), "dp", scatter_dimension=1, tiled=True
        ).astype(jnp.float32),
        lax.psum_scatter(
            row_grads[2].astype(jnp.bfloat16), "dp", scatter_dimension=1, tiled=True
        ).astype(jnp.float32),
        lax.psum_scatter(
            row_grads[3].astype(jnp.bfloat16), "dp", scatter_dimension=1, tiled=True
        ).astype(jnp.float32),
        lax.psum_scatter(
            row_grads[4].astype(jnp.bfloat16), "dp", scatter_dimension=1, tiled=True
        ).astype(jnp.float32),
    )
    grad_mask = lax.psum(grad_mask_part, ("dp", "band"))
    reduced = (red_qkv, red_proj, red_fc1, red_fc2, red_ada)
    local_squares = sum((jnp.sum(grad * grad) for grad in reduced))
    total_squares = lax.psum(local_squares, ("dp", "band")) + jnp.sum(grad_mask * grad_mask)
    norm_value = jnp.sqrt(total_squares)
    factor = clip_level / jnp.maximum(norm_value, clip_level)
    mask_new = adamw(mask_token, mask_first, mask_second, grad_mask * factor)
    qkv_new = adamw(w_qkv, first_qkv, second_qkv, red_qkv * factor)
    proj_new = adamw(w_proj, first_proj, second_proj, red_proj * factor)
    fc1_new = adamw(w_fc1, first_fc1, second_fc1, red_fc1 * factor)
    fc2_new = adamw(w_fc2, first_fc2, second_fc2, red_fc2 * factor)
    ada_new = adamw(w_ada, first_ada, second_ada, red_ada * factor)
    return (
        block_out,
        kept_grad,
        norm_value,
        mask_new[0],
        qkv_new[0],
        proj_new[0],
        fc1_new[0],
        fc2_new[0],
        ada_new[0],
        mask_new[1],
        qkv_new[1],
        proj_new[1],
        fc1_new[1],
        fc2_new[1],
        ada_new[1],
        mask_new[2],
        qkv_new[2],
        proj_new[2],
        fc1_new[2],
        fc2_new[2],
        ada_new[2],
    )


MASKED = -1e30
SCORE_SCALE = HEAD_DIM ** (-0.5)
LOG2E = math.log2(math.e)
VMEM_LIMIT = 63 * 1024 * 1024


def dot_nn(left, right):
    return lax.dot_general(
        left, right, (((1,), (0,)), ((), ())), preferred_element_type=jnp.float32
    )


def dot_nt(left, right):
    return lax.dot_general(
        left, right, (((1,), (1,)), ((), ())), preferred_element_type=jnp.float32
    )


def masked_scores(keys, queries, block, other):
    raw = dot_nn(keys, queries)
    parts = [
        raw[r * REGION : (r + 1) * REGION] + (0.0 if r == block else other)
        for r in range(keys.shape[0] // REGION)
    ]
    return jnp.concatenate(parts, axis=0)


def attn_head(other, queries, keys_t, values_t, out_ref, rows, lse_ref):
    keys = jnp.transpose(keys_t)
    for block in range(keys.shape[0] // REGION):
        cols = slice(block * REGION, (block + 1) * REGION)
        scores = masked_scores(keys, queries[:, cols], block, other)
        peak = jnp.max(scores, axis=0, keepdims=True)
        weights = jnp.exp2((scores - peak) * (SCORE_SCALE * LOG2E))
        total = jnp.sum(weights, axis=0, keepdims=True)
        mixed = dot_nn(values_t, weights.astype(jnp.bfloat16))
        out_ref[rows, cols] = (mixed / total).astype(jnp.bfloat16)
        lse_ref[:, cols] = peak * (SCORE_SCALE * LOG2E) + jnp.log2(total)


def attn_head_back(other, queries, keys_t, values_t, out, grad, lse_ref, grads_ref, rows):
    tokens = queries.shape[1]
    keys = jnp.transpose(keys_t)
    values = jnp.transpose(values_t)
    grad_keys = jnp.zeros((HEAD_DIM, tokens), jnp.float32)
    grad_values = jnp.zeros((HEAD_DIM, tokens), jnp.float32)
    dots = jnp.sum(out.astype(jnp.float32) * grad.astype(jnp.float32), axis=0, keepdims=True)
    for block in range(tokens // REGION):
        cols = slice(block * REGION, (block + 1) * REGION)
        scores = masked_scores(keys, queries[:, cols], block, other)
        weights = jnp.exp2(scores * (SCORE_SCALE * LOG2E) - lse_ref[:, cols])
        grad_weights = dot_nn(values, grad[:, cols])
        grad_scores = (weights * (grad_weights - dots[:, cols])).astype(jnp.bfloat16)
        grad_values += dot_nt(grad[:, cols], weights.astype(jnp.bfloat16))
        grad_keys += dot_nt(queries[:, cols], grad_scores)
        grads_ref[0, rows, cols] = (dot_nn(keys_t, grad_scores) * SCORE_SCALE).astype(jnp.bfloat16)
    grads_ref[1, rows] = (grad_keys * SCORE_SCALE).astype(jnp.bfloat16)
    grads_ref[2, rows] = grad_values.astype(jnp.bfloat16)


GELU_A = math.sqrt(2.0 / math.pi)
GELU_B = 0.044715


def mlp_kernel(h_ref, ht_ref, g_ref, gt_ref, up_ref, down_ref, out_ref, grad_ref, gup_ref, gdown_ref):
    step = pl.program_id(0)

    @pl.when(step == 0)
    def _():
        out_ref[...] = jnp.zeros_like(out_ref)
        grad_ref[...] = jnp.zeros_like(grad_ref)

    up = up_ref[...]
    down = down_ref[...]
    upward = dot_nn(h_ref[...], up)
    square = upward * upward
    curve = jnp.tanh(GELU_A * upward * (1.0 + GELU_B * square))
    half = 0.5 * (1.0 + curve)
    active = (upward * half).astype(jnp.bfloat16)
    slope = half + 0.5 * upward * (1.0 - curve * curve) * GELU_A * (
        1.0 + 3.0 * GELU_B * square
    )
    grad_upward = (dot_nn(g_ref[...], down) * slope).astype(jnp.bfloat16)
    out_ref[...] += dot_nt(active, down)
    grad_ref[...] += dot_nt(grad_upward, up)
    gup_ref[...] = dot_nn(ht_ref[...], grad_upward).astype(jnp.bfloat16)
    gdown_ref[...] = dot_nn(gt_ref[...], active).astype(jnp.bfloat16)


def mlp_both(hidden, hidden_t, grad, grad_t, up, down_t, tile):
    tokens, width = hidden.shape
    wide = up.shape[1]
    whole = lambda shape: pl.BlockSpec(shape, lambda f: (0, 0))
    part = pl.BlockSpec((width, tile), lambda f: (0, f))
    return pl.pallas_call(
        mlp_kernel,
        grid=(wide // tile,),
        in_specs=[
            whole((tokens, width)),
            whole((width, tokens)),
            whole((tokens, width)),
            whole((width, tokens)),
            part,
            part,
        ],
        out_specs=[whole((tokens, width)), whole((tokens, width)), part, part],
        out_shape=[
            jax.ShapeDtypeStruct((tokens, width), jnp.float32),
            jax.ShapeDtypeStruct((tokens, width), jnp.float32),
            jax.ShapeDtypeStruct((width, wide), jnp.bfloat16),
            jax.ShapeDtypeStruct((width, wide), jnp.bfloat16),
        ],
        compiler_params=pltpu.CompilerParams(vmem_limit_bytes=VMEM_LIMIT),
        name="mlp_both",
    )(hidden, hidden_t, grad, grad_t, up, down_t)


BLOCK_ROWS = 144
BLOCK_COLS = 1152
def flip(index):
    return index + 1 - 2 * (index % 2)


def along_z(z, step):
    return (z, flip(z), (z + 2) % 4, 3 - z)[step]


class Place:
    def __init__(self):
        dp = lax.axis_index("dp")
        band = lax.axis_index("band")
        self.z, self.y, self.x, self.core = dp // 2, dp % 2, band // 2, band % 2

    def chip(self, i, a, b):
        return (along_z(self.z, i), flip(self.y) if a else self.y, flip(self.x) if b else self.x)

    def device(self, i=0, a=0, b=0, core=0):
        z, y, x = self.chip(i, a, b)
        return (z * 2 + y, x * 2 + (flip(self.core) if core else self.core))

    def partners(self, band=False, dp=False):
        found = [
            self.device(core=1),
            self.device(b=1),
            self.device(a=1),
            self.device(i=1),
            self.device(i=2),
            self.device(i=3),
        ]
        if band:
            found.append(self.device(b=1, core=1))
        if dp:
            found += [self.device(i=i, a=1) for i in (1, 2, 3)]
        return found

    def dp(self, i=0, a=0):
        z, y, _ = self.chip(i, a, 0)
        return z * 2 + y

    def band(self, b=0, core=0):
        x = flip(self.x) if b else self.x
        return x * 2 + (flip(self.core) if core else self.core)

    def block(self, by_rows, i, a, b, core=0):
        z, y, x = self.chip(i, a, b)
        c = flip(self.core) if core else self.core
        if by_rows:
            row, col = z * 2 + y, x * 2 + c
        else:
            row, col = (x * 2 + c) * 2 + y, z
        return (
            pl.ds(pl.multiple_of(row * BLOCK_ROWS, 16), BLOCK_ROWS),
            pl.ds(pl.multiple_of(col * BLOCK_COLS, 128), BLOCK_COLS),
        )


def greet(place, band=False, dp=False):
    barrier = pltpu.get_barrier_semaphore()
    partners = place.partners(band, dp)
    for partner in partners:
        pl.semaphore_signal(
            barrier, inc=1, device_id=partner, device_id_type=pl.DeviceIdType.MESH
        )
    pl.semaphore_wait(barrier, len(partners))


def send(source, target, send_sem, recv_sem, device):
    return pltpu.make_async_remote_copy(
        src_ref=source,
        dst_ref=target,
        send_sem=send_sem,
        recv_sem=recv_sem,
        device_id=device,
        device_id_type=pl.DeviceIdType.MESH,
    )


CHIPS = [(i, a, b) for i in range(4) for a in range(2) for b in range(2)]


def slot(piece):
    return piece[0] * 4 + piece[1] * 2 + piece[2]


def parent(piece, via_x, sides_by_z):
    i, a, b = piece
    if a and b:
        return (0, 0, 1) if i in via_x else (0, 1, 0)
    if (a or b) and not (i == 1 and sides_by_z):
        return (0, a, b)
    return (i, 0, 0)


def moved(piece, step):
    return (piece[0] ^ step[0], piece[1] ^ step[1], piece[2] ^ step[2])


def children(piece, via_x, sides_by_z):
    return [
        (other, parent(other, via_x, sides_by_z))
        for other in CHIPS
        if any(other) and moved(other, parent(other, via_x, sides_by_z)) == piece
    ]


GATHER_SENDS = 31
ARRIVALS = [
    (1, 0, 0), (0, 1, 0), (0, 0, 1), (3, 0, 0), (1, 0, 1), (1, 1, 0), (2, 0, 0), (3, 1, 0),
    (3, 0, 1), (2, 0, 1), (2, 1, 0), (0, 1, 1), (1, 1, 1), (3, 1, 1), (2, 1, 1),
]


def gather_actions(
    place, plans, own_refs, full_refs, local_sems, send_sems, link_sems, core_sems, meet=None
):
    weights = range(len(own_refs))
    counts = [0] * len(own_refs)

    def ship(w, source, piece, name, sems, device):
        target = full_refs[w].at[place.block(plans[w][0], *piece)]
        send(source, target, send_sems.at[w, counts[w]], sems.at[w, slot(name)], device).start()
        counts[w] += 1

    def pass_on(w, source, piece):
        for child, step in children(piece, plans[w][1], False):
            ship(w, source, piece, child, link_sems, place.device(*step))
        ship(w, source, piece, piece, core_sems, place.device(core=1))

    def arrive(w, piece, core=0):
        target = full_refs[w].at[place.block(plans[w][0], *piece, core)]
        sems = core_sems if core else link_sems
        send(
            target, target, send_sems.at[w, 0], sems.at[w, slot(piece)], place.device(core=1)
        ).wait_recv()
        return target

    def keep(w):
        return pltpu.make_async_copy(
            own_refs[w], full_refs[w].at[place.block(plans[w][0], 0, 0, 0)], local_sems.at[w]
        )

    def begin():
        (meet or greet)(place)
        for w in weights:
            keep(w).start()
            pass_on(w, own_refs[w], (0, 0, 0))

    def relay(w, piece):
        def step():
            pass_on(w, arrive(w, piece), piece)

        return step

    def finish():
        for w in weights:
            for piece in CHIPS:
                arrive(w, piece, core=1)
            keep(w).wait()
            for n in range(counts[w]):
                send(
                    own_refs[w], own_refs[w], send_sems.at[w, n], link_sems.at[w, 0],
                    place.device(core=1),
                ).wait_send()

    return [begin] + [relay(w, piece) for w in weights for piece in ARRIVALS] + [finish]


def gather_scratch(count):
    return [
        pltpu.SemaphoreType.DMA((count,)),
        pltpu.SemaphoreType.DMA((count, GATHER_SENDS)),
        pltpu.SemaphoreType.DMA((count, 16)),
        pltpu.SemaphoreType.DMA((count, 16)),
    ]


BAND_PEERS = ((0, 1), (1, 0), (1, 1))
DP_PEERS = ((1, 0), (0, 1), (3, 0), (1, 1), (2, 0), (3, 1), (2, 1))


def swap_band(place, source, target, local_sem, send_sems, recv_sems):
    def copies():
        found = []
        for n, (b, core) in enumerate(BAND_PEERS):
            found.append(
                send(
                    source.at[place.band(b, core)],
                    target.at[place.band()],
                    send_sems.at[n],
                    recv_sems.at[n],
                    place.device(b=b, core=core),
                )
            )
        local = pltpu.make_async_copy(
            source.at[place.band()], target.at[place.band()], local_sem.at[0]
        )
        return found, local

    def start():
        found, local = copies()
        for copy in found:
            copy.start()
        local.start()

    def wait():
        found, local = copies()
        for copy in found:
            copy.wait()
        local.wait()

    return start, wait


def swap_scratch():
    return [
        pltpu.SemaphoreType.DMA((1,)),
        pltpu.SemaphoreType.DMA((3,)),
        pltpu.SemaphoreType.DMA((3,)),
    ]


def head_kernel(
    block_ref,
    cond_ref,
    ada_ref,
    kept_ref,
    index_ref,
    full_ref,
    mod_ref,
    conds_ref,
    kept_out,
    index_out,
    part_ref,
    got_ref,
    sums_ref,
    cond_sends,
    cond_recvs,
    part_sends,
    part_recvs,
    mod_sends,
    mod_recvs,
    *rest,
):
    place = Place()
    slots, _, _, cols = part_ref.shape
    images = part_ref.shape[2]
    plans = ((False, (0,)),)
    actions = gather_actions(
        place, plans, [block_ref], [full_ref], *rest[:4], meet=lambda _: None
    )
    kept_start, kept_wait = swap_band(place, kept_ref, kept_out, *rest[4:7])
    index_start, index_wait = swap_band(place, index_ref, index_out, *rest[7:10])

    def to_dp(n, source, target, sends, recvs):
        i, a = DP_PEERS[n]
        return send(source, target, sends.at[n], recvs.at[n], place.device(i=i, a=a))

    greet(place, band=True, dp=True)
    own = place.dp()
    cond_copies = [
        to_dp(n, cond_ref, conds_ref.at[own], cond_sends, cond_recvs) for n in range(7)
    ]
    for copy in cond_copies:
        copy.start()
    actions[0]()
    index_start()
    conds_ref[own] = cond_ref[...]
    for copy in cond_copies:
        copy.wait()
    for s in range(slots):
        rows = conds_ref[:, s].reshape(-1, cond_ref.shape[-1]).astype(jnp.bfloat16)
        product = dot_nn(rows, ada_ref[...])
        part_ref[s] = product.reshape(-1, cond_ref.shape[1], cols)[:, :images]
    part_copies = [
        send(
            part_ref.at[place.band(b, core)],
            got_ref.at[n],
            part_sends.at[n],
            part_recvs.at[n],
            place.device(b=b, core=core),
        )
        for n, (b, core) in enumerate(BAND_PEERS)
    ]
    for copy in part_copies:
        copy.start()
    for action in actions[1:4]:
        action()
    kept_start()
    for action in actions[4:8]:
        action()
    for copy in part_copies:
        copy.wait()
    sums_ref[...] = part_ref[place.band()] + got_ref[0] + got_ref[1] + got_ref[2]
    mod_copies = [
        to_dp(n, sums_ref.at[place.dp(*DP_PEERS[n])], mod_ref.at[own], mod_sends, mod_recvs)
        for n in range(7)
    ]
    for copy in mod_copies:
        copy.start()
    mod_ref[own] = sums_ref[own]
    for action in actions[8:]:
        action()
    for copy in mod_copies:
        copy.wait()
    index_wait()
    kept_wait()


def head(block, cond, ada, kept, index, collective_id):
    slots, images_pad, width = cond.shape
    images = 4
    cols = ada.shape[1]
    groups = lax.axis_size("dp")
    vmem = pl.BlockSpec(memory_space=pltpu.VMEM)
    hbm = pl.BlockSpec(memory_space=pl.ANY)
    f32 = jnp.float32
    return pl.pallas_call(
        head_kernel,
        in_specs=[vmem, vmem, vmem, hbm, hbm],
        out_specs=[hbm, vmem, vmem, hbm, hbm],
        out_shape=[
            jax.ShapeDtypeStruct((8 * BLOCK_ROWS, 4 * BLOCK_COLS), jnp.bfloat16),
            jax.ShapeDtypeStruct((groups, images, cols), f32),
            jax.ShapeDtypeStruct((groups,) + cond.shape, f32),
            jax.ShapeDtypeStruct(kept.shape, kept.dtype),
            jax.ShapeDtypeStruct(index.shape, index.dtype),
        ],
        scratch_shapes=[
            pltpu.VMEM((slots, groups, images, cols), f32),
            pltpu.VMEM((3, groups, images, cols), f32),
            pltpu.VMEM((groups, images, cols), f32),
            pltpu.SemaphoreType.DMA((7,)),
            pltpu.SemaphoreType.DMA((7,)),
            pltpu.SemaphoreType.DMA((3,)),
            pltpu.SemaphoreType.DMA((3,)),
            pltpu.SemaphoreType.DMA((7,)),
            pltpu.SemaphoreType.DMA((7,)),
        ]
        + gather_scratch(1)
        + swap_scratch()
        + swap_scratch(),
        compiler_params=pltpu.CompilerParams(
            collective_id=collective_id, has_side_effects=True, vmem_limit_bytes=VMEM_LIMIT
        ),
        name="head",
    )(block, cond, ada, kept, index)


FOLDS = [
    (1, 1, 1), (3, 1, 1), (2, 1, 1), (0, 1, 1), (1, 0, 0), (1, 1, 0), (1, 0, 1), (3, 1, 0),
    (3, 0, 1), (2, 1, 0), (2, 0, 1), (0, 1, 0), (0, 0, 1), (3, 0, 0), (2, 0, 0), (0, 0, 0),
]
STAGES = 4


def scatter_actions(
    place,
    plans,
    grad_refs,
    out_refs,
    held_refs,
    over_refs,
    stage,
    stage_sems,
    send_sems,
    held_sems,
    over_sems,
    meet=None,
):
    weights = range(len(grad_refs))
    counts = [0] * len(grad_refs)
    order = [(w, piece) for w in weights for piece in FOLDS]

    def ship(w, source, target, recv_sem, device):
        send(source, target, send_sems.at[w, counts[w]], recv_sem, device).start()
        counts[w] += 1

    def landed(target, recv_sem):
        send(target, target, send_sems.at[0, 0], recv_sem, place.device(core=1)).wait_recv()

    def begin():
        (meet or greet)(place)
        for w, piece in order:
            source = grad_refs[w].at[place.block(plans[w][0], *piece, 1)]
            s = slot(piece)
            ship(w, source, held_refs.at[w, s], held_sems.at[w, s], place.device(core=1))

    def load(n):
        w, piece = order[n]
        return pltpu.make_async_copy(
            grad_refs[w].at[place.block(plans[w][0], *piece)],
            stage.at[n % STAGES],
            stage_sems.at[n % STAGES],
        )

    def up(w, piece):
        step = parent(piece, plans[w][1], True)
        s = slot(piece)
        ship(
            w, held_refs.at[w, s], over_refs.at[w, s - 1], over_sems.at[w, s - 1], place.device(*step)
        )

    def fold(n):
        def step():
            if n == 0:
                for ahead in range(STAGES - 1):
                    load(ahead).start()
            if n + STAGES - 1 < len(order):
                load(n + STAGES - 1).start()
            w, piece = order[n]
            s = slot(piece)
            load(n).wait()
            landed(held_refs.at[w, s], held_sems.at[w, s])
            held = held_refs.at[w, s]
            held[...] = held[...] + stage[n % STAGES]
            if not children(piece, plans[w][1], True):
                up(w, piece)

        return step

    def combine(w, piece):
        def step():
            held = held_refs.at[w, slot(piece)]
            total = held[...].astype(jnp.float32)
            for child, _ in children(piece, plans[w][1], True):
                k = slot(child) - 1
                landed(over_refs.at[w, k], over_sems.at[w, k])
                total = total + over_refs[w, k].astype(jnp.float32)
            if any(piece):
                held[...] = total.astype(jnp.bfloat16)
                up(w, piece)
            else:
                out_refs[w][...] = total.astype(jnp.bfloat16)

        return step

    def finish():
        for w in weights:
            block = held_refs.at[w, 0]
            for n in range(counts[w]):
                send(
                    block, block, send_sems.at[w, n], held_sems.at[w, 0], place.device(core=1)
                ).wait_send()

    inner = lambda w: [p for p in FOLDS if any(p) and children(p, plans[w][1], True)]
    early = [[p for p in inner(w) if p[0] and (p[1] or p[2])] for w in weights]
    late = [[p for p in inner(w) if p not in early[w]] for w in weights]
    steps = [begin] + [fold(n) for n in range(len(order))]
    steps += [combine(w, p) for w in weights for p in early[w]]
    steps += [combine(w, p) for w in weights for p in late[w]]
    steps += [combine(w, (0, 0, 0)) for w in weights]
    return steps + [finish]


def scatter_scratch(count):
    blocks = lambda n: pltpu.VMEM((count, n, BLOCK_ROWS, BLOCK_COLS), jnp.bfloat16)
    return [
        blocks(16),
        blocks(15),
        pltpu.VMEM((STAGES, BLOCK_ROWS, BLOCK_COLS), jnp.bfloat16),
        pltpu.SemaphoreType.DMA((STAGES,)),
        pltpu.SemaphoreType.DMA((count, 31)),
        pltpu.SemaphoreType.DMA((count, 16)),
        pltpu.SemaphoreType.DMA((count, 15)),
    ]


def to_dp_peer(place, n, source, target, sends, recvs):
    i, a = DP_PEERS[n]
    return send(source, target, sends.at[n], recvs.at[n], place.device(i=i, a=a))


def to_band_peer(place, n, source, target, sends, recvs):
    b, core = BAND_PEERS[n]
    return send(source, target, sends.at[n], recvs.at[n], place.device(b=b, core=core))


def square_sum(values):
    wide = values.astype(jnp.float32)
    return jnp.sum(jnp.sum(wide * wide, axis=0, keepdims=True), axis=1, keepdims=True)


def tail_kernel(
    grad_ref,
    kind_ref,
    fc1_ref,
    fc2_ref,
    index_ref,
    index_t_ref,
    scales_ref,
    sums_ref,
    conds_ref,
    tokens_hbm,
    middle_hbm,
    hidden_hbm,
    own_ref,
    other_ref,
    fc1_other_ref,
    ada_ref,
    mask_out,
    square_out,
    kept_out,
    tokens,
    grad_middle,
    grad_hidden,
    kept_total,
    kept,
    six,
    mask_own,
    mods_own,
    mods_dp,
    mods_all,
    mask_band,
    mask_sum,
    mask_dp,
    square_own,
    square_band,
    square_sum_ref,
    square_dp,
    load_sems,
    y_sends,
    y_recvs,
    dp_sends,
    dp_recvs,
    band_sends,
    band_recvs,
    *rest,
):
    place = Place()
    plans = ((False, (0,)),)
    actions = scatter_actions(
        place, plans, [grad_ref], [own_ref], *rest[:7], meet=lambda _: None
    )
    kept_start, kept_wait = swap_band(place, kept, kept_out, *rest[7:10])
    across = lambda n, source, target: send(
        source, target, y_sends.at[n], y_recvs.at[n], place.device(a=1)
    )
    to_dp = lambda k, n, source, target: to_dp_peer(
        place, n, source, target, dp_sends.at[k], dp_recvs.at[k]
    )
    to_band = lambda k, n, source, target: to_band_peer(
        place, n, source, target, band_sends.at[k], band_recvs.at[k]
    )
    greet(place, band=True, dp=True)
    own = place.dp()
    loads = [
        pltpu.make_async_copy(source, target, load_sems.at[n])
        for n, (source, target) in enumerate(
            [(tokens_hbm, tokens), (middle_hbm, grad_middle), (hidden_hbm, grad_hidden)]
        )
    ]
    for copy in loads:
        copy.start()
    actions[0]()
    fc1_copy = across(0, fc1_ref, fc1_other_ref)
    fc1_copy.start()
    for action in actions[1:6]:
        action()
    for copy in loads:
        copy.wait()

    count = tokens.shape[0]
    regions = count // REGION
    done = 6
    for region in range(regions):
        spot = slice(region * REGION, (region + 1) * REGION)
        grad = grad_hidden[spot]
        normal, root = norm_parts(tokens[spot])
        scale = scales_ref[SCALE_ATTN, region : region + 1]
        grad_tokens = grad_middle[spot] + norm_back(grad, normal, root, scale)
        six[0, region : region + 1] = column_sum(grad)
        six[1, region : region + 1] = column_sum(grad * normal)
        for k in range(4):
            six[2 + k, region : region + 1] = sums_ref[region, k : k + 1]
        unfilled = 1.0 - jnp.sum(chosen_rows(index_ref, region), axis=1, keepdims=True)
        masked = column_sum(unfilled * grad_tokens)
        columns = lax.broadcasted_iota(jnp.int32, (index_t_ref.shape[0], REGION), 1)
        select = (index_t_ref[...] == columns + region * REGION).astype(jnp.float32)
        added = dot_nn(select.astype(jnp.bfloat16), grad_tokens.astype(jnp.bfloat16))
        if region == 0:
            mask_own[...] = jnp.broadcast_to(masked, mask_own.shape)
            kept_total[...] = added
        else:
            mask_own[...] += jnp.broadcast_to(masked, mask_own.shape)
            kept_total[...] += added
        for action in actions[done : done + 3]:
            action()
        done += 3
    kept[...] = kept_total[...].astype(jnp.bfloat16).reshape(kept.shape)
    images = six.shape[1]
    first = lax.broadcasted_iota(jnp.int32, six.shape[1:], 0) == 0
    flat = []
    for k in range(6):
        part = six[k]
        flat.append(
            jnp.where(kind_ref[0] == 1, part, jnp.where(first, column_sum(part), 0.0))
        )
    flat = jnp.concatenate(flat, axis=1)
    groups, padded, cols = mods_own.shape
    for d in range(groups):
        mods_own[d, :images] = flat[:, d * cols : (d + 1) * cols]
        mods_own[d, images:] = jnp.zeros((padded - images, cols), jnp.float32)

    early = [to_dp(0, n, mods_own.at[place.dp(*DP_PEERS[n])], mods_dp.at[own]) for n in range(7)]
    early += [to_band(0, n, mask_own, mask_band.at[n]) for n in range(3)]
    for copy in early:
        copy.start()
    kept_start()
    mods_dp[own] = mods_own[own]
    for action in actions[done : done + 3]:
        action()
    done += 3
    for copy in early:
        copy.wait()
    mask_sum[...] = mask_own[...] + mask_band[0] + mask_band[1] + mask_band[2]
    second = [to_band(1, n, mods_dp, mods_all.at[place.band()]) for n in range(3)]
    second += [to_dp(1, n, mask_sum, mask_dp.at[n]) for n in range(7)]
    for copy in second:
        copy.start()
    mods_all[place.band()] = mods_dp[...]
    fc1_copy.wait()
    for action in actions[done : done + 3]:
        action()
    done += 3
    for copy in second:
        copy.wait()
    total = mask_sum[...]
    for n in range(7):
        total = total + mask_dp[n]
    mask_out[...] = total
    width = ada_ref.shape[0]
    ada = jnp.zeros(ada_ref.shape, jnp.float32)
    for s in range(conds_ref.shape[1]):
        ada += lax.dot_general(
            conds_ref[:, s].reshape(-1, width),
            mods_all[s].reshape(-1, ada_ref.shape[1]),
            (((0,), (0,)), ((), ())),
            precision=lax.Precision.HIGHEST,
            preferred_element_type=jnp.float32,
        )
    ada_ref[...] = ada
    squares = square_sum(ada) + square_sum(fc1_ref[...]) + square_sum(fc2_ref[...])
    for action in actions[done:-1]:
        action()
    last = across(1, own_ref, other_ref)
    last.start()
    squares = squares + square_sum(own_ref[...])
    square_own[...] = jnp.broadcast_to(squares, square_own.shape)
    third = [to_band(2, n, square_own, square_band.at[n]) for n in range(3)]
    for copy in third:
        copy.start()
    for copy in third:
        copy.wait()
    square_sum_ref[...] = square_own[...] + square_band[0] + square_band[1] + square_band[2]
    fourth = [to_dp(2, n, square_sum_ref, square_dp.at[n]) for n in range(7)]
    for copy in fourth:
        copy.start()
    for copy in fourth:
        copy.wait()
    total = square_sum_ref[...]
    for n in range(7):
        total = total + square_dp[n]
    square_out[...] = total
    last.wait()
    kept_wait()
    actions[-1]()


def tail(
    grad, kind, fc1, fc2, index, mod, sums, conds, tokens, grad_middle, grad_hidden, bands, collective_id
):
    f32, bf16 = jnp.float32, jnp.bfloat16
    vmem = pl.BlockSpec(memory_space=pltpu.VMEM)
    hbm = pl.BlockSpec(memory_space=pl.ANY)
    block = jax.ShapeDtypeStruct((BLOCK_ROWS, BLOCK_COLS), bf16)
    squares = (8, 128)
    mask = (8, D)
    count, width = tokens.shape
    places = index.shape[1]
    groups, _, padded, rows_ada = conds.shape
    cols_ada = 6 * D // groups
    mods = (groups, padded, cols_ada)
    kept = (bands, places // bands, width)
    dma = pltpu.SemaphoreType.DMA
    return pl.pallas_call(
        tail_kernel,
        in_specs=[hbm, pl.BlockSpec(memory_space=pltpu.SMEM)] + [vmem] * 7 + [hbm] * 3,
        out_specs=[vmem] * 6 + [hbm],
        out_shape=[
            block,
            block,
            block,
            jax.ShapeDtypeStruct((rows_ada, cols_ada), f32),
            jax.ShapeDtypeStruct(mask, f32),
            jax.ShapeDtypeStruct(squares, f32),
            jax.ShapeDtypeStruct(kept, bf16),
        ],
        scratch_shapes=[
            pltpu.VMEM((count, width), f32),
            pltpu.VMEM((count, width), f32),
            pltpu.VMEM((count, width), f32),
            pltpu.VMEM((places, width), f32),
            pltpu.VMEM(kept, bf16),
            pltpu.VMEM(mod.shape, f32),
            pltpu.VMEM(mask, f32),
            pltpu.VMEM(mods, f32),
            pltpu.VMEM(mods, f32),
            pltpu.VMEM((bands,) + mods, f32),
            pltpu.VMEM((3,) + mask, f32),
            pltpu.VMEM(mask, f32),
            pltpu.VMEM((7,) + mask, f32),
            pltpu.VMEM(squares, f32),
            pltpu.VMEM((3,) + squares, f32),
            pltpu.VMEM(squares, f32),
            pltpu.VMEM((7,) + squares, f32),
            dma((3,)),
            dma((2,)),
            dma((2,)),
            dma((3, 7)),
            dma((3, 7)),
            dma((3, 3)),
            dma((3, 3)),
        ]
        + scatter_scratch(1)
        + swap_scratch(),
        compiler_params=pltpu.CompilerParams(
            collective_id=collective_id, has_side_effects=True, vmem_limit_bytes=VMEM_LIMIT
        ),
        name="tail",
    )(
        grad, kind, fc1, fc2, index, index.reshape(places, 1), mod, sums, conds,
        tokens, grad_middle, grad_hidden,
    )


def adam_kernel(odd_ref, factor_ref, own_ref, other_ref, fc1_ref, fc1_other_ref, fc2_ref, ada_ref, *refs):
    weights, outs = refs[:15], refs[15:]
    odd = odd_ref[0] == 1
    factor = factor_ref[0]
    qkv = weights[0].shape[1]
    proj = weights[1].shape[0]
    fc1 = weights[2].shape[1]

    def pair(own, other):
        own, other = own[...].astype(jnp.float32), other[...].astype(jnp.float32)
        return jnp.where(odd, other, own), jnp.where(odd, own, other)

    def half(block, first, cols):
        return jnp.where(
            odd, block[:, first + cols : first + 2 * cols], block[:, first : first + cols]
        )

    def step(n, rows, grad):
        new = adamw(weights[n][rows], weights[5 + n][rows], weights[10 + n][rows], grad * factor)
        for k in range(3):
            outs[5 * k + n][rows] = new[k]

    projs = []
    for k, block in enumerate(pair(own_ref, other_ref)):
        rows = slice(k * BLOCK_ROWS, (k + 1) * BLOCK_ROWS)
        step(0, rows, half(block, 0, qkv))
        projs.append(half(block, 2 * qkv, proj))
    step(1, slice(None), jnp.transpose(jnp.concatenate(projs, axis=0)))
    for k, block in enumerate(pair(fc1_ref, fc1_other_ref)):
        rows = slice(k * BLOCK_ROWS, (k + 1) * BLOCK_ROWS)
        step(2, rows, half(block, 0, fc1))
    step(3, slice(None), fc2_ref[...].astype(jnp.float32))
    step(4, slice(None), ada_ref[...])


def adam_all(odd, factor, sums, weights):
    turn = lambda values: [v.T if n % 5 in (1, 3) else v for n, v in enumerate(values)]
    weights = turn(weights)
    vmem = pl.BlockSpec(memory_space=pltpu.VMEM)
    smem = pl.BlockSpec(memory_space=pltpu.SMEM)
    new = pl.pallas_call(
        adam_kernel,
        in_specs=[smem, smem] + [vmem] * (6 + 15),
        out_specs=[vmem] * 15,
        out_shape=[jax.ShapeDtypeStruct(w.shape, w.dtype) for w in weights],
        compiler_params=pltpu.CompilerParams(vmem_limit_bytes=VMEM_LIMIT),
        name="adam_all",
    )(odd, factor, *sums, *weights)
    return turn(new)


def spread(actions, slots):
    middle = actions[1:-1]
    groups = [[] for _ in range(slots)]
    groups[0].append(actions[0])
    for n, action in enumerate(middle):
        groups[1 + n * (slots - 1) // len(middle)].append(action)
    return groups, actions[-1]


def run_slot(step, groups, first, count, stride=1):
    for k in range(count):
        group = groups[first + k * stride]

        @pl.when(step == k)
        def _():
            for action in group:
                action()


def fixed(*shape):
    return pl.BlockSpec(shape, lambda *_: (0,) * len(shape))


def once(*shape):
    return pl.BlockSpec(shape, lambda *_: (0,) * len(shape), pipeline_mode=pl.Buffered(1))


def chosen_rows(index_ref, region):
    rows = lax.broadcasted_iota(jnp.int32, (REGION, index_ref.shape[1]), 0) + region * REGION
    return (rows == index_ref[...]).astype(jnp.float32)


GATHER_PLANS = ((False, (0,)), (True, (3,)))
SCATTER_PLANS = ((False, (0, 3)), (True, (0, 3)))
SHIFT_ATTN, SCALE_ATTN, GATE_ATTN, SHIFT_MLP, SCALE_MLP, GATE_MLP = range(6)
GRANULE = 16
PAIR = 2 * HEAD_DIM
PAIRS = HEADS // 2


def embed_tokens(kind_ref, kept_ref, index_ref, mask_ref, table_ref, mod_ref, tokens, hidden, hidden_t):
    count = tokens.shape[0]
    small = kind_ref[0] == 1
    for region in range(count // REGION):
        select = chosen_rows(index_ref, region)
        placed = dot_nn(select.astype(jnp.bfloat16), kept_ref[...])
        unfilled = 1.0 - jnp.sum(select, axis=1, keepdims=True)
        tokens[pl.ds(region * REGION, REGION)] = placed + unfilled * mask_ref[...]

    def add_place(g, carry):
        first = pl.multiple_of((g % 2) * GRANULE, GRANULE)
        wide = table_ref[0, pl.ds(g // 2, 1), :] + table_ref[1, pl.ds(first, GRANULE), :]
        narrow = table_ref[0, pl.ds(g % 16, 1), :] + table_ref[1, :GRANULE]
        place = jnp.where(small, narrow, wide)
        spot = pl.ds(pl.multiple_of(g * GRANULE, GRANULE), GRANULE)
        tokens[spot, :] = tokens[spot, :] + place
        return carry

    lax.fori_loop(0, count // GRANULE, add_place, 0)
    for region in range(count // REGION):
        spot = slice(region * REGION, (region + 1) * REGION)
        normal, _ = norm_parts(tokens[spot])
        value = normal * (1.0 + mod_ref[SCALE_ATTN, region : region + 1])
        value = (value + mod_ref[SHIFT_ATTN, region : region + 1]).astype(jnp.bfloat16)
        hidden[spot] = value
        hidden_t[:, spot] = jnp.transpose(value)


def forward_kernel(
    kind_ref,
    kept_ref,
    index_ref,
    mask_ref,
    table_ref,
    mod_ref,
    weight_ref,
    fc1_ref,
    fc2_ref,
    swap_ref,
    qkv_out,
    attended_out,
    lse_out,
    branch_out,
    middle_out,
    hidden_out,
    hidden_t_out,
    gated_out,
    gated_t_out,
    tokens_hbm,
    normed_t_hbm,
    proj_hbm,
    grad_hbm,
    fc1_full,
    fc2_full,
    tokens,
    normed,
    normed_t,
    qkv,
    attended,
    proj,
    grad,
    out_sems,
    *sems,
):
    step = pl.program_id(0)
    rows = qkv_out.shape[0]
    groups = qkv.shape[0] // rows
    regions = tokens.shape[0] // REGION
    cols = D // groups
    place = Place()
    meet = functools.partial(greet, band=True)
    actions = gather_actions(
        place, GATHER_PLANS, [fc1_ref, fc2_ref], [fc1_full, fc2_full], *sems[:4], meet=meet
    )
    swap_start, swap_wait = swap_band(place, swap_ref, grad, *sems[4:])
    actions.insert(4, swap_start)
    slots, finish = spread(actions, groups + 2 * PAIRS + regions)
    outward = [
        pltpu.make_async_copy(source, target, out_sems.at[n])
        for n, (source, target) in enumerate(
            [(tokens, tokens_hbm), (normed_t, normed_t_hbm), (proj, proj_hbm), (grad, grad_hbm)]
        )
    ]

    run_slot(step, slots, 0, groups)

    @pl.when(step == 0)
    def _():
        embed_tokens(
            kind_ref, kept_ref, index_ref, mask_ref, table_ref, mod_ref, tokens, normed, normed_t
        )
        outward[0].start()
        outward[1].start()

    @pl.when(step < groups)
    def _():
        span = -(-rows // 128) * 128
        wide = dot_nn(normed[...], weight_ref[:, :span]).astype(jnp.bfloat16)
        part = jnp.transpose(wide)[:rows]
        qkv_out[...] = part
        qkv[pl.ds(pl.multiple_of(step * rows, 16), rows), :] = part
        for g in range(groups):

            @pl.when(step == g)
            def _():
                proj[:, g * cols : (g + 1) * cols] = weight_ref[:, rows:]

    pair = step - groups

    @pl.when((pair >= 0) & (pair < PAIRS))
    def _():
        @pl.when(pair == 0)
        def _():
            outward[2].start()

        other = jnp.where(kind_ref[0] == 1, MASKED, 0.0)
        spot = lambda part: pl.ds(pl.multiple_of(part * D + pair * PAIR, 16), PAIR)
        for half in range(2):
            run_slot(pair, slots, groups + half, PAIRS, 2)
            head = slice(half * HEAD_DIM, (half + 1) * HEAD_DIM)
            attn_head(
                other,
                qkv[spot(0), :][head],
                qkv[spot(1), :][head],
                qkv[spot(2), :][head],
                attended_out,
                head,
                lse_out.at[half],
            )
        attended[spot(0), :] = attended_out[...]

    region = step - groups - PAIRS
    run_slot(region, slots, groups + 2 * PAIRS, regions)

    @pl.when(region >= 0)
    def _():
        @pl.when(region == 0)
        def _():
            swap_wait()
            outward[3].start()

        spot = pl.ds(pl.multiple_of(region * REGION, REGION), REGION)
        part = lambda k: mod_ref[k, pl.ds(region, 1), :]
        branch = dot_nn(jnp.transpose(attended[:, spot]), proj[...])
        middle = tokens[spot, :] + part(GATE_ATTN) * branch
        normal, _ = norm_parts(middle)
        hidden = (normal * (1.0 + part(SCALE_MLP)) + part(SHIFT_MLP)).astype(jnp.bfloat16)
        gated = (part(GATE_MLP) * grad[region].astype(jnp.float32)).astype(jnp.bfloat16)
        branch_out[...] = branch
        middle_out[...] = middle
        hidden_out[...] = hidden
        hidden_t_out[...] = jnp.transpose(hidden)
        gated_out[...] = gated
        gated_t_out[...] = jnp.transpose(gated)

    @pl.when(region == regions - 1)
    def _():
        finish()
        for copy in outward:
            copy.wait()


def forward(kind, kept, index, mask, tables, mod, weights, blocks, swap, collective_id):
    width = kept.shape[1]
    regions = mod.shape[1]
    count = regions * REGION
    groups = weights.shape[1] // BLOCK_COLS
    rows = 3 * D // groups
    shape = jax.ShapeDtypeStruct
    bf16, f32 = jnp.bfloat16, jnp.float32
    group = lambda s: jnp.minimum(s, groups - 1)
    pair = lambda s: jnp.clip(s - groups, 0, PAIRS - 1)
    region = lambda s: jnp.clip(s - groups - PAIRS, 0, regions - 1)
    token_rows = pl.BlockSpec((REGION, width), lambda s: (region(s), 0))
    token_cols = pl.BlockSpec((width, REGION), lambda s: (0, region(s)))
    hbm = pl.BlockSpec(memory_space=pl.ANY)
    whole = shape((8 * BLOCK_ROWS, 4 * BLOCK_COLS), bf16)
    return pl.pallas_call(
        forward_kernel,
        grid=(groups + PAIRS + regions,),
        in_specs=[
            pl.BlockSpec(memory_space=pltpu.SMEM),
            once(*kept.shape),
            once(*index.shape),
            once(1, width),
            once(*tables.shape),
            once(*mod.shape),
            pl.BlockSpec((width, BLOCK_COLS), lambda s: (0, group(s))),
            once(BLOCK_ROWS, BLOCK_COLS),
            once(BLOCK_ROWS, BLOCK_COLS),
            hbm,
        ],
        out_specs=[
            pl.BlockSpec((rows, count), lambda s: (group(s), 0)),
            pl.BlockSpec((PAIR, count), lambda s: (pair(s), 0)),
            pl.BlockSpec((2, 1, count), lambda s: (pair(s), 0, 0)),
            token_rows,
            token_rows,
            token_rows,
            token_cols,
            token_rows,
            token_cols,
        ]
        + [hbm] * 6,
        out_shape=[
            shape((3 * D, count), bf16),
            shape((D, count), bf16),
            shape((HEADS, 1, count), f32),
            shape((count, width), f32),
            shape((count, width), f32),
            shape((count, width), bf16),
            shape((width, count), bf16),
            shape((count, width), bf16),
            shape((width, count), bf16),
            shape((count, width), f32),
            shape((width, count), bf16),
            shape((width, width), bf16),
            shape(swap.shape, swap.dtype),
            whole,
            whole,
        ],
        scratch_shapes=[
            pltpu.VMEM((count, width), f32),
            pltpu.VMEM((count, width), bf16),
            pltpu.VMEM((width, count), bf16),
            pltpu.VMEM((3 * D, count), bf16),
            pltpu.VMEM((D, count), bf16),
            pltpu.VMEM((width, width), bf16),
            pltpu.VMEM(swap.shape, swap.dtype),
            pltpu.SemaphoreType.DMA((4,)),
        ]
        + gather_scratch(2)
        + swap_scratch(),
        compiler_params=pltpu.CompilerParams(
            collective_id=collective_id, has_side_effects=True, vmem_limit_bytes=VMEM_LIMIT
        ),
        name="forward",
    )(kind, kept, index, mask, tables, mod, weights, *blocks, swap)


def backward_kernel(
    kind_ref,
    q_ref,
    k_ref,
    v_ref,
    attended_ref,
    grad_ref,
    lse_ref,
    weight_ref,
    normed_t_ref,
    proj_ref,
    fc1_ref,
    fc2_ref,
    swap_ref,
    out_ref,
    fc1_sum,
    fc2_sum,
    hidden_hbm,
    swapped_hbm,
    grads,
    staged,
    grad_hidden,
    out_sem,
    *sems,
):
    step = pl.program_id(0)
    rows = grads.shape[0] // (pl.num_programs(0) - PAIRS)
    groups = grads.shape[0] // rows
    cols = BLOCK_COLS - rows
    place = Place()
    meet = functools.partial(greet, band=True)
    swap_start, swap_wait = swap_band(place, swap_ref, swapped_hbm, *sems[7:])
    actions = scatter_actions(
        place, SCATTER_PLANS, [fc1_ref, fc2_ref], [fc1_sum, fc2_sum], *sems[:7], meet=meet
    )
    actions.insert(len(actions) // 2, swap_start)
    slots, finish = spread(actions, 2 * PAIRS + groups)

    @pl.when(step < PAIRS)
    def _():
        other = jnp.where(kind_ref[0] == 1, MASKED, 0.0)
        for half in range(2):
            run_slot(step, slots, half, PAIRS, 2)
            head = slice(half * HEAD_DIM, (half + 1) * HEAD_DIM)
            attn_head_back(
                other,
                q_ref[head],
                k_ref[head],
                v_ref[head],
                attended_ref[head],
                grad_ref[head],
                lse_ref.at[half],
                staged,
                head,
            )
        for part in range(3):
            spot = pl.ds(pl.multiple_of(part * D + step * PAIR, 16), PAIR)
            grads[spot, :] = staged[part]

    group = step - PAIRS
    run_slot(group, slots, 2 * PAIRS, groups)

    @pl.when(group >= 0)
    def _():
        grad = grads[pl.ds(pl.multiple_of(group * rows, 16), rows), :]
        added = dot_nt(jnp.transpose(grad), weight_ref[:, :rows])

        @pl.when(group == 0)
        def _():
            grad_hidden[...] = added

        @pl.when(group > 0)
        def _():
            grad_hidden[...] += added

        out_ref[:, :rows] = dot_nt(normed_t_ref[...], grad).astype(jnp.bfloat16)
        for g in range(groups):

            @pl.when(group == g)
            def _():
                out_ref[:, rows:] = proj_ref[:, g * cols : (g + 1) * cols]

    @pl.when(group == groups - 1)
    def _():
        outward = pltpu.make_async_copy(grad_hidden, hidden_hbm, out_sem.at[0])
        outward.start()
        finish()
        swap_wait()
        outward.wait()


def backward(
    kind, qkv, attended, grad_attended, lse, weights, normed_t, grad_proj, grads, swap, collective_id
):
    width, count = normed_t.shape
    groups = weights.shape[1] // BLOCK_COLS
    shape = jax.ShapeDtypeStruct
    bf16, f32 = jnp.bfloat16, jnp.float32
    pair = lambda s: jnp.minimum(s, PAIRS - 1)
    group = lambda s: jnp.maximum(s - PAIRS, 0)
    heads = lambda part: pl.BlockSpec((PAIR, count), lambda s: (pair(s) + part * PAIRS, 0))
    hbm = pl.BlockSpec(memory_space=pl.ANY)
    block = shape((BLOCK_ROWS, BLOCK_COLS), bf16)
    return pl.pallas_call(
        backward_kernel,
        grid=(PAIRS + groups,),
        in_specs=[
            pl.BlockSpec(memory_space=pltpu.SMEM),
            heads(0),
            heads(1),
            heads(2),
            heads(0),
            heads(0),
            pl.BlockSpec((2, 1, count), lambda s: (pair(s), 0, 0)),
            pl.BlockSpec((width, BLOCK_COLS), lambda s: (0, group(s))),
            once(width, count),
            once(width, D),
            hbm,
            hbm,
            hbm,
        ],
        out_specs=[
            pl.BlockSpec((width, BLOCK_COLS), lambda s: (0, group(s))),
            fixed(BLOCK_ROWS, BLOCK_COLS),
            fixed(BLOCK_ROWS, BLOCK_COLS),
            hbm,
            hbm,
        ],
        out_shape=[
            shape(weights.shape, bf16),
            block,
            block,
            shape((count, width), f32),
            shape(swap.shape, swap.dtype),
        ],
        scratch_shapes=[
            pltpu.VMEM((3 * D, count), bf16),
            pltpu.VMEM((3, PAIR, count), bf16),
            pltpu.VMEM((count, width), f32),
            pltpu.SemaphoreType.DMA((1,)),
        ]
        + scatter_scratch(2)
        + swap_scratch(),
        compiler_params=pltpu.CompilerParams(
            collective_id=collective_id, has_side_effects=True, vmem_limit_bytes=VMEM_LIMIT
        ),
        name="backward",
    )(kind, qkv, qkv, qkv, attended, grad_attended, lse, weights, normed_t, grad_proj, *grads, swap)


def local_call(kernel, grid, in_specs, out_specs, out_shape, scratch, name, *operands):
    return pl.pallas_call(
        kernel,
        grid=grid,
        in_specs=in_specs,
        out_specs=out_specs,
        out_shape=out_shape,
        scratch_shapes=scratch,
        compiler_params=pltpu.CompilerParams(vmem_limit_bytes=VMEM_LIMIT),
        name=name,
    )(*operands)


def column_sum(values):
    return jnp.sum(values, axis=0, keepdims=True)


def after_kernel(
    output_ref,
    grad_hidden_ref,
    middle_ref,
    branch_ref,
    grad_ref,
    attended_ref,
    proj_ref,
    mod_ref,
    block_ref,
    grad_middle_ref,
    grad_proj_ref,
    grad_attended_ref,
    sums_ref,
    total_ref,
):
    region = pl.program_id(0)
    part = lambda k: mod_ref[k, pl.ds(region, 1), :]
    output = output_ref[...]
    grad_hidden = grad_hidden_ref[...]
    middle = middle_ref[...]
    grad = grad_ref[...].astype(jnp.float32)
    block_ref[...] = (middle + part(GATE_MLP) * output).astype(jnp.bfloat16)
    normal, root = norm_parts(middle)
    grad_middle = grad + norm_back(grad_hidden, normal, root, part(SCALE_MLP))
    grad_middle_ref[...] = grad_middle
    sums_ref[0, 0:1] = column_sum(grad_middle * branch_ref[...])
    sums_ref[0, 1:2] = column_sum(grad_hidden)
    sums_ref[0, 2:3] = column_sum(grad_hidden * normal)
    sums_ref[0, 3:4] = column_sum(grad * output)
    grad_branch = (part(GATE_ATTN) * grad_middle).astype(jnp.bfloat16)
    grad_attended_ref[...] = dot_nt(proj_ref[...], grad_branch).astype(jnp.bfloat16)
    added = dot_nn(attended_ref[...], grad_branch)

    @pl.when(region == 0)
    def _():
        total_ref[...] = added

    @pl.when(region > 0)
    def _():
        total_ref[...] += added

    @pl.when(region == pl.num_programs(0) - 1)
    def _():
        grad_proj_ref[...] = total_ref[...].astype(jnp.bfloat16)


def after_mlp(output, grad_hidden, middle, branch, grad, attended_t, proj, mod):
    count, width = middle.shape
    regions = count // REGION
    rows = pl.BlockSpec((REGION, width), lambda r: (r, 0))
    columns = pl.BlockSpec((width, REGION), lambda r: (0, r))
    shape = jax.ShapeDtypeStruct
    return local_call(
        after_kernel,
        (regions,),
        [rows, rows, rows, rows, rows, columns, fixed(width, width), fixed(*mod.shape)],
        [
            rows,
            rows,
            fixed(width, width),
            columns,
            pl.BlockSpec((1, 4, width), lambda r: (r, 0, 0)),
        ],
        [
            shape((count, width), jnp.bfloat16),
            shape((count, width), jnp.float32),
            shape((width, width), jnp.bfloat16),
            shape((width, count), jnp.bfloat16),
            shape((regions, 4, width), jnp.float32),
        ],
        [pltpu.VMEM((width, width), jnp.float32)],
        "after_mlp",
        output,
        grad_hidden,
        middle,
        branch,
        grad,
        attended_t,
        proj,
        mod,
    )


def swap_columns(shard):
    pairs = [(d, d ^ 1) for d in range(lax.axis_size("dp"))]
    odd = lax.axis_index("dp") % 2
    rows = shard.shape[0] // 2
    own = lax.dynamic_slice_in_dim(shard, odd * rows, rows, axis=0)
    other = lax.dynamic_slice_in_dim(shard, (1 - odd) * rows, rows, axis=0)
    other = lax.ppermute(other, "dp", pairs)
    return jnp.where(odd == 0, jnp.stack([own, other], 1), jnp.stack([other, own], 1))


def norm_parts(values):
    center = jnp.mean(values, axis=-1, keepdims=True)
    spread = jnp.mean((values - center) ** 2, axis=-1, keepdims=True)
    root = lax.rsqrt(spread + 1e-06)
    return ((values - center) * root, root)


def norm_back(grad, normal, root, scales):
    inner = grad * (1.0 + scales)
    return root * (
        inner
        - jnp.mean(inner, axis=-1, keepdims=True)
        - normal * jnp.mean(inner * normal, axis=-1, keepdims=True)
    )


def embed_tables(count):
    quarter = D // 4
    omegas = 1.0 / 10000.0 ** (jnp.arange(quarter, dtype=jnp.float32) / quarter)
    angles = jnp.arange(count, dtype=jnp.float32)[:, None] * omegas
    return jnp.concatenate([jnp.sin(angles), jnp.cos(angles)], axis=-1)


def slot_device(
    kept_tokens,
    kept_index,
    resolution,
    labels,
    timesteps,
    class_table,
    cotangent,
    mask_token,
    w_qkv,
    w_proj,
    w_fc1,
    w_fc2,
    w_ada,
    mask_first,
    first_qkv,
    first_proj,
    first_fc1,
    first_fc2,
    first_ada,
    mask_second,
    second_qkv,
    second_proj,
    second_fc1,
    second_fc2,
    second_ada,
):
    highest = lax.Precision.HIGHEST
    bf16 = jnp.bfloat16
    bands = lax.axis_size("band")
    groups = lax.axis_size("dp")
    band = lax.axis_index("band")
    slots, local_rows, _ = cotangent.shape
    tokens_count = bands * local_rows
    regions = tokens_count // REGION
    images = labels.shape[1]

    qkv_cols, proj_cols, fc1_cols = w_qkv.shape[1], w_proj.shape[1], w_fc1.shape[1]
    swapped = swap_columns(jnp.concatenate([w_qkv, w_proj, w_fc1], axis=1).astype(bf16))
    joined_block = jnp.concatenate(
        [
            swapped[:, :, :qkv_cols].reshape(-1, 2 * qkv_cols),
            swapped[:, :, qkv_cols:-fc1_cols].reshape(-1, 2 * proj_cols),
        ],
        axis=1,
    )
    fc1_block = swapped[:, :, -fc1_cols:].reshape(-1, 2 * fc1_cols)
    fc2_block = w_fc2.astype(bf16).T

    rows_ada, cols_ada = w_ada.shape
    table_part = lax.dynamic_slice_in_dim(class_table, band * rows_ada, rows_ada, axis=1)
    chosen = labels.reshape(-1, 1) == jnp.arange(class_table.shape[0])[None, :]
    features = band * rows_ada + jnp.arange(rows_ada)
    half_width = D // 2
    frequency = jnp.exp(
        -math.log(10000.0) * (features % half_width).astype(jnp.float32) / half_width
    )
    angles = timesteps.reshape(-1, 1).astype(jnp.float32) * frequency
    waves = jnp.where(features < half_width, jnp.cos(angles), jnp.sin(angles))
    condition = jnp.matmul(chosen.astype(jnp.float32), table_part, precision=highest) + waves
    cond = jax.nn.silu(condition).astype(bf16).astype(jnp.float32)
    cond = jnp.pad(cond.reshape(slots, images, rows_ada), ((0, 0), (0, 8 - images), (0, 0)))

    kind = lax.dynamic_slice_in_dim(resolution, band, 1)
    joined_full, modulation, conds, kept, index = head(
        joined_block, cond, w_ada.astype(bf16), kept_tokens, kept_index[:, None, :], 0
    )
    kept = kept.reshape(-1, D)
    index = index.reshape(1, -1)
    modulation = modulation.transpose(1, 0, 2).reshape(images, 6, D).transpose(1, 0, 2)
    mod = jnp.where(kind[0] == 1, modulation, modulation[:, :1])
    table = embed_tables(SIDE)
    blank = jnp.zeros_like(table)
    tables = jnp.stack(
        [jnp.concatenate([table, blank], axis=1), jnp.concatenate([blank, table], axis=1)]
    )
    (
        qkv,
        attended_t,
        lse,
        branch,
        middle,
        hidden_mlp,
        hidden_mlp_t,
        grad_output,
        grad_output_t,
        tokens,
        normed_t,
        proj_full,
        grad_out,
        fc1_full,
        fc2_full,
    ) = forward(
        kind,
        kept,
        index,
        mask_token[None],
        tables,
        mod,
        joined_full,
        [fc1_block, fc2_block],
        cotangent,
        1,
    )
    grad_out = grad_out.reshape(tokens_count, D)
    output, grad_hidden_mlp, grad_fc1, grad_fc2 = mlp_both(
        hidden_mlp, hidden_mlp_t, grad_output, grad_output_t, fc1_full, fc2_full, 512
    )
    block_slot, grad_middle, grad_proj, grad_attended, sums_mlp = after_mlp(
        output, grad_hidden_mlp, middle, branch, grad_out, attended_t, proj_full, mod
    )
    grad_joined, sum_fc1, sum_fc2, grad_hidden, block_out = backward(
        kind,
        qkv,
        attended_t,
        grad_attended,
        lse,
        joined_full,
        normed_t,
        grad_proj,
        [grad_fc1, grad_fc2],
        block_slot.reshape(bands, local_rows, D),
        2,
    )
    sum_joined, other_joined, other_fc1, red_ada, grad_mask, squares, grad_kept = tail(
        grad_joined,
        kind,
        sum_fc1,
        sum_fc2,
        index,
        mod,
        sums_mlp,
        conds,
        tokens,
        grad_middle,
        grad_hidden,
        bands,
        3,
    )
    kept_grad = grad_kept.astype(jnp.float32)
    grad_mask = grad_mask[0]
    norm_value = jnp.sqrt(squares[0, 0] + jnp.sum(grad_mask * grad_mask))
    factor = clip_level / jnp.maximum(norm_value, clip_level)
    mask_new = adamw(mask_token, mask_first, mask_second, grad_mask * factor)
    odd = (lax.axis_index("dp") % 2).astype(jnp.int32)
    new = adam_all(
        odd[None],
        factor[None],
        [sum_joined, other_joined, sum_fc1, other_fc1, sum_fc2, red_ada],
        [
            w_qkv, w_proj, w_fc1, w_fc2, w_ada,
            first_qkv, first_proj, first_fc1, first_fc2, first_ada,
            second_qkv, second_proj, second_fc1, second_fc2, second_ada,
        ],
    )
    return (
        (block_out, kept_grad, norm_value)
        + (mask_new[0], *new[:5])
        + (mask_new[1], *new[5:10])
        + (mask_new[2], *new[10:])
    )


def per_device(*arguments):
    cotangent = arguments[6]
    if (lax.axis_size("dp"), lax.axis_size("band")) == (8, cotangent.shape[0]):
        return slot_device(*arguments)
    return general_device(*arguments)


def solution(mesh):
    in_specs = (
        P("dp", "band", None),
        P("dp", "band"),
        P("dp"),
        P("dp", None),
        P("dp", None),
        P(),
        P("dp", "band", None),
        P(),
        P("band", "dp"),
        P("band", "dp"),
        P("band", "dp"),
        P("band", "dp"),
        P("band", "dp"),
        P(),
        P("band", "dp"),
        P("band", "dp"),
        P("band", "dp"),
        P("band", "dp"),
        P("band", "dp"),
        P(),
        P("band", "dp"),
        P("band", "dp"),
        P("band", "dp"),
        P("band", "dp"),
        P("band", "dp"),
    )
    out_specs = (
        P("dp", "band", None),
        P("dp", "band", None),
        P(),
        P(),
        P("band", "dp"),
        P("band", "dp"),
        P("band", "dp"),
        P("band", "dp"),
        P("band", "dp"),
        P(),
        P("band", "dp"),
        P("band", "dp"),
        P("band", "dp"),
        P("band", "dp"),
        P("band", "dp"),
        P(),
        P("band", "dp"),
        P("band", "dp"),
        P("band", "dp"),
        P("band", "dp"),
        P("band", "dp"),
    )
    return jax.shard_map(
        per_device, mesh=mesh, in_specs=in_specs, out_specs=out_specs, check_vma=False
    )
```

```python
import functools
import math

import jax
import jax.numpy as jnp
from jax import lax
from jax.experimental import pallas as pl
from jax.experimental.pallas import tpu as pltpu
from jax.sharding import PartitionSpec as P

D = 1152
HEADS = 16
HEAD_DIM = 72
SIDE = 32
STEP = 10
REGION = 256


learn_rate = 0.1
beta_first = 0.9
beta_second = 0.95
adam_eps = 1e-08
decay_rate = 0.1
clip_level = 1.0


def time_embed(timestep):
    half_width = D // 2
    frequency = jnp.exp(-math.log(10000.0) * jnp.arange(half_width, dtype=jnp.float32) / half_width)
    angles = timestep.astype(jnp.float32)[..., None] * frequency
    return jnp.concatenate([jnp.cos(angles), jnp.sin(angles)], axis=-1)


def grid_embed(grid_rows, grid_cols):
    quarter = D // 4
    omegas = 1.0 / 10000.0 ** (jnp.arange(quarter, dtype=jnp.float32) / quarter)
    row_angle = grid_rows.astype(jnp.float32)[..., None] * omegas
    col_angle = grid_cols.astype(jnp.float32)[..., None] * omegas
    return jnp.concatenate(
        [jnp.sin(row_angle), jnp.cos(row_angle), jnp.sin(col_angle), jnp.cos(col_angle)], axis=-1
    )


def slot_layout(positions, slot_kinds):
    small_side = SIDE // 2
    region = positions // REGION
    inside = positions % REGION
    grid_rows = jnp.where(slot_kinds == 1, inside // small_side, positions // SIDE)
    grid_cols = jnp.where(slot_kinds == 1, inside % small_side, positions % SIDE)
    image_id = jnp.where(slot_kinds == 1, region, 0)
    return (grid_rows, grid_cols, image_id)


def modulate(values, shifts, scales):
    center = jnp.mean(values, axis=-1, keepdims=True)
    spread = jnp.mean((values - center) ** 2, axis=-1, keepdims=True)
    return (values - center) * lax.rsqrt(spread + 1e-06) * (1.0 + scales) + shifts


def gelu_tanh(values):
    return jax.nn.gelu(values, approximate=True)


def pick_rows(table_rows, picks):
    return table_rows[picks]


def allowed_pairs(query_pos, key_pos, slot_kinds):
    same_region = (query_pos // REGION)[None, :, None] == (key_pos // REGION)[None, None, :]
    return (slot_kinds[:, None, None] == 0) | same_region


def attend(queries, keys_in, values_in, allowed):

    def one_slot(pieces):
        query_s, key_s, value_s, allow_s = pieces
        scores = jnp.einsum(
            "qhd,khd->hqk", query_s, key_s, preferred_element_type=jnp.float32
        ) * HEAD_DIM ** (-0.5)
        scores = jnp.where(allow_s[None], scores, -1e30)
        row_peak = jnp.max(scores, axis=-1, keepdims=True)
        row_total = jnp.sum(jnp.exp(scores - row_peak), axis=-1, keepdims=True)
        log_total = row_peak + jnp.log(row_total)
        weights_soft = jnp.exp(scores - log_total).astype(jnp.bfloat16)
        result = jnp.einsum(
            "hqk,khd->qhd", weights_soft, value_s, preferred_element_type=jnp.float32
        )
        return (result.astype(jnp.bfloat16), log_total)

    return lax.map(one_slot, (queries, keys_in, values_in, allowed))


def attend_back(queries, keys_in, values_in, allowed, log_total, grad_attended):

    def one_slot(pieces):
        query_s, key_s, value_s, allow_s, total_s, grad_s = pieces
        scores = jnp.einsum(
            "qhd,khd->hqk", query_s, key_s, preferred_element_type=jnp.float32
        ) * HEAD_DIM ** (-0.5)
        scores = jnp.where(allow_s[None], scores, -1e30)
        weights_full = jnp.exp(scores - total_s)
        weights_soft = weights_full.astype(jnp.bfloat16)
        grad_weights = jnp.einsum(
            "qhd,khd->hqk", grad_s, value_s, preferred_element_type=jnp.float32
        )
        row_dot = jnp.sum(weights_full * grad_weights, axis=-1, keepdims=True)
        grad_scores = (weights_full * (grad_weights - row_dot) * HEAD_DIM ** (-0.5)).astype(
            jnp.bfloat16
        )
        grad_queries = jnp.einsum(
            "hqk,khd->qhd", grad_scores, key_s, preferred_element_type=jnp.float32
        )
        grad_keys = jnp.einsum(
            "hqk,qhd->khd", grad_scores, query_s, preferred_element_type=jnp.float32
        )
        grad_values = jnp.einsum(
            "hqk,qhd->khd", weights_soft, grad_s, preferred_element_type=jnp.float32
        )
        return (grad_queries, grad_keys, grad_values)

    return lax.map(one_slot, (queries, keys_in, values_in, allowed, log_total, grad_attended))


def adamw(weight, first, second, grad):
    first_new = beta_first * first + (1.0 - beta_first) * grad
    second_new = beta_second * second + (1.0 - beta_second) * grad * grad
    first_hat = first_new / (1.0 - beta_first**STEP)
    second_hat = second_new / (1.0 - beta_second**STEP)
    weight_new = weight - learn_rate * (
        first_hat / (jnp.sqrt(second_hat) + adam_eps) + decay_rate * weight
    )
    return (weight_new, first_new, second_new)


def general_device(
    kept_tokens,
    kept_index,
    resolution,
    labels,
    timesteps,
    class_table,
    cotangent,
    mask_token,
    w_qkv,
    w_proj,
    w_fc1,
    w_fc2,
    w_ada,
    mask_first,
    first_qkv,
    first_proj,
    first_fc1,
    first_fc2,
    first_ada,
    mask_second,
    second_qkv,
    second_proj,
    second_fc1,
    second_fc2,
    second_ada,
):
    highest = lax.Precision.HIGHEST
    band_index = lax.axis_index("band")
    slot_count = cotangent.shape[0]
    local_rows = cotangent.shape[1]
    qkv_low = w_qkv.astype(jnp.bfloat16)
    proj_low = w_proj.astype(jnp.bfloat16)
    fc1_low = w_fc1.astype(jnp.bfloat16)
    fc2_low = w_fc2.astype(jnp.bfloat16)
    ada_low = w_ada.astype(jnp.bfloat16)
    cols_qkv, cols_proj, cols_fc1, cols_fc2, cols_ada = (
        lax.all_gather(qkv_low, "dp", axis=1, tiled=True),
        lax.all_gather(proj_low, "dp", axis=1, tiled=True),
        lax.all_gather(fc1_low, "dp", axis=1, tiled=True),
        lax.all_gather(fc2_low, "dp", axis=1, tiled=True),
        lax.all_gather(ada_low, "dp", axis=1, tiled=True),
    )
    condition = jnp.take(class_table, labels, axis=0) + time_embed(timesteps)
    cond_low = jax.nn.silu(condition).astype(jnp.bfloat16)
    qkv_full, proj_full, fc1_full, fc2_full, ada_full = (
        lax.all_gather(cols_qkv, "band", axis=0, tiled=True),
        lax.all_gather(cols_proj, "band", axis=0, tiled=True),
        lax.all_gather(cols_fc1, "band", axis=0, tiled=True),
        lax.all_gather(cols_fc2, "band", axis=0, tiled=True),
        lax.all_gather(cols_ada, "band", axis=0, tiled=True),
    )
    modulation = jnp.einsum("sid,de->sie", cond_low, ada_full, preferred_element_type=jnp.float32)
    kept_all, index_all = (
        lax.all_gather(kept_tokens, "band", axis=1, tiled=True),
        lax.all_gather(kept_index, "band", axis=1, tiled=True),
    )
    positions = band_index * local_rows + jnp.arange(local_rows)
    select = index_all[:, None, :] == positions[None, :, None]
    placed = jnp.einsum(
        "spj,sjd->spd", select.astype(jnp.bfloat16), kept_all, preferred_element_type=jnp.float32
    )
    unfilled = 1.0 - jnp.sum(select.astype(jnp.float32), axis=2)
    grid_rows, grid_cols, image_id = slot_layout(positions[None, :], resolution[:, None])
    tokens = placed + unfilled[..., None] * mask_token + grid_embed(grid_rows, grid_cols)
    token_mod = jax.vmap(pick_rows)(modulation, image_id)
    shift_attn, scale_attn, gate_attn, shift_mlp, scale_mlp, gate_mlp = jnp.split(
        token_mod, 6, axis=-1
    )
    attn_value, attn_pull = jax.vjp(modulate, tokens, shift_attn, scale_attn)
    hidden = attn_value.astype(jnp.bfloat16)
    qkv = jnp.einsum("std,de->ste", hidden, qkv_full, preferred_element_type=jnp.float32).astype(
        jnp.bfloat16
    )
    queries = qkv[..., :D].reshape(slot_count, local_rows, HEADS, HEAD_DIM)
    keys_in = qkv[..., D : 2 * D].reshape(slot_count, local_rows, HEADS, HEAD_DIM)
    values_in = qkv[..., 2 * D :].reshape(slot_count, local_rows, HEADS, HEAD_DIM)
    keys_all, values_all = (
        lax.all_gather(keys_in, "band", axis=1, tiled=True),
        lax.all_gather(values_in, "band", axis=1, tiled=True),
    )
    allowed = allowed_pairs(positions, jnp.arange(keys_all.shape[1]), resolution)
    attended, log_total = attend(queries, keys_all, values_all, allowed)
    attended_flat = attended.reshape(slot_count, local_rows, D)
    branch = jnp.einsum("std,de->ste", attended_flat, proj_full, preferred_element_type=jnp.float32)
    middle = tokens + gate_attn * branch
    mlp_value, mlp_pull = jax.vjp(modulate, middle, shift_mlp, scale_mlp)
    hidden_mlp = mlp_value.astype(jnp.bfloat16)
    upward = jnp.einsum("std,df->stf", hidden_mlp, fc1_full, preferred_element_type=jnp.float32)
    active_value, gelu_pull = jax.vjp(gelu_tanh, upward)
    active = active_value.astype(jnp.bfloat16)
    output = jnp.einsum("stf,fd->std", active, fc2_full, preferred_element_type=jnp.float32)
    block_out = (middle + gate_mlp * output).astype(jnp.bfloat16)
    grad_out = cotangent.astype(jnp.float32)
    grad_gate_mlp = grad_out * output
    grad_output = (gate_mlp * grad_out).astype(jnp.bfloat16)
    grad_fc2 = jnp.einsum("stf,std->fd", active, grad_output, preferred_element_type=jnp.float32)
    grad_active = jnp.einsum(
        "std,fd->stf", grad_output, fc2_full, preferred_element_type=jnp.float32
    )
    grad_upward = gelu_pull(grad_active)[0].astype(jnp.bfloat16)
    grad_fc1 = jnp.einsum(
        "std,stf->df", hidden_mlp, grad_upward, preferred_element_type=jnp.float32
    )
    grad_hidden_mlp = jnp.einsum(
        "stf,df->std", grad_upward, fc1_full, preferred_element_type=jnp.float32
    )
    grad_mid_norm, grad_shift_mlp, grad_scale_mlp = mlp_pull(grad_hidden_mlp)
    grad_middle = grad_out + grad_mid_norm
    grad_gate_attn = grad_middle * branch
    grad_branch = (gate_attn * grad_middle).astype(jnp.bfloat16)
    grad_proj = jnp.einsum(
        "std,ste->de", attended_flat, grad_branch, preferred_element_type=jnp.float32
    )
    grad_attended = jnp.einsum(
        "ste,de->std", grad_branch, proj_full, preferred_element_type=jnp.float32
    ).astype(jnp.bfloat16)
    grad_attended = grad_attended.reshape(slot_count, local_rows, HEADS, HEAD_DIM)
    grad_queries, grad_keys_part, grad_values_part = attend_back(
        queries, keys_all, values_all, allowed, log_total, grad_attended
    )
    grad_keys, grad_values = (
        lax.psum_scatter(
            grad_keys_part.astype(jnp.bfloat16), "band", scatter_dimension=1, tiled=True
        ).astype(jnp.float32),
        lax.psum_scatter(
            grad_values_part.astype(jnp.bfloat16), "band", scatter_dimension=1, tiled=True
        ).astype(jnp.float32),
    )
    grad_qkv = jnp.concatenate(
        [
            grad_queries.reshape(slot_count, local_rows, D),
            grad_keys.reshape(slot_count, local_rows, D),
            grad_values.reshape(slot_count, local_rows, D),
        ],
        axis=-1,
    ).astype(jnp.bfloat16)
    grad_qkv_weight = jnp.einsum(
        "std,ste->de", hidden, grad_qkv, preferred_element_type=jnp.float32
    )
    grad_hidden = jnp.einsum("ste,de->std", grad_qkv, qkv_full, preferred_element_type=jnp.float32)
    grad_tok_norm, grad_shift_attn, grad_scale_attn = attn_pull(grad_hidden)
    grad_tokens = grad_middle + grad_tok_norm
    grad_mod_tok = jnp.concatenate(
        [
            grad_shift_attn,
            grad_scale_attn,
            grad_gate_attn,
            grad_shift_mlp,
            grad_scale_mlp,
            grad_gate_mlp,
        ],
        axis=-1,
    )
    image_onehot = (image_id[..., None] == jnp.arange(4)).astype(jnp.float32)
    grad_modulation = jnp.einsum("spi,spe->sie", image_onehot, grad_mod_tok, precision=highest)
    grad_mask_part = jnp.sum(unfilled[..., None] * grad_tokens, axis=(0, 1))
    grad_kept_all = jnp.einsum(
        "spj,spd->sjd", select.astype(jnp.float32), grad_tokens, precision=highest
    )
    kept_grad = lax.psum_scatter(
        grad_kept_all.astype(jnp.bfloat16), "band", scatter_dimension=1, tiled=True
    ).astype(jnp.float32)
    grad_ada = jnp.einsum(
        "sid,sie->de", cond_low.astype(jnp.float32), grad_modulation, precision=highest
    )
    row_grads = (
        lax.psum_scatter(
            grad_qkv_weight.astype(jnp.bfloat16), "band", scatter_dimension=0, tiled=True
        ).astype(jnp.float32),
        lax.psum_scatter(
            grad_proj.astype(jnp.bfloat16), "band", scatter_dimension=0, tiled=True
        ).astype(jnp.float32),
        lax.psum_scatter(
            grad_fc1.astype(jnp.bfloat16), "band", scatter_dimension=0, tiled=True
        ).astype(jnp.float32),
        lax.psum_scatter(
            grad_fc2.astype(jnp.bfloat16), "band", scatter_dimension=0, tiled=True
        ).astype(jnp.float32),
        lax.psum_scatter(
            grad_ada.astype(jnp.bfloat16), "band", scatter_dimension=0, tiled=True
        ).astype(jnp.float32),
    )
    red_qkv, red_proj, red_fc1, red_fc2, red_ada = (
        lax.psum_scatter(
            row_grads[0].astype(jnp.bfloat16), "dp", scatter_dimension=1, tiled=True
        ).astype(jnp.float32),
        lax.psum_scatter(
            row_grads[1].astype(jnp.bfloat16), "dp", scatter_dimension=1, tiled=True
        ).astype(jnp.float32),
        lax.psum_scatter(
            row_grads[2].astype(jnp.bfloat16), "dp", scatter_dimension=1, tiled=True
        ).astype(jnp.float32),
        lax.psum_scatter(
            row_grads[3].astype(jnp.bfloat16), "dp", scatter_dimension=1, tiled=True
        ).astype(jnp.float32),
        lax.psum_scatter(
            row_grads[4].astype(jnp.bfloat16), "dp", scatter_dimension=1, tiled=True
        ).astype(jnp.float32),
    )
    grad_mask = lax.psum(grad_mask_part, ("dp", "band"))
    reduced = (red_qkv, red_proj, red_fc1, red_fc2, red_ada)
    local_squares = sum((jnp.sum(grad * grad) for grad in reduced))
    total_squares = lax.psum(local_squares, ("dp", "band")) + jnp.sum(grad_mask * grad_mask)
    norm_value = jnp.sqrt(total_squares)
    factor = clip_level / jnp.maximum(norm_value, clip_level)
    mask_new = adamw(mask_token, mask_first, mask_second, grad_mask * factor)
    qkv_new = adamw(w_qkv, first_qkv, second_qkv, red_qkv * factor)
    proj_new = adamw(w_proj, first_proj, second_proj, red_proj * factor)
    fc1_new = adamw(w_fc1, first_fc1, second_fc1, red_fc1 * factor)
    fc2_new = adamw(w_fc2, first_fc2, second_fc2, red_fc2 * factor)
    ada_new = adamw(w_ada, first_ada, second_ada, red_ada * factor)
    return (
        block_out,
        kept_grad,
        norm_value,
        mask_new[0],
        qkv_new[0],
        proj_new[0],
        fc1_new[0],
        fc2_new[0],
        ada_new[0],
        mask_new[1],
        qkv_new[1],
        proj_new[1],
        fc1_new[1],
        fc2_new[1],
        ada_new[1],
        mask_new[2],
        qkv_new[2],
        proj_new[2],
        fc1_new[2],
        fc2_new[2],
        ada_new[2],
    )


MASKED = -1e30
SCORE_SCALE = HEAD_DIM ** (-0.5)
LOG2E = math.log2(math.e)
VMEM_LIMIT = 63 * 1024 * 1024


def dot_nn(left, right):
    return lax.dot_general(
        left, right, (((1,), (0,)), ((), ())), preferred_element_type=jnp.float32
    )


def dot_nt(left, right):
    return lax.dot_general(
        left, right, (((1,), (1,)), ((), ())), preferred_element_type=jnp.float32
    )


def masked_scores(keys, queries, block, other):
    raw = dot_nn(keys, queries)
    parts = [
        raw[r * REGION : (r + 1) * REGION] + (0.0 if r == block else other)
        for r in range(keys.shape[0] // REGION)
    ]
    return jnp.concatenate(parts, axis=0)


def attn_head(other, queries, keys_t, values_t, out_ref, rows, lse_ref):
    keys = jnp.transpose(keys_t)
    for block in range(keys.shape[0] // REGION):
        cols = slice(block * REGION, (block + 1) * REGION)
        scores = masked_scores(keys, queries[:, cols], block, other)
        peak = jnp.max(scores, axis=0, keepdims=True)
        weights = jnp.exp2((scores - peak) * (SCORE_SCALE * LOG2E))
        total = jnp.sum(weights, axis=0, keepdims=True)
        mixed = dot_nn(values_t, weights.astype(jnp.bfloat16))
        out_ref[rows, cols] = (mixed / total).astype(jnp.bfloat16)
        lse_ref[:, cols] = peak * (SCORE_SCALE * LOG2E) + jnp.log2(total)


def attn_head_back(other, queries, keys_t, values_t, out, grad, lse_ref, grads_ref, rows):
    tokens = queries.shape[1]
    keys = jnp.transpose(keys_t)
    values = jnp.transpose(values_t)
    grad_keys = jnp.zeros((HEAD_DIM, tokens), jnp.float32)
    grad_values = jnp.zeros((HEAD_DIM, tokens), jnp.float32)
    dots = jnp.sum(out.astype(jnp.float32) * grad.astype(jnp.float32), axis=0, keepdims=True)
    for block in range(tokens // REGION):
        cols = slice(block * REGION, (block + 1) * REGION)
        scores = masked_scores(keys, queries[:, cols], block, other)
        weights = jnp.exp2(scores * (SCORE_SCALE * LOG2E) - lse_ref[:, cols])
        grad_weights = dot_nn(values, grad[:, cols])
        grad_scores = (weights * (grad_weights - dots[:, cols])).astype(jnp.bfloat16)
        grad_values += dot_nt(grad[:, cols], weights.astype(jnp.bfloat16))
        grad_keys += dot_nt(queries[:, cols], grad_scores)
        grads_ref[0, rows, cols] = (dot_nn(keys_t, grad_scores) * SCORE_SCALE).astype(jnp.bfloat16)
    grads_ref[1, rows] = (grad_keys * SCORE_SCALE).astype(jnp.bfloat16)
    grads_ref[2, rows] = grad_values.astype(jnp.bfloat16)


GELU_A = math.sqrt(2.0 / math.pi)
GELU_B = 0.044715


def mlp_kernel(h_ref, ht_ref, g_ref, gt_ref, up_ref, down_ref, out_ref, grad_ref, gup_ref, gdown_ref):
    step = pl.program_id(0)

    @pl.when(step == 0)
    def _():
        out_ref[...] = jnp.zeros_like(out_ref)
        grad_ref[...] = jnp.zeros_like(grad_ref)

    up = up_ref[...]
    down = down_ref[...]
    upward = dot_nn(h_ref[...], up)
    square = upward * upward
    curve = jnp.tanh(GELU_A * upward * (1.0 + GELU_B * square))
    half = 0.5 * (1.0 + curve)
    active = (upward * half).astype(jnp.bfloat16)
    slope = half + 0.5 * upward * (1.0 - curve * curve) * GELU_A * (
        1.0 + 3.0 * GELU_B * square
    )
    grad_upward = (dot_nn(g_ref[...], down) * slope).astype(jnp.bfloat16)
    out_ref[...] += dot_nt(active, down)
    grad_ref[...] += dot_nt(grad_upward, up)
    gup_ref[...] = dot_nn(ht_ref[...], grad_upward).astype(jnp.bfloat16)
    gdown_ref[...] = dot_nn(gt_ref[...], active).astype(jnp.bfloat16)


def mlp_both(hidden, hidden_t, grad, grad_t, up, down_t, tile):
    tokens, width = hidden.shape
    wide = up.shape[1]
    whole = lambda shape: pl.BlockSpec(shape, lambda f: (0, 0))
    part = pl.BlockSpec((width, tile), lambda f: (0, f))
    return pl.pallas_call(
        mlp_kernel,
        grid=(wide // tile,),
        in_specs=[
            whole((tokens, width)),
            whole((width, tokens)),
            whole((tokens, width)),
            whole((width, tokens)),
            part,
            part,
        ],
        out_specs=[whole((tokens, width)), whole((tokens, width)), part, part],
        out_shape=[
            jax.ShapeDtypeStruct((tokens, width), jnp.float32),
            jax.ShapeDtypeStruct((tokens, width), jnp.float32),
            jax.ShapeDtypeStruct((width, wide), jnp.bfloat16),
            jax.ShapeDtypeStruct((width, wide), jnp.bfloat16),
        ],
        compiler_params=pltpu.CompilerParams(vmem_limit_bytes=VMEM_LIMIT),
        name="mlp_both",
    )(hidden, hidden_t, grad, grad_t, up, down_t)


BLOCK_ROWS = 144
BLOCK_COLS = 1152
def flip(index):
    return index + 1 - 2 * (index % 2)


def along_z(z, step):
    return (z, flip(z), (z + 2) % 4, 3 - z)[step]


class Place:
    def __init__(self):
        dp = lax.axis_index("dp")
        band = lax.axis_index("band")
        self.z, self.y, self.x, self.core = dp // 2, dp % 2, band // 2, band % 2

    def chip(self, i, a, b):
        return (along_z(self.z, i), flip(self.y) if a else self.y, flip(self.x) if b else self.x)

    def device(self, i=0, a=0, b=0, core=0):
        z, y, x = self.chip(i, a, b)
        return (z * 2 + y, x * 2 + (flip(self.core) if core else self.core))

    def partners(self, band=False, dp=False):
        found = [
            self.device(core=1),
            self.device(b=1),
            self.device(a=1),
            self.device(i=1),
            self.device(i=2),
            self.device(i=3),
        ]
        if band:
            found.append(self.device(b=1, core=1))
        if dp:
            found += [self.device(i=i, a=1) for i in (1, 2, 3)]
        return found

    def dp(self, i=0, a=0):
        z, y, _ = self.chip(i, a, 0)
        return z * 2 + y

    def band(self, b=0, core=0):
        x = flip(self.x) if b else self.x
        return x * 2 + (flip(self.core) if core else self.core)

    def block(self, by_rows, i, a, b, core=0):
        z, y, x = self.chip(i, a, b)
        c = flip(self.core) if core else self.core
        if by_rows:
            row, col = z * 2 + y, x * 2 + c
        else:
            row, col = (x * 2 + c) * 2 + y, z
        return (
            pl.ds(pl.multiple_of(row * BLOCK_ROWS, 16), BLOCK_ROWS),
            pl.ds(pl.multiple_of(col * BLOCK_COLS, 128), BLOCK_COLS),
        )


def greet(place, band=False, dp=False):
    barrier = pltpu.get_barrier_semaphore()
    partners = place.partners(band, dp)
    for partner in partners:
        pl.semaphore_signal(
            barrier, inc=1, device_id=partner, device_id_type=pl.DeviceIdType.MESH
        )
    pl.semaphore_wait(barrier, len(partners))


def send(source, target, send_sem, recv_sem, device):
    return pltpu.make_async_remote_copy(
        src_ref=source,
        dst_ref=target,
        send_sem=send_sem,
        recv_sem=recv_sem,
        device_id=device,
        device_id_type=pl.DeviceIdType.MESH,
    )


CHIPS = [(i, a, b) for i in range(4) for a in range(2) for b in range(2)]


def slot(piece):
    return piece[0] * 4 + piece[1] * 2 + piece[2]


def parent(piece, via_x, sides_by_z):
    i, a, b = piece
    if a and b:
        return (0, 0, 1) if i in via_x else (0, 1, 0)
    if (a or b) and not (i == 1 and sides_by_z):
        return (0, a, b)
    return (i, 0, 0)


def moved(piece, step):
    return (piece[0] ^ step[0], piece[1] ^ step[1], piece[2] ^ step[2])


def children(piece, via_x, sides_by_z):
    return [
        (other, parent(other, via_x, sides_by_z))
        for other in CHIPS
        if any(other) and moved(other, parent(other, via_x, sides_by_z)) == piece
    ]


GATHER_SENDS = 31


def gather_actions(place, plans, own_refs, full_refs, local_sems, send_sems, link_sems, core_sems):
    weights = range(len(own_refs))
    counts = [0] * len(own_refs)

    def ship(w, source, piece, name, sems, device):
        target = full_refs[w].at[place.block(plans[w][0], *piece)]
        send(source, target, send_sems.at[w, counts[w]], sems.at[w, slot(name)], device).start()
        counts[w] += 1

    def pass_on(w, source, piece):
        for child, step in children(piece, plans[w][1], False):
            if step[0] < 2:
                ship(w, source, piece, child, link_sems, place.device(*step))
        ship(w, source, piece, piece, core_sems, place.device(core=1))

    def arrive(w, piece, core=0):
        target = full_refs[w].at[place.block(plans[w][0], *piece, core)]
        sems = core_sems if core else link_sems
        send(
            target, target, send_sems.at[w, 0], sems.at[w, slot(piece)], place.device(core=1)
        ).wait_recv()
        return target

    def keep(w):
        return pltpu.make_async_copy(
            own_refs[w], full_refs[w].at[place.block(plans[w][0], 0, 0, 0)], local_sems.at[w]
        )

    def begin():
        for w in weights:
            keep(w).start()
            pass_on(w, own_refs[w], (0, 0, 0))

    def relay(w, *piece):
        pass_on(w, arrive(w, piece), piece)

    def late(w, i):
        ship(w, own_refs[w], (0, 0, 0), (i, 0, 0), link_sems, place.device(i))

    def finish():
        for w in weights:
            for piece in CHIPS:
                arrive(w, piece, core=1)
            keep(w).wait()
            for n in range(counts[w]):
                send(
                    own_refs[w], own_refs[w], send_sems.at[w, n], link_sems.at[w, 0],
                    place.device(core=1),
                ).wait_send()

    return begin, relay, late, finish


def gather_scratch(count):
    return [
        pltpu.SemaphoreType.DMA((count,)),
        pltpu.SemaphoreType.DMA((count, GATHER_SENDS)),
        pltpu.SemaphoreType.DMA((count, 16)),
        pltpu.SemaphoreType.DMA((count, 16)),
    ]


BAND_PEERS = ((0, 1), (1, 0), (1, 1))
DP_PEERS = ((1, 0), (0, 1), (3, 0), (1, 1), (2, 0), (3, 1), (2, 1))


def swap_band(place, source, target, local_sem, send_sems, recv_sems):
    def copies():
        found = []
        for n, (b, core) in enumerate(BAND_PEERS):
            found.append(
                send(
                    source.at[place.band(b, core)],
                    target.at[place.band()],
                    send_sems.at[n],
                    recv_sems.at[n],
                    place.device(b=b, core=core),
                )
            )
        local = pltpu.make_async_copy(
            source.at[place.band()], target.at[place.band()], local_sem.at[0]
        )
        return found, local

    def start():
        found, local = copies()
        for copy in found:
            copy.start()
        local.start()

    def wait():
        found, local = copies()
        for copy in found:
            copy.wait()
        local.wait()

    return start, wait


def swap_scratch():
    return [
        pltpu.SemaphoreType.DMA((1,)),
        pltpu.SemaphoreType.DMA((3,)),
        pltpu.SemaphoreType.DMA((3,)),
    ]


def head_kernel(
    block_ref,
    cond_ref,
    ada_ref,
    kept_ref,
    index_ref,
    full_ref,
    mod_ref,
    conds_ref,
    kept_out,
    index_out,
    part_ref,
    got_ref,
    sums_ref,
    cond_sends,
    cond_recvs,
    part_sends,
    part_recvs,
    mod_sends,
    mod_recvs,
    *rest,
):
    place = Place()
    slots, _, _, cols = part_ref.shape
    images = part_ref.shape[2]
    plans = ((False, (0,)),)
    begin, relay, late, finish = gather_actions(
        place, plans, [block_ref], [full_ref], *rest[:4]
    )

    def relays(*pieces):
        for piece in pieces:
            relay(0, *piece)

    kept_start, kept_wait = swap_band(place, kept_ref, kept_out, *rest[4:7])
    index_start, index_wait = swap_band(place, index_ref, index_out, *rest[7:10])

    def to_dp(n, source, target, sends, recvs):
        i, a = DP_PEERS[n]
        return send(source, target, sends.at[n], recvs.at[n], place.device(i=i, a=a))

    greet(place, band=True, dp=True)
    own = place.dp()
    cond_copies = [
        to_dp(n, cond_ref, conds_ref.at[own], cond_sends, cond_recvs) for n in range(7)
    ]
    for copy in cond_copies:
        copy.start()
    begin()
    index_start()
    conds_ref[own] = cond_ref[...]
    late(0, 3)
    relays((1, 0, 0))
    for copy in cond_copies:
        copy.wait()
    for s in range(slots):
        rows = conds_ref[:, s].reshape(-1, cond_ref.shape[-1]).astype(jnp.bfloat16)
        product = dot_nn(rows, ada_ref[...])
        part_ref[s] = product.reshape(-1, cond_ref.shape[1], cols)[:, :images]
    relays((0, 1, 0))
    late(0, 2)
    relays((1, 0, 1), (1, 1, 0), (3, 0, 0))
    part_copies = [
        send(
            part_ref.at[place.band(b, core)],
            got_ref.at[n],
            part_sends.at[n],
            part_recvs.at[n],
            place.device(b=b, core=core),
        )
        for n, (b, core) in enumerate(BAND_PEERS)
    ]
    for copy in part_copies:
        copy.start()
    relays((3, 0, 1), (2, 0, 0), (0, 0, 1), (0, 1, 1), (3, 1, 0))
    kept_start()
    for copy in part_copies:
        copy.wait()
    sums_ref[...] = part_ref[place.band()] + got_ref[0] + got_ref[1] + got_ref[2]
    relays((1, 1, 1))
    mod_copies = [
        to_dp(n, sums_ref.at[place.dp(*DP_PEERS[n])], mod_ref.at[own], mod_sends, mod_recvs)
        for n in range(7)
    ]
    for copy in mod_copies:
        copy.start()
    mod_ref[own] = sums_ref[own]
    relays((2, 0, 1), (3, 1, 1), (2, 1, 0), (2, 1, 1))
    finish()
    for copy in mod_copies:
        copy.wait()
    index_wait()
    kept_wait()


def head(block, cond, ada, kept, index, collective_id):
    slots, images_pad, width = cond.shape
    images = 4
    cols = ada.shape[1]
    groups = lax.axis_size("dp")
    vmem = pl.BlockSpec(memory_space=pltpu.VMEM)
    hbm = pl.BlockSpec(memory_space=pl.ANY)
    f32 = jnp.float32
    return pl.pallas_call(
        head_kernel,
        in_specs=[vmem, vmem, vmem, hbm, hbm],
        out_specs=[hbm, vmem, vmem, hbm, hbm],
        out_shape=[
            jax.ShapeDtypeStruct((8 * BLOCK_ROWS, 4 * BLOCK_COLS), jnp.bfloat16),
            jax.ShapeDtypeStruct((groups, images, cols), f32),
            jax.ShapeDtypeStruct((groups,) + cond.shape, f32),
            jax.ShapeDtypeStruct(kept.shape, kept.dtype),
            jax.ShapeDtypeStruct(index.shape, index.dtype),
        ],
        scratch_shapes=[
            pltpu.VMEM((slots, groups, images, cols), f32),
            pltpu.VMEM((3, groups, images, cols), f32),
            pltpu.VMEM((groups, images, cols), f32),
            pltpu.SemaphoreType.DMA((7,)),
            pltpu.SemaphoreType.DMA((7,)),
            pltpu.SemaphoreType.DMA((3,)),
            pltpu.SemaphoreType.DMA((3,)),
            pltpu.SemaphoreType.DMA((7,)),
            pltpu.SemaphoreType.DMA((7,)),
        ]
        + gather_scratch(1)
        + swap_scratch()
        + swap_scratch(),
        compiler_params=pltpu.CompilerParams(
            collective_id=collective_id, has_side_effects=True, vmem_limit_bytes=VMEM_LIMIT
        ),
        name="head",
    )(block, cond, ada, kept, index)


STAGES = 4


def scatter_actions(
    place,
    plans,
    order,
    grad_refs,
    out_refs,
    held_refs,
    over_refs,
    stage,
    stage_sems,
    send_sems,
    held_sems,
    over_sems,
):
    weights = range(len(grad_refs))
    counts = [0] * len(grad_refs)

    def ship(w, source, target, recv_sem, device):
        send(source, target, send_sems.at[w, counts[w]], recv_sem, device).start()
        counts[w] += 1

    def landed(target, recv_sem):
        send(target, target, send_sems.at[0, 0], recv_sem, place.device(core=1)).wait_recv()

    def begin():
        for ahead in range(STAGES - 1):
            load(ahead).start()
        for w, *piece in order:
            source = grad_refs[w].at[place.block(plans[w][0], *piece, 1)]
            s = slot(piece)
            ship(w, source, held_refs.at[w, s], held_sems.at[w, s], place.device(core=1))

    def load(n):
        w, *piece = order[n]
        return pltpu.make_async_copy(
            grad_refs[w].at[place.block(plans[w][0], *piece)],
            stage.at[n % STAGES],
            stage_sems.at[n % STAGES],
        )

    def up(w, piece):
        step = parent(piece, plans[w][1], True)
        s = slot(piece)
        ship(
            w, held_refs.at[w, s], over_refs.at[w, s - 1], over_sems.at[w, s - 1], place.device(*step)
        )

    def fold(n):
        if n + STAGES - 1 < len(order):
            load(n + STAGES - 1).start()
        w, *piece = order[n]
        s = slot(piece)
        load(n).wait()
        landed(held_refs.at[w, s], held_sems.at[w, s])
        held = held_refs.at[w, s]
        held[...] = held[...] + stage[n % STAGES]
        if not children(tuple(piece), plans[w][1], True):
            up(w, piece)

    def combine(w, *piece):
        held = held_refs.at[w, slot(piece)]
        total = held[...].astype(jnp.float32)
        for child, _ in children(piece, plans[w][1], True):
            k = slot(child) - 1
            landed(over_refs.at[w, k], over_sems.at[w, k])
            total = total + over_refs[w, k].astype(jnp.float32)
        if any(piece):
            held[...] = total.astype(jnp.bfloat16)
            up(w, piece)
        else:
            out_refs[w][...] = total.astype(jnp.bfloat16)

    def finish():
        for w in weights:
            block = held_refs.at[w, 0]
            for n in range(counts[w]):
                send(
                    block, block, send_sems.at[w, n], held_sems.at[w, 0], place.device(core=1)
                ).wait_send()

    return begin, fold, combine, finish


def scatter_scratch(count):
    blocks = lambda n: pltpu.VMEM((count, n, BLOCK_ROWS, BLOCK_COLS), jnp.bfloat16)
    return [
        blocks(16),
        blocks(15),
        pltpu.VMEM((STAGES, BLOCK_ROWS, BLOCK_COLS), jnp.bfloat16),
        pltpu.SemaphoreType.DMA((STAGES,)),
        pltpu.SemaphoreType.DMA((count, 31)),
        pltpu.SemaphoreType.DMA((count, 16)),
        pltpu.SemaphoreType.DMA((count, 15)),
    ]


def to_dp_peer(place, n, source, target, sends, recvs):
    i, a = DP_PEERS[n]
    return send(source, target, sends.at[n], recvs.at[n], place.device(i=i, a=a))


def to_band_peer(place, n, source, target, sends, recvs):
    b, core = BAND_PEERS[n]
    return send(source, target, sends.at[n], recvs.at[n], place.device(b=b, core=core))


def square_sum(values):
    wide = values.astype(jnp.float32)
    return jnp.sum(jnp.sum(wide * wide, axis=0, keepdims=True), axis=1, keepdims=True)


def tail_kernel(
    grad_ref,
    kind_ref,
    fc1_ref,
    fc2_ref,
    index_ref,
    index_t_ref,
    scales_ref,
    sums_ref,
    conds_ref,
    tokens_hbm,
    middle_hbm,
    hidden_hbm,
    own_ref,
    other_ref,
    fc1_other_ref,
    ada_ref,
    mask_out,
    square_out,
    kept_out,
    tokens,
    grad_middle,
    grad_hidden,
    kept_total,
    kept,
    six,
    mask_own,
    mods_own,
    mods_dp,
    mods_all,
    mask_band,
    mask_sum,
    mask_dp,
    square_own,
    square_band,
    square_sum_ref,
    square_dp,
    load_sems,
    y_sends,
    y_recvs,
    dp_sends,
    dp_recvs,
    band_sends,
    band_recvs,
    *rest,
):
    place = Place()
    plans = ((False, (0,)),)
    order = [
        (3, 1, 1), (0, 1, 1), (3, 0, 1), (1, 0, 0), (1, 1, 0), (2, 1, 1), (3, 1, 0), (3, 0, 0),
        (1, 1, 1), (2, 0, 1), (1, 0, 1), (2, 1, 0), (0, 0, 1), (0, 0, 0), (0, 1, 0), (2, 0, 0),
    ]
    begin, fold, combine, finish = scatter_actions(
        place, plans, [(0,) + piece for piece in order], [grad_ref], [own_ref], *rest[:7]
    )

    left = list(range(len(order)))

    def folds(count):
        for _ in range(count):
            fold(left.pop(0))

    kept_start, kept_wait = swap_band(place, kept, kept_out, *rest[7:10])
    across = lambda n, source, target: send(
        source, target, y_sends.at[n], y_recvs.at[n], place.device(a=1)
    )
    to_dp = lambda k, n, source, target: to_dp_peer(
        place, n, source, target, dp_sends.at[k], dp_recvs.at[k]
    )
    to_band = lambda k, n, source, target: to_band_peer(
        place, n, source, target, band_sends.at[k], band_recvs.at[k]
    )
    greet(place, band=True, dp=True)
    own = place.dp()
    loads = [
        pltpu.make_async_copy(source, target, load_sems.at[n])
        for n, (source, target) in enumerate(
            [(tokens_hbm, tokens), (middle_hbm, grad_middle), (hidden_hbm, grad_hidden)]
        )
    ]
    for copy in loads:
        copy.start()
    begin()
    fc1_copy = across(0, fc1_ref, fc1_other_ref)
    fc1_copy.start()
    folds(4)
    for copy in loads:
        copy.wait()

    count = tokens.shape[0]
    regions = count // REGION
    for region in range(regions):
        if region == 2:
            combine(0, 3, 0, 1)
        folds((0, 2, 2, 2)[region])
        if region == 3:
            combine(0, 2, 0, 1)
        spot = slice(region * REGION, (region + 1) * REGION)
        grad = grad_hidden[spot]
        normal, root = norm_parts(tokens[spot])
        scale = scales_ref[SCALE_ATTN, region : region + 1]
        grad_tokens = grad_middle[spot] + norm_back(grad, normal, root, scale)
        six[0, region : region + 1] = column_sum(grad)
        six[1, region : region + 1] = column_sum(grad * normal)
        for k in range(4):
            six[2 + k, region : region + 1] = sums_ref[region, k : k + 1]
        unfilled = 1.0 - jnp.sum(chosen_rows(index_ref, region), axis=1, keepdims=True)
        masked = column_sum(unfilled * grad_tokens)
        columns = lax.broadcasted_iota(jnp.int32, (index_t_ref.shape[0], REGION), 1)
        select = (index_t_ref[...] == columns + region * REGION).astype(jnp.float32)
        added = dot_nn(select.astype(jnp.bfloat16), grad_tokens.astype(jnp.bfloat16))
        if region == 0:
            mask_own[...] = jnp.broadcast_to(masked, mask_own.shape)
            kept_total[...] = added
        else:
            mask_own[...] += jnp.broadcast_to(masked, mask_own.shape)
            kept_total[...] += added
    kept[...] = kept_total[...].astype(jnp.bfloat16).reshape(kept.shape)
    images = six.shape[1]
    first = lax.broadcasted_iota(jnp.int32, six.shape[1:], 0) == 0
    flat = []
    for k in range(6):
        part = six[k]
        flat.append(
            jnp.where(kind_ref[0] == 1, part, jnp.where(first, column_sum(part), 0.0))
        )
    flat = jnp.concatenate(flat, axis=1)
    groups, padded, cols = mods_own.shape
    for d in range(groups):
        mods_own[d, :images] = flat[:, d * cols : (d + 1) * cols]
        mods_own[d, images:] = jnp.zeros((padded - images, cols), jnp.float32)

    early = [to_dp(0, n, mods_own.at[place.dp(*DP_PEERS[n])], mods_dp.at[own]) for n in range(7)]
    early += [to_band(0, n, mask_own, mask_band.at[n]) for n in range(3)]
    for copy in early:
        copy.start()
    kept_start()
    mods_dp[own] = mods_own[own]
    combine(0, 3, 0, 0)
    folds(5)
    combine(0, 1, 0, 1)
    folds(1)
    for copy in early:
        copy.wait()
    mask_sum[...] = mask_own[...] + mask_band[0] + mask_band[1] + mask_band[2]
    second = [to_band(1, n, mods_dp, mods_all.at[place.band()]) for n in range(3)]
    second += [to_dp(1, n, mask_sum, mask_dp.at[n]) for n in range(7)]
    for copy in second:
        copy.start()
    mods_all[place.band()] = mods_dp[...]
    fc1_copy.wait()
    combine(0, 2, 0, 0)
    combine(0, 0, 1, 0)
    combine(0, 0, 0, 1)
    for copy in second:
        copy.wait()
    total = mask_sum[...]
    for n in range(7):
        total = total + mask_dp[n]
    mask_out[...] = total
    width = ada_ref.shape[0]
    ada = jnp.zeros(ada_ref.shape, jnp.float32)
    for s in range(conds_ref.shape[1]):
        ada += lax.dot_general(
            conds_ref[:, s].reshape(-1, width),
            mods_all[s].reshape(-1, ada_ref.shape[1]),
            (((0,), (0,)), ((), ())),
            precision=lax.Precision.HIGHEST,
            preferred_element_type=jnp.float32,
        )
    ada_ref[...] = ada
    squares = square_sum(ada) + square_sum(fc1_ref[...]) + square_sum(fc2_ref[...])
    combine(0, 0, 0, 0)
    last = across(1, own_ref, other_ref)
    last.start()
    squares = squares + square_sum(own_ref[...])
    square_own[...] = jnp.broadcast_to(squares, square_own.shape)
    third = [to_band(2, n, square_own, square_band.at[n]) for n in range(3)]
    for copy in third:
        copy.start()
    for copy in third:
        copy.wait()
    square_sum_ref[...] = square_own[...] + square_band[0] + square_band[1] + square_band[2]
    fourth = [to_dp(2, n, square_sum_ref, square_dp.at[n]) for n in range(7)]
    for copy in fourth:
        copy.start()
    for copy in fourth:
        copy.wait()
    total = square_sum_ref[...]
    for n in range(7):
        total = total + square_dp[n]
    square_out[...] = total
    last.wait()
    kept_wait()
    finish()


def tail(
    grad, kind, fc1, fc2, index, mod, sums, conds, tokens, grad_middle, grad_hidden, bands, collective_id
):
    f32, bf16 = jnp.float32, jnp.bfloat16
    vmem = pl.BlockSpec(memory_space=pltpu.VMEM)
    hbm = pl.BlockSpec(memory_space=pl.ANY)
    block = jax.ShapeDtypeStruct((BLOCK_ROWS, BLOCK_COLS), bf16)
    squares = (8, 128)
    mask = (8, D)
    count, width = tokens.shape
    places = index.shape[1]
    groups, _, padded, rows_ada = conds.shape
    cols_ada = 6 * D // groups
    mods = (groups, padded, cols_ada)
    kept = (bands, places // bands, width)
    dma = pltpu.SemaphoreType.DMA
    return pl.pallas_call(
        tail_kernel,
        in_specs=[hbm, pl.BlockSpec(memory_space=pltpu.SMEM)] + [vmem] * 7 + [hbm] * 3,
        out_specs=[vmem] * 6 + [hbm],
        out_shape=[
            block,
            block,
            block,
            jax.ShapeDtypeStruct((rows_ada, cols_ada), f32),
            jax.ShapeDtypeStruct(mask, f32),
            jax.ShapeDtypeStruct(squares, f32),
            jax.ShapeDtypeStruct(kept, bf16),
        ],
        scratch_shapes=[
            pltpu.VMEM((count, width), f32),
            pltpu.VMEM((count, width), f32),
            pltpu.VMEM((count, width), f32),
            pltpu.VMEM((places, width), f32),
            pltpu.VMEM(kept, bf16),
            pltpu.VMEM(mod.shape, f32),
            pltpu.VMEM(mask, f32),
            pltpu.VMEM(mods, f32),
            pltpu.VMEM(mods, f32),
            pltpu.VMEM((bands,) + mods, f32),
            pltpu.VMEM((3,) + mask, f32),
            pltpu.VMEM(mask, f32),
            pltpu.VMEM((7,) + mask, f32),
            pltpu.VMEM(squares, f32),
            pltpu.VMEM((3,) + squares, f32),
            pltpu.VMEM(squares, f32),
            pltpu.VMEM((7,) + squares, f32),
            dma((3,)),
            dma((2,)),
            dma((2,)),
            dma((3, 7)),
            dma((3, 7)),
            dma((3, 3)),
            dma((3, 3)),
        ]
        + scatter_scratch(1)
        + swap_scratch(),
        compiler_params=pltpu.CompilerParams(
            collective_id=collective_id, has_side_effects=True, vmem_limit_bytes=VMEM_LIMIT
        ),
        name="tail",
    )(
        grad, kind, fc1, fc2, index, index.reshape(places, 1), mod, sums, conds,
        tokens, grad_middle, grad_hidden,
    )


def adam_kernel(odd_ref, factor_ref, own_ref, other_ref, fc1_ref, fc1_other_ref, fc2_ref, ada_ref, *refs):
    weights, outs = refs[:15], refs[15:]
    odd = odd_ref[0] == 1
    factor = factor_ref[0]
    qkv = weights[0].shape[1]
    proj = weights[1].shape[0]
    fc1 = weights[2].shape[1]

    def pair(own, other):
        own, other = own[...].astype(jnp.float32), other[...].astype(jnp.float32)
        return jnp.where(odd, other, own), jnp.where(odd, own, other)

    def half(block, first, cols):
        return jnp.where(
            odd, block[:, first + cols : first + 2 * cols], block[:, first : first + cols]
        )

    def step(n, rows, grad):
        new = adamw(weights[n][rows], weights[5 + n][rows], weights[10 + n][rows], grad * factor)
        for k in range(3):
            outs[5 * k + n][rows] = new[k]

    projs = []
    for k, block in enumerate(pair(own_ref, other_ref)):
        rows = slice(k * BLOCK_ROWS, (k + 1) * BLOCK_ROWS)
        step(0, rows, half(block, 0, qkv))
        projs.append(half(block, 2 * qkv, proj))
    step(1, slice(None), jnp.transpose(jnp.concatenate(projs, axis=0)))
    for k, block in enumerate(pair(fc1_ref, fc1_other_ref)):
        rows = slice(k * BLOCK_ROWS, (k + 1) * BLOCK_ROWS)
        step(2, rows, half(block, 0, fc1))
    step(3, slice(None), fc2_ref[...].astype(jnp.float32))
    step(4, slice(None), ada_ref[...])


def adam_all(odd, factor, sums, weights):
    turn = lambda values: [v.T if n % 5 in (1, 3) else v for n, v in enumerate(values)]
    weights = turn(weights)
    vmem = pl.BlockSpec(memory_space=pltpu.VMEM)
    smem = pl.BlockSpec(memory_space=pltpu.SMEM)
    new = pl.pallas_call(
        adam_kernel,
        in_specs=[smem, smem] + [vmem] * (6 + 15),
        out_specs=[vmem] * 15,
        out_shape=[jax.ShapeDtypeStruct(w.shape, w.dtype) for w in weights],
        compiler_params=pltpu.CompilerParams(vmem_limit_bytes=VMEM_LIMIT),
        name="adam_all",
    )(odd, factor, *sums, *weights)
    return turn(new)


def run(actions):
    for action in actions:
        action()


def run_slot(step, groups, first, count, stride=1):
    for k in range(count):
        group = groups[first + k * stride]

        @pl.when(step == k)
        def _():
            run(group)


def fixed(*shape):
    return pl.BlockSpec(shape, lambda *_: (0,) * len(shape))


def once(*shape):
    return pl.BlockSpec(shape, lambda *_: (0,) * len(shape), pipeline_mode=pl.Buffered(1))


def chosen_rows(index_ref, region):
    rows = lax.broadcasted_iota(jnp.int32, (REGION, index_ref.shape[1]), 0) + region * REGION
    return (rows == index_ref[...]).astype(jnp.float32)


GATHER_PLANS = ((False, (0,)), (True, (3,)))
SCATTER_PLANS = ((False, (0,)), (True, (0, 3)))
FORWARD_STEPS = [
    (0, 1, 3), (5, 0, 1, 0, 0), (5, 0, 3), (6, 0, 0, 1, 0), (6, 0, 0, 0, 1), (9, 1, 0, 0, 1),
    (12, 0, 1, 0, 1), (12, 0, 1, 1, 0), (12, 1, 1, 0, 0), (13, 0, 2), (14, 0, 3, 0, 0), (15,),
    (16, 1, 0, 1, 0), (16, 1, 3, 0, 0), (16, 0, 3, 0, 1), (17, 1, 2), (18, 0, 0, 1, 1),
    (21, 0, 1, 1, 1), (22, 0, 2, 0, 0), (22, 1, 1, 0, 1), (22, 1, 2, 0, 0), (26, 1, 1, 1, 0),
    (27, 0, 2, 1, 0), (27, 1, 3, 1, 0), (28, 1, 3, 0, 1), (29, 0, 2, 0, 1), (30, 1, 0, 1, 1),
    (30, 1, 1, 1, 1), (30, 1, 2, 0, 1), (31, 0, 3, 1, 0), (31, 0, 2, 1, 1), (32, 0, 3, 1, 1),
    (32, 1, 3, 1, 1), (32, 1, 2, 1, 0), (32, 1, 2, 1, 1),
]
BACKWARD_STEPS = [
    (0, 0, 0, 1, 1, 0), (0,), (0, 0, 0, 0, 0, 1), (0, 0, 0, 3, 1, 1), (0, 0, 0, 1, 1, 1),
    (0, 0, 0, 1, 0, 1), (1, 0, 1, 1, 0, 0), (1, 0, 1, 1, 1, 1), (1, 0, 1, 3, 1, 1),
    (2, 0, 1, 1, 1, 0), (2, 0, 0, 2, 0, 0), (2, 0, 0, 3, 0, 1), (3, 1, 0, 3, 0, 1),
    (3, 0, 0, 2, 1, 1), (3, 0, 1, 3, 0, 1), (4, 0, 1, 0, 1, 1), (4, 0, 0, 3, 0, 0),
    (6, 1, 0, 1, 0, 1), (6, 0, 0, 3, 1, 0), (6, 0, 1, 1, 0, 1), (6, 0, 1, 2, 1, 0),
    (7, 0, 1, 3, 1, 0), (7, 0, 1, 0, 0, 0), (7, 0, 0, 0, 0, 0), (10, 0, 0, 1, 0, 0),
    (10, 0, 1, 2, 0, 1), (10, 1, 0, 3, 0, 0), (10, 1, 1, 3, 1, 0), (11, 0, 1, 3, 0, 0),
    (11, 0, 1, 2, 1, 1), (11, 0, 1, 0, 1, 0), (11, 0, 0, 2, 0, 1), (12, 0, 0, 0, 1, 0),
    (13, 1, 0, 2, 0, 1), (13, 1, 1, 3, 0, 0), (14, 0, 0, 2, 1, 0), (14, 1, 1, 1, 0, 1),
    (15, 0, 0, 0, 1, 1), (17, 1, 0, 2, 0, 0), (17, 0, 1, 2, 0, 0), (17, 1, 1, 2, 0, 1),
    (17, 0, 1, 0, 0, 1), (18, 1, 0, 0, 1, 0), (19, 1, 0, 0, 0, 1), (19, 1, 1, 2, 0, 0),
    (19, 1, 1, 0, 0, 1), (20, 1, 1, 0, 1, 0), (21, 1, 0, 0, 0, 0), (23, 1, 1, 0, 0, 0),
]
SHIFT_ATTN, SCALE_ATTN, GATE_ATTN, SHIFT_MLP, SCALE_MLP, GATE_MLP = range(6)
GRANULE = 16
PAIR = 2 * HEAD_DIM
PAIRS = HEADS // 2


def embed_tokens(
    slots, kind_ref, kept_ref, index_ref, mask_ref, table_ref, mod_ref, tokens, hidden, hidden_t
):
    count = tokens.shape[0]
    small = kind_ref[0] == 1
    for region in range(count // REGION):
        run(slots[region])
        select = chosen_rows(index_ref, region)
        placed = dot_nn(select.astype(jnp.bfloat16), kept_ref[...])
        unfilled = 1.0 - jnp.sum(select, axis=1, keepdims=True)
        tokens[pl.ds(region * REGION, REGION)] = placed + unfilled * mask_ref[...]

    def add_place(g, carry):
        first = pl.multiple_of((g % 2) * GRANULE, GRANULE)
        wide = table_ref[0, pl.ds(g // 2, 1), :] + table_ref[1, pl.ds(first, GRANULE), :]
        narrow = table_ref[0, pl.ds(g % 16, 1), :] + table_ref[1, :GRANULE]
        place = jnp.where(small, narrow, wide)
        spot = pl.ds(pl.multiple_of(g * GRANULE, GRANULE), GRANULE)
        tokens[spot, :] = tokens[spot, :] + place
        return carry

    lax.fori_loop(0, count // GRANULE, add_place, 0)
    for region in range(count // REGION):
        run(slots[count // REGION + region])
        spot = slice(region * REGION, (region + 1) * REGION)
        normal, _ = norm_parts(tokens[spot])
        value = normal * (1.0 + mod_ref[SCALE_ATTN, region : region + 1])
        value = (value + mod_ref[SHIFT_ATTN, region : region + 1]).astype(jnp.bfloat16)
        hidden[spot] = value
        hidden_t[:, spot] = jnp.transpose(value)


def forward_kernel(
    kind_ref,
    kept_ref,
    index_ref,
    mask_ref,
    table_ref,
    mod_ref,
    weight_ref,
    fc1_ref,
    fc2_ref,
    swap_ref,
    qkv_out,
    attended_out,
    lse_out,
    branch_out,
    middle_out,
    hidden_out,
    hidden_t_out,
    gated_out,
    gated_t_out,
    tokens_hbm,
    normed_t_hbm,
    proj_hbm,
    grad_hbm,
    fc1_full,
    fc2_full,
    tokens,
    normed,
    normed_t,
    qkv,
    attended,
    proj,
    grad,
    out_sems,
    *sems,
):
    step = pl.program_id(0)
    rows = qkv_out.shape[0]
    groups = qkv.shape[0] // rows
    regions = tokens.shape[0] // REGION
    cols = D // groups
    place = Place()
    begin, relay, late, finish = gather_actions(
        place, GATHER_PLANS, [fc1_ref, fc2_ref], [fc1_full, fc2_full], *sems[:4]
    )
    swap_start, swap_wait = swap_band(place, swap_ref, grad, *sems[4:])
    first_qkv = 1 + 2 * regions
    first_head = first_qkv + groups
    first_region = first_head + HEADS
    slots = [[] for _ in range(first_region + regions)]
    slots[0] += [functools.partial(greet, place, band=True), begin]
    for when, *what in FORWARD_STEPS:
        action = {0: swap_start, 2: late, 4: relay}[len(what)]
        slots[when].append(functools.partial(action, *what))
    outward = [
        pltpu.make_async_copy(source, target, out_sems.at[n])
        for n, (source, target) in enumerate(
            [(tokens, tokens_hbm), (normed_t, normed_t_hbm), (proj, proj_hbm), (grad, grad_hbm)]
        )
    ]

    @pl.when(step == 0)
    def _():
        run(slots[0])
        embed_tokens(
            slots[1:first_qkv],
            kind_ref,
            kept_ref,
            index_ref,
            mask_ref,
            table_ref,
            mod_ref,
            tokens,
            normed,
            normed_t,
        )
        outward[0].start()
        outward[1].start()

    run_slot(step, slots, first_qkv, groups)

    @pl.when(step < groups)
    def _():
        span = -(-rows // 128) * 128
        wide = dot_nn(normed[...], weight_ref[:, :span]).astype(jnp.bfloat16)
        part = jnp.transpose(wide)[:rows]
        qkv_out[...] = part
        qkv[pl.ds(pl.multiple_of(step * rows, 16), rows), :] = part
        for g in range(groups):

            @pl.when(step == g)
            def _():
                proj[:, g * cols : (g + 1) * cols] = weight_ref[:, rows:]

    pair = step - groups

    @pl.when((pair >= 0) & (pair < PAIRS))
    def _():
        @pl.when(pair == 0)
        def _():
            outward[2].start()

        other = jnp.where(kind_ref[0] == 1, MASKED, 0.0)
        spot = lambda part: pl.ds(pl.multiple_of(part * D + pair * PAIR, 16), PAIR)
        for half in range(2):
            run_slot(pair, slots, first_head + half, PAIRS, 2)
            head = slice(half * HEAD_DIM, (half + 1) * HEAD_DIM)
            attn_head(
                other,
                qkv[spot(0), :][head],
                qkv[spot(1), :][head],
                qkv[spot(2), :][head],
                attended_out,
                head,
                lse_out.at[half],
            )
        attended[spot(0), :] = attended_out[...]

    region = step - groups - PAIRS
    run_slot(region, slots, first_region, regions)

    @pl.when(region >= 0)
    def _():
        @pl.when(region == 0)
        def _():
            swap_wait()
            outward[3].start()

        spot = pl.ds(pl.multiple_of(region * REGION, REGION), REGION)
        part = lambda k: mod_ref[k, pl.ds(region, 1), :]
        branch = dot_nn(jnp.transpose(attended[:, spot]), proj[...])
        middle = tokens[spot, :] + part(GATE_ATTN) * branch
        normal, _ = norm_parts(middle)
        hidden = (normal * (1.0 + part(SCALE_MLP)) + part(SHIFT_MLP)).astype(jnp.bfloat16)
        gated = (part(GATE_MLP) * grad[region].astype(jnp.float32)).astype(jnp.bfloat16)
        branch_out[...] = branch
        middle_out[...] = middle
        hidden_out[...] = hidden
        hidden_t_out[...] = jnp.transpose(hidden)
        gated_out[...] = gated
        gated_t_out[...] = jnp.transpose(gated)

    @pl.when(region == regions - 1)
    def _():
        finish()
        for copy in outward:
            copy.wait()


def forward(kind, kept, index, mask, tables, mod, weights, blocks, swap, collective_id):
    width = kept.shape[1]
    regions = mod.shape[1]
    count = regions * REGION
    groups = weights.shape[1] // BLOCK_COLS
    rows = 3 * D // groups
    shape = jax.ShapeDtypeStruct
    bf16, f32 = jnp.bfloat16, jnp.float32
    group = lambda s: jnp.minimum(s, groups - 1)
    pair = lambda s: jnp.clip(s - groups, 0, PAIRS - 1)
    region = lambda s: jnp.clip(s - groups - PAIRS, 0, regions - 1)
    token_rows = pl.BlockSpec((REGION, width), lambda s: (region(s), 0))
    token_cols = pl.BlockSpec((width, REGION), lambda s: (0, region(s)))
    hbm = pl.BlockSpec(memory_space=pl.ANY)
    whole = shape((8 * BLOCK_ROWS, 4 * BLOCK_COLS), bf16)
    return pl.pallas_call(
        forward_kernel,
        grid=(groups + PAIRS + regions,),
        in_specs=[
            pl.BlockSpec(memory_space=pltpu.SMEM),
            once(*kept.shape),
            once(*index.shape),
            once(1, width),
            once(*tables.shape),
            once(*mod.shape),
            pl.BlockSpec((width, BLOCK_COLS), lambda s: (0, group(s))),
            once(BLOCK_ROWS, BLOCK_COLS),
            once(BLOCK_ROWS, BLOCK_COLS),
            hbm,
        ],
        out_specs=[
            pl.BlockSpec((rows, count), lambda s: (group(s), 0)),
            pl.BlockSpec((PAIR, count), lambda s: (pair(s), 0)),
            pl.BlockSpec((2, 1, count), lambda s: (pair(s), 0, 0)),
            token_rows,
            token_rows,
            token_rows,
            token_cols,
            token_rows,
            token_cols,
        ]
        + [hbm] * 6,
        out_shape=[
            shape((3 * D, count), bf16),
            shape((D, count), bf16),
            shape((HEADS, 1, count), f32),
            shape((count, width), f32),
            shape((count, width), f32),
            shape((count, width), bf16),
            shape((width, count), bf16),
            shape((count, width), bf16),
            shape((width, count), bf16),
            shape((count, width), f32),
            shape((width, count), bf16),
            shape((width, width), bf16),
            shape(swap.shape, swap.dtype),
            whole,
            whole,
        ],
        scratch_shapes=[
            pltpu.VMEM((count, width), f32),
            pltpu.VMEM((count, width), bf16),
            pltpu.VMEM((width, count), bf16),
            pltpu.VMEM((3 * D, count), bf16),
            pltpu.VMEM((D, count), bf16),
            pltpu.VMEM((width, width), bf16),
            pltpu.VMEM(swap.shape, swap.dtype),
            pltpu.SemaphoreType.DMA((4,)),
        ]
        + gather_scratch(2)
        + swap_scratch(),
        compiler_params=pltpu.CompilerParams(
            collective_id=collective_id, has_side_effects=True, vmem_limit_bytes=VMEM_LIMIT
        ),
        name="forward",
    )(kind, kept, index, mask, tables, mod, weights, *blocks, swap)


def backward_kernel(
    kind_ref,
    q_ref,
    k_ref,
    v_ref,
    attended_ref,
    grad_ref,
    lse_ref,
    weight_ref,
    normed_t_ref,
    proj_ref,
    fc1_ref,
    fc2_ref,
    swap_ref,
    out_ref,
    fc1_sum,
    fc2_sum,
    hidden_hbm,
    swapped_hbm,
    grads,
    staged,
    grad_hidden,
    out_sem,
    *sems,
):
    step = pl.program_id(0)
    rows = grads.shape[0] // (pl.num_programs(0) - PAIRS)
    groups = grads.shape[0] // rows
    cols = BLOCK_COLS - rows
    place = Place()
    swap_start, swap_wait = swap_band(place, swap_ref, swapped_hbm, *sems[7:])
    order = [what[1:] for _, *what in BACKWARD_STEPS if what and not what[0]]
    begin, fold, combine, finish = scatter_actions(
        place, SCATTER_PLANS, order, [fc1_ref, fc2_ref], [fc1_sum, fc2_sum], *sems[:7]
    )
    slots = [[] for _ in range(HEADS + 2 * groups)]
    slots[0] += [functools.partial(greet, place, band=True), begin]
    folded = 0
    for when, *what in BACKWARD_STEPS:
        if not what:
            slots[when].append(swap_start)
        elif what[0]:
            slots[when].append(functools.partial(combine, *what[1:]))
        else:
            slots[when].append(functools.partial(fold, folded))
            folded += 1

    @pl.when(step < PAIRS)
    def _():
        other = jnp.where(kind_ref[0] == 1, MASKED, 0.0)
        for half in range(2):
            run_slot(step, slots, half, PAIRS, 2)
            head = slice(half * HEAD_DIM, (half + 1) * HEAD_DIM)
            attn_head_back(
                other,
                q_ref[head],
                k_ref[head],
                v_ref[head],
                attended_ref[head],
                grad_ref[head],
                lse_ref.at[half],
                staged,
                head,
            )
        for part in range(3):
            spot = pl.ds(pl.multiple_of(part * D + step * PAIR, 16), PAIR)
            grads[spot, :] = staged[part]

    group = step - PAIRS
    run_slot(group, slots, HEADS, groups, 2)

    @pl.when(group >= 0)
    def _():
        grad = grads[pl.ds(pl.multiple_of(group * rows, 16), rows), :]
        added = dot_nt(jnp.transpose(grad), weight_ref[:, :rows])

        @pl.when(group == 0)
        def _():
            grad_hidden[...] = added

        @pl.when(group > 0)
        def _():
            grad_hidden[...] += added

        run_slot(group, slots, HEADS + 1, groups, 2)
        out_ref[:, :rows] = dot_nt(normed_t_ref[...], grad).astype(jnp.bfloat16)
        for g in range(groups):

            @pl.when(group == g)
            def _():
                out_ref[:, rows:] = proj_ref[:, g * cols : (g + 1) * cols]

    @pl.when(group == groups - 1)
    def _():
        outward = pltpu.make_async_copy(grad_hidden, hidden_hbm, out_sem.at[0])
        outward.start()
        finish()
        swap_wait()
        outward.wait()


def backward(
    kind, qkv, attended, grad_attended, lse, weights, normed_t, grad_proj, grads, swap, collective_id
):
    width, count = normed_t.shape
    groups = weights.shape[1] // BLOCK_COLS
    shape = jax.ShapeDtypeStruct
    bf16, f32 = jnp.bfloat16, jnp.float32
    pair = lambda s: jnp.minimum(s, PAIRS - 1)
    group = lambda s: jnp.maximum(s - PAIRS, 0)
    heads = lambda part: pl.BlockSpec((PAIR, count), lambda s: (pair(s) + part * PAIRS, 0))
    hbm = pl.BlockSpec(memory_space=pl.ANY)
    block = shape((BLOCK_ROWS, BLOCK_COLS), bf16)
    return pl.pallas_call(
        backward_kernel,
        grid=(PAIRS + groups,),
        in_specs=[
            pl.BlockSpec(memory_space=pltpu.SMEM),
            heads(0),
            heads(1),
            heads(2),
            heads(0),
            heads(0),
            pl.BlockSpec((2, 1, count), lambda s: (pair(s), 0, 0)),
            pl.BlockSpec((width, BLOCK_COLS), lambda s: (0, group(s))),
            once(width, count),
            once(width, D),
            hbm,
            hbm,
            hbm,
        ],
        out_specs=[
            pl.BlockSpec((width, BLOCK_COLS), lambda s: (0, group(s))),
            fixed(BLOCK_ROWS, BLOCK_COLS),
            fixed(BLOCK_ROWS, BLOCK_COLS),
            hbm,
            hbm,
        ],
        out_shape=[
            shape(weights.shape, bf16),
            block,
            block,
            shape((count, width), f32),
            shape(swap.shape, swap.dtype),
        ],
        scratch_shapes=[
            pltpu.VMEM((3 * D, count), bf16),
            pltpu.VMEM((3, PAIR, count), bf16),
            pltpu.VMEM((count, width), f32),
            pltpu.SemaphoreType.DMA((1,)),
        ]
        + scatter_scratch(2)
        + swap_scratch(),
        compiler_params=pltpu.CompilerParams(
            collective_id=collective_id, has_side_effects=True, vmem_limit_bytes=VMEM_LIMIT
        ),
        name="backward",
    )(kind, qkv, qkv, qkv, attended, grad_attended, lse, weights, normed_t, grad_proj, *grads, swap)


def local_call(kernel, grid, in_specs, out_specs, out_shape, scratch, name, *operands):
    return pl.pallas_call(
        kernel,
        grid=grid,
        in_specs=in_specs,
        out_specs=out_specs,
        out_shape=out_shape,
        scratch_shapes=scratch,
        compiler_params=pltpu.CompilerParams(vmem_limit_bytes=VMEM_LIMIT),
        name=name,
    )(*operands)


def column_sum(values):
    return jnp.sum(values, axis=0, keepdims=True)


def after_kernel(
    output_ref,
    grad_hidden_ref,
    middle_ref,
    branch_ref,
    grad_ref,
    attended_ref,
    proj_ref,
    mod_ref,
    block_ref,
    grad_middle_ref,
    grad_proj_ref,
    grad_attended_ref,
    sums_ref,
    total_ref,
):
    region = pl.program_id(0)
    part = lambda k: mod_ref[k, pl.ds(region, 1), :]
    output = output_ref[...]
    grad_hidden = grad_hidden_ref[...]
    middle = middle_ref[...]
    grad = grad_ref[...].astype(jnp.float32)
    block_ref[...] = (middle + part(GATE_MLP) * output).astype(jnp.bfloat16)
    normal, root = norm_parts(middle)
    grad_middle = grad + norm_back(grad_hidden, normal, root, part(SCALE_MLP))
    grad_middle_ref[...] = grad_middle
    sums_ref[0, 0:1] = column_sum(grad_middle * branch_ref[...])
    sums_ref[0, 1:2] = column_sum(grad_hidden)
    sums_ref[0, 2:3] = column_sum(grad_hidden * normal)
    sums_ref[0, 3:4] = column_sum(grad * output)
    grad_branch = (part(GATE_ATTN) * grad_middle).astype(jnp.bfloat16)
    grad_attended_ref[...] = dot_nt(proj_ref[...], grad_branch).astype(jnp.bfloat16)
    added = dot_nn(attended_ref[...], grad_branch)

    @pl.when(region == 0)
    def _():
        total_ref[...] = added

    @pl.when(region > 0)
    def _():
        total_ref[...] += added

    @pl.when(region == pl.num_programs(0) - 1)
    def _():
        grad_proj_ref[...] = total_ref[...].astype(jnp.bfloat16)


def after_mlp(output, grad_hidden, middle, branch, grad, attended_t, proj, mod):
    count, width = middle.shape
    regions = count // REGION
    rows = pl.BlockSpec((REGION, width), lambda r: (r, 0))
    columns = pl.BlockSpec((width, REGION), lambda r: (0, r))
    shape = jax.ShapeDtypeStruct
    return local_call(
        after_kernel,
        (regions,),
        [rows, rows, rows, rows, rows, columns, fixed(width, width), fixed(*mod.shape)],
        [
            rows,
            rows,
            fixed(width, width),
            columns,
            pl.BlockSpec((1, 4, width), lambda r: (r, 0, 0)),
        ],
        [
            shape((count, width), jnp.bfloat16),
            shape((count, width), jnp.float32),
            shape((width, width), jnp.bfloat16),
            shape((width, count), jnp.bfloat16),
            shape((regions, 4, width), jnp.float32),
        ],
        [pltpu.VMEM((width, width), jnp.float32)],
        "after_mlp",
        output,
        grad_hidden,
        middle,
        branch,
        grad,
        attended_t,
        proj,
        mod,
    )


def swap_columns(shard):
    pairs = [(d, d ^ 1) for d in range(lax.axis_size("dp"))]
    odd = lax.axis_index("dp") % 2
    rows = shard.shape[0] // 2
    own = lax.dynamic_slice_in_dim(shard, odd * rows, rows, axis=0)
    other = lax.dynamic_slice_in_dim(shard, (1 - odd) * rows, rows, axis=0)
    other = lax.ppermute(other, "dp", pairs)
    return jnp.where(odd == 0, jnp.stack([own, other], 1), jnp.stack([other, own], 1))


def norm_parts(values):
    center = jnp.mean(values, axis=-1, keepdims=True)
    spread = jnp.mean((values - center) ** 2, axis=-1, keepdims=True)
    root = lax.rsqrt(spread + 1e-06)
    return ((values - center) * root, root)


def norm_back(grad, normal, root, scales):
    inner = grad * (1.0 + scales)
    return root * (
        inner
        - jnp.mean(inner, axis=-1, keepdims=True)
        - normal * jnp.mean(inner * normal, axis=-1, keepdims=True)
    )


def embed_tables(count):
    quarter = D // 4
    omegas = 1.0 / 10000.0 ** (jnp.arange(quarter, dtype=jnp.float32) / quarter)
    angles = jnp.arange(count, dtype=jnp.float32)[:, None] * omegas
    return jnp.concatenate([jnp.sin(angles), jnp.cos(angles)], axis=-1)


def slot_device(
    kept_tokens,
    kept_index,
    resolution,
    labels,
    timesteps,
    class_table,
    cotangent,
    mask_token,
    w_qkv,
    w_proj,
    w_fc1,
    w_fc2,
    w_ada,
    mask_first,
    first_qkv,
    first_proj,
    first_fc1,
    first_fc2,
    first_ada,
    mask_second,
    second_qkv,
    second_proj,
    second_fc1,
    second_fc2,
    second_ada,
):
    highest = lax.Precision.HIGHEST
    bf16 = jnp.bfloat16
    bands = lax.axis_size("band")
    groups = lax.axis_size("dp")
    band = lax.axis_index("band")
    slots, local_rows, _ = cotangent.shape
    tokens_count = bands * local_rows
    regions = tokens_count // REGION
    images = labels.shape[1]

    qkv_cols, proj_cols, fc1_cols = w_qkv.shape[1], w_proj.shape[1], w_fc1.shape[1]
    swapped = swap_columns(jnp.concatenate([w_qkv, w_proj, w_fc1], axis=1).astype(bf16))
    joined_block = jnp.concatenate(
        [
            swapped[:, :, :qkv_cols].reshape(-1, 2 * qkv_cols),
            swapped[:, :, qkv_cols:-fc1_cols].reshape(-1, 2 * proj_cols),
        ],
        axis=1,
    )
    fc1_block = swapped[:, :, -fc1_cols:].reshape(-1, 2 * fc1_cols)
    fc2_block = w_fc2.astype(bf16).T

    rows_ada, cols_ada = w_ada.shape
    table_part = lax.dynamic_slice_in_dim(class_table, band * rows_ada, rows_ada, axis=1)
    chosen = labels.reshape(-1, 1) == jnp.arange(class_table.shape[0])[None, :]
    features = band * rows_ada + jnp.arange(rows_ada)
    half_width = D // 2
    frequency = jnp.exp(
        -math.log(10000.0) * (features % half_width).astype(jnp.float32) / half_width
    )
    angles = timesteps.reshape(-1, 1).astype(jnp.float32) * frequency
    waves = jnp.where(features < half_width, jnp.cos(angles), jnp.sin(angles))
    condition = jnp.matmul(chosen.astype(jnp.float32), table_part, precision=highest) + waves
    cond = jax.nn.silu(condition).astype(bf16).astype(jnp.float32)
    cond = jnp.pad(cond.reshape(slots, images, rows_ada), ((0, 0), (0, 8 - images), (0, 0)))

    kind = lax.dynamic_slice_in_dim(resolution, band, 1)
    joined_full, modulation, conds, kept, index = head(
        joined_block, cond, w_ada.astype(bf16), kept_tokens, kept_index[:, None, :], 0
    )
    kept = kept.reshape(-1, D)
    index = index.reshape(1, -1)
    modulation = modulation.transpose(1, 0, 2).reshape(images, 6, D).transpose(1, 0, 2)
    mod = jnp.where(kind[0] == 1, modulation, modulation[:, :1])
    table = embed_tables(SIDE)
    blank = jnp.zeros_like(table)
    tables = jnp.stack(
        [jnp.concatenate([table, blank], axis=1), jnp.concatenate([blank, table], axis=1)]
    )
    (
        qkv,
        attended_t,
        lse,
        branch,
        middle,
        hidden_mlp,
        hidden_mlp_t,
        grad_output,
        grad_output_t,
        tokens,
        normed_t,
        proj_full,
        grad_out,
        fc1_full,
        fc2_full,
    ) = forward(
        kind,
        kept,
        index,
        mask_token[None],
        tables,
        mod,
        joined_full,
        [fc1_block, fc2_block],
        cotangent,
        1,
    )
    grad_out = grad_out.reshape(tokens_count, D)
    output, grad_hidden_mlp, grad_fc1, grad_fc2 = mlp_both(
        hidden_mlp, hidden_mlp_t, grad_output, grad_output_t, fc1_full, fc2_full, 512
    )
    block_slot, grad_middle, grad_proj, grad_attended, sums_mlp = after_mlp(
        output, grad_hidden_mlp, middle, branch, grad_out, attended_t, proj_full, mod
    )
    grad_joined, sum_fc1, sum_fc2, grad_hidden, block_out = backward(
        kind,
        qkv,
        attended_t,
        grad_attended,
        lse,
        joined_full,
        normed_t,
        grad_proj,
        [grad_fc1, grad_fc2],
        block_slot.reshape(bands, local_rows, D),
        2,
    )
    sum_joined, other_joined, other_fc1, red_ada, grad_mask, squares, grad_kept = tail(
        grad_joined,
        kind,
        sum_fc1,
        sum_fc2,
        index,
        mod,
        sums_mlp,
        conds,
        tokens,
        grad_middle,
        grad_hidden,
        bands,
        3,
    )
    kept_grad = grad_kept.astype(jnp.float32)
    grad_mask = grad_mask[0]
    norm_value = jnp.sqrt(squares[0, 0] + jnp.sum(grad_mask * grad_mask))
    factor = clip_level / jnp.maximum(norm_value, clip_level)
    mask_new = adamw(mask_token, mask_first, mask_second, grad_mask * factor)
    odd = (lax.axis_index("dp") % 2).astype(jnp.int32)
    new = adam_all(
        odd[None],
        factor[None],
        [sum_joined, other_joined, sum_fc1, other_fc1, sum_fc2, red_ada],
        [
            w_qkv, w_proj, w_fc1, w_fc2, w_ada,
            first_qkv, first_proj, first_fc1, first_fc2, first_ada,
            second_qkv, second_proj, second_fc1, second_fc2, second_ada,
        ],
    )
    return (
        (block_out, kept_grad, norm_value)
        + (mask_new[0], *new[:5])
        + (mask_new[1], *new[5:10])
        + (mask_new[2], *new[10:])
    )


def per_device(*arguments):
    cotangent = arguments[6]
    if (lax.axis_size("dp"), lax.axis_size("band")) == (8, cotangent.shape[0]):
        return slot_device(*arguments)
    return general_device(*arguments)


def solution(mesh):
    in_specs = (
        P("dp", "band", None),
        P("dp", "band"),
        P("dp"),
        P("dp", None),
        P("dp", None),
        P(),
        P("dp", "band", None),
        P(),
        P("band", "dp"),
        P("band", "dp"),
        P("band", "dp"),
        P("band", "dp"),
        P("band", "dp"),
        P(),
        P("band", "dp"),
        P("band", "dp"),
        P("band", "dp"),
        P("band", "dp"),
        P("band", "dp"),
        P(),
        P("band", "dp"),
        P("band", "dp"),
        P("band", "dp"),
        P("band", "dp"),
        P("band", "dp"),
    )
    out_specs = (
        P("dp", "band", None),
        P("dp", "band", None),
        P(),
        P(),
        P("band", "dp"),
        P("band", "dp"),
        P("band", "dp"),
        P("band", "dp"),
        P("band", "dp"),
        P(),
        P("band", "dp"),
        P("band", "dp"),
        P("band", "dp"),
        P("band", "dp"),
        P("band", "dp"),
        P(),
        P("band", "dp"),
        P("band", "dp"),
        P("band", "dp"),
        P("band", "dp"),
        P("band", "dp"),
    )
    return jax.shard_map(
        per_device, mesh=mesh, in_specs=in_specs, out_specs=out_specs, check_vma=False
    )
```

```python
import functools
import math

import jax
import jax.numpy as jnp
from jax import lax
from jax.experimental import pallas as pl
from jax.experimental.pallas import tpu as pltpu
from jax.sharding import PartitionSpec as P

D = 1152
HEADS = 16
HEAD_DIM = 72
SIDE = 32
STEP = 10
REGION = 256


learn_rate = 0.1
beta_first = 0.9
beta_second = 0.95
adam_eps = 1e-08
decay_rate = 0.1
clip_level = 1.0


def time_embed(timestep):
    half_width = D // 2
    frequency = jnp.exp(-math.log(10000.0) * jnp.arange(half_width, dtype=jnp.float32) / half_width)
    angles = timestep.astype(jnp.float32)[..., None] * frequency
    return jnp.concatenate([jnp.cos(angles), jnp.sin(angles)], axis=-1)


def grid_embed(grid_rows, grid_cols):
    quarter = D // 4
    omegas = 1.0 / 10000.0 ** (jnp.arange(quarter, dtype=jnp.float32) / quarter)
    row_angle = grid_rows.astype(jnp.float32)[..., None] * omegas
    col_angle = grid_cols.astype(jnp.float32)[..., None] * omegas
    return jnp.concatenate(
        [jnp.sin(row_angle), jnp.cos(row_angle), jnp.sin(col_angle), jnp.cos(col_angle)], axis=-1
    )


def slot_layout(positions, slot_kinds):
    small_side = SIDE // 2
    region = positions // REGION
    inside = positions % REGION
    grid_rows = jnp.where(slot_kinds == 1, inside // small_side, positions // SIDE)
    grid_cols = jnp.where(slot_kinds == 1, inside % small_side, positions % SIDE)
    image_id = jnp.where(slot_kinds == 1, region, 0)
    return (grid_rows, grid_cols, image_id)


def modulate(values, shifts, scales):
    center = jnp.mean(values, axis=-1, keepdims=True)
    spread = jnp.mean((values - center) ** 2, axis=-1, keepdims=True)
    return (values - center) * lax.rsqrt(spread + 1e-06) * (1.0 + scales) + shifts


def gelu_tanh(values):
    return jax.nn.gelu(values, approximate=True)


def pick_rows(table_rows, picks):
    return table_rows[picks]


def allowed_pairs(query_pos, key_pos, slot_kinds):
    same_region = (query_pos // REGION)[None, :, None] == (key_pos // REGION)[None, None, :]
    return (slot_kinds[:, None, None] == 0) | same_region


def attend(queries, keys_in, values_in, allowed):

    def one_slot(pieces):
        query_s, key_s, value_s, allow_s = pieces
        scores = jnp.einsum(
            "qhd,khd->hqk", query_s, key_s, preferred_element_type=jnp.float32
        ) * HEAD_DIM ** (-0.5)
        scores = jnp.where(allow_s[None], scores, -1e30)
        row_peak = jnp.max(scores, axis=-1, keepdims=True)
        row_total = jnp.sum(jnp.exp(scores - row_peak), axis=-1, keepdims=True)
        log_total = row_peak + jnp.log(row_total)
        weights_soft = jnp.exp(scores - log_total).astype(jnp.bfloat16)
        result = jnp.einsum(
            "hqk,khd->qhd", weights_soft, value_s, preferred_element_type=jnp.float32
        )
        return (result.astype(jnp.bfloat16), log_total)

    return lax.map(one_slot, (queries, keys_in, values_in, allowed))


def attend_back(queries, keys_in, values_in, allowed, log_total, grad_attended):

    def one_slot(pieces):
        query_s, key_s, value_s, allow_s, total_s, grad_s = pieces
        scores = jnp.einsum(
            "qhd,khd->hqk", query_s, key_s, preferred_element_type=jnp.float32
        ) * HEAD_DIM ** (-0.5)
        scores = jnp.where(allow_s[None], scores, -1e30)
        weights_full = jnp.exp(scores - total_s)
        weights_soft = weights_full.astype(jnp.bfloat16)
        grad_weights = jnp.einsum(
            "qhd,khd->hqk", grad_s, value_s, preferred_element_type=jnp.float32
        )
        row_dot = jnp.sum(weights_full * grad_weights, axis=-1, keepdims=True)
        grad_scores = (weights_full * (grad_weights - row_dot) * HEAD_DIM ** (-0.5)).astype(
            jnp.bfloat16
        )
        grad_queries = jnp.einsum(
            "hqk,khd->qhd", grad_scores, key_s, preferred_element_type=jnp.float32
        )
        grad_keys = jnp.einsum(
            "hqk,qhd->khd", grad_scores, query_s, preferred_element_type=jnp.float32
        )
        grad_values = jnp.einsum(
            "hqk,qhd->khd", weights_soft, grad_s, preferred_element_type=jnp.float32
        )
        return (grad_queries, grad_keys, grad_values)

    return lax.map(one_slot, (queries, keys_in, values_in, allowed, log_total, grad_attended))


def adamw(weight, first, second, grad):
    first_new = beta_first * first + (1.0 - beta_first) * grad
    second_new = beta_second * second + (1.0 - beta_second) * grad * grad
    first_hat = first_new / (1.0 - beta_first**STEP)
    second_hat = second_new / (1.0 - beta_second**STEP)
    weight_new = weight - learn_rate * (
        first_hat / (jnp.sqrt(second_hat) + adam_eps) + decay_rate * weight
    )
    return (weight_new, first_new, second_new)


def general_device(
    kept_tokens,
    kept_index,
    resolution,
    labels,
    timesteps,
    class_table,
    cotangent,
    mask_token,
    w_qkv,
    w_proj,
    w_fc1,
    w_fc2,
    w_ada,
    mask_first,
    first_qkv,
    first_proj,
    first_fc1,
    first_fc2,
    first_ada,
    mask_second,
    second_qkv,
    second_proj,
    second_fc1,
    second_fc2,
    second_ada,
):
    highest = lax.Precision.HIGHEST
    band_index = lax.axis_index("band")
    slot_count = cotangent.shape[0]
    local_rows = cotangent.shape[1]
    qkv_low = w_qkv.astype(jnp.bfloat16)
    proj_low = w_proj.astype(jnp.bfloat16)
    fc1_low = w_fc1.astype(jnp.bfloat16)
    fc2_low = w_fc2.astype(jnp.bfloat16)
    ada_low = w_ada.astype(jnp.bfloat16)
    cols_qkv, cols_proj, cols_fc1, cols_fc2, cols_ada = (
        lax.all_gather(qkv_low, "dp", axis=1, tiled=True),
        lax.all_gather(proj_low, "dp", axis=1, tiled=True),
        lax.all_gather(fc1_low, "dp", axis=1, tiled=True),
        lax.all_gather(fc2_low, "dp", axis=1, tiled=True),
        lax.all_gather(ada_low, "dp", axis=1, tiled=True),
    )
    condition = jnp.take(class_table, labels, axis=0) + time_embed(timesteps)
    cond_low = jax.nn.silu(condition).astype(jnp.bfloat16)
    qkv_full, proj_full, fc1_full, fc2_full, ada_full = (
        lax.all_gather(cols_qkv, "band", axis=0, tiled=True),
        lax.all_gather(cols_proj, "band", axis=0, tiled=True),
        lax.all_gather(cols_fc1, "band", axis=0, tiled=True),
        lax.all_gather(cols_fc2, "band", axis=0, tiled=True),
        lax.all_gather(cols_ada, "band", axis=0, tiled=True),
    )
    modulation = jnp.einsum("sid,de->sie", cond_low, ada_full, preferred_element_type=jnp.float32)
    kept_all, index_all = (
        lax.all_gather(kept_tokens, "band", axis=1, tiled=True),
        lax.all_gather(kept_index, "band", axis=1, tiled=True),
    )
    positions = band_index * local_rows + jnp.arange(local_rows)
    select = index_all[:, None, :] == positions[None, :, None]
    placed = jnp.einsum(
        "spj,sjd->spd", select.astype(jnp.bfloat16), kept_all, preferred_element_type=jnp.float32
    )
    unfilled = 1.0 - jnp.sum(select.astype(jnp.float32), axis=2)
    grid_rows, grid_cols, image_id = slot_layout(positions[None, :], resolution[:, None])
    tokens = placed + unfilled[..., None] * mask_token + grid_embed(grid_rows, grid_cols)
    token_mod = jax.vmap(pick_rows)(modulation, image_id)
    shift_attn, scale_attn, gate_attn, shift_mlp, scale_mlp, gate_mlp = jnp.split(
        token_mod, 6, axis=-1
    )
    attn_value, attn_pull = jax.vjp(modulate, tokens, shift_attn, scale_attn)
    hidden = attn_value.astype(jnp.bfloat16)
    qkv = jnp.einsum("std,de->ste", hidden, qkv_full, preferred_element_type=jnp.float32).astype(
        jnp.bfloat16
    )
    queries = qkv[..., :D].reshape(slot_count, local_rows, HEADS, HEAD_DIM)
    keys_in = qkv[..., D : 2 * D].reshape(slot_count, local_rows, HEADS, HEAD_DIM)
    values_in = qkv[..., 2 * D :].reshape(slot_count, local_rows, HEADS, HEAD_DIM)
    keys_all, values_all = (
        lax.all_gather(keys_in, "band", axis=1, tiled=True),
        lax.all_gather(values_in, "band", axis=1, tiled=True),
    )
    allowed = allowed_pairs(positions, jnp.arange(keys_all.shape[1]), resolution)
    attended, log_total = attend(queries, keys_all, values_all, allowed)
    attended_flat = attended.reshape(slot_count, local_rows, D)
    branch = jnp.einsum("std,de->ste", attended_flat, proj_full, preferred_element_type=jnp.float32)
    middle = tokens + gate_attn * branch
    mlp_value, mlp_pull = jax.vjp(modulate, middle, shift_mlp, scale_mlp)
    hidden_mlp = mlp_value.astype(jnp.bfloat16)
    upward = jnp.einsum("std,df->stf", hidden_mlp, fc1_full, preferred_element_type=jnp.float32)
    active_value, gelu_pull = jax.vjp(gelu_tanh, upward)
    active = active_value.astype(jnp.bfloat16)
    output = jnp.einsum("stf,fd->std", active, fc2_full, preferred_element_type=jnp.float32)
    block_out = (middle + gate_mlp * output).astype(jnp.bfloat16)
    grad_out = cotangent.astype(jnp.float32)
    grad_gate_mlp = grad_out * output
    grad_output = (gate_mlp * grad_out).astype(jnp.bfloat16)
    grad_fc2 = jnp.einsum("stf,std->fd", active, grad_output, preferred_element_type=jnp.float32)
    grad_active = jnp.einsum(
        "std,fd->stf", grad_output, fc2_full, preferred_element_type=jnp.float32
    )
    grad_upward = gelu_pull(grad_active)[0].astype(jnp.bfloat16)
    grad_fc1 = jnp.einsum(
        "std,stf->df", hidden_mlp, grad_upward, preferred_element_type=jnp.float32
    )
    grad_hidden_mlp = jnp.einsum(
        "stf,df->std", grad_upward, fc1_full, preferred_element_type=jnp.float32
    )
    grad_mid_norm, grad_shift_mlp, grad_scale_mlp = mlp_pull(grad_hidden_mlp)
    grad_middle = grad_out + grad_mid_norm
    grad_gate_attn = grad_middle * branch
    grad_branch = (gate_attn * grad_middle).astype(jnp.bfloat16)
    grad_proj = jnp.einsum(
        "std,ste->de", attended_flat, grad_branch, preferred_element_type=jnp.float32
    )
    grad_attended = jnp.einsum(
        "ste,de->std", grad_branch, proj_full, preferred_element_type=jnp.float32
    ).astype(jnp.bfloat16)
    grad_attended = grad_attended.reshape(slot_count, local_rows, HEADS, HEAD_DIM)
    grad_queries, grad_keys_part, grad_values_part = attend_back(
        queries, keys_all, values_all, allowed, log_total, grad_attended
    )
    grad_keys, grad_values = (
        lax.psum_scatter(
            grad_keys_part.astype(jnp.bfloat16), "band", scatter_dimension=1, tiled=True
        ).astype(jnp.float32),
        lax.psum_scatter(
            grad_values_part.astype(jnp.bfloat16), "band", scatter_dimension=1, tiled=True
        ).astype(jnp.float32),
    )
    grad_qkv = jnp.concatenate(
        [
            grad_queries.reshape(slot_count, local_rows, D),
            grad_keys.reshape(slot_count, local_rows, D),
            grad_values.reshape(slot_count, local_rows, D),
        ],
        axis=-1,
    ).astype(jnp.bfloat16)
    grad_qkv_weight = jnp.einsum(
        "std,ste->de", hidden, grad_qkv, preferred_element_type=jnp.float32
    )
    grad_hidden = jnp.einsum("ste,de->std", grad_qkv, qkv_full, preferred_element_type=jnp.float32)
    grad_tok_norm, grad_shift_attn, grad_scale_attn = attn_pull(grad_hidden)
    grad_tokens = grad_middle + grad_tok_norm
    grad_mod_tok = jnp.concatenate(
        [
            grad_shift_attn,
            grad_scale_attn,
            grad_gate_attn,
            grad_shift_mlp,
            grad_scale_mlp,
            grad_gate_mlp,
        ],
        axis=-1,
    )
    image_onehot = (image_id[..., None] == jnp.arange(4)).astype(jnp.float32)
    grad_modulation = jnp.einsum("spi,spe->sie", image_onehot, grad_mod_tok, precision=highest)
    grad_mask_part = jnp.sum(unfilled[..., None] * grad_tokens, axis=(0, 1))
    grad_kept_all = jnp.einsum(
        "spj,spd->sjd", select.astype(jnp.float32), grad_tokens, precision=highest
    )
    kept_grad = lax.psum_scatter(
        grad_kept_all.astype(jnp.bfloat16), "band", scatter_dimension=1, tiled=True
    ).astype(jnp.float32)
    grad_ada = jnp.einsum(
        "sid,sie->de", cond_low.astype(jnp.float32), grad_modulation, precision=highest
    )
    row_grads = (
        lax.psum_scatter(
            grad_qkv_weight.astype(jnp.bfloat16), "band", scatter_dimension=0, tiled=True
        ).astype(jnp.float32),
        lax.psum_scatter(
            grad_proj.astype(jnp.bfloat16), "band", scatter_dimension=0, tiled=True
        ).astype(jnp.float32),
        lax.psum_scatter(
            grad_fc1.astype(jnp.bfloat16), "band", scatter_dimension=0, tiled=True
        ).astype(jnp.float32),
        lax.psum_scatter(
            grad_fc2.astype(jnp.bfloat16), "band", scatter_dimension=0, tiled=True
        ).astype(jnp.float32),
        lax.psum_scatter(
            grad_ada.astype(jnp.bfloat16), "band", scatter_dimension=0, tiled=True
        ).astype(jnp.float32),
    )
    red_qkv, red_proj, red_fc1, red_fc2, red_ada = (
        lax.psum_scatter(
            row_grads[0].astype(jnp.bfloat16), "dp", scatter_dimension=1, tiled=True
        ).astype(jnp.float32),
        lax.psum_scatter(
            row_grads[1].astype(jnp.bfloat16), "dp", scatter_dimension=1, tiled=True
        ).astype(jnp.float32),
        lax.psum_scatter(
            row_grads[2].astype(jnp.bfloat16), "dp", scatter_dimension=1, tiled=True
        ).astype(jnp.float32),
        lax.psum_scatter(
            row_grads[3].astype(jnp.bfloat16), "dp", scatter_dimension=1, tiled=True
        ).astype(jnp.float32),
        lax.psum_scatter(
            row_grads[4].astype(jnp.bfloat16), "dp", scatter_dimension=1, tiled=True
        ).astype(jnp.float32),
    )
    grad_mask = lax.psum(grad_mask_part, ("dp", "band"))
    reduced = (red_qkv, red_proj, red_fc1, red_fc2, red_ada)
    local_squares = sum((jnp.sum(grad * grad) for grad in reduced))
    total_squares = lax.psum(local_squares, ("dp", "band")) + jnp.sum(grad_mask * grad_mask)
    norm_value = jnp.sqrt(total_squares)
    factor = clip_level / jnp.maximum(norm_value, clip_level)
    mask_new = adamw(mask_token, mask_first, mask_second, grad_mask * factor)
    qkv_new = adamw(w_qkv, first_qkv, second_qkv, red_qkv * factor)
    proj_new = adamw(w_proj, first_proj, second_proj, red_proj * factor)
    fc1_new = adamw(w_fc1, first_fc1, second_fc1, red_fc1 * factor)
    fc2_new = adamw(w_fc2, first_fc2, second_fc2, red_fc2 * factor)
    ada_new = adamw(w_ada, first_ada, second_ada, red_ada * factor)
    return (
        block_out,
        kept_grad,
        norm_value,
        mask_new[0],
        qkv_new[0],
        proj_new[0],
        fc1_new[0],
        fc2_new[0],
        ada_new[0],
        mask_new[1],
        qkv_new[1],
        proj_new[1],
        fc1_new[1],
        fc2_new[1],
        ada_new[1],
        mask_new[2],
        qkv_new[2],
        proj_new[2],
        fc1_new[2],
        fc2_new[2],
        ada_new[2],
    )


MASKED = -1e30
SCORE_SCALE = HEAD_DIM ** (-0.5)
LOG2E = math.log2(math.e)
VMEM_LIMIT = 63 * 1024 * 1024


def dot_nn(left, right):
    return lax.dot_general(
        left, right, (((1,), (0,)), ((), ())), preferred_element_type=jnp.float32
    )


def dot_nt(left, right):
    return lax.dot_general(
        left, right, (((1,), (1,)), ((), ())), preferred_element_type=jnp.float32
    )


def masked_scores(keys, queries, block, other):
    raw = dot_nn(keys, queries)
    parts = [
        raw[r * REGION : (r + 1) * REGION] + (0.0 if r == block else other)
        for r in range(keys.shape[0] // REGION)
    ]
    return jnp.concatenate(parts, axis=0)


def attn_head(other, queries, keys_t, values_t, out_ref, rows, lse_ref):
    keys = jnp.transpose(keys_t)
    for block in range(keys.shape[0] // REGION):
        cols = slice(block * REGION, (block + 1) * REGION)
        scores = masked_scores(keys, queries[:, cols], block, other)
        peak = jnp.max(scores, axis=0, keepdims=True)
        weights = jnp.exp2((scores - peak) * (SCORE_SCALE * LOG2E))
        total = jnp.sum(weights, axis=0, keepdims=True)
        mixed = dot_nn(values_t, weights.astype(jnp.bfloat16))
        out_ref[rows, cols] = (mixed / total).astype(jnp.bfloat16)
        lse_ref[:, cols] = peak * (SCORE_SCALE * LOG2E) + jnp.log2(total)


def attn_head_back(other, queries, keys_t, values_t, out, grad, lse_ref, grads_ref, rows):
    tokens = queries.shape[1]
    keys = jnp.transpose(keys_t)
    values = jnp.transpose(values_t)
    grad_keys = jnp.zeros((HEAD_DIM, tokens), jnp.float32)
    grad_values = jnp.zeros((HEAD_DIM, tokens), jnp.float32)
    dots = jnp.sum(out.astype(jnp.float32) * grad.astype(jnp.float32), axis=0, keepdims=True)
    for block in range(tokens // REGION):
        cols = slice(block * REGION, (block + 1) * REGION)
        scores = masked_scores(keys, queries[:, cols], block, other)
        weights = jnp.exp2(scores * (SCORE_SCALE * LOG2E) - lse_ref[:, cols])
        grad_weights = dot_nn(values, grad[:, cols])
        grad_scores = (weights * (grad_weights - dots[:, cols])).astype(jnp.bfloat16)
        grad_values += dot_nt(grad[:, cols], weights.astype(jnp.bfloat16))
        grad_keys += dot_nt(queries[:, cols], grad_scores)
        grads_ref[0, rows, cols] = (dot_nn(keys_t, grad_scores) * SCORE_SCALE).astype(jnp.bfloat16)
    grads_ref[1, rows] = (grad_keys * SCORE_SCALE).astype(jnp.bfloat16)
    grads_ref[2, rows] = grad_values.astype(jnp.bfloat16)


GELU_A = math.sqrt(2.0 / math.pi)
GELU_B = 0.044715


def mlp_tile(h_ref, ht_ref, g_ref, gt_ref, up_ref, down_ref, out_ref, grad_ref, gup_ref, gdown_ref):
    up = up_ref[...]
    down = down_ref[...]
    upward = dot_nn(h_ref[...], up)
    square = upward * upward
    curve = jnp.tanh(GELU_A * upward * (1.0 + GELU_B * square))
    half = 0.5 * (1.0 + curve)
    active = (upward * half).astype(jnp.bfloat16)
    slope = half + 0.5 * upward * (1.0 - curve * curve) * GELU_A * (
        1.0 + 3.0 * GELU_B * square
    )
    grad_upward = (dot_nn(g_ref[...], down) * slope).astype(jnp.bfloat16)
    out_ref[...] += dot_nt(active, down)
    grad_ref[...] += dot_nt(grad_upward, up)
    gup_ref[...] = dot_nn(ht_ref[...], grad_upward).astype(jnp.bfloat16)
    gdown_ref[...] = dot_nn(gt_ref[...], active).astype(jnp.bfloat16)


BLOCK_ROWS = 144
BLOCK_COLS = 1152
def flip(index):
    return index + 1 - 2 * (index % 2)


def along_z(z, step):
    return (z, flip(z), (z + 2) % 4, 3 - z)[step]


class Place:
    def __init__(self):
        dp = lax.axis_index("dp")
        band = lax.axis_index("band")
        self.z, self.y, self.x, self.core = dp // 2, dp % 2, band // 2, band % 2

    def chip(self, i, a, b):
        return (along_z(self.z, i), flip(self.y) if a else self.y, flip(self.x) if b else self.x)

    def device(self, i=0, a=0, b=0, core=0):
        z, y, x = self.chip(i, a, b)
        return (z * 2 + y, x * 2 + (flip(self.core) if core else self.core))

    def partners(self, band=False, dp=False):
        found = [
            self.device(core=1),
            self.device(b=1),
            self.device(a=1),
            self.device(i=1),
            self.device(i=2),
            self.device(i=3),
        ]
        if band:
            found.append(self.device(b=1, core=1))
        if dp:
            found += [self.device(i=i, a=1) for i in (1, 2, 3)]
        return found

    def dp(self, i=0, a=0):
        z, y, _ = self.chip(i, a, 0)
        return z * 2 + y

    def band(self, b=0, core=0):
        x = flip(self.x) if b else self.x
        return x * 2 + (flip(self.core) if core else self.core)

    def block(self, by_rows, i, a, b, core=0):
        z, y, x = self.chip(i, a, b)
        c = flip(self.core) if core else self.core
        if by_rows:
            row, col = z * 2 + y, x * 2 + c
        else:
            row, col = (x * 2 + c) * 2 + y, z
        return (
            pl.ds(pl.multiple_of(row * BLOCK_ROWS, 16), BLOCK_ROWS),
            pl.ds(pl.multiple_of(col * BLOCK_COLS, 128), BLOCK_COLS),
        )


def greet(place, band=False, dp=False):
    barrier = pltpu.get_barrier_semaphore()
    partners = place.partners(band, dp)
    for partner in partners:
        pl.semaphore_signal(
            barrier, inc=1, device_id=partner, device_id_type=pl.DeviceIdType.MESH
        )
    pl.semaphore_wait(barrier, len(partners))


def send(source, target, send_sem, recv_sem, device):
    return pltpu.make_async_remote_copy(
        src_ref=source,
        dst_ref=target,
        send_sem=send_sem,
        recv_sem=recv_sem,
        device_id=device,
        device_id_type=pl.DeviceIdType.MESH,
    )


CHIPS = [(i, a, b) for i in range(4) for a in range(2) for b in range(2)]


def slot(piece):
    return piece[0] * 4 + piece[1] * 2 + piece[2]


def parent(piece, via_x, sides_by_z):
    i, a, b = piece
    if a and b:
        return (0, 0, 1) if i in via_x else (0, 1, 0)
    if (a or b) and not (i == 1 and sides_by_z):
        return (0, a, b)
    return (i, 0, 0)


def moved(piece, step):
    return (piece[0] ^ step[0], piece[1] ^ step[1], piece[2] ^ step[2])


def children(piece, via_x, sides_by_z):
    return [
        (other, parent(other, via_x, sides_by_z))
        for other in CHIPS
        if any(other) and moved(other, parent(other, via_x, sides_by_z)) == piece
    ]


GATHER_SENDS = 31


def gather_actions(place, plans, own_refs, full_refs, local_sems, send_sems, link_sems, core_sems):
    weights = range(len(own_refs))
    counts = [0] * len(own_refs)

    def ship(w, source, piece, name, sems, device):
        target = full_refs[w].at[place.block(plans[w][0], *piece)]
        send(source, target, send_sems.at[w, counts[w]], sems.at[w, slot(name)], device).start()
        counts[w] += 1

    def pass_on(w, source, piece):
        for child, step in children(piece, plans[w][1], False):
            if step[0] < 2:
                ship(w, source, piece, child, link_sems, place.device(*step))
        ship(w, source, piece, piece, core_sems, place.device(core=1))

    def arrive(w, piece, core=0):
        target = full_refs[w].at[place.block(plans[w][0], *piece, core)]
        sems = core_sems if core else link_sems
        send(
            target, target, send_sems.at[w, 0], sems.at[w, slot(piece)], place.device(core=1)
        ).wait_recv()
        return target

    def keep(w):
        return pltpu.make_async_copy(
            own_refs[w], full_refs[w].at[place.block(plans[w][0], 0, 0, 0)], local_sems.at[w]
        )

    def begin():
        for w in weights:
            keep(w).start()
            pass_on(w, own_refs[w], (0, 0, 0))

    def relay(w, *piece):
        pass_on(w, arrive(w, piece), piece)

    def late(w, i):
        ship(w, own_refs[w], (0, 0, 0), (i, 0, 0), link_sems, place.device(i))

    def finish():
        for w in weights:
            for piece in CHIPS:
                arrive(w, piece, core=1)
            keep(w).wait()
            for n in range(counts[w]):
                send(
                    own_refs[w], own_refs[w], send_sems.at[w, n], link_sems.at[w, 0],
                    place.device(core=1),
                ).wait_send()

    return begin, relay, late, finish


def gather_scratch(count):
    return [
        pltpu.SemaphoreType.DMA((count,)),
        pltpu.SemaphoreType.DMA((count, GATHER_SENDS)),
        pltpu.SemaphoreType.DMA((count, 16)),
        pltpu.SemaphoreType.DMA((count, 16)),
    ]


BAND_PEERS = ((0, 1), (1, 0), (1, 1))
DP_PEERS = ((1, 0), (0, 1), (3, 0), (1, 1), (2, 0), (3, 1), (2, 1))


def swap_band(place, source, target, local_sem, send_sems, recv_sems):
    def copies():
        found = []
        for n, (b, core) in enumerate(BAND_PEERS):
            found.append(
                send(
                    source.at[place.band(b, core)],
                    target.at[place.band()],
                    send_sems.at[n],
                    recv_sems.at[n],
                    place.device(b=b, core=core),
                )
            )
        local = pltpu.make_async_copy(
            source.at[place.band()], target.at[place.band()], local_sem.at[0]
        )
        return found, local

    def start():
        found, local = copies()
        for copy in found:
            copy.start()
        local.start()

    def wait():
        found, local = copies()
        for copy in found:
            copy.wait()
        local.wait()

    return start, wait


def swap_scratch():
    return [
        pltpu.SemaphoreType.DMA((1,)),
        pltpu.SemaphoreType.DMA((3,)),
        pltpu.SemaphoreType.DMA((3,)),
    ]


def head_kernel(
    block_ref,
    cond_ref,
    ada_ref,
    kept_ref,
    index_ref,
    full_ref,
    mod_ref,
    conds_ref,
    kept_out,
    index_out,
    part_ref,
    got_ref,
    sums_ref,
    cond_sends,
    cond_recvs,
    part_sends,
    part_recvs,
    mod_sends,
    mod_recvs,
    *rest,
):
    place = Place()
    slots, _, _, cols = part_ref.shape
    images = part_ref.shape[2]
    plans = ((False, (0,)),)
    begin, relay, late, finish = gather_actions(
        place, plans, [block_ref], [full_ref], *rest[:4]
    )

    def relays(*pieces):
        for piece in pieces:
            relay(0, *piece)

    kept_start, kept_wait = swap_band(place, kept_ref, kept_out, *rest[4:7])
    index_start, index_wait = swap_band(place, index_ref, index_out, *rest[7:10])

    def to_dp(n, source, target, sends, recvs):
        i, a = DP_PEERS[n]
        return send(source, target, sends.at[n], recvs.at[n], place.device(i=i, a=a))

    greet(place, band=True, dp=True)
    own = place.dp()
    cond_copies = [
        to_dp(n, cond_ref, conds_ref.at[own], cond_sends, cond_recvs) for n in range(7)
    ]
    for copy in cond_copies:
        copy.start()
    begin()
    index_start()
    conds_ref[own] = cond_ref[...]
    late(0, 3)
    relays((1, 0, 0))
    for copy in cond_copies:
        copy.wait()
    for s in range(slots):
        rows = conds_ref[:, s].reshape(-1, cond_ref.shape[-1]).astype(jnp.bfloat16)
        product = dot_nn(rows, ada_ref[...])
        part_ref[s] = product.reshape(-1, cond_ref.shape[1], cols)[:, :images]
    relays((0, 1, 0))
    late(0, 2)
    relays((1, 0, 1), (1, 1, 0), (3, 0, 0))
    part_copies = [
        send(
            part_ref.at[place.band(b, core)],
            got_ref.at[n],
            part_sends.at[n],
            part_recvs.at[n],
            place.device(b=b, core=core),
        )
        for n, (b, core) in enumerate(BAND_PEERS)
    ]
    for copy in part_copies:
        copy.start()
    relays((3, 0, 1), (2, 0, 0), (0, 0, 1), (0, 1, 1), (3, 1, 0))
    kept_start()
    for copy in part_copies:
        copy.wait()
    sums_ref[...] = part_ref[place.band()] + got_ref[0] + got_ref[1] + got_ref[2]
    relays((1, 1, 1))
    mod_copies = [
        to_dp(n, sums_ref.at[place.dp(*DP_PEERS[n])], mod_ref.at[own], mod_sends, mod_recvs)
        for n in range(7)
    ]
    for copy in mod_copies:
        copy.start()
    mod_ref[own] = sums_ref[own]
    relays((2, 0, 1), (3, 1, 1), (2, 1, 0), (2, 1, 1))
    finish()
    for copy in mod_copies:
        copy.wait()
    index_wait()
    kept_wait()


def head(block, cond, ada, kept, index, collective_id):
    slots, images_pad, width = cond.shape
    images = 4
    cols = ada.shape[1]
    groups = lax.axis_size("dp")
    vmem = pl.BlockSpec(memory_space=pltpu.VMEM)
    hbm = pl.BlockSpec(memory_space=pl.ANY)
    f32 = jnp.float32
    return pl.pallas_call(
        head_kernel,
        in_specs=[vmem, vmem, vmem, hbm, hbm],
        out_specs=[hbm, vmem, vmem, hbm, hbm],
        out_shape=[
            jax.ShapeDtypeStruct((8 * BLOCK_ROWS, 4 * BLOCK_COLS), jnp.bfloat16),
            jax.ShapeDtypeStruct((groups, images, cols), f32),
            jax.ShapeDtypeStruct((groups,) + cond.shape, f32),
            jax.ShapeDtypeStruct(kept.shape, kept.dtype),
            jax.ShapeDtypeStruct(index.shape, index.dtype),
        ],
        scratch_shapes=[
            pltpu.VMEM((slots, groups, images, cols), f32),
            pltpu.VMEM((3, groups, images, cols), f32),
            pltpu.VMEM((groups, images, cols), f32),
            pltpu.SemaphoreType.DMA((7,)),
            pltpu.SemaphoreType.DMA((7,)),
            pltpu.SemaphoreType.DMA((3,)),
            pltpu.SemaphoreType.DMA((3,)),
            pltpu.SemaphoreType.DMA((7,)),
            pltpu.SemaphoreType.DMA((7,)),
        ]
        + gather_scratch(1)
        + swap_scratch()
        + swap_scratch(),
        compiler_params=pltpu.CompilerParams(
            collective_id=collective_id, has_side_effects=True, vmem_limit_bytes=VMEM_LIMIT
        ),
        name="head",
    )(block, cond, ada, kept, index)


STAGES = 4


def scatter_actions(
    place,
    plans,
    order,
    grad_refs,
    out_refs,
    held_refs,
    over_refs,
    stage,
    stage_sems,
    send_sems,
    held_sems,
    over_sems,
):
    weights = range(len(grad_refs))
    counts = [0] * len(grad_refs)

    def ship(w, source, target, recv_sem, device):
        send(source, target, send_sems.at[w, counts[w]], recv_sem, device).start()
        counts[w] += 1

    def landed(target, recv_sem):
        send(target, target, send_sems.at[0, 0], recv_sem, place.device(core=1)).wait_recv()

    def begin():
        for ahead in range(STAGES - 1):
            load(ahead).start()
        for w, *piece in order:
            source = grad_refs[w].at[place.block(plans[w][0], *piece, 1)]
            s = slot(piece)
            ship(w, source, held_refs.at[w, s], held_sems.at[w, s], place.device(core=1))

    def load(n):
        w, *piece = order[n]
        return pltpu.make_async_copy(
            grad_refs[w].at[place.block(plans[w][0], *piece)],
            stage.at[n % STAGES],
            stage_sems.at[n % STAGES],
        )

    def up(w, piece):
        step = parent(piece, plans[w][1], True)
        s = slot(piece)
        ship(
            w, held_refs.at[w, s], over_refs.at[w, s - 1], over_sems.at[w, s - 1], place.device(*step)
        )

    def fold(n):
        if n + STAGES - 1 < len(order):
            load(n + STAGES - 1).start()
        w, *piece = order[n]
        s = slot(piece)
        load(n).wait()
        landed(held_refs.at[w, s], held_sems.at[w, s])
        held = held_refs.at[w, s]
        held[...] = held[...] + stage[n % STAGES]
        if not children(tuple(piece), plans[w][1], True):
            up(w, piece)

    def combine(w, *piece):
        held = held_refs.at[w, slot(piece)]
        total = held[...].astype(jnp.float32)
        for child, _ in children(piece, plans[w][1], True):
            k = slot(child) - 1
            landed(over_refs.at[w, k], over_sems.at[w, k])
            total = total + over_refs[w, k].astype(jnp.float32)
        if any(piece):
            held[...] = total.astype(jnp.bfloat16)
            up(w, piece)
        else:
            out_refs[w][...] = total.astype(jnp.bfloat16)

    def finish():
        for w in weights:
            block = held_refs.at[w, 0]
            for n in range(counts[w]):
                send(
                    block, block, send_sems.at[w, n], held_sems.at[w, 0], place.device(core=1)
                ).wait_send()

    return begin, fold, combine, finish


def scatter_scratch(count):
    blocks = lambda n: pltpu.VMEM((count, n, BLOCK_ROWS, BLOCK_COLS), jnp.bfloat16)
    return [
        blocks(16),
        blocks(15),
        pltpu.VMEM((STAGES, BLOCK_ROWS, BLOCK_COLS), jnp.bfloat16),
        pltpu.SemaphoreType.DMA((STAGES,)),
        pltpu.SemaphoreType.DMA((count, 31)),
        pltpu.SemaphoreType.DMA((count, 16)),
        pltpu.SemaphoreType.DMA((count, 15)),
    ]


def to_dp_peer(place, n, source, target, sends, recvs):
    i, a = DP_PEERS[n]
    return send(source, target, sends.at[n], recvs.at[n], place.device(i=i, a=a))


def to_band_peer(place, n, source, target, sends, recvs):
    b, core = BAND_PEERS[n]
    return send(source, target, sends.at[n], recvs.at[n], place.device(b=b, core=core))


def square_sum(values):
    wide = values.astype(jnp.float32)
    return jnp.sum(jnp.sum(wide * wide, axis=0, keepdims=True), axis=1, keepdims=True)


def tail_kernel(
    grad_ref,
    kind_ref,
    fc1_ref,
    fc2_ref,
    index_ref,
    scales_ref,
    sums_ref,
    conds_ref,
    tokens_hbm,
    middle_hbm,
    hidden_hbm,
    own_ref,
    other_ref,
    fc1_other_ref,
    ada_ref,
    mask_out,
    square_out,
    kept_out,
    tokens,
    grad_middle,
    grad_hidden,
    kept_total,
    kept,
    six,
    mask_own,
    mods_own,
    mods_dp,
    mods_all,
    mask_band,
    mask_sum,
    mask_dp,
    square_own,
    square_band,
    square_sum_ref,
    square_dp,
    load_sems,
    y_sends,
    y_recvs,
    dp_sends,
    dp_recvs,
    band_sends,
    band_recvs,
    *rest,
):
    place = Place()
    plans = ((False, (0,)),)
    order = [
        (3, 1, 1), (0, 1, 1), (3, 0, 1), (1, 0, 0), (1, 1, 0), (2, 1, 1), (3, 1, 0), (3, 0, 0),
        (1, 1, 1), (2, 0, 1), (1, 0, 1), (2, 1, 0), (0, 0, 1), (0, 0, 0), (0, 1, 0), (2, 0, 0),
    ]
    begin, fold, combine, finish = scatter_actions(
        place, plans, [(0,) + piece for piece in order], [grad_ref], [own_ref], *rest[:7]
    )

    left = list(range(len(order)))

    def folds(count):
        for _ in range(count):
            fold(left.pop(0))

    kept_start, kept_wait = swap_band(place, kept, kept_out, *rest[7:10])
    across = lambda n, source, target: send(
        source, target, y_sends.at[n], y_recvs.at[n], place.device(a=1)
    )
    to_dp = lambda k, n, source, target: to_dp_peer(
        place, n, source, target, dp_sends.at[k], dp_recvs.at[k]
    )
    to_band = lambda k, n, source, target: to_band_peer(
        place, n, source, target, band_sends.at[k], band_recvs.at[k]
    )
    greet(place, band=True, dp=True)
    own = place.dp()
    loads = [
        pltpu.make_async_copy(source, target, load_sems.at[n])
        for n, (source, target) in enumerate(
            [(tokens_hbm, tokens), (middle_hbm, grad_middle), (hidden_hbm, grad_hidden)]
        )
    ]
    for copy in loads:
        copy.start()
    begin()
    fc1_copy = across(0, fc1_ref, fc1_other_ref)
    fc1_copy.start()
    folds(4)
    for copy in loads:
        copy.wait()

    count = tokens.shape[0]
    regions = count // REGION
    for region in range(regions):
        if region == 2:
            combine(0, 3, 0, 1)
        folds((0, 2, 2, 2)[region])
        if region == 3:
            combine(0, 2, 0, 1)
        spot = slice(region * REGION, (region + 1) * REGION)
        grad = grad_hidden[spot]
        normal, root = norm_parts(tokens[spot])
        scale = scales_ref[SCALE_ATTN, region : region + 1]
        grad_tokens = grad_middle[spot] + norm_back(grad, normal, root, scale)
        six[0, region : region + 1] = column_sum(grad)
        six[1, region : region + 1] = column_sum(grad * normal)
        for k in range(4):
            six[2 + k, region : region + 1] = sums_ref[region, k : k + 1]
        select = chosen_rows(index_ref, region)
        unfilled = 1.0 - jnp.sum(select, axis=1, keepdims=True)
        masked = column_sum(unfilled * grad_tokens)
        select = jnp.transpose(select).astype(jnp.bfloat16)
        added = dot_nn(select, grad_tokens.astype(jnp.bfloat16))
        if region == 0:
            mask_own[...] = jnp.broadcast_to(masked, mask_own.shape)
            kept_total[...] = added
        else:
            mask_own[...] += jnp.broadcast_to(masked, mask_own.shape)
            kept_total[...] += added
    kept[...] = kept_total[...].astype(jnp.bfloat16).reshape(kept.shape)
    images = six.shape[1]
    first = lax.broadcasted_iota(jnp.int32, six.shape[1:], 0) == 0
    flat = []
    for k in range(6):
        part = six[k]
        flat.append(
            jnp.where(kind_ref[0] == 1, part, jnp.where(first, column_sum(part), 0.0))
        )
    flat = jnp.concatenate(flat, axis=1)
    groups, padded, cols = mods_own.shape
    for d in range(groups):
        mods_own[d, :images] = flat[:, d * cols : (d + 1) * cols]
        mods_own[d, images:] = jnp.zeros((padded - images, cols), jnp.float32)

    early = [to_dp(0, n, mods_own.at[place.dp(*DP_PEERS[n])], mods_dp.at[own]) for n in range(7)]
    early += [to_band(0, n, mask_own, mask_band.at[n]) for n in range(3)]
    for copy in early:
        copy.start()
    kept_start()
    mods_dp[own] = mods_own[own]
    combine(0, 3, 0, 0)
    folds(5)
    combine(0, 1, 0, 1)
    folds(1)
    for copy in early:
        copy.wait()
    mask_sum[...] = mask_own[...] + mask_band[0] + mask_band[1] + mask_band[2]
    second = [to_band(1, n, mods_dp, mods_all.at[place.band()]) for n in range(3)]
    second += [to_dp(1, n, mask_sum, mask_dp.at[n]) for n in range(7)]
    for copy in second:
        copy.start()
    mods_all[place.band()] = mods_dp[...]
    fc1_copy.wait()
    combine(0, 2, 0, 0)
    combine(0, 0, 1, 0)
    combine(0, 0, 0, 1)
    for copy in second:
        copy.wait()
    total = mask_sum[...]
    for n in range(7):
        total = total + mask_dp[n]
    mask_out[...] = total
    width = ada_ref.shape[0]
    ada = jnp.zeros(ada_ref.shape, jnp.float32)
    for s in range(conds_ref.shape[1]):
        ada += lax.dot_general(
            conds_ref[:, s].reshape(-1, width),
            mods_all[s].reshape(-1, ada_ref.shape[1]),
            (((0,), (0,)), ((), ())),
            precision=lax.Precision.HIGHEST,
            preferred_element_type=jnp.float32,
        )
    ada_ref[...] = ada
    squares = square_sum(ada) + square_sum(fc1_ref[...]) + square_sum(fc2_ref[...])
    combine(0, 0, 0, 0)
    last = across(1, own_ref, other_ref)
    last.start()
    squares = squares + square_sum(own_ref[...])
    square_own[...] = jnp.broadcast_to(squares, square_own.shape)
    third = [to_band(2, n, square_own, square_band.at[n]) for n in range(3)]
    for copy in third:
        copy.start()
    for copy in third:
        copy.wait()
    square_sum_ref[...] = square_own[...] + square_band[0] + square_band[1] + square_band[2]
    fourth = [to_dp(2, n, square_sum_ref, square_dp.at[n]) for n in range(7)]
    for copy in fourth:
        copy.start()
    for copy in fourth:
        copy.wait()
    total = square_sum_ref[...]
    for n in range(7):
        total = total + square_dp[n]
    square_out[...] = total
    last.wait()
    kept_wait()
    finish()


def tail(
    grad, kind, fc1, fc2, index, mod, sums, conds, tokens, grad_middle, grad_hidden, bands, collective_id
):
    f32, bf16 = jnp.float32, jnp.bfloat16
    vmem = pl.BlockSpec(memory_space=pltpu.VMEM)
    hbm = pl.BlockSpec(memory_space=pl.ANY)
    block = jax.ShapeDtypeStruct((BLOCK_ROWS, BLOCK_COLS), bf16)
    squares = (8, 128)
    mask = (8, D)
    count, width = tokens.shape
    places = index.shape[1]
    groups, _, padded, rows_ada = conds.shape
    cols_ada = 6 * D // groups
    mods = (groups, padded, cols_ada)
    kept = (bands, places // bands, width)
    dma = pltpu.SemaphoreType.DMA
    return pl.pallas_call(
        tail_kernel,
        in_specs=[hbm, pl.BlockSpec(memory_space=pltpu.SMEM)] + [vmem] * 6 + [hbm] * 3,
        out_specs=[vmem] * 6 + [hbm],
        out_shape=[
            block,
            block,
            block,
            jax.ShapeDtypeStruct((rows_ada, cols_ada), f32),
            jax.ShapeDtypeStruct(mask, f32),
            jax.ShapeDtypeStruct(squares, f32),
            jax.ShapeDtypeStruct(kept, bf16),
        ],
        scratch_shapes=[
            pltpu.VMEM((count, width), f32),
            pltpu.VMEM((count, width), f32),
            pltpu.VMEM((count, width), f32),
            pltpu.VMEM((places, width), f32),
            pltpu.VMEM(kept, bf16),
            pltpu.VMEM(mod.shape, f32),
            pltpu.VMEM(mask, f32),
            pltpu.VMEM(mods, f32),
            pltpu.VMEM(mods, f32),
            pltpu.VMEM((bands,) + mods, f32),
            pltpu.VMEM((3,) + mask, f32),
            pltpu.VMEM(mask, f32),
            pltpu.VMEM((7,) + mask, f32),
            pltpu.VMEM(squares, f32),
            pltpu.VMEM((3,) + squares, f32),
            pltpu.VMEM(squares, f32),
            pltpu.VMEM((7,) + squares, f32),
            dma((3,)),
            dma((2,)),
            dma((2,)),
            dma((3, 7)),
            dma((3, 7)),
            dma((3, 3)),
            dma((3, 3)),
        ]
        + scatter_scratch(1)
        + swap_scratch(),
        compiler_params=pltpu.CompilerParams(
            collective_id=collective_id, has_side_effects=True, vmem_limit_bytes=VMEM_LIMIT
        ),
        name="tail",
    )(
        grad, kind, fc1, fc2, index, mod, sums, conds,
        tokens, grad_middle, grad_hidden,
    )


def finish_kernel(
    odd_ref,
    square_ref,
    mask_grad_ref,
    kept_ref,
    block_ref,
    own_ref,
    other_ref,
    fc1_ref,
    fc1_other_ref,
    fc2_ref,
    ada_ref,
    *refs,
):
    weights, outs = refs[:18], refs[18:36]
    norm_ref, kept_out, block_out = refs[36:]
    odd = odd_ref[0] == 1
    mask_grad = mask_grad_ref[0:1]
    norm = jnp.sqrt(square_ref[0:1, 0:1] + square_sum(mask_grad))
    factor = clip_level / jnp.maximum(norm, clip_level)
    norm_ref[...] = norm
    qkv = weights[0].shape[1]
    proj = weights[1].shape[0]
    fc1 = weights[2].shape[1]

    def pair(own, other):
        own, other = own[...].astype(jnp.float32), other[...].astype(jnp.float32)
        return jnp.where(odd, other, own), jnp.where(odd, own, other)

    def half(block, first, cols):
        return jnp.where(
            odd, block[:, first + cols : first + 2 * cols], block[:, first : first + cols]
        )

    def step(n, rows, grad):
        new = adamw(weights[n][rows], weights[6 + n][rows], weights[12 + n][rows], grad * factor)
        for k in range(3):
            outs[6 * k + n][rows] = new[k]

    projs = []
    for k, block in enumerate(pair(own_ref, other_ref)):
        rows = slice(k * BLOCK_ROWS, (k + 1) * BLOCK_ROWS)
        step(0, rows, half(block, 0, qkv))
        projs.append(half(block, 2 * qkv, proj))
    step(1, slice(None), jnp.transpose(jnp.concatenate(projs, axis=0)))
    for k, block in enumerate(pair(fc1_ref, fc1_other_ref)):
        rows = slice(k * BLOCK_ROWS, (k + 1) * BLOCK_ROWS)
        step(2, rows, half(block, 0, fc1))
    step(3, slice(None), fc2_ref[...].astype(jnp.float32))
    step(4, slice(None), ada_ref[...])
    step(5, slice(None), mask_grad)
    kept_out[...] = kept_ref[...].astype(jnp.float32)
    block_out[...] = block_ref[...]


def finish_all(odd, squares, mask_grad, kept, block, sums, weights):
    turn = lambda values: [v.T if n % 6 in (1, 3) else v for n, v in enumerate(values)]
    weights = turn(weights)
    vmem = pl.BlockSpec(memory_space=pltpu.VMEM)
    shape = jax.ShapeDtypeStruct
    found = pl.pallas_call(
        finish_kernel,
        in_specs=[pl.BlockSpec(memory_space=pltpu.SMEM)] + [vmem] * (4 + 6 + 18),
        out_specs=[vmem] * 21,
        out_shape=[shape(w.shape, w.dtype) for w in weights]
        + [
            shape((1, 1), jnp.float32),
            shape(kept.shape, jnp.float32),
            shape(block.shape, block.dtype),
        ],
        compiler_params=pltpu.CompilerParams(vmem_limit_bytes=VMEM_LIMIT),
        name="finish_all",
    )(odd, squares, mask_grad, kept, block, *sums, *weights)
    return turn(found[:18]), *found[18:]


def run(actions):
    for action in actions:
        action()


def run_slot(step, groups, first, count, stride=1):
    for k in range(count):
        group = groups[first + k * stride]

        @pl.when(step == k)
        def _():
            run(group)


def fixed(*shape):
    return pl.BlockSpec(shape, lambda *_: (0,) * len(shape))


def once(*shape):
    return pl.BlockSpec(shape, lambda *_: (0,) * len(shape), pipeline_mode=pl.Buffered(1))


def chosen_rows(index_ref, region):
    rows = lax.broadcasted_iota(jnp.int32, (REGION, index_ref.shape[1]), 0) + region * REGION
    return (rows == index_ref[...]).astype(jnp.float32)


GATHER_PLANS = ((False, (0,)), (True, (3,)))
SCATTER_PLANS = ((False, (0,)), (True, (0, 3)))
FORWARD_STEPS = [
    (0, 1, 3), (5, 0, 1, 0, 0), (5, 0, 3), (6, 0, 0, 1, 0), (6, 0, 0, 0, 1), (9, 1, 0, 0, 1),
    (12, 0, 1, 0, 1), (12, 0, 1, 1, 0), (12, 1, 1, 0, 0), (13, 0, 2), (14, 0, 3, 0, 0), (15,),
    (16, 1, 0, 1, 0), (16, 1, 3, 0, 0), (16, 0, 3, 0, 1), (17, 1, 2), (18, 0, 0, 1, 1),
    (21, 0, 1, 1, 1), (22, 0, 2, 0, 0), (22, 1, 1, 0, 1), (22, 1, 2, 0, 0), (26, 1, 1, 1, 0),
    (27, 0, 2, 1, 0), (27, 1, 3, 1, 0), (28, 1, 3, 0, 1), (29, 0, 2, 0, 1), (30, 1, 0, 1, 1),
    (30, 1, 1, 1, 1), (30, 1, 2, 0, 1), (31, 0, 3, 1, 0), (31, 0, 2, 1, 1), (32, 0, 3, 1, 1),
    (32, 1, 3, 1, 1), (32, 1, 2, 1, 0), (32, 1, 2, 1, 1),
]
BACKWARD_STEPS = [
    (0, 0, 0, 1, 1, 0), (0,), (0, 0, 0, 0, 0, 1), (0, 0, 0, 3, 1, 1), (0, 0, 0, 1, 1, 1),
    (0, 0, 0, 1, 0, 1), (1, 0, 1, 1, 0, 0), (1, 0, 1, 1, 1, 1), (1, 0, 1, 3, 1, 1),
    (2, 0, 1, 1, 1, 0), (2, 0, 0, 2, 0, 0), (2, 0, 0, 3, 0, 1), (3, 1, 0, 3, 0, 1),
    (3, 0, 0, 2, 1, 1), (3, 0, 1, 3, 0, 1), (4, 0, 1, 0, 1, 1), (4, 0, 0, 3, 0, 0),
    (6, 1, 0, 1, 0, 1), (6, 0, 0, 3, 1, 0), (6, 0, 1, 1, 0, 1), (6, 0, 1, 2, 1, 0),
    (7, 0, 1, 3, 1, 0), (7, 0, 1, 0, 0, 0), (7, 0, 0, 0, 0, 0), (10, 0, 0, 1, 0, 0),
    (10, 0, 1, 2, 0, 1), (10, 1, 0, 3, 0, 0), (10, 1, 1, 3, 1, 0), (11, 0, 1, 3, 0, 0),
    (11, 0, 1, 2, 1, 1), (11, 0, 1, 0, 1, 0), (11, 0, 0, 2, 0, 1), (12, 0, 0, 0, 1, 0),
    (13, 1, 0, 2, 0, 1), (13, 1, 1, 3, 0, 0), (14, 0, 0, 2, 1, 0), (14, 1, 1, 1, 0, 1),
    (15, 0, 0, 0, 1, 1), (17, 1, 0, 2, 0, 0), (17, 0, 1, 2, 0, 0), (17, 1, 1, 2, 0, 1),
    (17, 0, 1, 0, 0, 1), (18, 1, 0, 0, 1, 0), (19, 1, 0, 0, 0, 1), (19, 1, 1, 2, 0, 0),
    (19, 1, 1, 0, 0, 1), (20, 1, 1, 0, 1, 0), (21, 1, 0, 0, 0, 0), (23, 1, 1, 0, 0, 0),
]
SHIFT_ATTN, SCALE_ATTN, GATE_ATTN, SHIFT_MLP, SCALE_MLP, GATE_MLP = range(6)
GRANULE = 16
PAIR = 2 * HEAD_DIM
PAIRS = HEADS // 2


def embed_tokens(
    slots, kind_ref, kept_ref, index_ref, mask_ref, table_ref, mod_ref, tokens, hidden, hidden_t
):
    count = tokens.shape[0]
    small = kind_ref[0] == 1
    for region in range(count // REGION):
        run(slots[region])
        select = chosen_rows(index_ref, region)
        placed = dot_nn(select.astype(jnp.bfloat16), kept_ref[...])
        unfilled = 1.0 - jnp.sum(select, axis=1, keepdims=True)
        tokens[pl.ds(region * REGION, REGION)] = placed + unfilled * mask_ref[...]

    def add_place(g, carry):
        first = pl.multiple_of((g % 2) * GRANULE, GRANULE)
        wide = table_ref[0, pl.ds(g // 2, 1), :] + table_ref[1, pl.ds(first, GRANULE), :]
        narrow = table_ref[0, pl.ds(g % 16, 1), :] + table_ref[1, :GRANULE]
        place = jnp.where(small, narrow, wide)
        spot = pl.ds(pl.multiple_of(g * GRANULE, GRANULE), GRANULE)
        tokens[spot, :] = tokens[spot, :] + place
        return carry

    lax.fori_loop(0, count // GRANULE, add_place, 0)
    for region in range(count // REGION):
        run(slots[count // REGION + region])
        spot = slice(region * REGION, (region + 1) * REGION)
        normal, _ = norm_parts(tokens[spot])
        value = normal * (1.0 + mod_ref[SCALE_ATTN, region : region + 1])
        value = (value + mod_ref[SHIFT_ATTN, region : region + 1]).astype(jnp.bfloat16)
        hidden[spot] = value
        hidden_t[:, spot] = jnp.transpose(value)


def forward_kernel(
    kind_ref,
    kept_ref,
    index_ref,
    mask_ref,
    table_ref,
    mod_ref,
    weight_ref,
    fc1_ref,
    fc2_ref,
    swap_ref,
    qkv_out,
    attended_out,
    lse_out,
    branch_out,
    middle_out,
    hidden_out,
    hidden_t_out,
    gated_out,
    gated_t_out,
    tokens_hbm,
    normed_t_hbm,
    proj_hbm,
    grad_hbm,
    fc1_full,
    fc2_full,
    tokens,
    normed,
    normed_t,
    qkv,
    attended,
    proj,
    grad,
    out_sems,
    *sems,
):
    step = pl.program_id(0)
    rows = qkv_out.shape[0]
    groups = qkv.shape[0] // rows
    regions = tokens.shape[0] // REGION
    cols = D // groups
    place = Place()
    begin, relay, late, finish = gather_actions(
        place, GATHER_PLANS, [fc1_ref, fc2_ref], [fc1_full, fc2_full], *sems[:4]
    )
    swap_start, swap_wait = swap_band(place, swap_ref, grad, *sems[4:])
    first_qkv = 1 + 2 * regions
    first_head = first_qkv + groups
    first_region = first_head + HEADS
    slots = [[] for _ in range(first_region + regions)]
    slots[0] += [functools.partial(greet, place, band=True), begin]
    for when, *what in FORWARD_STEPS:
        action = {0: swap_start, 2: late, 4: relay}[len(what)]
        slots[when].append(functools.partial(action, *what))
    outward = [
        pltpu.make_async_copy(source, target, out_sems.at[n])
        for n, (source, target) in enumerate(
            [(tokens, tokens_hbm), (normed_t, normed_t_hbm), (proj, proj_hbm), (grad, grad_hbm)]
        )
    ]

    @pl.when(step == 0)
    def _():
        run(slots[0])
        embed_tokens(
            slots[1:first_qkv],
            kind_ref,
            kept_ref,
            index_ref,
            mask_ref,
            table_ref,
            mod_ref,
            tokens,
            normed,
            normed_t,
        )
        outward[0].start()
        outward[1].start()

    run_slot(step, slots, first_qkv, groups)

    @pl.when(step < groups)
    def _():
        span = -(-rows // 128) * 128
        wide = dot_nn(normed[...], weight_ref[:, :span]).astype(jnp.bfloat16)
        part = jnp.transpose(wide)[:rows]
        qkv_out[...] = part
        qkv[pl.ds(pl.multiple_of(step * rows, 16), rows), :] = part
        for g in range(groups):

            @pl.when(step == g)
            def _():
                proj[:, g * cols : (g + 1) * cols] = weight_ref[:, rows:]

    pair = step - groups

    @pl.when((pair >= 0) & (pair < PAIRS))
    def _():
        @pl.when(pair == 0)
        def _():
            outward[2].start()

        other = jnp.where(kind_ref[0] == 1, MASKED, 0.0)
        spot = lambda part: pl.ds(pl.multiple_of(part * D + pair * PAIR, 16), PAIR)
        for half in range(2):
            run_slot(pair, slots, first_head + half, PAIRS, 2)
            head = slice(half * HEAD_DIM, (half + 1) * HEAD_DIM)
            attn_head(
                other,
                qkv[spot(0), :][head],
                qkv[spot(1), :][head],
                qkv[spot(2), :][head],
                attended_out,
                head,
                lse_out.at[half],
            )
        attended[spot(0), :] = attended_out[...]

    region = step - groups - PAIRS
    run_slot(region, slots, first_region, regions)

    @pl.when(region >= 0)
    def _():
        @pl.when(region == 0)
        def _():
            swap_wait()
            outward[3].start()

        spot = pl.ds(pl.multiple_of(region * REGION, REGION), REGION)
        part = lambda k: mod_ref[k, pl.ds(region, 1), :]
        branch = dot_nn(jnp.transpose(attended[:, spot]), proj[...])
        middle = tokens[spot, :] + part(GATE_ATTN) * branch
        normal, _ = norm_parts(middle)
        hidden = (normal * (1.0 + part(SCALE_MLP)) + part(SHIFT_MLP)).astype(jnp.bfloat16)
        gated = (part(GATE_MLP) * grad[region].astype(jnp.float32)).astype(jnp.bfloat16)
        branch_out[...] = branch
        middle_out[...] = middle
        hidden_out[...] = hidden
        hidden_t_out[...] = jnp.transpose(hidden)
        gated_out[...] = gated
        gated_t_out[...] = jnp.transpose(gated)

    @pl.when(region == regions - 1)
    def _():
        finish()
        for copy in outward:
            copy.wait()


def forward(kind, kept, index, mask, tables, mod, weights, blocks, swap, collective_id):
    width = kept.shape[1]
    regions = mod.shape[1]
    count = regions * REGION
    groups = weights.shape[1] // BLOCK_COLS
    rows = 3 * D // groups
    shape = jax.ShapeDtypeStruct
    bf16, f32 = jnp.bfloat16, jnp.float32
    group = lambda s: jnp.minimum(s, groups - 1)
    pair = lambda s: jnp.clip(s - groups, 0, PAIRS - 1)
    region = lambda s: jnp.clip(s - groups - PAIRS, 0, regions - 1)
    token_rows = pl.BlockSpec((REGION, width), lambda s: (region(s), 0))
    token_cols = pl.BlockSpec((width, REGION), lambda s: (0, region(s)))
    hbm = pl.BlockSpec(memory_space=pl.ANY)
    whole = shape((8 * BLOCK_ROWS, 4 * BLOCK_COLS), bf16)
    return pl.pallas_call(
        forward_kernel,
        grid=(groups + PAIRS + regions,),
        in_specs=[
            pl.BlockSpec(memory_space=pltpu.SMEM),
            once(*kept.shape),
            once(*index.shape),
            once(1, width),
            once(*tables.shape),
            once(*mod.shape),
            pl.BlockSpec((width, BLOCK_COLS), lambda s: (0, group(s))),
            once(BLOCK_ROWS, BLOCK_COLS),
            once(BLOCK_ROWS, BLOCK_COLS),
            hbm,
        ],
        out_specs=[
            pl.BlockSpec((rows, count), lambda s: (group(s), 0)),
            pl.BlockSpec((PAIR, count), lambda s: (pair(s), 0)),
            pl.BlockSpec((2, 1, count), lambda s: (pair(s), 0, 0)),
            token_rows,
            token_rows,
            token_rows,
            token_cols,
            token_rows,
            token_cols,
        ]
        + [hbm] * 6,
        out_shape=[
            shape((3 * D, count), bf16),
            shape((D, count), bf16),
            shape((HEADS, 1, count), f32),
            shape((count, width), f32),
            shape((count, width), f32),
            shape((count, width), bf16),
            shape((width, count), bf16),
            shape((count, width), bf16),
            shape((width, count), bf16),
            shape((count, width), f32),
            shape((width, count), bf16),
            shape((width, width), bf16),
            shape(swap.shape, swap.dtype),
            whole,
            whole,
        ],
        scratch_shapes=[
            pltpu.VMEM((count, width), f32),
            pltpu.VMEM((count, width), bf16),
            pltpu.VMEM((width, count), bf16),
            pltpu.VMEM((3 * D, count), bf16),
            pltpu.VMEM((D, count), bf16),
            pltpu.VMEM((width, width), bf16),
            pltpu.VMEM(swap.shape, swap.dtype),
            pltpu.SemaphoreType.DMA((4,)),
        ]
        + gather_scratch(2)
        + swap_scratch(),
        compiler_params=pltpu.CompilerParams(
            collective_id=collective_id, has_side_effects=True, vmem_limit_bytes=VMEM_LIMIT
        ),
        name="forward",
    )(kind, kept, index, mask, tables, mod, weights, *blocks, swap)


def backward_kernel(
    kind_ref,
    q_ref,
    k_ref,
    v_ref,
    attended_ref,
    grad_ref,
    lse_ref,
    weight_ref,
    normed_t_ref,
    proj_ref,
    fc1_ref,
    fc2_ref,
    swap_ref,
    out_ref,
    fc1_sum,
    fc2_sum,
    hidden_hbm,
    swapped_hbm,
    grads,
    staged,
    grad_hidden,
    out_sem,
    *sems,
):
    step = pl.program_id(0)
    rows = grads.shape[0] // (pl.num_programs(0) - PAIRS)
    groups = grads.shape[0] // rows
    cols = BLOCK_COLS - rows
    place = Place()
    swap_start, swap_wait = swap_band(place, swap_ref, swapped_hbm, *sems[7:])
    order = [what[1:] for _, *what in BACKWARD_STEPS if what and not what[0]]
    begin, fold, combine, finish = scatter_actions(
        place, SCATTER_PLANS, order, [fc1_ref, fc2_ref], [fc1_sum, fc2_sum], *sems[:7]
    )
    slots = [[] for _ in range(HEADS + 2 * groups)]
    slots[0] += [functools.partial(greet, place, band=True), begin]
    folded = 0
    for when, *what in BACKWARD_STEPS:
        if not what:
            slots[when].append(swap_start)
        elif what[0]:
            slots[when].append(functools.partial(combine, *what[1:]))
        else:
            slots[when].append(functools.partial(fold, folded))
            folded += 1

    @pl.when(step < PAIRS)
    def _():
        other = jnp.where(kind_ref[0] == 1, MASKED, 0.0)
        for half in range(2):
            run_slot(step, slots, half, PAIRS, 2)
            head = slice(half * HEAD_DIM, (half + 1) * HEAD_DIM)
            attn_head_back(
                other,
                q_ref[head],
                k_ref[head],
                v_ref[head],
                attended_ref[head],
                grad_ref[head],
                lse_ref.at[half],
                staged,
                head,
            )
        for part in range(3):
            spot = pl.ds(pl.multiple_of(part * D + step * PAIR, 16), PAIR)
            grads[spot, :] = staged[part]

    group = step - PAIRS
    run_slot(group, slots, HEADS, groups, 2)

    @pl.when(group >= 0)
    def _():
        grad = grads[pl.ds(pl.multiple_of(group * rows, 16), rows), :]
        added = dot_nt(jnp.transpose(grad), weight_ref[:, :rows])

        @pl.when(group == 0)
        def _():
            grad_hidden[...] = added

        @pl.when(group > 0)
        def _():
            grad_hidden[...] += added

        run_slot(group, slots, HEADS + 1, groups, 2)
        out_ref[:, :rows] = dot_nt(normed_t_ref[...], grad).astype(jnp.bfloat16)
        for g in range(groups):

            @pl.when(group == g)
            def _():
                out_ref[:, rows:] = proj_ref[:, g * cols : (g + 1) * cols]

    @pl.when(group == groups - 1)
    def _():
        outward = pltpu.make_async_copy(grad_hidden, hidden_hbm, out_sem.at[0])
        outward.start()
        finish()
        swap_wait()
        outward.wait()


def backward(
    kind, qkv, attended, grad_attended, lse, weights, normed_t, grad_proj, grads, swap, collective_id
):
    width, count = normed_t.shape
    groups = weights.shape[1] // BLOCK_COLS
    shape = jax.ShapeDtypeStruct
    bf16, f32 = jnp.bfloat16, jnp.float32
    pair = lambda s: jnp.minimum(s, PAIRS - 1)
    group = lambda s: jnp.maximum(s - PAIRS, 0)
    heads = lambda part: pl.BlockSpec((PAIR, count), lambda s: (pair(s) + part * PAIRS, 0))
    hbm = pl.BlockSpec(memory_space=pl.ANY)
    block = shape((BLOCK_ROWS, BLOCK_COLS), bf16)
    return pl.pallas_call(
        backward_kernel,
        grid=(PAIRS + groups,),
        in_specs=[
            pl.BlockSpec(memory_space=pltpu.SMEM),
            heads(0),
            heads(1),
            heads(2),
            heads(0),
            heads(0),
            pl.BlockSpec((2, 1, count), lambda s: (pair(s), 0, 0)),
            pl.BlockSpec((width, BLOCK_COLS), lambda s: (0, group(s))),
            once(width, count),
            once(width, D),
            hbm,
            hbm,
            hbm,
        ],
        out_specs=[
            pl.BlockSpec((width, BLOCK_COLS), lambda s: (0, group(s))),
            fixed(BLOCK_ROWS, BLOCK_COLS),
            fixed(BLOCK_ROWS, BLOCK_COLS),
            hbm,
            hbm,
        ],
        out_shape=[
            shape(weights.shape, bf16),
            block,
            block,
            shape((count, width), f32),
            shape(swap.shape, swap.dtype),
        ],
        scratch_shapes=[
            pltpu.VMEM((3 * D, count), bf16),
            pltpu.VMEM((3, PAIR, count), bf16),
            pltpu.VMEM((count, width), f32),
            pltpu.SemaphoreType.DMA((1,)),
        ]
        + scatter_scratch(2)
        + swap_scratch(),
        compiler_params=pltpu.CompilerParams(
            collective_id=collective_id, has_side_effects=True, vmem_limit_bytes=VMEM_LIMIT
        ),
        name="backward",
    )(kind, qkv, qkv, qkv, attended, grad_attended, lse, weights, normed_t, grad_proj, *grads, swap)


def column_sum(values):
    return jnp.sum(values, axis=0, keepdims=True)


def mlp_kernel(
    h_ref,
    ht_ref,
    g_ref,
    gt_ref,
    up_ref,
    down_ref,
    middle_ref,
    branch_ref,
    grad_ref,
    attended_ref,
    proj_ref,
    mod_ref,
    gup_ref,
    gdown_ref,
    block_ref,
    grad_middle_ref,
    grad_proj_ref,
    grad_attended_ref,
    sums_ref,
    output_ref,
    grad_hidden_ref,
    total_ref,
):
    step = pl.program_id(0)
    regions = mod_ref.shape[1]
    region = step - (pl.num_programs(0) - regions)

    @pl.when(step == 0)
    def _():
        output_ref[...] = jnp.zeros_like(output_ref)
        grad_hidden_ref[...] = jnp.zeros_like(grad_hidden_ref)

    @pl.when(region < 0)
    def _():
        mlp_tile(
            h_ref, ht_ref, g_ref, gt_ref, up_ref, down_ref, output_ref, grad_hidden_ref, gup_ref, gdown_ref
        )

    @pl.when(region >= 0)
    def _():
        spot = pl.ds(pl.multiple_of(region * REGION, REGION), REGION)
        part = lambda k: mod_ref[k, pl.ds(region, 1), :]
        output = output_ref[spot, :]
        grad_hidden = grad_hidden_ref[spot, :]
        middle = middle_ref[...]
        grad = grad_ref[...].astype(jnp.float32)
        block_ref[...] = (middle + part(GATE_MLP) * output).astype(jnp.bfloat16)
        normal, root = norm_parts(middle)
        grad_middle = grad + norm_back(grad_hidden, normal, root, part(SCALE_MLP))
        grad_middle_ref[...] = grad_middle
        sums_ref[0, 0:1] = column_sum(grad_middle * branch_ref[...])
        sums_ref[0, 1:2] = column_sum(grad_hidden)
        sums_ref[0, 2:3] = column_sum(grad_hidden * normal)
        sums_ref[0, 3:4] = column_sum(grad * output)
        grad_branch = (part(GATE_ATTN) * grad_middle).astype(jnp.bfloat16)
        grad_attended_ref[...] = dot_nt(proj_ref[...], grad_branch).astype(jnp.bfloat16)
        added = dot_nn(attended_ref[...], grad_branch)

        @pl.when(region == 0)
        def _():
            total_ref[...] = added

        @pl.when(region > 0)
        def _():
            total_ref[...] += added

        @pl.when(region == regions - 1)
        def _():
            grad_proj_ref[...] = total_ref[...].astype(jnp.bfloat16)


def mlp_both(hidden, hidden_t, gated, gated_t, up, down_t, middle, branch, grad, attended_t, proj, mod):
    count, width = hidden.shape
    wide = up.shape[1]
    tile = 512
    tiles = wide // tile
    regions = count // REGION
    region = lambda s: jnp.maximum(s - tiles, 0)
    rows = pl.BlockSpec((REGION, width), lambda s: (region(s), 0))
    columns = pl.BlockSpec((width, REGION), lambda s: (0, region(s)))
    part = pl.BlockSpec((width, tile), lambda s: (0, jnp.minimum(s, tiles - 1)))
    shape = jax.ShapeDtypeStruct
    bf16, f32 = jnp.bfloat16, jnp.float32
    return pl.pallas_call(
        mlp_kernel,
        grid=(tiles + regions,),
        in_specs=[
            once(count, width),
            once(width, count),
            once(count, width),
            once(width, count),
            part,
            part,
            rows,
            rows,
            rows,
            columns,
            once(width, width),
            once(*mod.shape),
        ],
        out_specs=[
            part,
            part,
            rows,
            rows,
            once(width, width),
            columns,
            pl.BlockSpec((1, 4, width), lambda s: (region(s), 0, 0)),
        ],
        out_shape=[
            shape((width, wide), bf16),
            shape((width, wide), bf16),
            shape((count, width), bf16),
            shape((count, width), f32),
            shape((width, width), bf16),
            shape((width, count), bf16),
            shape((regions, 4, width), f32),
        ],
        scratch_shapes=[
            pltpu.VMEM((count, width), f32),
            pltpu.VMEM((count, width), f32),
            pltpu.VMEM((width, width), f32),
        ],
        compiler_params=pltpu.CompilerParams(vmem_limit_bytes=VMEM_LIMIT),
        name="mlp_both",
    )(hidden, hidden_t, gated, gated_t, up, down_t, middle, branch, grad, attended_t, proj, mod)


def swap_columns(shard):
    pairs = [(d, d ^ 1) for d in range(lax.axis_size("dp"))]
    odd = lax.axis_index("dp") % 2
    rows = shard.shape[0] // 2
    own = lax.dynamic_slice_in_dim(shard, odd * rows, rows, axis=0)
    other = lax.dynamic_slice_in_dim(shard, (1 - odd) * rows, rows, axis=0)
    other = lax.ppermute(other, "dp", pairs)
    return jnp.where(odd == 0, jnp.stack([own, other], 1), jnp.stack([other, own], 1))


def norm_parts(values):
    center = jnp.mean(values, axis=-1, keepdims=True)
    spread = jnp.mean((values - center) ** 2, axis=-1, keepdims=True)
    root = lax.rsqrt(spread + 1e-06)
    return ((values - center) * root, root)


def norm_back(grad, normal, root, scales):
    inner = grad * (1.0 + scales)
    return root * (
        inner
        - jnp.mean(inner, axis=-1, keepdims=True)
        - normal * jnp.mean(inner * normal, axis=-1, keepdims=True)
    )


def embed_tables(count):
    quarter = D // 4
    omegas = 1.0 / 10000.0 ** (jnp.arange(quarter, dtype=jnp.float32) / quarter)
    angles = jnp.arange(count, dtype=jnp.float32)[:, None] * omegas
    return jnp.concatenate([jnp.sin(angles), jnp.cos(angles)], axis=-1)


def slot_device(
    kept_tokens,
    kept_index,
    resolution,
    labels,
    timesteps,
    class_table,
    cotangent,
    mask_token,
    w_qkv,
    w_proj,
    w_fc1,
    w_fc2,
    w_ada,
    mask_first,
    first_qkv,
    first_proj,
    first_fc1,
    first_fc2,
    first_ada,
    mask_second,
    second_qkv,
    second_proj,
    second_fc1,
    second_fc2,
    second_ada,
):
    highest = lax.Precision.HIGHEST
    bf16 = jnp.bfloat16
    bands = lax.axis_size("band")
    groups = lax.axis_size("dp")
    band = lax.axis_index("band")
    slots, local_rows, _ = cotangent.shape
    tokens_count = bands * local_rows
    regions = tokens_count // REGION
    images = labels.shape[1]

    qkv_cols, proj_cols, fc1_cols = w_qkv.shape[1], w_proj.shape[1], w_fc1.shape[1]
    swapped = swap_columns(jnp.concatenate([w_qkv, w_proj, w_fc1], axis=1).astype(bf16))
    joined_block = jnp.concatenate(
        [
            swapped[:, :, :qkv_cols].reshape(-1, 2 * qkv_cols),
            swapped[:, :, qkv_cols:-fc1_cols].reshape(-1, 2 * proj_cols),
        ],
        axis=1,
    )
    fc1_block = swapped[:, :, -fc1_cols:].reshape(-1, 2 * fc1_cols)
    fc2_block = w_fc2.astype(bf16).T

    rows_ada, cols_ada = w_ada.shape
    table_part = lax.dynamic_slice_in_dim(class_table, band * rows_ada, rows_ada, axis=1)
    chosen = labels.reshape(-1, 1) == jnp.arange(class_table.shape[0])[None, :]
    features = band * rows_ada + jnp.arange(rows_ada)
    half_width = D // 2
    frequency = jnp.exp(
        -math.log(10000.0) * (features % half_width).astype(jnp.float32) / half_width
    )
    angles = timesteps.reshape(-1, 1).astype(jnp.float32) * frequency
    waves = jnp.where(features < half_width, jnp.cos(angles), jnp.sin(angles))
    condition = jnp.matmul(chosen.astype(jnp.float32), table_part, precision=highest) + waves
    cond = jax.nn.silu(condition).astype(bf16).astype(jnp.float32)
    cond = jnp.pad(cond.reshape(slots, images, rows_ada), ((0, 0), (0, 8 - images), (0, 0)))

    kind = lax.dynamic_slice_in_dim(resolution, band, 1)
    joined_full, modulation, conds, kept, index = head(
        joined_block, cond, w_ada.astype(bf16), kept_tokens, kept_index[:, None, :], 0
    )
    kept = kept.reshape(-1, D)
    index = index.reshape(1, -1)
    modulation = modulation.transpose(1, 0, 2).reshape(images, 6, D).transpose(1, 0, 2)
    mod = jnp.where(kind[0] == 1, modulation, modulation[:, :1])
    table = embed_tables(SIDE)
    blank = jnp.zeros_like(table)
    tables = jnp.stack(
        [jnp.concatenate([table, blank], axis=1), jnp.concatenate([blank, table], axis=1)]
    )
    (
        qkv,
        attended_t,
        lse,
        branch,
        middle,
        hidden_mlp,
        hidden_mlp_t,
        grad_output,
        grad_output_t,
        tokens,
        normed_t,
        proj_full,
        grad_out,
        fc1_full,
        fc2_full,
    ) = forward(
        kind,
        kept,
        index,
        mask_token[None],
        tables,
        mod,
        joined_full,
        [fc1_block, fc2_block],
        cotangent,
        1,
    )
    grad_out = grad_out.reshape(tokens_count, D)
    grad_fc1, grad_fc2, block_slot, grad_middle, grad_proj, grad_attended, sums_mlp = mlp_both(
        hidden_mlp,
        hidden_mlp_t,
        grad_output,
        grad_output_t,
        fc1_full,
        fc2_full,
        middle,
        branch,
        grad_out,
        attended_t,
        proj_full,
        mod,
    )
    grad_joined, sum_fc1, sum_fc2, grad_hidden, block_out = backward(
        kind,
        qkv,
        attended_t,
        grad_attended,
        lse,
        joined_full,
        normed_t,
        grad_proj,
        [grad_fc1, grad_fc2],
        block_slot.reshape(bands, local_rows, D),
        2,
    )
    sum_joined, other_joined, other_fc1, red_ada, grad_mask, squares, grad_kept = tail(
        grad_joined,
        kind,
        sum_fc1,
        sum_fc2,
        index,
        mod,
        sums_mlp,
        conds,
        tokens,
        grad_middle,
        grad_hidden,
        bands,
        3,
    )
    odd = (lax.axis_index("dp") % 2).astype(jnp.int32)
    new, norm_value, kept_grad, block_out = finish_all(
        odd[None],
        squares,
        grad_mask,
        grad_kept,
        block_out,
        [sum_joined, other_joined, sum_fc1, other_fc1, sum_fc2, red_ada],
        [
            w_qkv, w_proj, w_fc1, w_fc2, w_ada, mask_token[None],
            first_qkv, first_proj, first_fc1, first_fc2, first_ada, mask_first[None],
            second_qkv, second_proj, second_fc1, second_fc2, second_ada, mask_second[None],
        ],
    )
    return (
        (block_out, kept_grad, norm_value[0, 0])
        + (new[5][0], *new[:5])
        + (new[11][0], *new[6:11])
        + (new[17][0], *new[12:17])
    )


def per_device(*arguments):
    cotangent = arguments[6]
    if (lax.axis_size("dp"), lax.axis_size("band")) == (8, cotangent.shape[0]):
        return slot_device(*arguments)
    return general_device(*arguments)


def solution(mesh):
    in_specs = (
        P("dp", "band", None),
        P("dp", "band"),
        P("dp"),
        P("dp", None),
        P("dp", None),
        P(),
        P("dp", "band", None),
        P(),
        P("band", "dp"),
        P("band", "dp"),
        P("band", "dp"),
        P("band", "dp"),
        P("band", "dp"),
        P(),
        P("band", "dp"),
        P("band", "dp"),
        P("band", "dp"),
        P("band", "dp"),
        P("band", "dp"),
        P(),
        P("band", "dp"),
        P("band", "dp"),
        P("band", "dp"),
        P("band", "dp"),
        P("band", "dp"),
    )
    out_specs = (
        P("dp", "band", None),
        P("dp", "band", None),
        P(),
        P(),
        P("band", "dp"),
        P("band", "dp"),
        P("band", "dp"),
        P("band", "dp"),
        P("band", "dp"),
        P(),
        P("band", "dp"),
        P("band", "dp"),
        P("band", "dp"),
        P("band", "dp"),
        P("band", "dp"),
        P(),
        P("band", "dp"),
        P("band", "dp"),
        P("band", "dp"),
        P("band", "dp"),
        P("band", "dp"),
    )
    return jax.shard_map(
        per_device, mesh=mesh, in_specs=in_specs, out_specs=out_specs, check_vma=False
    )
```

```python
import functools
import math

import jax
import jax.numpy as jnp
from jax import lax
from jax.experimental import pallas as pl
from jax.experimental.pallas import tpu as pltpu
from jax.sharding import PartitionSpec as P

D = 1152
HEADS = 16
HEAD_DIM = 72
SIDE = 32
STEP = 10
REGION = 256


learn_rate = 0.1
beta_first = 0.9
beta_second = 0.95
adam_eps = 1e-08
decay_rate = 0.1
clip_level = 1.0


def time_embed(timestep):
    half_width = D // 2
    frequency = jnp.exp(-math.log(10000.0) * jnp.arange(half_width, dtype=jnp.float32) / half_width)
    angles = timestep.astype(jnp.float32)[..., None] * frequency
    return jnp.concatenate([jnp.cos(angles), jnp.sin(angles)], axis=-1)


def grid_embed(grid_rows, grid_cols):
    quarter = D // 4
    omegas = 1.0 / 10000.0 ** (jnp.arange(quarter, dtype=jnp.float32) / quarter)
    row_angle = grid_rows.astype(jnp.float32)[..., None] * omegas
    col_angle = grid_cols.astype(jnp.float32)[..., None] * omegas
    return jnp.concatenate(
        [jnp.sin(row_angle), jnp.cos(row_angle), jnp.sin(col_angle), jnp.cos(col_angle)], axis=-1
    )


def slot_layout(positions, slot_kinds):
    small_side = SIDE // 2
    region = positions // REGION
    inside = positions % REGION
    grid_rows = jnp.where(slot_kinds == 1, inside // small_side, positions // SIDE)
    grid_cols = jnp.where(slot_kinds == 1, inside % small_side, positions % SIDE)
    image_id = jnp.where(slot_kinds == 1, region, 0)
    return (grid_rows, grid_cols, image_id)


def modulate(values, shifts, scales):
    center = jnp.mean(values, axis=-1, keepdims=True)
    spread = jnp.mean((values - center) ** 2, axis=-1, keepdims=True)
    return (values - center) * lax.rsqrt(spread + 1e-06) * (1.0 + scales) + shifts


def gelu_tanh(values):
    return jax.nn.gelu(values, approximate=True)


def pick_rows(table_rows, picks):
    return table_rows[picks]


def allowed_pairs(query_pos, key_pos, slot_kinds):
    same_region = (query_pos // REGION)[None, :, None] == (key_pos // REGION)[None, None, :]
    return (slot_kinds[:, None, None] == 0) | same_region


def attend(queries, keys_in, values_in, allowed):

    def one_slot(pieces):
        query_s, key_s, value_s, allow_s = pieces
        scores = jnp.einsum(
            "qhd,khd->hqk", query_s, key_s, preferred_element_type=jnp.float32
        ) * HEAD_DIM ** (-0.5)
        scores = jnp.where(allow_s[None], scores, -1e30)
        row_peak = jnp.max(scores, axis=-1, keepdims=True)
        row_total = jnp.sum(jnp.exp(scores - row_peak), axis=-1, keepdims=True)
        log_total = row_peak + jnp.log(row_total)
        weights_soft = jnp.exp(scores - log_total).astype(jnp.bfloat16)
        result = jnp.einsum(
            "hqk,khd->qhd", weights_soft, value_s, preferred_element_type=jnp.float32
        )
        return (result.astype(jnp.bfloat16), log_total)

    return lax.map(one_slot, (queries, keys_in, values_in, allowed))


def attend_back(queries, keys_in, values_in, allowed, log_total, grad_attended):

    def one_slot(pieces):
        query_s, key_s, value_s, allow_s, total_s, grad_s = pieces
        scores = jnp.einsum(
            "qhd,khd->hqk", query_s, key_s, preferred_element_type=jnp.float32
        ) * HEAD_DIM ** (-0.5)
        scores = jnp.where(allow_s[None], scores, -1e30)
        weights_full = jnp.exp(scores - total_s)
        weights_soft = weights_full.astype(jnp.bfloat16)
        grad_weights = jnp.einsum(
            "qhd,khd->hqk", grad_s, value_s, preferred_element_type=jnp.float32
        )
        row_dot = jnp.sum(weights_full * grad_weights, axis=-1, keepdims=True)
        grad_scores = (weights_full * (grad_weights - row_dot) * HEAD_DIM ** (-0.5)).astype(
            jnp.bfloat16
        )
        grad_queries = jnp.einsum(
            "hqk,khd->qhd", grad_scores, key_s, preferred_element_type=jnp.float32
        )
        grad_keys = jnp.einsum(
            "hqk,qhd->khd", grad_scores, query_s, preferred_element_type=jnp.float32
        )
        grad_values = jnp.einsum(
            "hqk,qhd->khd", weights_soft, grad_s, preferred_element_type=jnp.float32
        )
        return (grad_queries, grad_keys, grad_values)

    return lax.map(one_slot, (queries, keys_in, values_in, allowed, log_total, grad_attended))


def adamw(weight, first, second, grad):
    first_new = beta_first * first + (1.0 - beta_first) * grad
    second_new = beta_second * second + (1.0 - beta_second) * grad * grad
    first_hat = first_new / (1.0 - beta_first**STEP)
    second_hat = second_new / (1.0 - beta_second**STEP)
    weight_new = weight - learn_rate * (
        first_hat / (jnp.sqrt(second_hat) + adam_eps) + decay_rate * weight
    )
    return (weight_new, first_new, second_new)


def general_device(
    kept_tokens,
    kept_index,
    resolution,
    labels,
    timesteps,
    class_table,
    cotangent,
    mask_token,
    w_qkv,
    w_proj,
    w_fc1,
    w_fc2,
    w_ada,
    mask_first,
    first_qkv,
    first_proj,
    first_fc1,
    first_fc2,
    first_ada,
    mask_second,
    second_qkv,
    second_proj,
    second_fc1,
    second_fc2,
    second_ada,
):
    highest = lax.Precision.HIGHEST
    band_index = lax.axis_index("band")
    slot_count = cotangent.shape[0]
    local_rows = cotangent.shape[1]
    qkv_low = w_qkv.astype(jnp.bfloat16)
    proj_low = w_proj.astype(jnp.bfloat16)
    fc1_low = w_fc1.astype(jnp.bfloat16)
    fc2_low = w_fc2.astype(jnp.bfloat16)
    ada_low = w_ada.astype(jnp.bfloat16)
    cols_qkv, cols_proj, cols_fc1, cols_fc2, cols_ada = (
        lax.all_gather(qkv_low, "dp", axis=1, tiled=True),
        lax.all_gather(proj_low, "dp", axis=1, tiled=True),
        lax.all_gather(fc1_low, "dp", axis=1, tiled=True),
        lax.all_gather(fc2_low, "dp", axis=1, tiled=True),
        lax.all_gather(ada_low, "dp", axis=1, tiled=True),
    )
    condition = jnp.take(class_table, labels, axis=0) + time_embed(timesteps)
    cond_low = jax.nn.silu(condition).astype(jnp.bfloat16)
    qkv_full, proj_full, fc1_full, fc2_full, ada_full = (
        lax.all_gather(cols_qkv, "band", axis=0, tiled=True),
        lax.all_gather(cols_proj, "band", axis=0, tiled=True),
        lax.all_gather(cols_fc1, "band", axis=0, tiled=True),
        lax.all_gather(cols_fc2, "band", axis=0, tiled=True),
        lax.all_gather(cols_ada, "band", axis=0, tiled=True),
    )
    modulation = jnp.einsum("sid,de->sie", cond_low, ada_full, preferred_element_type=jnp.float32)
    kept_all, index_all = (
        lax.all_gather(kept_tokens, "band", axis=1, tiled=True),
        lax.all_gather(kept_index, "band", axis=1, tiled=True),
    )
    positions = band_index * local_rows + jnp.arange(local_rows)
    select = index_all[:, None, :] == positions[None, :, None]
    placed = jnp.einsum(
        "spj,sjd->spd", select.astype(jnp.bfloat16), kept_all, preferred_element_type=jnp.float32
    )
    unfilled = 1.0 - jnp.sum(select.astype(jnp.float32), axis=2)
    grid_rows, grid_cols, image_id = slot_layout(positions[None, :], resolution[:, None])
    tokens = placed + unfilled[..., None] * mask_token + grid_embed(grid_rows, grid_cols)
    token_mod = jax.vmap(pick_rows)(modulation, image_id)
    shift_attn, scale_attn, gate_attn, shift_mlp, scale_mlp, gate_mlp = jnp.split(
        token_mod, 6, axis=-1
    )
    attn_value, attn_pull = jax.vjp(modulate, tokens, shift_attn, scale_attn)
    hidden = attn_value.astype(jnp.bfloat16)
    qkv = jnp.einsum("std,de->ste", hidden, qkv_full, preferred_element_type=jnp.float32).astype(
        jnp.bfloat16
    )
    queries = qkv[..., :D].reshape(slot_count, local_rows, HEADS, HEAD_DIM)
    keys_in = qkv[..., D : 2 * D].reshape(slot_count, local_rows, HEADS, HEAD_DIM)
    values_in = qkv[..., 2 * D :].reshape(slot_count, local_rows, HEADS, HEAD_DIM)
    keys_all, values_all = (
        lax.all_gather(keys_in, "band", axis=1, tiled=True),
        lax.all_gather(values_in, "band", axis=1, tiled=True),
    )
    allowed = allowed_pairs(positions, jnp.arange(keys_all.shape[1]), resolution)
    attended, log_total = attend(queries, keys_all, values_all, allowed)
    attended_flat = attended.reshape(slot_count, local_rows, D)
    branch = jnp.einsum("std,de->ste", attended_flat, proj_full, preferred_element_type=jnp.float32)
    middle = tokens + gate_attn * branch
    mlp_value, mlp_pull = jax.vjp(modulate, middle, shift_mlp, scale_mlp)
    hidden_mlp = mlp_value.astype(jnp.bfloat16)
    upward = jnp.einsum("std,df->stf", hidden_mlp, fc1_full, preferred_element_type=jnp.float32)
    active_value, gelu_pull = jax.vjp(gelu_tanh, upward)
    active = active_value.astype(jnp.bfloat16)
    output = jnp.einsum("stf,fd->std", active, fc2_full, preferred_element_type=jnp.float32)
    block_out = (middle + gate_mlp * output).astype(jnp.bfloat16)
    grad_out = cotangent.astype(jnp.float32)
    grad_gate_mlp = grad_out * output
    grad_output = (gate_mlp * grad_out).astype(jnp.bfloat16)
    grad_fc2 = jnp.einsum("stf,std->fd", active, grad_output, preferred_element_type=jnp.float32)
    grad_active = jnp.einsum(
        "std,fd->stf", grad_output, fc2_full, preferred_element_type=jnp.float32
    )
    grad_upward = gelu_pull(grad_active)[0].astype(jnp.bfloat16)
    grad_fc1 = jnp.einsum(
        "std,stf->df", hidden_mlp, grad_upward, preferred_element_type=jnp.float32
    )
    grad_hidden_mlp = jnp.einsum(
        "stf,df->std", grad_upward, fc1_full, preferred_element_type=jnp.float32
    )
    grad_mid_norm, grad_shift_mlp, grad_scale_mlp = mlp_pull(grad_hidden_mlp)
    grad_middle = grad_out + grad_mid_norm
    grad_gate_attn = grad_middle * branch
    grad_branch = (gate_attn * grad_middle).astype(jnp.bfloat16)
    grad_proj = jnp.einsum(
        "std,ste->de", attended_flat, grad_branch, preferred_element_type=jnp.float32
    )
    grad_attended = jnp.einsum(
        "ste,de->std", grad_branch, proj_full, preferred_element_type=jnp.float32
    ).astype(jnp.bfloat16)
    grad_attended = grad_attended.reshape(slot_count, local_rows, HEADS, HEAD_DIM)
    grad_queries, grad_keys_part, grad_values_part = attend_back(
        queries, keys_all, values_all, allowed, log_total, grad_attended
    )
    grad_keys, grad_values = (
        lax.psum_scatter(
            grad_keys_part.astype(jnp.bfloat16), "band", scatter_dimension=1, tiled=True
        ).astype(jnp.float32),
        lax.psum_scatter(
            grad_values_part.astype(jnp.bfloat16), "band", scatter_dimension=1, tiled=True
        ).astype(jnp.float32),
    )
    grad_qkv = jnp.concatenate(
        [
            grad_queries.reshape(slot_count, local_rows, D),
            grad_keys.reshape(slot_count, local_rows, D),
            grad_values.reshape(slot_count, local_rows, D),
        ],
        axis=-1,
    ).astype(jnp.bfloat16)
    grad_qkv_weight = jnp.einsum(
        "std,ste->de", hidden, grad_qkv, preferred_element_type=jnp.float32
    )
    grad_hidden = jnp.einsum("ste,de->std", grad_qkv, qkv_full, preferred_element_type=jnp.float32)
    grad_tok_norm, grad_shift_attn, grad_scale_attn = attn_pull(grad_hidden)
    grad_tokens = grad_middle + grad_tok_norm
    grad_mod_tok = jnp.concatenate(
        [
            grad_shift_attn,
            grad_scale_attn,
            grad_gate_attn,
            grad_shift_mlp,
            grad_scale_mlp,
            grad_gate_mlp,
        ],
        axis=-1,
    )
    image_onehot = (image_id[..., None] == jnp.arange(4)).astype(jnp.float32)
    grad_modulation = jnp.einsum("spi,spe->sie", image_onehot, grad_mod_tok, precision=highest)
    grad_mask_part = jnp.sum(unfilled[..., None] * grad_tokens, axis=(0, 1))
    grad_kept_all = jnp.einsum(
        "spj,spd->sjd", select.astype(jnp.float32), grad_tokens, precision=highest
    )
    kept_grad = lax.psum_scatter(
        grad_kept_all.astype(jnp.bfloat16), "band", scatter_dimension=1, tiled=True
    ).astype(jnp.float32)
    grad_ada = jnp.einsum(
        "sid,sie->de", cond_low.astype(jnp.float32), grad_modulation, precision=highest
    )
    row_grads = (
        lax.psum_scatter(
            grad_qkv_weight.astype(jnp.bfloat16), "band", scatter_dimension=0, tiled=True
        ).astype(jnp.float32),
        lax.psum_scatter(
            grad_proj.astype(jnp.bfloat16), "band", scatter_dimension=0, tiled=True
        ).astype(jnp.float32),
        lax.psum_scatter(
            grad_fc1.astype(jnp.bfloat16), "band", scatter_dimension=0, tiled=True
        ).astype(jnp.float32),
        lax.psum_scatter(
            grad_fc2.astype(jnp.bfloat16), "band", scatter_dimension=0, tiled=True
        ).astype(jnp.float32),
        lax.psum_scatter(
            grad_ada.astype(jnp.bfloat16), "band", scatter_dimension=0, tiled=True
        ).astype(jnp.float32),
    )
    red_qkv, red_proj, red_fc1, red_fc2, red_ada = (
        lax.psum_scatter(
            row_grads[0].astype(jnp.bfloat16), "dp", scatter_dimension=1, tiled=True
        ).astype(jnp.float32),
        lax.psum_scatter(
            row_grads[1].astype(jnp.bfloat16), "dp", scatter_dimension=1, tiled=True
        ).astype(jnp.float32),
        lax.psum_scatter(
            row_grads[2].astype(jnp.bfloat16), "dp", scatter_dimension=1, tiled=True
        ).astype(jnp.float32),
        lax.psum_scatter(
            row_grads[3].astype(jnp.bfloat16), "dp", scatter_dimension=1, tiled=True
        ).astype(jnp.float32),
        lax.psum_scatter(
            row_grads[4].astype(jnp.bfloat16), "dp", scatter_dimension=1, tiled=True
        ).astype(jnp.float32),
    )
    grad_mask = lax.psum(grad_mask_part, ("dp", "band"))
    reduced = (red_qkv, red_proj, red_fc1, red_fc2, red_ada)
    local_squares = sum((jnp.sum(grad * grad) for grad in reduced))
    total_squares = lax.psum(local_squares, ("dp", "band")) + jnp.sum(grad_mask * grad_mask)
    norm_value = jnp.sqrt(total_squares)
    factor = clip_level / jnp.maximum(norm_value, clip_level)
    mask_new = adamw(mask_token, mask_first, mask_second, grad_mask * factor)
    qkv_new = adamw(w_qkv, first_qkv, second_qkv, red_qkv * factor)
    proj_new = adamw(w_proj, first_proj, second_proj, red_proj * factor)
    fc1_new = adamw(w_fc1, first_fc1, second_fc1, red_fc1 * factor)
    fc2_new = adamw(w_fc2, first_fc2, second_fc2, red_fc2 * factor)
    ada_new = adamw(w_ada, first_ada, second_ada, red_ada * factor)
    return (
        block_out,
        kept_grad,
        norm_value,
        mask_new[0],
        qkv_new[0],
        proj_new[0],
        fc1_new[0],
        fc2_new[0],
        ada_new[0],
        mask_new[1],
        qkv_new[1],
        proj_new[1],
        fc1_new[1],
        fc2_new[1],
        ada_new[1],
        mask_new[2],
        qkv_new[2],
        proj_new[2],
        fc1_new[2],
        fc2_new[2],
        ada_new[2],
    )


MASKED = -1e30
SCORE_SCALE = HEAD_DIM ** (-0.5)
LOG2E = math.log2(math.e)
VMEM_LIMIT = 63 * 1024 * 1024


def dot_nn(left, right):
    return lax.dot_general(
        left, right, (((1,), (0,)), ((), ())), preferred_element_type=jnp.float32
    )


def dot_nt(left, right):
    return lax.dot_general(
        left, right, (((1,), (1,)), ((), ())), preferred_element_type=jnp.float32
    )


def masked_scores(keys, queries, block, other):
    raw = dot_nn(keys, queries)
    parts = [
        raw[r * REGION : (r + 1) * REGION] + (0.0 if r == block else other)
        for r in range(keys.shape[0] // REGION)
    ]
    return jnp.concatenate(parts, axis=0)


def attn_head(other, queries, keys_t, values_t, out_ref, rows, lse_ref):
    keys = jnp.transpose(keys_t)
    for block in range(keys.shape[0] // REGION):
        cols = slice(block * REGION, (block + 1) * REGION)
        scores = masked_scores(keys, queries[:, cols], block, other)
        peak = jnp.max(scores, axis=0, keepdims=True)
        weights = jnp.exp2((scores - peak) * (SCORE_SCALE * LOG2E))
        total = jnp.sum(weights, axis=0, keepdims=True)
        mixed = dot_nn(values_t, weights.astype(jnp.bfloat16))
        out_ref[rows, cols] = (mixed / total).astype(jnp.bfloat16)
        lse_ref[:, cols] = peak * (SCORE_SCALE * LOG2E) + jnp.log2(total)


def attn_head_back(other, queries, keys_t, values_t, out, grad, lse_ref, grads_ref, rows):
    tokens = queries.shape[1]
    keys = jnp.transpose(keys_t)
    values = jnp.transpose(values_t)
    grad_keys = jnp.zeros((HEAD_DIM, tokens), jnp.float32)
    grad_values = jnp.zeros((HEAD_DIM, tokens), jnp.float32)
    dots = jnp.sum(out.astype(jnp.float32) * grad.astype(jnp.float32), axis=0, keepdims=True)
    for block in range(tokens // REGION):
        cols = slice(block * REGION, (block + 1) * REGION)
        scores = masked_scores(keys, queries[:, cols], block, other)
        weights = jnp.exp2(scores * (SCORE_SCALE * LOG2E) - lse_ref[:, cols])
        grad_weights = dot_nn(values, grad[:, cols])
        grad_scores = (weights * (grad_weights - dots[:, cols])).astype(jnp.bfloat16)
        grad_values += dot_nt(grad[:, cols], weights.astype(jnp.bfloat16))
        grad_keys += dot_nt(queries[:, cols], grad_scores)
        grads_ref[0, rows, cols] = (dot_nn(keys_t, grad_scores) * SCORE_SCALE).astype(jnp.bfloat16)
    grads_ref[1, rows] = (grad_keys * SCORE_SCALE).astype(jnp.bfloat16)
    grads_ref[2, rows] = grad_values.astype(jnp.bfloat16)


GELU_A = math.sqrt(2.0 / math.pi)
GELU_B = 0.044715


def mlp_tile(h_ref, ht_ref, g_ref, gt_ref, up_ref, down_ref, out_ref, grad_ref, gup_ref, gdown_ref):
    up = up_ref[...]
    down = down_ref[...]
    upward = dot_nn(h_ref[...], up)
    square = upward * upward
    curve = jnp.tanh(GELU_A * upward * (1.0 + GELU_B * square))
    half = 0.5 * (1.0 + curve)
    active = (upward * half).astype(jnp.bfloat16)
    slope = half + 0.5 * upward * (1.0 - curve * curve) * GELU_A * (
        1.0 + 3.0 * GELU_B * square
    )
    grad_upward = (dot_nn(g_ref[...], down) * slope).astype(jnp.bfloat16)
    out_ref[...] += dot_nt(active, down)
    grad_ref[...] += dot_nt(grad_upward, up)
    gup_ref[...] = dot_nn(ht_ref[...], grad_upward).astype(jnp.bfloat16)
    gdown_ref[...] = dot_nn(gt_ref[...], active).astype(jnp.bfloat16)


BLOCK_ROWS = 144
BLOCK_COLS = 1152
def flip(index):
    return index + 1 - 2 * (index % 2)


def along_z(z, step):
    return (z, flip(z), (z + 2) % 4, 3 - z)[step]


class Place:
    def __init__(self):
        dp = lax.axis_index("dp")
        band = lax.axis_index("band")
        self.z, self.y, self.x, self.core = dp // 2, dp % 2, band // 2, band % 2

    def chip(self, i, a, b):
        return (along_z(self.z, i), flip(self.y) if a else self.y, flip(self.x) if b else self.x)

    def device(self, i=0, a=0, b=0, core=0):
        z, y, x = self.chip(i, a, b)
        return (z * 2 + y, x * 2 + (flip(self.core) if core else self.core))

    def partners(self, band=False, dp=False):
        found = [
            self.device(core=1),
            self.device(b=1),
            self.device(a=1),
            self.device(i=1),
            self.device(i=2),
            self.device(i=3),
        ]
        if band:
            found.append(self.device(b=1, core=1))
        if dp:
            found += [self.device(i=i, a=1) for i in (1, 2, 3)]
        return found

    def dp(self, i=0, a=0):
        z, y, _ = self.chip(i, a, 0)
        return z * 2 + y

    def band(self, b=0, core=0):
        x = flip(self.x) if b else self.x
        return x * 2 + (flip(self.core) if core else self.core)

    def block(self, by_rows, i, a, b, core=0):
        z, y, x = self.chip(i, a, b)
        c = flip(self.core) if core else self.core
        if by_rows:
            row, col = z * 2 + y, x * 2 + c
        else:
            row, col = (x * 2 + c) * 2 + y, z
        return (
            pl.ds(pl.multiple_of(row * BLOCK_ROWS, 16), BLOCK_ROWS),
            pl.ds(pl.multiple_of(col * BLOCK_COLS, 128), BLOCK_COLS),
        )


def greet(place, band=False, dp=False):
    barrier = pltpu.get_barrier_semaphore()
    partners = place.partners(band, dp)
    for partner in partners:
        pl.semaphore_signal(
            barrier, inc=1, device_id=partner, device_id_type=pl.DeviceIdType.MESH
        )
    pl.semaphore_wait(barrier, len(partners))


def send(source, target, send_sem, recv_sem, device):
    return pltpu.make_async_remote_copy(
        src_ref=source,
        dst_ref=target,
        send_sem=send_sem,
        recv_sem=recv_sem,
        device_id=device,
        device_id_type=pl.DeviceIdType.MESH,
    )


CHIPS = [(i, a, b) for i in range(4) for a in range(2) for b in range(2)]


def slot(piece):
    return piece[0] * 4 + piece[1] * 2 + piece[2]


def parent(piece, via_x, sides_by_z):
    i, a, b = piece
    if a and b:
        return (0, 0, 1) if i in via_x else (0, 1, 0)
    if (a or b) and not (i == 1 and sides_by_z):
        return (0, a, b)
    return (i, 0, 0)


def moved(piece, step):
    return (piece[0] ^ step[0], piece[1] ^ step[1], piece[2] ^ step[2])


def children(piece, via_x, sides_by_z):
    return [
        (other, parent(other, via_x, sides_by_z))
        for other in CHIPS
        if any(other) and moved(other, parent(other, via_x, sides_by_z)) == piece
    ]


GATHER_SENDS = 31


def gather_actions(place, plans, own_refs, full_refs, local_sems, send_sems, link_sems, core_sems):
    weights = range(len(own_refs))
    counts = [0] * len(own_refs)

    def ship(w, source, piece, name, sems, device):
        target = full_refs[w].at[place.block(plans[w][0], *piece)]
        send(source, target, send_sems.at[w, counts[w]], sems.at[w, slot(name)], device).start()
        counts[w] += 1

    def pass_on(w, source, piece):
        for child, step in children(piece, plans[w][1], False):
            if step[0] < 2:
                ship(w, source, piece, child, link_sems, place.device(*step))
        ship(w, source, piece, piece, core_sems, place.device(core=1))

    def arrive(w, piece, core=0):
        target = full_refs[w].at[place.block(plans[w][0], *piece, core)]
        sems = core_sems if core else link_sems
        send(
            target, target, send_sems.at[w, 0], sems.at[w, slot(piece)], place.device(core=1)
        ).wait_recv()
        return target

    def keep(w):
        return pltpu.make_async_copy(
            own_refs[w], full_refs[w].at[place.block(plans[w][0], 0, 0, 0)], local_sems.at[w]
        )

    def begin():
        for w in weights:
            keep(w).start()
            pass_on(w, own_refs[w], (0, 0, 0))

    def relay(w, *piece):
        pass_on(w, arrive(w, piece), piece)

    def late(w, i):
        ship(w, own_refs[w], (0, 0, 0), (i, 0, 0), link_sems, place.device(i))

    def finish():
        for w in weights:
            for piece in CHIPS:
                arrive(w, piece, core=1)
            keep(w).wait()
            for n in range(counts[w]):
                send(
                    own_refs[w], own_refs[w], send_sems.at[w, n], link_sems.at[w, 0],
                    place.device(core=1),
                ).wait_send()

    return begin, relay, late, finish


def gather_scratch(count):
    return [
        pltpu.SemaphoreType.DMA((count,)),
        pltpu.SemaphoreType.DMA((count, GATHER_SENDS)),
        pltpu.SemaphoreType.DMA((count, 16)),
        pltpu.SemaphoreType.DMA((count, 16)),
    ]


BAND_PEERS = ((0, 1), (1, 0), (1, 1))
DP_PEERS = ((1, 0), (0, 1), (3, 0), (1, 1), (2, 0), (3, 1), (2, 1))


def swap_band(place, source, target, local_sem, send_sems, recv_sems):
    def copies():
        found = []
        for n, (b, core) in enumerate(BAND_PEERS):
            found.append(
                send(
                    source.at[place.band(b, core)],
                    target.at[place.band()],
                    send_sems.at[n],
                    recv_sems.at[n],
                    place.device(b=b, core=core),
                )
            )
        local = pltpu.make_async_copy(
            source.at[place.band()], target.at[place.band()], local_sem.at[0]
        )
        return found, local

    def start():
        found, local = copies()
        for copy in found:
            copy.start()
        local.start()

    def wait():
        found, local = copies()
        for copy in found:
            copy.wait()
        local.wait()

    return start, wait


def swap_scratch():
    return [
        pltpu.SemaphoreType.DMA((1,)),
        pltpu.SemaphoreType.DMA((3,)),
        pltpu.SemaphoreType.DMA((3,)),
    ]


def head_kernel(
    block_ref,
    cond_ref,
    ada_ref,
    kept_ref,
    index_ref,
    full_ref,
    mod_ref,
    conds_ref,
    kept_out,
    index_out,
    part_ref,
    got_ref,
    sums_ref,
    cond_sends,
    cond_recvs,
    part_sends,
    part_recvs,
    mod_sends,
    mod_recvs,
    *rest,
):
    place = Place()
    slots, _, _, cols = part_ref.shape
    images = part_ref.shape[2]
    plans = ((False, (0,)),)
    begin, relay, late, finish = gather_actions(
        place, plans, [block_ref], [full_ref], *rest[:4]
    )

    def relays(*pieces):
        for piece in pieces:
            relay(0, *piece)

    kept_start, kept_wait = swap_band(place, kept_ref, kept_out, *rest[4:7])
    index_start, index_wait = swap_band(place, index_ref, index_out, *rest[7:10])

    def to_dp(n, source, target, sends, recvs):
        i, a = DP_PEERS[n]
        return send(source, target, sends.at[n], recvs.at[n], place.device(i=i, a=a))

    greet(place, band=True, dp=True)
    own = place.dp()
    cond_copies = [
        to_dp(n, cond_ref, conds_ref.at[own], cond_sends, cond_recvs) for n in range(7)
    ]
    for copy in cond_copies:
        copy.start()
    begin()
    index_start()
    conds_ref[own] = cond_ref[...]
    late(0, 3)
    relays((1, 0, 0))
    for copy in cond_copies:
        copy.wait()
    for s in range(slots):
        rows = conds_ref[:, s].reshape(-1, cond_ref.shape[-1]).astype(jnp.bfloat16)
        product = dot_nn(rows, ada_ref[...])
        part_ref[s] = product.reshape(-1, cond_ref.shape[1], cols)[:, :images]
    relays((0, 1, 0))
    late(0, 2)
    relays((1, 0, 1), (1, 1, 0), (3, 0, 0))
    part_copies = [
        send(
            part_ref.at[place.band(b, core)],
            got_ref.at[n],
            part_sends.at[n],
            part_recvs.at[n],
            place.device(b=b, core=core),
        )
        for n, (b, core) in enumerate(BAND_PEERS)
    ]
    for copy in part_copies:
        copy.start()
    relays((3, 0, 1), (2, 0, 0), (0, 0, 1), (0, 1, 1), (3, 1, 0))
    kept_start()
    for copy in part_copies:
        copy.wait()
    sums_ref[...] = part_ref[place.band()] + got_ref[0] + got_ref[1] + got_ref[2]
    relays((1, 1, 1))
    mod_copies = [
        to_dp(n, sums_ref.at[place.dp(*DP_PEERS[n])], mod_ref.at[own], mod_sends, mod_recvs)
        for n in range(7)
    ]
    for copy in mod_copies:
        copy.start()
    mod_ref[own] = sums_ref[own]
    relays((2, 0, 1), (3, 1, 1), (2, 1, 0), (2, 1, 1))
    finish()
    for copy in mod_copies:
        copy.wait()
    index_wait()
    kept_wait()


def head(block, cond, ada, kept, index, collective_id):
    slots, images_pad, width = cond.shape
    images = 4
    cols = ada.shape[1]
    groups = lax.axis_size("dp")
    vmem = pl.BlockSpec(memory_space=pltpu.VMEM)
    hbm = pl.BlockSpec(memory_space=pl.ANY)
    f32 = jnp.float32
    return pl.pallas_call(
        head_kernel,
        in_specs=[vmem, vmem, vmem, hbm, hbm],
        out_specs=[hbm, vmem, vmem, hbm, hbm],
        out_shape=[
            jax.ShapeDtypeStruct((8 * BLOCK_ROWS, 4 * BLOCK_COLS), jnp.bfloat16),
            jax.ShapeDtypeStruct((groups, images, cols), f32),
            jax.ShapeDtypeStruct((groups,) + cond.shape, f32),
            jax.ShapeDtypeStruct(kept.shape, kept.dtype),
            jax.ShapeDtypeStruct(index.shape, index.dtype),
        ],
        scratch_shapes=[
            pltpu.VMEM((slots, groups, images, cols), f32),
            pltpu.VMEM((3, groups, images, cols), f32),
            pltpu.VMEM((groups, images, cols), f32),
            pltpu.SemaphoreType.DMA((7,)),
            pltpu.SemaphoreType.DMA((7,)),
            pltpu.SemaphoreType.DMA((3,)),
            pltpu.SemaphoreType.DMA((3,)),
            pltpu.SemaphoreType.DMA((7,)),
            pltpu.SemaphoreType.DMA((7,)),
        ]
        + gather_scratch(1)
        + swap_scratch()
        + swap_scratch(),
        compiler_params=pltpu.CompilerParams(
            collective_id=collective_id, has_side_effects=True, vmem_limit_bytes=VMEM_LIMIT
        ),
        name="head",
    )(block, cond, ada, kept, index)


STAGES = 4


def scatter_actions(
    place,
    plans,
    order,
    grad_refs,
    out_refs,
    held_refs,
    over_refs,
    stage,
    stage_sems,
    send_sems,
    held_sems,
    over_sems,
):
    weights = range(len(grad_refs))
    counts = [0] * len(grad_refs)

    def ship(w, source, target, recv_sem, device):
        send(source, target, send_sems.at[w, counts[w]], recv_sem, device).start()
        counts[w] += 1

    def landed(target, recv_sem):
        send(target, target, send_sems.at[0, 0], recv_sem, place.device(core=1)).wait_recv()

    def begin():
        for ahead in range(STAGES - 1):
            load(ahead).start()
        for w, *piece in order:
            source = grad_refs[w].at[place.block(plans[w][0], *piece, 1)]
            s = slot(piece)
            ship(w, source, held_refs.at[w, s], held_sems.at[w, s], place.device(core=1))

    def load(n):
        w, *piece = order[n]
        return pltpu.make_async_copy(
            grad_refs[w].at[place.block(plans[w][0], *piece)],
            stage.at[n % STAGES],
            stage_sems.at[n % STAGES],
        )

    def up(w, piece):
        step = parent(piece, plans[w][1], True)
        s = slot(piece)
        ship(
            w, held_refs.at[w, s], over_refs.at[w, s - 1], over_sems.at[w, s - 1], place.device(*step)
        )

    def fold(n):
        if n + STAGES - 1 < len(order):
            load(n + STAGES - 1).start()
        w, *piece = order[n]
        s = slot(piece)
        load(n).wait()
        landed(held_refs.at[w, s], held_sems.at[w, s])
        held = held_refs.at[w, s]
        held[...] = held[...] + stage[n % STAGES]
        if not children(tuple(piece), plans[w][1], True):
            up(w, piece)

    def combine(w, *piece):
        held = held_refs.at[w, slot(piece)]
        total = held[...].astype(jnp.float32)
        for child, _ in children(piece, plans[w][1], True):
            k = slot(child) - 1
            landed(over_refs.at[w, k], over_sems.at[w, k])
            total = total + over_refs[w, k].astype(jnp.float32)
        if any(piece):
            held[...] = total.astype(jnp.bfloat16)
            up(w, piece)
        else:
            out_refs[w][...] = total.astype(jnp.bfloat16)

    def finish():
        for w in weights:
            block = held_refs.at[w, 0]
            for n in range(counts[w]):
                send(
                    block, block, send_sems.at[w, n], held_sems.at[w, 0], place.device(core=1)
                ).wait_send()

    return begin, fold, combine, finish


def scatter_scratch(count):
    blocks = lambda n: pltpu.VMEM((count, n, BLOCK_ROWS, BLOCK_COLS), jnp.bfloat16)
    return [
        blocks(16),
        blocks(15),
        pltpu.VMEM((STAGES, BLOCK_ROWS, BLOCK_COLS), jnp.bfloat16),
        pltpu.SemaphoreType.DMA((STAGES,)),
        pltpu.SemaphoreType.DMA((count, 31)),
        pltpu.SemaphoreType.DMA((count, 16)),
        pltpu.SemaphoreType.DMA((count, 15)),
    ]


def to_dp_peer(place, n, source, target, sends, recvs):
    i, a = DP_PEERS[n]
    return send(source, target, sends.at[n], recvs.at[n], place.device(i=i, a=a))


def to_band_peer(place, n, source, target, sends, recvs):
    b, core = BAND_PEERS[n]
    return send(source, target, sends.at[n], recvs.at[n], place.device(b=b, core=core))


def square_sum(values):
    wide = values.astype(jnp.float32)
    return jnp.sum(jnp.sum(wide * wide, axis=0, keepdims=True), axis=1, keepdims=True)


def tail_kernel(
    grad_ref,
    kind_ref,
    fc1_ref,
    fc2_ref,
    index_ref,
    scales_ref,
    sums_ref,
    conds_ref,
    tokens_hbm,
    middle_hbm,
    hidden_hbm,
    own_ref,
    other_ref,
    fc1_other_ref,
    ada_ref,
    mask_out,
    square_out,
    kept_out,
    tokens,
    grad_middle,
    grad_hidden,
    kept_total,
    kept,
    six,
    mask_own,
    mods_own,
    mods_dp,
    mods_all,
    mask_band,
    mask_sum,
    mask_dp,
    square_own,
    square_band,
    square_sum_ref,
    square_dp,
    load_sems,
    y_sends,
    y_recvs,
    dp_sends,
    dp_recvs,
    band_sends,
    band_recvs,
    *rest,
):
    place = Place()
    plans = ((False, (2,)),)
    order = [
        (2, 1, 1), (3, 1, 1), (3, 1, 0), (1, 0, 0), (1, 1, 0), (2, 0, 1), (3, 0, 1), (1, 1, 1),
        (3, 0, 0), (2, 0, 0), (1, 0, 1), (2, 1, 0), (0, 1, 0), (0, 1, 1), (0, 0, 0), (0, 0, 1),
    ]
    begin, fold, combine, finish = scatter_actions(
        place, plans, [(0,) + piece for piece in order], [grad_ref], [own_ref], *rest[:7]
    )

    left = list(range(len(order)))

    def folds(count):
        for _ in range(count):
            fold(left.pop(0))

    kept_start, kept_wait = swap_band(place, kept, kept_out, *rest[7:10])
    across = lambda n, source, target: send(
        source, target, y_sends.at[n], y_recvs.at[n], place.device(a=1)
    )
    to_dp = lambda k, n, source, target: to_dp_peer(
        place, n, source, target, dp_sends.at[k], dp_recvs.at[k]
    )
    to_band = lambda k, n, source, target: to_band_peer(
        place, n, source, target, band_sends.at[k], band_recvs.at[k]
    )
    greet(place, band=True, dp=True)
    own = place.dp()
    loads = [
        pltpu.make_async_copy(source, target, load_sems.at[n])
        for n, (source, target) in enumerate(
            [(tokens_hbm, tokens), (middle_hbm, grad_middle), (hidden_hbm, grad_hidden)]
        )
    ]
    for copy in loads:
        copy.start()
    begin()
    fc1_copy = across(0, fc1_ref, fc1_other_ref)
    fc1_copy.start()
    folds(6)
    for copy in loads:
        copy.wait()

    count = tokens.shape[0]
    regions = count // REGION
    for region in range(regions):
        if region == 2:
            folds(1)
        if region == 3:
            combine(0, 3, 0, 1)
        spot = slice(region * REGION, (region + 1) * REGION)
        grad = grad_hidden[spot]
        normal, root = norm_parts(tokens[spot])
        scale = scales_ref[SCALE_ATTN, region : region + 1]
        grad_tokens = grad_middle[spot] + norm_back(grad, normal, root, scale)
        six[0, region : region + 1] = column_sum(grad)
        six[1, region : region + 1] = column_sum(grad * normal)
        for k in range(4):
            six[2 + k, region : region + 1] = sums_ref[region, k : k + 1]
        select = chosen_rows(index_ref, region)
        unfilled = 1.0 - jnp.sum(select, axis=1, keepdims=True)
        masked = column_sum(unfilled * grad_tokens)
        select = jnp.transpose(select).astype(jnp.bfloat16)
        added = dot_nn(select, grad_tokens.astype(jnp.bfloat16))
        if region == 0:
            mask_own[...] = jnp.broadcast_to(masked, mask_own.shape)
            kept_total[...] = added
        else:
            mask_own[...] += jnp.broadcast_to(masked, mask_own.shape)
            kept_total[...] += added
    kept[...] = kept_total[...].astype(jnp.bfloat16).reshape(kept.shape)
    images = six.shape[1]
    first = lax.broadcasted_iota(jnp.int32, six.shape[1:], 0) == 0
    flat = []
    for k in range(6):
        part = six[k]
        flat.append(
            jnp.where(kind_ref[0] == 1, part, jnp.where(first, column_sum(part), 0.0))
        )
    flat = jnp.concatenate(flat, axis=1)
    groups, padded, cols = mods_own.shape
    for d in range(groups):
        mods_own[d, :images] = flat[:, d * cols : (d + 1) * cols]
        mods_own[d, images:] = jnp.zeros((padded - images, cols), jnp.float32)

    early = [to_dp(0, n, mods_own.at[place.dp(*DP_PEERS[n])], mods_dp.at[own]) for n in range(7)]
    early += [to_band(0, n, mask_own, mask_band.at[n]) for n in range(3)]
    for copy in early:
        copy.start()
    mods_dp[own] = mods_own[own]
    folds(2)
    kept_start()
    combine(0, 3, 0, 0)
    for copy in early:
        copy.wait()
    folds(4)
    combine(0, 2, 1, 0)
    folds(1)
    mask_sum[...] = mask_own[...] + mask_band[0] + mask_band[1] + mask_band[2]
    second = [to_band(1, n, mods_dp, mods_all.at[place.band()]) for n in range(3)]
    second += [to_dp(1, n, mask_sum, mask_dp.at[n]) for n in range(7)]
    for copy in second:
        copy.start()
    mods_all[place.band()] = mods_dp[...]
    combine(0, 0, 1, 0)
    combine(0, 1, 0, 1)
    combine(0, 2, 0, 0)
    folds(2)
    fc1_copy.wait()
    combine(0, 0, 0, 1)
    for copy in second:
        copy.wait()
    total = mask_sum[...]
    for n in range(7):
        total = total + mask_dp[n]
    mask_out[...] = total
    width = ada_ref.shape[0]
    ada = jnp.zeros(ada_ref.shape, jnp.float32)
    for s in range(conds_ref.shape[1]):
        ada += lax.dot_general(
            conds_ref[:, s].reshape(-1, width),
            mods_all[s].reshape(-1, ada_ref.shape[1]),
            (((0,), (0,)), ((), ())),
            precision=lax.Precision.HIGHEST,
            preferred_element_type=jnp.float32,
        )
    ada_ref[...] = ada
    squares = square_sum(ada) + square_sum(fc1_ref[...]) + square_sum(fc2_ref[...])
    combine(0, 0, 0, 0)
    last = across(1, own_ref, other_ref)
    last.start()
    squares = squares + square_sum(own_ref[...])
    square_own[...] = jnp.broadcast_to(squares, square_own.shape)
    third = [to_band(2, n, square_own, square_band.at[n]) for n in range(3)]
    for copy in third:
        copy.start()
    for copy in third:
        copy.wait()
    square_sum_ref[...] = square_own[...] + square_band[0] + square_band[1] + square_band[2]
    fourth = [to_dp(2, n, square_sum_ref, square_dp.at[n]) for n in range(7)]
    for copy in fourth:
        copy.start()
    for copy in fourth:
        copy.wait()
    total = square_sum_ref[...]
    for n in range(7):
        total = total + square_dp[n]
    square_out[...] = total
    last.wait()
    kept_wait()
    finish()


def tail(
    grad, kind, fc1, fc2, index, mod, sums, conds, tokens, grad_middle, grad_hidden, bands, collective_id
):
    f32, bf16 = jnp.float32, jnp.bfloat16
    vmem = pl.BlockSpec(memory_space=pltpu.VMEM)
    hbm = pl.BlockSpec(memory_space=pl.ANY)
    block = jax.ShapeDtypeStruct((BLOCK_ROWS, BLOCK_COLS), bf16)
    squares = (8, 128)
    mask = (8, D)
    count, width = tokens.shape
    places = index.shape[1]
    groups, _, padded, rows_ada = conds.shape
    cols_ada = 6 * D // groups
    mods = (groups, padded, cols_ada)
    kept = (bands, places // bands, width)
    dma = pltpu.SemaphoreType.DMA
    return pl.pallas_call(
        tail_kernel,
        in_specs=[hbm, pl.BlockSpec(memory_space=pltpu.SMEM)] + [vmem] * 6 + [hbm] * 3,
        out_specs=[vmem] * 6 + [hbm],
        out_shape=[
            block,
            block,
            block,
            jax.ShapeDtypeStruct((rows_ada, cols_ada), f32),
            jax.ShapeDtypeStruct(mask, f32),
            jax.ShapeDtypeStruct(squares, f32),
            jax.ShapeDtypeStruct(kept, bf16),
        ],
        scratch_shapes=[
            pltpu.VMEM((count, width), f32),
            pltpu.VMEM((count, width), f32),
            pltpu.VMEM((count, width), f32),
            pltpu.VMEM((places, width), f32),
            pltpu.VMEM(kept, bf16),
            pltpu.VMEM(mod.shape, f32),
            pltpu.VMEM(mask, f32),
            pltpu.VMEM(mods, f32),
            pltpu.VMEM(mods, f32),
            pltpu.VMEM((bands,) + mods, f32),
            pltpu.VMEM((3,) + mask, f32),
            pltpu.VMEM(mask, f32),
            pltpu.VMEM((7,) + mask, f32),
            pltpu.VMEM(squares, f32),
            pltpu.VMEM((3,) + squares, f32),
            pltpu.VMEM(squares, f32),
            pltpu.VMEM((7,) + squares, f32),
            dma((3,)),
            dma((2,)),
            dma((2,)),
            dma((3, 7)),
            dma((3, 7)),
            dma((3, 3)),
            dma((3, 3)),
        ]
        + scatter_scratch(1)
        + swap_scratch(),
        compiler_params=pltpu.CompilerParams(
            collective_id=collective_id, has_side_effects=True, vmem_limit_bytes=VMEM_LIMIT
        ),
        name="tail",
    )(
        grad, kind, fc1, fc2, index, mod, sums, conds,
        tokens, grad_middle, grad_hidden,
    )


def finish_kernel(
    odd_ref,
    square_ref,
    mask_grad_ref,
    kept_ref,
    block_ref,
    own_ref,
    other_ref,
    fc1_ref,
    fc1_other_ref,
    fc2_ref,
    ada_ref,
    *refs,
):
    weights, outs = refs[:18], refs[18:36]
    norm_ref, kept_out, block_out = refs[36:]
    odd = odd_ref[0] == 1
    mask_grad = mask_grad_ref[0:1]
    norm = jnp.sqrt(square_ref[0:1, 0:1] + square_sum(mask_grad))
    factor = clip_level / jnp.maximum(norm, clip_level)
    norm_ref[...] = norm
    qkv = weights[0].shape[1]
    proj = weights[1].shape[0]
    fc1 = weights[2].shape[1]

    def pair(own, other):
        own, other = own[...].astype(jnp.float32), other[...].astype(jnp.float32)
        return jnp.where(odd, other, own), jnp.where(odd, own, other)

    def half(block, first, cols):
        return jnp.where(
            odd, block[:, first + cols : first + 2 * cols], block[:, first : first + cols]
        )

    def step(n, rows, grad):
        new = adamw(weights[n][rows], weights[6 + n][rows], weights[12 + n][rows], grad * factor)
        for k in range(3):
            outs[6 * k + n][rows] = new[k]

    projs = []
    for k, block in enumerate(pair(own_ref, other_ref)):
        rows = slice(k * BLOCK_ROWS, (k + 1) * BLOCK_ROWS)
        step(0, rows, half(block, 0, qkv))
        projs.append(half(block, 2 * qkv, proj))
    step(1, slice(None), jnp.transpose(jnp.concatenate(projs, axis=0)))
    for k, block in enumerate(pair(fc1_ref, fc1_other_ref)):
        rows = slice(k * BLOCK_ROWS, (k + 1) * BLOCK_ROWS)
        step(2, rows, half(block, 0, fc1))
    step(3, slice(None), fc2_ref[...].astype(jnp.float32))
    step(4, slice(None), ada_ref[...])
    step(5, slice(None), mask_grad)
    kept_out[...] = kept_ref[...].astype(jnp.float32)
    block_out[...] = block_ref[...]


def finish_all(odd, squares, mask_grad, kept, block, sums, weights):
    turn = lambda values: [v.T if n % 6 in (1, 3) else v for n, v in enumerate(values)]
    weights = turn(weights)
    vmem = pl.BlockSpec(memory_space=pltpu.VMEM)
    shape = jax.ShapeDtypeStruct
    found = pl.pallas_call(
        finish_kernel,
        in_specs=[pl.BlockSpec(memory_space=pltpu.SMEM)] + [vmem] * (4 + 6 + 18),
        out_specs=[vmem] * 21,
        out_shape=[shape(w.shape, w.dtype) for w in weights]
        + [
            shape((1, 1), jnp.float32),
            shape(kept.shape, jnp.float32),
            shape(block.shape, block.dtype),
        ],
        compiler_params=pltpu.CompilerParams(vmem_limit_bytes=VMEM_LIMIT),
        name="finish_all",
    )(odd, squares, mask_grad, kept, block, *sums, *weights)
    return turn(found[:18]), *found[18:]


def run(actions):
    for action in actions:
        action()


def run_slot(step, groups, first, count, stride=1):
    for k in range(count):
        group = groups[first + k * stride]

        @pl.when(step == k)
        def _():
            run(group)


def fixed(*shape):
    return pl.BlockSpec(shape, lambda *_: (0,) * len(shape))


def once(*shape):
    return pl.BlockSpec(shape, lambda *_: (0,) * len(shape), pipeline_mode=pl.Buffered(1))


def chosen_rows(index_ref, region):
    rows = lax.broadcasted_iota(jnp.int32, (REGION, index_ref.shape[1]), 0) + region * REGION
    return (rows == index_ref[...]).astype(jnp.float32)


GATHER_PLANS = ((False, (0,)), (True, (3,)))
SCATTER_PLANS = ((False, (0,)), (True, (0, 3)))
FORWARD_STEPS = [
    (0, 1, 3), (5, 0, 1, 0, 0), (5, 0, 3), (6, 0, 0, 1, 0), (6, 0, 0, 0, 1), (9, 1, 0, 0, 1),
    (12, 0, 1, 0, 1), (12, 0, 1, 1, 0), (12, 1, 1, 0, 0), (13, 0, 2), (14, 0, 3, 0, 0), (15,),
    (16, 1, 0, 1, 0), (16, 1, 3, 0, 0), (16, 0, 3, 0, 1), (17, 1, 2), (18, 0, 0, 1, 1),
    (21, 0, 1, 1, 1), (22, 0, 2, 0, 0), (22, 1, 1, 0, 1), (22, 1, 2, 0, 0), (26, 1, 1, 1, 0),
    (27, 0, 2, 1, 0), (27, 1, 3, 1, 0), (28, 1, 3, 0, 1), (29, 0, 2, 0, 1), (30, 1, 0, 1, 1),
    (30, 1, 1, 1, 1), (30, 1, 2, 0, 1), (31, 0, 3, 1, 0), (31, 0, 2, 1, 1), (32, 0, 3, 1, 1),
    (32, 1, 3, 1, 1), (32, 1, 2, 1, 0), (32, 1, 2, 1, 1),
]
BACKWARD_STEPS = [
    (0, 0, 0, 1, 1, 0), (0,), (0, 0, 0, 0, 0, 1), (0, 0, 0, 3, 1, 1), (0, 0, 0, 1, 1, 1),
    (0, 0, 0, 1, 0, 1), (1, 0, 1, 1, 0, 0), (1, 0, 1, 1, 1, 1), (1, 0, 1, 3, 1, 1),
    (2, 0, 1, 1, 1, 0), (2, 0, 0, 2, 0, 0), (2, 0, 0, 3, 0, 1), (3, 1, 0, 3, 0, 1),
    (3, 0, 0, 2, 1, 1), (3, 0, 1, 3, 0, 1), (4, 0, 1, 0, 1, 1), (4, 0, 0, 3, 0, 0),
    (6, 1, 0, 1, 0, 1), (6, 0, 0, 3, 1, 0), (6, 0, 1, 1, 0, 1), (6, 0, 1, 2, 1, 0),
    (7, 0, 1, 3, 1, 0), (7, 0, 1, 0, 0, 0), (7, 0, 0, 0, 0, 0), (10, 0, 0, 1, 0, 0),
    (10, 0, 1, 2, 0, 1), (10, 1, 0, 3, 0, 0), (10, 1, 1, 3, 1, 0), (11, 0, 1, 3, 0, 0),
    (11, 0, 1, 2, 1, 1), (11, 0, 1, 0, 1, 0), (11, 0, 0, 2, 0, 1), (12, 0, 0, 0, 1, 0),
    (13, 1, 0, 2, 0, 1), (13, 1, 1, 3, 0, 0), (14, 0, 0, 2, 1, 0), (14, 1, 1, 1, 0, 1),
    (15, 0, 0, 0, 1, 1), (17, 1, 0, 2, 0, 0), (17, 0, 1, 2, 0, 0), (17, 1, 1, 2, 0, 1),
    (17, 0, 1, 0, 0, 1), (18, 1, 0, 0, 1, 0), (19, 1, 0, 0, 0, 1), (19, 1, 1, 2, 0, 0),
    (19, 1, 1, 0, 0, 1), (20, 1, 1, 0, 1, 0), (21, 1, 0, 0, 0, 0), (23, 1, 1, 0, 0, 0),
]
SHIFT_ATTN, SCALE_ATTN, GATE_ATTN, SHIFT_MLP, SCALE_MLP, GATE_MLP = range(6)
GRANULE = 16
PAIR = 2 * HEAD_DIM
PAIRS = HEADS // 2


def embed_tokens(
    slots, kind_ref, kept_ref, index_ref, mask_ref, table_ref, mod_ref, tokens, hidden, hidden_t
):
    count = tokens.shape[0]
    small = kind_ref[0] == 1
    for region in range(count // REGION):
        run(slots[region])
        select = chosen_rows(index_ref, region)
        placed = dot_nn(select.astype(jnp.bfloat16), kept_ref[...])
        unfilled = 1.0 - jnp.sum(select, axis=1, keepdims=True)
        tokens[pl.ds(region * REGION, REGION)] = placed + unfilled * mask_ref[...]

    def add_place(g, carry):
        first = pl.multiple_of((g % 2) * GRANULE, GRANULE)
        wide = table_ref[0, pl.ds(g // 2, 1), :] + table_ref[1, pl.ds(first, GRANULE), :]
        narrow = table_ref[0, pl.ds(g % 16, 1), :] + table_ref[1, :GRANULE]
        place = jnp.where(small, narrow, wide)
        spot = pl.ds(pl.multiple_of(g * GRANULE, GRANULE), GRANULE)
        tokens[spot, :] = tokens[spot, :] + place
        return carry

    lax.fori_loop(0, count // GRANULE, add_place, 0)
    for region in range(count // REGION):
        run(slots[count // REGION + region])
        spot = slice(region * REGION, (region + 1) * REGION)
        normal, _ = norm_parts(tokens[spot])
        value = normal * (1.0 + mod_ref[SCALE_ATTN, region : region + 1])
        value = (value + mod_ref[SHIFT_ATTN, region : region + 1]).astype(jnp.bfloat16)
        hidden[spot] = value
        hidden_t[:, spot] = jnp.transpose(value)


def forward_kernel(
    kind_ref,
    kept_ref,
    index_ref,
    mask_ref,
    table_ref,
    mod_ref,
    weight_ref,
    fc1_ref,
    fc2_ref,
    swap_ref,
    qkv_out,
    attended_out,
    lse_out,
    branch_out,
    middle_out,
    hidden_out,
    hidden_t_out,
    gated_out,
    gated_t_out,
    tokens_hbm,
    normed_t_hbm,
    proj_hbm,
    grad_hbm,
    fc1_full,
    fc2_full,
    tokens,
    normed,
    normed_t,
    qkv,
    attended,
    proj,
    grad,
    out_sems,
    *sems,
):
    step = pl.program_id(0)
    rows = qkv_out.shape[0]
    groups = qkv.shape[0] // rows
    regions = tokens.shape[0] // REGION
    cols = D // groups
    place = Place()
    begin, relay, late, finish = gather_actions(
        place, GATHER_PLANS, [fc1_ref, fc2_ref], [fc1_full, fc2_full], *sems[:4]
    )
    swap_start, swap_wait = swap_band(place, swap_ref, grad, *sems[4:])
    first_qkv = 1 + 2 * regions
    first_head = first_qkv + groups
    first_region = first_head + HEADS
    slots = [[] for _ in range(first_region + regions)]
    slots[0] += [functools.partial(greet, place, band=True), begin]
    for when, *what in FORWARD_STEPS:
        action = {0: swap_start, 2: late, 4: relay}[len(what)]
        slots[when].append(functools.partial(action, *what))
    outward = [
        pltpu.make_async_copy(source, target, out_sems.at[n])
        for n, (source, target) in enumerate(
            [(tokens, tokens_hbm), (normed_t, normed_t_hbm), (proj, proj_hbm), (grad, grad_hbm)]
        )
    ]

    @pl.when(step == 0)
    def _():
        run(slots[0])
        embed_tokens(
            slots[1:first_qkv],
            kind_ref,
            kept_ref,
            index_ref,
            mask_ref,
            table_ref,
            mod_ref,
            tokens,
            normed,
            normed_t,
        )
        outward[0].start()
        outward[1].start()

    run_slot(step, slots, first_qkv, groups)

    @pl.when(step < groups)
    def _():
        span = -(-rows // 128) * 128
        wide = dot_nn(normed[...], weight_ref[:, :span]).astype(jnp.bfloat16)
        part = jnp.transpose(wide)[:rows]
        qkv_out[...] = part
        qkv[pl.ds(pl.multiple_of(step * rows, 16), rows), :] = part
        for g in range(groups):

            @pl.when(step == g)
            def _():
                proj[:, g * cols : (g + 1) * cols] = weight_ref[:, rows:]

    pair = step - groups

    @pl.when((pair >= 0) & (pair < PAIRS))
    def _():
        @pl.when(pair == 0)
        def _():
            outward[2].start()

        other = jnp.where(kind_ref[0] == 1, MASKED, 0.0)
        spot = lambda part: pl.ds(pl.multiple_of(part * D + pair * PAIR, 16), PAIR)
        for half in range(2):
            run_slot(pair, slots, first_head + half, PAIRS, 2)
            head = slice(half * HEAD_DIM, (half + 1) * HEAD_DIM)
            attn_head(
                other,
                qkv[spot(0), :][head],
                qkv[spot(1), :][head],
                qkv[spot(2), :][head],
                attended_out,
                head,
                lse_out.at[half],
            )
        attended[spot(0), :] = attended_out[...]

    region = step - groups - PAIRS
    run_slot(region, slots, first_region, regions)

    @pl.when(region >= 0)
    def _():
        @pl.when(region == 0)
        def _():
            swap_wait()
            outward[3].start()

        spot = pl.ds(pl.multiple_of(region * REGION, REGION), REGION)
        part = lambda k: mod_ref[k, pl.ds(region, 1), :]
        branch = dot_nn(jnp.transpose(attended[:, spot]), proj[...])
        middle = tokens[spot, :] + part(GATE_ATTN) * branch
        normal, _ = norm_parts(middle)
        hidden = (normal * (1.0 + part(SCALE_MLP)) + part(SHIFT_MLP)).astype(jnp.bfloat16)
        gated = (part(GATE_MLP) * grad[region].astype(jnp.float32)).astype(jnp.bfloat16)
        branch_out[...] = branch
        middle_out[...] = middle
        hidden_out[...] = hidden
        hidden_t_out[...] = jnp.transpose(hidden)
        gated_out[...] = gated
        gated_t_out[...] = jnp.transpose(gated)

    @pl.when(region == regions - 1)
    def _():
        finish()
        for copy in outward:
            copy.wait()


def forward(kind, kept, index, mask, tables, mod, weights, blocks, swap, collective_id):
    width = kept.shape[1]
    regions = mod.shape[1]
    count = regions * REGION
    groups = weights.shape[1] // BLOCK_COLS
    rows = 3 * D // groups
    shape = jax.ShapeDtypeStruct
    bf16, f32 = jnp.bfloat16, jnp.float32
    group = lambda s: jnp.minimum(s, groups - 1)
    pair = lambda s: jnp.clip(s - groups, 0, PAIRS - 1)
    region = lambda s: jnp.clip(s - groups - PAIRS, 0, regions - 1)
    token_rows = pl.BlockSpec((REGION, width), lambda s: (region(s), 0))
    token_cols = pl.BlockSpec((width, REGION), lambda s: (0, region(s)))
    hbm = pl.BlockSpec(memory_space=pl.ANY)
    whole = shape((8 * BLOCK_ROWS, 4 * BLOCK_COLS), bf16)
    return pl.pallas_call(
        forward_kernel,
        grid=(groups + PAIRS + regions,),
        in_specs=[
            pl.BlockSpec(memory_space=pltpu.SMEM),
            once(*kept.shape),
            once(*index.shape),
            once(1, width),
            once(*tables.shape),
            once(*mod.shape),
            pl.BlockSpec((width, BLOCK_COLS), lambda s: (0, group(s))),
            once(BLOCK_ROWS, BLOCK_COLS),
            once(BLOCK_ROWS, BLOCK_COLS),
            hbm,
        ],
        out_specs=[
            pl.BlockSpec((rows, count), lambda s: (group(s), 0)),
            pl.BlockSpec((PAIR, count), lambda s: (pair(s), 0)),
            pl.BlockSpec((2, 1, count), lambda s: (pair(s), 0, 0)),
            token_rows,
            token_rows,
            token_rows,
            token_cols,
            token_rows,
            token_cols,
        ]
        + [hbm] * 6,
        out_shape=[
            shape((3 * D, count), bf16),
            shape((D, count), bf16),
            shape((HEADS, 1, count), f32),
            shape((count, width), f32),
            shape((count, width), f32),
            shape((count, width), bf16),
            shape((width, count), bf16),
            shape((count, width), bf16),
            shape((width, count), bf16),
            shape((count, width), f32),
            shape((width, count), bf16),
            shape((width, width), bf16),
            shape(swap.shape, swap.dtype),
            whole,
            whole,
        ],
        scratch_shapes=[
            pltpu.VMEM((count, width), f32),
            pltpu.VMEM((count, width), bf16),
            pltpu.VMEM((width, count), bf16),
            pltpu.VMEM((3 * D, count), bf16),
            pltpu.VMEM((D, count), bf16),
            pltpu.VMEM((width, width), bf16),
            pltpu.VMEM(swap.shape, swap.dtype),
            pltpu.SemaphoreType.DMA((4,)),
        ]
        + gather_scratch(2)
        + swap_scratch(),
        compiler_params=pltpu.CompilerParams(
            collective_id=collective_id, has_side_effects=True, vmem_limit_bytes=VMEM_LIMIT
        ),
        name="forward",
    )(kind, kept, index, mask, tables, mod, weights, *blocks, swap)


def backward_kernel(
    kind_ref,
    q_ref,
    k_ref,
    v_ref,
    attended_ref,
    grad_ref,
    lse_ref,
    weight_ref,
    normed_t_ref,
    proj_ref,
    fc1_ref,
    fc2_ref,
    swap_ref,
    out_ref,
    fc1_sum,
    fc2_sum,
    hidden_hbm,
    swapped_hbm,
    grads,
    staged,
    grad_hidden,
    out_sem,
    *sems,
):
    step = pl.program_id(0)
    rows = grads.shape[0] // (pl.num_programs(0) - PAIRS)
    groups = grads.shape[0] // rows
    cols = BLOCK_COLS - rows
    place = Place()
    swap_start, swap_wait = swap_band(place, swap_ref, swapped_hbm, *sems[7:])
    order = [what[1:] for _, *what in BACKWARD_STEPS if what and not what[0]]
    begin, fold, combine, finish = scatter_actions(
        place, SCATTER_PLANS, order, [fc1_ref, fc2_ref], [fc1_sum, fc2_sum], *sems[:7]
    )
    slots = [[] for _ in range(HEADS + 2 * groups)]
    slots[0] += [functools.partial(greet, place, band=True), begin]
    folded = 0
    for when, *what in BACKWARD_STEPS:
        if not what:
            slots[when].append(swap_start)
        elif what[0]:
            slots[when].append(functools.partial(combine, *what[1:]))
        else:
            slots[when].append(functools.partial(fold, folded))
            folded += 1

    @pl.when(step < PAIRS)
    def _():
        other = jnp.where(kind_ref[0] == 1, MASKED, 0.0)
        for half in range(2):
            run_slot(step, slots, half, PAIRS, 2)
            head = slice(half * HEAD_DIM, (half + 1) * HEAD_DIM)
            attn_head_back(
                other,
                q_ref[head],
                k_ref[head],
                v_ref[head],
                attended_ref[head],
                grad_ref[head],
                lse_ref.at[half],
                staged,
                head,
            )
        for part in range(3):
            spot = pl.ds(pl.multiple_of(part * D + step * PAIR, 16), PAIR)
            grads[spot, :] = staged[part]

    group = step - PAIRS
    run_slot(group, slots, HEADS, groups, 2)

    @pl.when(group >= 0)
    def _():
        grad = grads[pl.ds(pl.multiple_of(group * rows, 16), rows), :]
        added = dot_nt(jnp.transpose(grad), weight_ref[:, :rows])

        @pl.when(group == 0)
        def _():
            grad_hidden[...] = added

        @pl.when(group > 0)
        def _():
            grad_hidden[...] += added

        run_slot(group, slots, HEADS + 1, groups, 2)
        out_ref[:, :rows] = dot_nt(normed_t_ref[...], grad).astype(jnp.bfloat16)
        for g in range(groups):

            @pl.when(group == g)
            def _():
                out_ref[:, rows:] = proj_ref[:, g * cols : (g + 1) * cols]

    @pl.when(group == groups - 1)
    def _():
        outward = pltpu.make_async_copy(grad_hidden, hidden_hbm, out_sem.at[0])
        outward.start()
        finish()
        swap_wait()
        outward.wait()


def backward(
    kind, qkv, attended, grad_attended, lse, weights, normed_t, grad_proj, grads, swap, collective_id
):
    width, count = normed_t.shape
    groups = weights.shape[1] // BLOCK_COLS
    shape = jax.ShapeDtypeStruct
    bf16, f32 = jnp.bfloat16, jnp.float32
    pair = lambda s: jnp.minimum(s, PAIRS - 1)
    group = lambda s: jnp.maximum(s - PAIRS, 0)
    heads = lambda part: pl.BlockSpec((PAIR, count), lambda s: (pair(s) + part * PAIRS, 0))
    hbm = pl.BlockSpec(memory_space=pl.ANY)
    block = shape((BLOCK_ROWS, BLOCK_COLS), bf16)
    return pl.pallas_call(
        backward_kernel,
        grid=(PAIRS + groups,),
        in_specs=[
            pl.BlockSpec(memory_space=pltpu.SMEM),
            heads(0),
            heads(1),
            heads(2),
            heads(0),
            heads(0),
            pl.BlockSpec((2, 1, count), lambda s: (pair(s), 0, 0)),
            pl.BlockSpec((width, BLOCK_COLS), lambda s: (0, group(s))),
            once(width, count),
            once(width, D),
            hbm,
            hbm,
            hbm,
        ],
        out_specs=[
            pl.BlockSpec((width, BLOCK_COLS), lambda s: (0, group(s))),
            fixed(BLOCK_ROWS, BLOCK_COLS),
            fixed(BLOCK_ROWS, BLOCK_COLS),
            hbm,
            hbm,
        ],
        out_shape=[
            shape(weights.shape, bf16),
            block,
            block,
            shape((count, width), f32),
            shape(swap.shape, swap.dtype),
        ],
        scratch_shapes=[
            pltpu.VMEM((3 * D, count), bf16),
            pltpu.VMEM((3, PAIR, count), bf16),
            pltpu.VMEM((count, width), f32),
            pltpu.SemaphoreType.DMA((1,)),
        ]
        + scatter_scratch(2)
        + swap_scratch(),
        compiler_params=pltpu.CompilerParams(
            collective_id=collective_id, has_side_effects=True, vmem_limit_bytes=VMEM_LIMIT
        ),
        name="backward",
    )(kind, qkv, qkv, qkv, attended, grad_attended, lse, weights, normed_t, grad_proj, *grads, swap)


def column_sum(values):
    return jnp.sum(values, axis=0, keepdims=True)


def mlp_kernel(
    h_ref,
    ht_ref,
    g_ref,
    gt_ref,
    up_ref,
    down_ref,
    middle_ref,
    branch_ref,
    grad_ref,
    attended_ref,
    proj_ref,
    mod_ref,
    gup_ref,
    gdown_ref,
    block_ref,
    grad_middle_ref,
    grad_proj_ref,
    grad_attended_ref,
    sums_ref,
    output_ref,
    grad_hidden_ref,
    total_ref,
):
    step = pl.program_id(0)
    regions = mod_ref.shape[1]
    region = step - (pl.num_programs(0) - regions)

    @pl.when(step == 0)
    def _():
        output_ref[...] = jnp.zeros_like(output_ref)
        grad_hidden_ref[...] = jnp.zeros_like(grad_hidden_ref)

    @pl.when(region < 0)
    def _():
        mlp_tile(
            h_ref, ht_ref, g_ref, gt_ref, up_ref, down_ref, output_ref, grad_hidden_ref, gup_ref, gdown_ref
        )

    @pl.when(region >= 0)
    def _():
        spot = pl.ds(pl.multiple_of(region * REGION, REGION), REGION)
        part = lambda k: mod_ref[k, pl.ds(region, 1), :]
        output = output_ref[spot, :]
        grad_hidden = grad_hidden_ref[spot, :]
        middle = middle_ref[...]
        grad = grad_ref[...].astype(jnp.float32)
        block_ref[...] = (middle + part(GATE_MLP) * output).astype(jnp.bfloat16)
        normal, root = norm_parts(middle)
        grad_middle = grad + norm_back(grad_hidden, normal, root, part(SCALE_MLP))
        grad_middle_ref[...] = grad_middle
        sums_ref[0, 0:1] = column_sum(grad_middle * branch_ref[...])
        sums_ref[0, 1:2] = column_sum(grad_hidden)
        sums_ref[0, 2:3] = column_sum(grad_hidden * normal)
        sums_ref[0, 3:4] = column_sum(grad * output)
        grad_branch = (part(GATE_ATTN) * grad_middle).astype(jnp.bfloat16)
        grad_attended_ref[...] = dot_nt(proj_ref[...], grad_branch).astype(jnp.bfloat16)
        added = dot_nn(attended_ref[...], grad_branch)

        @pl.when(region == 0)
        def _():
            total_ref[...] = added

        @pl.when(region > 0)
        def _():
            total_ref[...] += added

        @pl.when(region == regions - 1)
        def _():
            grad_proj_ref[...] = total_ref[...].astype(jnp.bfloat16)


def mlp_both(hidden, hidden_t, gated, gated_t, up, down_t, middle, branch, grad, attended_t, proj, mod):
    count, width = hidden.shape
    wide = up.shape[1]
    tile = 512
    tiles = wide // tile
    regions = count // REGION
    region = lambda s: jnp.maximum(s - tiles, 0)
    rows = pl.BlockSpec((REGION, width), lambda s: (region(s), 0))
    columns = pl.BlockSpec((width, REGION), lambda s: (0, region(s)))
    part = pl.BlockSpec((width, tile), lambda s: (0, jnp.minimum(s, tiles - 1)))
    shape = jax.ShapeDtypeStruct
    bf16, f32 = jnp.bfloat16, jnp.float32
    return pl.pallas_call(
        mlp_kernel,
        grid=(tiles + regions,),
        in_specs=[
            once(count, width),
            once(width, count),
            once(count, width),
            once(width, count),
            part,
            part,
            rows,
            rows,
            rows,
            columns,
            once(width, width),
            once(*mod.shape),
        ],
        out_specs=[
            part,
            part,
            rows,
            rows,
            once(width, width),
            columns,
            pl.BlockSpec((1, 4, width), lambda s: (region(s), 0, 0)),
        ],
        out_shape=[
            shape((width, wide), bf16),
            shape((width, wide), bf16),
            shape((count, width), bf16),
            shape((count, width), f32),
            shape((width, width), bf16),
            shape((width, count), bf16),
            shape((regions, 4, width), f32),
        ],
        scratch_shapes=[
            pltpu.VMEM((count, width), f32),
            pltpu.VMEM((count, width), f32),
            pltpu.VMEM((width, width), f32),
        ],
        compiler_params=pltpu.CompilerParams(vmem_limit_bytes=VMEM_LIMIT),
        name="mlp_both",
    )(hidden, hidden_t, gated, gated_t, up, down_t, middle, branch, grad, attended_t, proj, mod)


def swap_columns(shard):
    pairs = [(d, d ^ 1) for d in range(lax.axis_size("dp"))]
    odd = lax.axis_index("dp") % 2
    rows = shard.shape[0] // 2
    own = lax.dynamic_slice_in_dim(shard, odd * rows, rows, axis=0)
    other = lax.dynamic_slice_in_dim(shard, (1 - odd) * rows, rows, axis=0)
    other = lax.ppermute(other, "dp", pairs)
    return jnp.where(odd == 0, jnp.stack([own, other], 1), jnp.stack([other, own], 1))


def norm_parts(values):
    center = jnp.mean(values, axis=-1, keepdims=True)
    spread = jnp.mean((values - center) ** 2, axis=-1, keepdims=True)
    root = lax.rsqrt(spread + 1e-06)
    return ((values - center) * root, root)


def norm_back(grad, normal, root, scales):
    inner = grad * (1.0 + scales)
    return root * (
        inner
        - jnp.mean(inner, axis=-1, keepdims=True)
        - normal * jnp.mean(inner * normal, axis=-1, keepdims=True)
    )


def embed_tables(count):
    quarter = D // 4
    omegas = 1.0 / 10000.0 ** (jnp.arange(quarter, dtype=jnp.float32) / quarter)
    angles = jnp.arange(count, dtype=jnp.float32)[:, None] * omegas
    return jnp.concatenate([jnp.sin(angles), jnp.cos(angles)], axis=-1)


def slot_device(
    kept_tokens,
    kept_index,
    resolution,
    labels,
    timesteps,
    class_table,
    cotangent,
    mask_token,
    w_qkv,
    w_proj,
    w_fc1,
    w_fc2,
    w_ada,
    mask_first,
    first_qkv,
    first_proj,
    first_fc1,
    first_fc2,
    first_ada,
    mask_second,
    second_qkv,
    second_proj,
    second_fc1,
    second_fc2,
    second_ada,
):
    highest = lax.Precision.HIGHEST
    bf16 = jnp.bfloat16
    bands = lax.axis_size("band")
    groups = lax.axis_size("dp")
    band = lax.axis_index("band")
    slots, local_rows, _ = cotangent.shape
    tokens_count = bands * local_rows
    regions = tokens_count // REGION
    images = labels.shape[1]

    qkv_cols, proj_cols, fc1_cols = w_qkv.shape[1], w_proj.shape[1], w_fc1.shape[1]
    swapped = swap_columns(jnp.concatenate([w_qkv, w_proj, w_fc1], axis=1).astype(bf16))
    joined_block = jnp.concatenate(
        [
            swapped[:, :, :qkv_cols].reshape(-1, 2 * qkv_cols),
            swapped[:, :, qkv_cols:-fc1_cols].reshape(-1, 2 * proj_cols),
        ],
        axis=1,
    )
    fc1_block = swapped[:, :, -fc1_cols:].reshape(-1, 2 * fc1_cols)
    fc2_block = w_fc2.astype(bf16).T

    rows_ada, cols_ada = w_ada.shape
    table_part = lax.dynamic_slice_in_dim(class_table, band * rows_ada, rows_ada, axis=1)
    chosen = labels.reshape(-1, 1) == jnp.arange(class_table.shape[0])[None, :]
    features = band * rows_ada + jnp.arange(rows_ada)
    half_width = D // 2
    frequency = jnp.exp(
        -math.log(10000.0) * (features % half_width).astype(jnp.float32) / half_width
    )
    angles = timesteps.reshape(-1, 1).astype(jnp.float32) * frequency
    waves = jnp.where(features < half_width, jnp.cos(angles), jnp.sin(angles))
    condition = jnp.matmul(chosen.astype(jnp.float32), table_part, precision=highest) + waves
    cond = jax.nn.silu(condition).astype(bf16).astype(jnp.float32)
    cond = jnp.pad(cond.reshape(slots, images, rows_ada), ((0, 0), (0, 8 - images), (0, 0)))

    kind = lax.dynamic_slice_in_dim(resolution, band, 1)
    joined_full, modulation, conds, kept, index = head(
        joined_block, cond, w_ada.astype(bf16), kept_tokens, kept_index[:, None, :], 0
    )
    kept = kept.reshape(-1, D)
    index = index.reshape(1, -1)
    modulation = modulation.transpose(1, 0, 2).reshape(images, 6, D).transpose(1, 0, 2)
    mod = jnp.where(kind[0] == 1, modulation, modulation[:, :1])
    table = embed_tables(SIDE)
    blank = jnp.zeros_like(table)
    tables = jnp.stack(
        [jnp.concatenate([table, blank], axis=1), jnp.concatenate([blank, table], axis=1)]
    )
    (
        qkv,
        attended_t,
        lse,
        branch,
        middle,
        hidden_mlp,
        hidden_mlp_t,
        grad_output,
        grad_output_t,
        tokens,
        normed_t,
        proj_full,
        grad_out,
        fc1_full,
        fc2_full,
    ) = forward(
        kind,
        kept,
        index,
        mask_token[None],
        tables,
        mod,
        joined_full,
        [fc1_block, fc2_block],
        cotangent,
        1,
    )
    grad_out = grad_out.reshape(tokens_count, D)
    grad_fc1, grad_fc2, block_slot, grad_middle, grad_proj, grad_attended, sums_mlp = mlp_both(
        hidden_mlp,
        hidden_mlp_t,
        grad_output,
        grad_output_t,
        fc1_full,
        fc2_full,
        middle,
        branch,
        grad_out,
        attended_t,
        proj_full,
        mod,
    )
    grad_joined, sum_fc1, sum_fc2, grad_hidden, block_out = backward(
        kind,
        qkv,
        attended_t,
        grad_attended,
        lse,
        joined_full,
        normed_t,
        grad_proj,
        [grad_fc1, grad_fc2],
        block_slot.reshape(bands, local_rows, D),
        2,
    )
    sum_joined, other_joined, other_fc1, red_ada, grad_mask, squares, grad_kept = tail(
        grad_joined,
        kind,
        sum_fc1,
        sum_fc2,
        index,
        mod,
        sums_mlp,
        conds,
        tokens,
        grad_middle,
        grad_hidden,
        bands,
        3,
    )
    odd = (lax.axis_index("dp") % 2).astype(jnp.int32)
    new, norm_value, kept_grad, block_out = finish_all(
        odd[None],
        squares,
        grad_mask,
        grad_kept,
        block_out,
        [sum_joined, other_joined, sum_fc1, other_fc1, sum_fc2, red_ada],
        [
            w_qkv, w_proj, w_fc1, w_fc2, w_ada, mask_token[None],
            first_qkv, first_proj, first_fc1, first_fc2, first_ada, mask_first[None],
            second_qkv, second_proj, second_fc1, second_fc2, second_ada, mask_second[None],
        ],
    )
    return (
        (block_out, kept_grad, norm_value[0, 0])
        + (new[5][0], *new[:5])
        + (new[11][0], *new[6:11])
        + (new[17][0], *new[12:17])
    )


def per_device(*arguments):
    cotangent = arguments[6]
    if (lax.axis_size("dp"), lax.axis_size("band")) == (8, cotangent.shape[0]):
        return slot_device(*arguments)
    return general_device(*arguments)


def solution(mesh):
    in_specs = (
        P("dp", "band", None),
        P("dp", "band"),
        P("dp"),
        P("dp", None),
        P("dp", None),
        P(),
        P("dp", "band", None),
        P(),
        P("band", "dp"),
        P("band", "dp"),
        P("band", "dp"),
        P("band", "dp"),
        P("band", "dp"),
        P(),
        P("band", "dp"),
        P("band", "dp"),
        P("band", "dp"),
        P("band", "dp"),
        P("band", "dp"),
        P(),
        P("band", "dp"),
        P("band", "dp"),
        P("band", "dp"),
        P("band", "dp"),
        P("band", "dp"),
    )
    out_specs = (
        P("dp", "band", None),
        P("dp", "band", None),
        P(),
        P(),
        P("band", "dp"),
        P("band", "dp"),
        P("band", "dp"),
        P("band", "dp"),
        P("band", "dp"),
        P(),
        P("band", "dp"),
        P("band", "dp"),
        P("band", "dp"),
        P("band", "dp"),
        P("band", "dp"),
        P(),
        P("band", "dp"),
        P("band", "dp"),
        P("band", "dp"),
        P("band", "dp"),
        P("band", "dp"),
    )
    return jax.shard_map(
        per_device, mesh=mesh, in_specs=in_specs, out_specs=out_specs, check_vma=False
    )
```
